32 devices in a mesh: req: 8 (over z, y), head: 4 (over x, core).
Axes of the slice: x: 2, y: 2, z: 4, core: 2. Of those that a mesh axis runs over, the one named last changes fastest.
Arguments:
- hidden_in: bfloat16 [16, 2048], P(None, 'head'), may hold values from -1.5 to 1.5
- attention_gain: float32 [2048], replicated, may hold values from 0.1 to 1.9
- query_gain: float32 [64], replicated, may hold values from 0.5 to 2
- key_gain: float32 [64], replicated, may hold values from 1.5 to 4
- feedforward_gain: float32 [2048], replicated, may hold values from 0.1 to 1.9
- input_weight: bfloat16 [2048, 1920], P('req', 'head'), may hold values from -0.125 to 0.125
- output_weight: bfloat16 [1280, 2048], P('req', 'head'), may hold values from -0.15625 to 0.15625
- gate_weight: bfloat16 [2048, 5120], P('req', 'head'), may hold values from -0.125 to 0.125
- up_weight: bfloat16 [2048, 5120], P('req', 'head'), may hold values from -0.125 to 0.125
- down_weight: bfloat16 [5120, 2048], P('req', 'head'), may hold values from -0.078125 to 0.078125
- old_cache: bfloat16 [256, 128, 640], P(('req', 'head')), may hold values from -400 to 400
- keep_rows: int32 [256, 64], P(('req', 'head')), may hold values from -1 to 127, as said below
- drop_weights: float32 [256, 128], P(('req', 'head')), may hold values from 0.1 to 1
- dest_slots: int32 [32, 8], P(('req', 'head')), may hold values from 0 to 7, each once within a row
- lengths: int32 [16], replicated, may hold values from 1 to 16, 128 in all
- page_table: int32 [16, 16], P('req'), may hold values from 0 to 7, as said below
- source: int32 [8], replicated, may hold values from 0 to 7, each once
Outputs:
- compact_cache: bfloat16 [128, 128, 640], P(('req', 'head'))
- summary_rows: bfloat16 [256, 640], P(('req', 'head'))
- hidden_out: bfloat16 [16, 2048], P(None, 'head')
The draws below stay inside these ranges and needn't reach their ends.
Inputs may be any that keep to these rules, and one draw needn't show every extreme that they name: `keep_rows`: row p lists kept rows of page p in ascending order, from 32 to 64 of them, then -1 to the end; some page keeps 64. `page_table`: row g * 2 + k belongs to the k-th request held by index g of req; entry j is the slot, on the device with req index g and head index j % 4, of that request's j-th page. On every device the entries that point to it form a permutation of its 8 slots. `source`: A permutation of the continued requests over the held slots. `dest_slots`: each row is a permutation. `lengths`: they sum to 128 and the largest is 16.
All inputs are finite; a program needn't handle non-finite values.
Results may differ from the reference program's by a relative error of at most 0.015.
The reference program's roundings to bfloat16 on the way count: a program that leaves them out, or rounds other values in their place, can miss the bound.
Values may be sent and summed in bfloat16 or wider, within the bound.
No kernel may reach another device: no remote copies, remote signals or barrier semaphores. Data moves between devices by JAX's collectives and lax.ppermute only.
A program may use at most 64 MiB of HBM per device.

```python
import math
import jax
import jax.numpy as jnp
import numpy as np
from jax import lax

D = 2048
HEADS = 20
KVH = 5
HD = 64
FF = 5120
PAGE = 128
KEEP = 64
NP = 16
R_DEV = 2
REQS = 16
CONT = 8
PG_DEV = 8
PAGES = 256
KVW = 640
QKVW = 1920
N_REQ = 8
N_HEAD = 4


def draw_old_cache(key, part):
    first = jax.random.fold_in(key, 0)
    values = jnp.clip(jax.random.normal(first, (PAGES, PAGE, KVW), jnp.float32), -6.0, 6.0)
    return values.astype(jnp.bfloat16)


def draw_keep_rows(key, part):
    first, second, third = jax.random.split(key, 3)
    rows = jnp.arange(PAGE, dtype=jnp.int32)
    scores = jax.random.randint(first, (PAGES, PAGE), 0, 1 << 20, dtype=jnp.int32) * PAGE + rows[None, :]
    order = jnp.argsort(scores, axis=1).astype(jnp.int32)
    counts = jax.random.randint(second, (PAGES,), PAGE // 4, KEEP + 1, dtype=jnp.int32)
    forced = jax.random.randint(third, (PAGES,), 0, 4, dtype=jnp.int32) == 0
    counts = jnp.where(forced, KEEP, counts)
    chosen = order[:, :KEEP]
    slots = jnp.arange(KEEP, dtype=jnp.int32)
    marked = jnp.where(slots[None, :] < counts[:, None], chosen, 2 * PAGE)
    ordered = jnp.sort(marked, axis=1)
    return jnp.where(ordered >= PAGE, -1, ordered).astype(jnp.int32)


def draw_page_table(key, part):
    groups = REQS // R_DEV
    per_device = R_DEV * NP // N_HEAD
    device_keys = jax.random.split(key, groups * N_HEAD)
    shuffled = jax.vmap(lambda single: jax.random.permutation(single, per_device))(device_keys)
    table = shuffled.reshape(groups, N_HEAD, R_DEV, NP // N_HEAD)
    return jnp.transpose(table, (0, 2, 3, 1)).reshape(REQS, NP).astype(jnp.int32)


def shard_levels(rng, extent, shards, low, largest):
    def one(axis_at, shards_of):
        heights = jax.random.uniform(jax.random.fold_in(jax.random.fold_in(rng, 6), axis_at), (shards_of,), jnp.float32, low / len(shards), largest / len(shards))
        return jnp.repeat(jnp.exp(heights), extent[axis_at] // shards_of).reshape((-1,) + (1,) * (len(extent) - axis_at - 1))

    level = one(*shards[0])
    for cut in shards[1:]:
        level = level * one(*cut)
    return level


def length_profile(number_of, total, bound, slope):
    loads = [(1 << 20) // math.isqrt(standing ** slope) + 1 for standing in range(2, number_of + 1)]
    spare, given = total - bound - (number_of - 1), [1] * (number_of - 1)
    while spare > 0:
        free = [i for i in range(number_of - 1) if given[i] < bound]
        whole, left = sum([loads[i] for i in free]), spare
        for i in free:
            more = min(bound - given[i], max(1, left * loads[i] // whole), spare)
            given[i] = given[i] + more
            spare = spare - more
    return np.array([bound] + given)


def uneven(stream_key, amount, total, limit, skew):
    if amount == 2:
        one = jax.random.randint(stream_key, (), max(1, total - limit), min(limit, total - 1) + 1)
        return jnp.stack([one, total - one])
    tallies = jnp.asarray(length_profile(amount, total, limit, skew), jnp.int32)
    couples = (amount - 1) // 2
    donor, sink = tallies[1:1 + 2 * couples:2], tallies[2:2 + 2 * couples:2]
    slack = jnp.minimum(donor - 1, limit - sink)
    shifted = jax.random.randint(jax.random.fold_in(stream_key, 1), (couples,), 0, 1 << 20) % (slack + 1)
    tallies = tallies.at[1:1 + 2 * couples:2].set(donor - shifted).at[2:2 + 2 * couples:2].set(sink + shifted)
    return tallies[jax.random.permutation(jax.random.fold_in(stream_key, 2), amount)]


def normal_values(rng, dims, scale, reach, cuts=(), kind=jnp.bfloat16):
    values = jax.random.normal(rng, dims, jnp.float32) * scale
    if len(cuts) > 0:
        values = shard_levels(rng, dims, cuts, -0.22, 0.18) * values
    return jnp.clip(values, min=-reach, max=reach).astype(kind)


def setup_inputs(seed: int = 0) -> dict:
    key_list = jax.random.split(jax.random.key(seed), 18)
    return {
        "hidden_in": normal_values(key_list[0], (REQS, D), 0.1, 1.5, ((1, 4),)),
        "attention_gain": jnp.clip(1.0 + 0.18 * jax.random.normal(key_list[1], (D,), jnp.float32), 0.1, 1.9),
        "query_gain": jnp.clip(jax.random.uniform(key_list[2], (HD,), jnp.float32, 0.5, 2.0), 0.5, 2.0),
        "key_gain": jnp.clip(jax.random.uniform(key_list[3], (HD,), jnp.float32, 1.5, 4.0), 1.5, 4.0),
        "feedforward_gain": jnp.clip(1.0 + 0.18 * jax.random.normal(key_list[4], (D,), jnp.float32), 0.1, 1.9),
        "input_weight": normal_values(key_list[5], (D, QKVW), D ** -0.5, 0.125, ((0, 8), (1, 4))),
        "output_weight": normal_values(key_list[6], (HEADS * HD, D), (HEADS * HD) ** -0.5, 0.15625, ((0, 8), (1, 4))),
        "gate_weight": normal_values(key_list[7], (D, FF), D ** -0.5, 0.125, ((0, 8), (1, 4))),
        "up_weight": normal_values(key_list[8], (D, FF), D ** -0.5, 0.125, ((0, 8), (1, 4))),
        "down_weight": normal_values(key_list[9], (FF, D), FF ** -0.5, 0.078125, ((0, 8), (1, 4))),
        "old_cache": draw_old_cache(jax.random.fold_in(key_list[17], 71), 0),
        "keep_rows": draw_keep_rows(jax.random.fold_in(key_list[17], 71), 0),
        "drop_weights": jnp.clip(jnp.exp(math.log(1.0) - 2.3025851 * jax.random.uniform(key_list[12], (PAGES, PAGE), jnp.float32) ** shard_levels(key_list[12], (PAGES, PAGE), ((0, 32),), -0.2, 0.2)), 0.1, 1.0),
        "dest_slots": jax.vmap(lambda own: jax.random.permutation(own, PG_DEV))(jax.random.split(key_list[13], (N_REQ * N_HEAD))).reshape((N_REQ * N_HEAD, PG_DEV)).astype(jnp.int32),
        "lengths": uneven(key_list[14], REQS, REQS * NP // 2, NP, 1).astype(jnp.int32),
        "page_table": draw_page_table(jax.random.fold_in(key_list[17], 71), 0),
        "source": jax.random.permutation(key_list[16], CONT).astype(jnp.int32),
    }


epsilon = 1e-06
negative = -1e+30

def rms_rows(values, gain):
    mean_square = lax.optimization_barrier(jnp.mean(values * values, axis=-1, keepdims=True))
    return values * lax.rsqrt(mean_square + epsilon) * gain

def rotate(vectors, positions):
    half = vectors.shape[-1] // 2
    frequency = 10000.0 ** (-jnp.arange(half, dtype=jnp.float32) / half)
    angles = positions.astype(jnp.float32)[:, None] * frequency[None, :]
    cosine = jnp.cos(angles)[:, None, :]
    sine = jnp.sin(angles)[:, None, :]
    first = vectors[..., :half]
    second = vectors[..., half:]
    return jnp.concatenate([first * cosine - second * sine, second * cosine + first * sine], axis=-1)

def compact_block(block):
    pages, keep, weights = block
    rows = jnp.arange(pages.shape[1], dtype=jnp.int32)
    picks = (keep[:, :, None] == rows[None, None, :]).astype(jnp.float32)
    wide = pages.astype(jnp.float32)
    kept = jnp.einsum('pkr,prc->pkc', picks, wide, precision=lax.Precision.HIGHEST).astype(jnp.bfloat16)
    dropped = weights * (1.0 - lax.optimization_barrier(jnp.sum(picks, axis=1)))
    total = lax.optimization_barrier(jnp.sum(dropped, axis=1))
    means = jnp.einsum('pr,prc->pc', dropped, wide, precision=lax.Precision.HIGHEST) / total[:, None]
    return (kept, means.astype(jnp.bfloat16), jnp.log(total))

def reference(hidden_in, attention_gain, query_gain, key_gain, feedforward_gain, input_weight, output_weight, gate_weight, up_weight, down_weight, old_cache, keep_rows, drop_weights, dest_slots, lengths, page_table, source):
    devices = N_REQ * N_HEAD
    half = R_DEV // 2
    split = KVH * HD
    ratio = HEADS // KVH
    scale = HD ** (-0.5)
    blocks = (old_cache.reshape(devices, PG_DEV, PAGE, KVW), keep_rows.reshape(devices, PG_DEV, KEEP), drop_weights.reshape(devices, PG_DEV, PAGE))
    kept, means, bias = lax.map(compact_block, blocks)
    slot_ids = jnp.arange(PG_DEV, dtype=jnp.int32)
    inverse = lax.optimization_barrier(jnp.sum(jnp.where(dest_slots[:, None, :] == slot_ids[None, :, None], slot_ids[None, None, :], 0), axis=2)).astype(jnp.int32)
    fresh = jnp.take_along_axis(kept, inverse[:, :, None, None], axis=1)
    compact_cache = fresh.reshape(PAGES // 2, PAGE, KVW)
    summary_rows = jnp.take_along_axis(means, inverse[:, :, None], axis=1).reshape(PAGES, KVW)
    kept_flat = kept.reshape(PAGES, KEEP, KVW)
    means_flat = means.reshape(PAGES, KVW)
    bias_flat = bias.reshape(PAGES)
    normed = rms_rows(hidden_in.astype(jnp.float32), attention_gain).astype(jnp.bfloat16)
    qkv = jnp.dot(normed, input_weight, preferred_element_type=jnp.float32).astype(jnp.bfloat16)
    qkv = lax.optimization_barrier(qkv).astype(jnp.float32)
    positions = lengths * PAGE
    query = rotate(rms_rows(qkv[:, :HEADS * HD].reshape(REQS, HEADS, HD), query_gain), positions).astype(jnp.bfloat16)
    key_new = rotate(rms_rows(qkv[:, HEADS * HD:(HEADS + KVH) * HD].reshape(REQS, KVH, HD), key_gain), positions).astype(jnp.bfloat16)
    value_new = qkv[:, (HEADS + KVH) * HD:].reshape(REQS, KVH, HD)
    rows_all = jnp.arange(REQS, dtype=jnp.int32)
    inverse_source = jnp.zeros((CONT,), jnp.int32).at[source].set(jnp.arange(CONT, dtype=jnp.int32))
    position = rows_all % R_DEV
    slot = rows_all // R_DEV * half + position - half
    owner = inverse_source[jnp.clip(slot, 0, CONT - 1)]
    held_to_req = jnp.where(position < half, rows_all, owner // half * R_DEV + half + owner % half).astype(jnp.int32)

    def attend(row):
        group = row // R_DEV
        request = held_to_req[row]
        logical = jnp.arange(NP, dtype=jnp.int32)
        ids = ((group * N_HEAD + logical % N_HEAD) * PG_DEV + page_table[row]).astype(jnp.int32)
        live = logical < lengths[request]
        entries = kept_flat[ids].astype(jnp.float32)
        row_live = (keep_rows[ids] >= 0) & live[:, None]
        summary = means_flat[ids].astype(jnp.float32)
        query_here = query[request].astype(jnp.float32).reshape(KVH, ratio, HD)
        key_here = key_new[request].astype(jnp.float32)
        value_here = value_new[request]
        row_keys = entries[:, :, :split].reshape(NP, KEEP, KVH, HD)
        row_values = entries[:, :, split:].reshape(NP, KEEP, KVH, HD)
        row_scores = jnp.einsum('ngd,jmnd->ngjm', query_here, row_keys, precision=lax.Precision.HIGHEST) * scale
        row_scores = jnp.where(row_live[None, None], row_scores, negative)
        mean_scores = jnp.einsum('ngd,jnd->ngj', query_here, summary[:, :split].reshape(NP, KVH, HD), precision=lax.Precision.HIGHEST) * scale + bias_flat[ids][None, None, :]
        mean_scores = jnp.where(live[None, None], mean_scores, negative)
        own_score = jnp.einsum('ngd,nd->ng', query_here, key_here, precision=lax.Precision.HIGHEST) * scale
        top = jnp.maximum(jnp.maximum(lax.optimization_barrier(jnp.max(row_scores, axis=(2, 3))), lax.optimization_barrier(jnp.max(mean_scores, axis=2))), own_score)
        row_weight = jnp.where(row_live[None, None], jnp.exp(row_scores - top[:, :, None, None]), 0.0)
        mean_weight = jnp.where(live[None, None], jnp.exp(mean_scores - top[:, :, None]), 0.0)
        own_weight = jnp.exp(own_score - top)
        mass = lax.optimization_barrier(jnp.sum(row_weight, axis=(2, 3))) + lax.optimization_barrier(jnp.sum(mean_weight, axis=2)) + own_weight
        total = jnp.einsum('ngjm,jmnd->ngd', row_weight, row_values, precision=lax.Precision.HIGHEST)
        total = total + jnp.einsum('ngj,jnd->ngd', mean_weight, summary[:, split:].reshape(NP, KVH, HD), precision=lax.Precision.HIGHEST)
        total = total + own_weight[:, :, None] * value_here[:, None, :]
        return (total / mass[:, :, None]).reshape(HEADS * HD).astype(jnp.bfloat16)
    attention_held = lax.map(attend, rows_all)
    attention = jnp.zeros((REQS, HEADS * HD), jnp.bfloat16).at[held_to_req].set(attention_held)
    projected = jnp.dot(attention, output_weight, preferred_element_type=jnp.float32)
    mid = (hidden_in.astype(jnp.float32) + projected).astype(jnp.bfloat16)
    mid = lax.optimization_barrier(mid).astype(jnp.float32)
    normed_mid = rms_rows(mid, feedforward_gain).astype(jnp.bfloat16)
    gate = jnp.dot(normed_mid, gate_weight, preferred_element_type=jnp.float32)
    upper = jnp.dot(normed_mid, up_weight, preferred_element_type=jnp.float32)
    active = (jax.nn.silu(gate) * upper).astype(jnp.bfloat16)
    hidden_out = (mid + jnp.dot(active, down_weight, preferred_element_type=jnp.float32)).astype(jnp.bfloat16)
    return (compact_cache, summary_rows, hidden_out)
```

```python
import jax
import jax.numpy as jnp
from jax import lax
from jax.sharding import PartitionSpec as P

D = 2048
HEADS = 20
KVH = 5
HD = 64
FF = 5120
PAGE = 128
KEEP = 64
NP = 16
R_DEV = 2
KVW = 640

DIRECT = 8

epsilon = 1e-06
negative = -1e30
both_axes = ("req", "head")


def rms_scale(values):
    return lax.rsqrt(jnp.mean(values * values, axis=-1, keepdims=True) + epsilon)


def rms_rows(values, gain):
    return values * rms_scale(values) * gain


def rotate(vectors, positions):
    half = vectors.shape[-1] // 2
    frequency = 10000.0 ** (-jnp.arange(half, dtype=jnp.float32) / half)
    angles = positions.astype(jnp.float32)[:, None] * frequency[None, :]
    cosine = jnp.cos(angles)[:, None, :]
    sine = jnp.sin(angles)[:, None, :]
    first = vectors[..., :half]
    second = vectors[..., half:]
    return jnp.concatenate(
        [first * cosine - second * sine, second * cosine + first * sine], axis=-1
    )


def compact_pages(pages, keep, weights):
    rows = jnp.arange(pages.shape[1], dtype=jnp.int32)
    picks = keep[:, :, None] == rows[None, None, :]
    kept = jnp.einsum(
        "pkr,prc->pkc", picks.astype(jnp.bfloat16), pages, preferred_element_type=jnp.float32
    ).astype(jnp.bfloat16)
    dropped = weights * (1.0 - jnp.sum(picks.astype(jnp.float32), axis=1))
    total = jnp.sum(dropped, axis=1)
    means = (
        jnp.einsum(
            "pr,prc->pc", dropped, pages.astype(jnp.float32), precision=lax.Precision.HIGHEST
        )
        / total[:, None]
    )
    return (kept, means.astype(jnp.bfloat16), jnp.log(total))


def held_request(rows, source):
    half = R_DEV // 2
    position = rows % R_DEV
    slot = rows // R_DEV * half + position - half
    continued = jnp.arange(source.shape[0], dtype=jnp.int32)
    matches = source[None, :] == slot[:, None]
    owner_cont = jnp.sum(jnp.where(matches, continued[None, :], 0), axis=1)
    carried = owner_cont // half * R_DEV + half + owner_cont % half
    return jnp.where(position < half, rows, carried)


def pick_rows(order, rows):
    chosen = order[:, None] == jnp.arange(rows.shape[0], dtype=jnp.int32)[None, :]
    return jnp.dot(
        chosen.astype(jnp.bfloat16), rows, preferred_element_type=jnp.float32
    ).astype(jnp.bfloat16)


def block_pieces(partial):
    groups = lax.axis_size("req")
    lanes = lax.axis_size("head")
    per_lane = groups // lanes
    group = lax.axis_index("req")
    width = partial.shape[-1] // per_lane
    if groups > DIRECT:
        whole = lax.all_gather(lax.psum(partial, "req"), "head", axis=1, tiled=True)
        return [lax.dynamic_slice_in_dim(whole, group * width, width, 1)]
    pieces = []
    for turn in range(groups):
        pairs = []
        for g in range(groups):
            for h in range(lanes):
                m = g ^ turn
                pairs.append((g * lanes + h, (per_lane * h + m % per_lane) * lanes + m // per_lane))
        part = (group ^ turn) % per_lane
        block = lax.dynamic_slice_in_dim(partial, part * width, width, 1)
        pieces.append(lax.ppermute(block, both_axes, pairs))
    return pieces


def whole_sum(partial):
    if lax.axis_size("req") > DIRECT:
        return lax.psum(partial, "req")
    return jnp.sum(lax.all_gather(partial, "req"), axis=0)


def on_device(
    hidden_in,
    attention_gain,
    query_gain,
    key_gain,
    feedforward_gain,
    input_weight,
    output_weight,
    gate_weight,
    up_weight,
    down_weight,
    old_cache,
    keep_rows,
    drop_weights,
    dest_slots,
    lengths,
    page_table,
    source,
):
    groups = lax.axis_size("req")
    lanes = lax.axis_size("head")
    group = lax.axis_index("req")
    lane = lax.axis_index("head")
    requests = hidden_in.shape[0]
    half = R_DEV // 2
    split = KVH * HD
    ratio = HEADS // KVH
    scale = HD ** (-0.5)
    pages_here = old_cache.shape[0]
    everyone = jnp.arange(requests, dtype=jnp.int32)
    holders = held_request(everyone, source)
    held = lax.dynamic_slice_in_dim(holders, group * R_DEV, R_DEV, 0)
    held_len = lengths[held]
    positions = held_len * PAGE

    whole = lax.all_gather(hidden_in, "head", axis=1, tiled=True)
    normed = rms_rows(whole.astype(jnp.float32), attention_gain).astype(jnp.bfloat16)
    features = D // groups
    inputs = pick_rows(holders, lax.dynamic_slice_in_dim(normed, group * features, features, 1))
    partial_qkv = jnp.dot(inputs, input_weight, preferred_element_type=jnp.float32)
    sent = jnp.broadcast_to(
        partial_qkv.reshape(groups, 1, R_DEV, -1), (groups, lanes, R_DEV, partial_qkv.shape[1])
    ).reshape(groups * lanes, R_DEV, -1)
    got = lax.all_to_all(sent, both_axes, split_axis=0, concat_axis=0, tiled=True)
    mixed = jnp.sum(got.reshape(groups, lanes, R_DEV, -1), axis=0).astype(jnp.bfloat16)
    held_qkv = jnp.swapaxes(mixed, 0, 1).reshape(R_DEV, -1).astype(jnp.float32)

    query = rotate(
        rms_rows(held_qkv[:, : HEADS * HD].reshape(R_DEV, HEADS, HD), query_gain), positions
    ).astype(jnp.bfloat16)
    key_new = rotate(
        rms_rows(held_qkv[:, HEADS * HD : (HEADS + KVH) * HD].reshape(R_DEV, KVH, HD), key_gain),
        positions,
    ).astype(jnp.bfloat16)
    value_new = held_qkv[:, (HEADS + KVH) * HD :].reshape(R_DEV, KVH, HD)
    kept, means, bias = compact_pages(old_cache, keep_rows, drop_weights)
    destination = dest_slots[0]
    fresh_ids = jnp.arange(pages_here, dtype=jnp.int32)
    inverse = jnp.sum(
        jnp.where(destination[None, :] == fresh_ids[:, None], fresh_ids[None, :], 0), axis=1
    )
    compact = kept[inverse].reshape(pages_here // 2, PAGE, KVW)
    summaries = means[inverse]
    per_lane = NP // lanes
    table = page_table.reshape(R_DEV, per_lane, lanes)
    mine = lax.dynamic_slice_in_dim(table, lane, 1, 2)[:, :, 0]
    logical = jnp.arange(per_lane, dtype=jnp.int32) * lanes + lane
    live = logical[None, :] < held_len[:, None]
    owner = jnp.any((mine[:, :, None] == fresh_ids[None, None, :]) & live[:, :, None], axis=1)
    query_groups = query.reshape(R_DEV, KVH, ratio, HD)
    row_keys = kept[:, :, :split].reshape(pages_here, KEEP, KVH, HD)
    row_values = kept[:, :, split:].reshape(pages_here, KEEP, KVH, HD)
    row_live = keep_rows >= 0
    allowed = owner[:, None, None, :, None] & row_live[None, None, None, :, :]
    scores = (
        jnp.einsum("rngd,pmnd->rngpm", query_groups, row_keys, preferred_element_type=jnp.float32)
        * scale
    )
    scores = jnp.where(allowed, scores, negative)
    mean_keys = means[:, :split].reshape(pages_here, KVH, HD)
    mean_values = means[:, split:].reshape(pages_here, KVH, HD)
    mean_scores = (
        jnp.einsum("rngd,pnd->rngp", query_groups, mean_keys, preferred_element_type=jnp.float32)
        * scale
        + bias[None, None, None, :]
    )
    mean_allowed = owner[:, None, None, :]
    mean_scores = jnp.where(mean_allowed, mean_scores, negative)
    own_score = (
        jnp.einsum("rngd,rnd->rng", query_groups, key_new, preferred_element_type=jnp.float32)
        * scale
    )
    own_score = jnp.where(lane == 0, own_score, negative)
    top = jnp.maximum(jnp.max(scores, axis=(3, 4)), jnp.max(mean_scores, axis=3))
    top = jnp.maximum(top, own_score)
    row_weight = jnp.where(allowed, jnp.exp(scores - top[..., None, None]), 0.0)
    mean_weight = jnp.where(mean_allowed, jnp.exp(mean_scores - top[..., None]), 0.0)
    own_weight = jnp.where(lane == 0, jnp.exp(own_score - top), 0.0)
    mass = jnp.sum(row_weight, axis=(3, 4)) + jnp.sum(mean_weight, axis=3) + own_weight
    total = jnp.einsum(
        "rngpm,pmnd->rngd",
        row_weight,
        row_values.astype(jnp.float32),
        precision=lax.Precision.HIGHEST,
    )
    total = total + jnp.einsum(
        "rngp,pnd->rngd",
        mean_weight,
        mean_values.astype(jnp.float32),
        precision=lax.Precision.HIGHEST,
    )
    total = total + own_weight[..., None] * value_new[:, :, None, :]

    parts = jnp.stack(
        [
            jnp.broadcast_to(top[..., None], total.shape).reshape(R_DEV, HEADS * HD),
            jnp.broadcast_to(mass[..., None], total.shape).reshape(R_DEV, HEADS * HD),
            total.reshape(R_DEV, HEADS * HD),
        ]
    )
    own = HEADS * HD // groups
    parts = jnp.moveaxis(parts.reshape(3, R_DEV, groups, own), 2, 0)
    parts = jnp.broadcast_to(parts[:, None], (groups, lanes, 3, R_DEV, own))
    came = lax.all_to_all(
        parts.reshape(groups * lanes, 3, R_DEV, own), both_axes, 0, 0, tiled=True
    ).reshape(groups, lanes, 3, R_DEV, own)
    tops, masses, sums = came[:, :, 0], came[:, :, 1], came[:, :, 2]
    weights = jnp.exp(tops - jnp.max(tops, axis=1, keepdims=True))
    attention = jnp.sum(sums * weights, axis=1) / jnp.sum(masses * weights, axis=1)
    attention = attention.reshape(requests, own).astype(jnp.bfloat16)
    back = jnp.sum(
        jnp.where(holders[None, :] == everyone[:, None], everyone[None, :], 0), axis=1
    )
    projected = jnp.dot(
        pick_rows(back, attention), output_weight, preferred_element_type=jnp.float32
    )
    projected = projected + jnp.where(group == 0, hidden_in.astype(jnp.float32), 0.0)

    mid = sum(block_pieces(projected)).astype(jnp.bfloat16).astype(jnp.float32)
    squares = jnp.sum(mid * mid, axis=1, keepdims=True)
    mean_square = lax.all_gather(squares, "req", axis=1, tiled=True)
    mean_square = jnp.sum(mean_square, axis=1, keepdims=True) / D
    gain_here = lax.dynamic_slice_in_dim(feedforward_gain, group * features, features, 0)
    inputs_mid = (mid * lax.rsqrt(mean_square + epsilon) * gain_here).astype(jnp.bfloat16)
    local_units = gate_weight.shape[1]
    piece = local_units // groups
    gates = jnp.dot(inputs_mid, gate_weight, preferred_element_type=jnp.float32)
    ups = jnp.dot(inputs_mid, up_weight, preferred_element_type=jnp.float32)
    both = jnp.stack([gates.reshape(requests, groups, piece), ups.reshape(requests, groups, piece)])
    both = lax.all_to_all(jnp.moveaxis(both, 2, 0), "req", 0, 0, tiled=True)
    sums = jnp.sum(both, axis=0)
    active = (jax.nn.silu(sums[0]) * sums[1]).astype(jnp.bfloat16)
    active = lax.all_gather(active, ("head", "req"), axis=1, tiled=True)
    units = FF // groups
    active_here = lax.dynamic_slice_in_dim(active, group * units, units, 1)
    down = jnp.dot(active_here, down_weight, preferred_element_type=jnp.float32)
    share = groups // lanes
    residual = [jnp.where(group == lane * share + k, mid, 0.0) for k in range(share)]
    down = down + jnp.concatenate(residual, axis=1)
    result = whole_sum(down).astype(jnp.bfloat16)
    return (compact, summaries, result)


def solution(mesh):
    placed = (
        P(None, "head"),
        P(),
        P(),
        P(),
        P(),
        P("req", "head"),
        P("req", "head"),
        P("req", "head"),
        P("req", "head"),
        P("req", "head"),
        P(("req", "head"), None, None),
        P(("req", "head"), None),
        P(("req", "head"), None),
        P(("req", "head"), None),
        P(),
        P("req", None),
        P(),
    )
    return jax.shard_map(
        on_device,
        mesh=mesh,
        in_specs=placed,
        out_specs=(P(("req", "head"), None, None), P(("req", "head"), None), P(None, "head")),
        check_vma=False,
    )
```

```python
import jax
import jax.numpy as jnp
from jax import lax
from jax.sharding import PartitionSpec as P

D = 2048
HEADS = 20
KVH = 5
HD = 64
FF = 5120
PAGE = 128
KEEP = 64
NP = 16
R_DEV = 2
KVW = 640

DIRECT = 8

epsilon = 1e-06
negative = -1e30
both_axes = ("req", "head")


def rms_scale(values):
    return lax.rsqrt(jnp.mean(values * values, axis=-1, keepdims=True) + epsilon)


def rms_rows(values, gain):
    return values * rms_scale(values) * gain


def rotate(vectors, positions):
    half = vectors.shape[-1] // 2
    frequency = 10000.0 ** (-jnp.arange(half, dtype=jnp.float32) / half)
    angles = positions.astype(jnp.float32)[:, None] * frequency[None, :]
    cosine = jnp.cos(angles)[:, None, :]
    sine = jnp.sin(angles)[:, None, :]
    first = vectors[..., :half]
    second = vectors[..., half:]
    return jnp.concatenate(
        [first * cosine - second * sine, second * cosine + first * sine], axis=-1
    )


def compact_pages(pages, keep, weights):
    rows = jnp.arange(pages.shape[1], dtype=jnp.int32)
    picks = keep[:, :, None] == rows[None, None, :]
    kept = jnp.einsum(
        "pkr,prc->pkc", picks.astype(jnp.bfloat16), pages, preferred_element_type=jnp.float32
    ).astype(jnp.bfloat16)
    dropped = weights * (1.0 - jnp.sum(picks.astype(jnp.float32), axis=1))
    total = jnp.sum(dropped, axis=1)
    means = (
        jnp.einsum(
            "pr,prc->pc", dropped, pages.astype(jnp.float32), precision=lax.Precision.HIGHEST
        )
        / total[:, None]
    )
    return (kept, means.astype(jnp.bfloat16), jnp.log(total))


def held_request(rows, source):
    half = R_DEV // 2
    position = rows % R_DEV
    slot = rows // R_DEV * half + position - half
    continued = jnp.arange(source.shape[0], dtype=jnp.int32)
    matches = source[None, :] == slot[:, None]
    owner_cont = jnp.sum(jnp.where(matches, continued[None, :], 0), axis=1)
    carried = owner_cont // half * R_DEV + half + owner_cont % half
    return jnp.where(position < half, rows, carried)


def pick_rows(order, rows):
    chosen = order[:, None] == jnp.arange(rows.shape[0], dtype=jnp.int32)[None, :]
    return jnp.dot(
        chosen.astype(jnp.bfloat16), rows, preferred_element_type=jnp.float32
    ).astype(jnp.bfloat16)


def exchange(parts):
    return lax.all_to_all(parts, "req", split_axis=0, concat_axis=0, tiled=True)


def to_block_owner(rows):
    groups = lax.axis_size("req")
    lanes = lax.axis_size("head")
    per_lane = groups // lanes
    pairs = [
        (g * lanes + h, (per_lane * h + g // lanes) * lanes + g % lanes)
        for g in range(groups)
        for h in range(lanes)
    ]
    return lax.ppermute(rows, both_axes, pairs)


def whole_sum(partial):
    if lax.axis_size("req") > DIRECT:
        return lax.psum(partial, "req")
    groups = lax.axis_size("req")
    return jnp.sum(exchange(jnp.broadcast_to(partial[None], (groups,) + partial.shape)), axis=0)


def on_device(
    hidden_in,
    attention_gain,
    query_gain,
    key_gain,
    feedforward_gain,
    input_weight,
    output_weight,
    gate_weight,
    up_weight,
    down_weight,
    old_cache,
    keep_rows,
    drop_weights,
    dest_slots,
    lengths,
    page_table,
    source,
):
    groups = lax.axis_size("req")
    lanes = lax.axis_size("head")
    group = lax.axis_index("req")
    lane = lax.axis_index("head")
    requests = hidden_in.shape[0]
    half = R_DEV // 2
    split = KVH * HD
    ratio = HEADS // KVH
    scale = HD ** (-0.5)
    pages_here = old_cache.shape[0]
    everyone = jnp.arange(requests, dtype=jnp.int32)
    holders = held_request(everyone, source)
    held = lax.dynamic_slice_in_dim(holders, group * R_DEV, R_DEV, 0)
    held_len = lengths[held]
    positions = held_len * PAGE

    whole = lax.all_gather(hidden_in, "head", axis=1, tiled=True)
    normed = rms_rows(whole.astype(jnp.float32), attention_gain).astype(jnp.bfloat16)
    features = D // groups
    inputs = pick_rows(holders, lax.dynamic_slice_in_dim(normed, group * features, features, 1))
    partial_qkv = jnp.dot(inputs, input_weight, preferred_element_type=jnp.float32)
    sent = jnp.broadcast_to(
        partial_qkv.reshape(groups, 1, R_DEV, -1), (groups, lanes, R_DEV, partial_qkv.shape[1])
    ).reshape(groups * lanes, R_DEV, -1)
    got = lax.all_to_all(sent, both_axes, split_axis=0, concat_axis=0, tiled=True)
    mixed = jnp.sum(got.reshape(groups, lanes, R_DEV, -1), axis=0).astype(jnp.bfloat16)
    held_qkv = jnp.swapaxes(mixed, 0, 1).reshape(R_DEV, -1).astype(jnp.float32)

    query = rotate(
        rms_rows(held_qkv[:, : HEADS * HD].reshape(R_DEV, HEADS, HD), query_gain), positions
    ).astype(jnp.bfloat16)
    key_new = rotate(
        rms_rows(held_qkv[:, HEADS * HD : (HEADS + KVH) * HD].reshape(R_DEV, KVH, HD), key_gain),
        positions,
    ).astype(jnp.bfloat16)
    value_new = held_qkv[:, (HEADS + KVH) * HD :].reshape(R_DEV, KVH, HD)
    kept, means, bias = compact_pages(old_cache, keep_rows, drop_weights)
    destination = dest_slots[0]
    fresh_ids = jnp.arange(pages_here, dtype=jnp.int32)
    inverse = jnp.sum(
        jnp.where(destination[None, :] == fresh_ids[:, None], fresh_ids[None, :], 0), axis=1
    )
    compact = kept[inverse].reshape(pages_here // 2, PAGE, KVW)
    summaries = means[inverse]
    per_lane = NP // lanes
    table = page_table.reshape(R_DEV, per_lane, lanes)
    mine = lax.dynamic_slice_in_dim(table, lane, 1, 2)[:, :, 0]
    logical = jnp.arange(per_lane, dtype=jnp.int32) * lanes + lane
    live = logical[None, :] < held_len[:, None]
    owner = jnp.any((mine[:, :, None] == fresh_ids[None, None, :]) & live[:, :, None], axis=1)
    query_groups = query.reshape(R_DEV, KVH, ratio, HD)
    row_keys = kept[:, :, :split].reshape(pages_here, KEEP, KVH, HD)
    row_values = kept[:, :, split:].reshape(pages_here, KEEP, KVH, HD)
    row_live = keep_rows >= 0
    allowed = owner[:, None, None, :, None] & row_live[None, None, None, :, :]
    scores = (
        jnp.einsum("rngd,pmnd->rngpm", query_groups, row_keys, preferred_element_type=jnp.float32)
        * scale
    )
    scores = jnp.where(allowed, scores, negative)
    mean_keys = means[:, :split].reshape(pages_here, KVH, HD)
    mean_values = means[:, split:].reshape(pages_here, KVH, HD)
    mean_scores = (
        jnp.einsum("rngd,pnd->rngp", query_groups, mean_keys, preferred_element_type=jnp.float32)
        * scale
        + bias[None, None, None, :]
    )
    mean_allowed = owner[:, None, None, :]
    mean_scores = jnp.where(mean_allowed, mean_scores, negative)
    own_score = (
        jnp.einsum("rngd,rnd->rng", query_groups, key_new, preferred_element_type=jnp.float32)
        * scale
    )
    own_score = jnp.where(lane == 0, own_score, negative)
    top = jnp.maximum(jnp.max(scores, axis=(3, 4)), jnp.max(mean_scores, axis=3))
    top = jnp.maximum(top, own_score)
    row_weight = jnp.where(allowed, jnp.exp(scores - top[..., None, None]), 0.0)
    mean_weight = jnp.where(mean_allowed, jnp.exp(mean_scores - top[..., None]), 0.0)
    own_weight = jnp.where(lane == 0, jnp.exp(own_score - top), 0.0)
    mass = jnp.sum(row_weight, axis=(3, 4)) + jnp.sum(mean_weight, axis=3) + own_weight
    total = jnp.einsum(
        "rngpm,pmnd->rngd",
        row_weight,
        row_values.astype(jnp.float32),
        precision=lax.Precision.HIGHEST,
    )
    total = total + jnp.einsum(
        "rngp,pnd->rngd",
        mean_weight,
        mean_values.astype(jnp.float32),
        precision=lax.Precision.HIGHEST,
    )
    total = total + own_weight[..., None] * value_new[:, :, None, :]

    some = mass > 0.0
    level = jnp.where(some, top + jnp.log(jnp.where(some, mass, 1.0)), negative)
    means_out = total / jnp.where(some, mass, 1.0)[..., None]
    own = HEADS * HD // groups
    parts = jnp.stack([means_out, jnp.broadcast_to(level[..., None], total.shape)])
    parts = jnp.transpose(parts.reshape(2, R_DEV, groups, own), (2, 1, 0, 3))
    parts = jnp.broadcast_to(
        parts.reshape(groups, 1, R_DEV, 2 * own), (groups, lanes, R_DEV, 2 * own)
    ).reshape(groups * lanes, R_DEV, 2 * own)
    came = lax.all_to_all(parts, both_axes, 0, 0, tiled=True)
    came = came.reshape(groups, lanes, R_DEV, 2 * own)
    outs, levels = came[..., :own], came[..., own:]
    weights = jnp.exp(levels - jnp.max(levels, axis=1, keepdims=True))
    attention = jnp.sum(outs * weights, axis=1) / jnp.sum(weights, axis=1)
    attention = attention.reshape(requests, own).astype(jnp.bfloat16)
    back = jnp.sum(
        jnp.where(holders[None, :] == everyone[:, None], everyone[None, :], 0), axis=1
    )
    projected = jnp.dot(
        pick_rows(back, attention), output_weight, preferred_element_type=jnp.float32
    )
    projected = projected + jnp.where(group == 0, hidden_in.astype(jnp.float32), 0.0)

    share = groups // lanes
    blocks = jnp.moveaxis(projected.reshape(requests, share, 1, features), 0, 2)
    blocks = jnp.broadcast_to(blocks, (share, lanes, requests, features))
    mid = jnp.sum(exchange(blocks.reshape(groups, requests, features)), axis=0)
    mid = to_block_owner(mid.astype(jnp.bfloat16)).astype(jnp.float32)
    squares = jnp.sum(mid * mid, axis=1, keepdims=True)
    gain_here = lax.dynamic_slice_in_dim(feedforward_gain, group * features, features, 0)
    inputs_mid = (mid * gain_here).astype(jnp.bfloat16)
    local_units = gate_weight.shape[1]
    piece = local_units // groups
    gates = jnp.dot(inputs_mid, gate_weight, preferred_element_type=jnp.float32)
    ups = jnp.dot(inputs_mid, up_weight, preferred_element_type=jnp.float32)
    both = jnp.concatenate(
        [
            gates.reshape(requests, groups, piece),
            ups.reshape(requests, groups, piece),
            jnp.broadcast_to(squares[:, :, None], (requests, groups, 1)),
        ],
        axis=2,
    )
    sums = jnp.sum(exchange(jnp.swapaxes(both, 0, 1)), axis=0)
    factor = lax.rsqrt(sums[:, 2 * piece :] / D + epsilon)
    gate = sums[:, :piece] * factor
    active = (jax.nn.silu(gate) * (sums[:, piece : 2 * piece] * factor)).astype(jnp.bfloat16)
    active_here = lax.all_gather(to_block_owner(active), "head", axis=1, tiled=True)
    down = jnp.dot(active_here, down_weight, preferred_element_type=jnp.float32)
    residual = [jnp.where(group == lane * share + k, mid, 0.0) for k in range(share)]
    down = down + jnp.concatenate(residual, axis=1)
    result = whole_sum(down).astype(jnp.bfloat16)
    return (compact, summaries, result)


def solution(mesh):
    placed = (
        P(None, "head"),
        P(),
        P(),
        P(),
        P(),
        P("req", "head"),
        P("req", "head"),
        P("req", "head"),
        P("req", "head"),
        P("req", "head"),
        P(("req", "head"), None, None),
        P(("req", "head"), None),
        P(("req", "head"), None),
        P(("req", "head"), None),
        P(),
        P("req", None),
        P(),
    )
    return jax.shard_map(
        on_device,
        mesh=mesh,
        in_specs=placed,
        out_specs=(P(("req", "head"), None, None), P(("req", "head"), None), P(None, "head")),
        check_vma=False,
    )
```

```python
import jax
import jax.numpy as jnp
from jax import lax
from jax.sharding import PartitionSpec as P

D = 2048
HEADS = 20
KVH = 5
HD = 64
FF = 5120
PAGE = 128
KEEP = 64
NP = 16
R_DEV = 2
KVW = 640

DIRECT = 8

epsilon = 1e-06
negative = -1e30
both_axes = ("req", "head")


def rms_scale(values):
    return lax.rsqrt(jnp.mean(values * values, axis=-1, keepdims=True) + epsilon)


def rms_rows(values, gain):
    return values * rms_scale(values) * gain


def rotate(vectors, positions):
    half = vectors.shape[-1] // 2
    frequency = 10000.0 ** (-jnp.arange(half, dtype=jnp.float32) / half)
    angles = positions.astype(jnp.float32)[:, None] * frequency[None, :]
    cosine = jnp.cos(angles)[:, None, :]
    sine = jnp.sin(angles)[:, None, :]
    first = vectors[..., :half]
    second = vectors[..., half:]
    return jnp.concatenate(
        [first * cosine - second * sine, second * cosine + first * sine], axis=-1
    )


def compact_pages(pages, keep, weights):
    rows = jnp.arange(pages.shape[1], dtype=jnp.int32)
    picks = keep[:, :, None] == rows[None, None, :]
    kept = jnp.einsum(
        "pkr,prc->pkc", picks.astype(jnp.bfloat16), pages, preferred_element_type=jnp.float32
    ).astype(jnp.bfloat16)
    dropped = weights * (1.0 - jnp.sum(picks.astype(jnp.float32), axis=1))
    total = jnp.sum(dropped, axis=1)
    means = (
        jnp.einsum(
            "pr,prc->pc", dropped, pages.astype(jnp.float32), precision=lax.Precision.HIGHEST
        )
        / total[:, None]
    )
    return (kept, means.astype(jnp.bfloat16), jnp.log(total))


def held_request(rows, source):
    half = R_DEV // 2
    position = rows % R_DEV
    slot = rows // R_DEV * half + position - half
    continued = jnp.arange(source.shape[0], dtype=jnp.int32)
    matches = source[None, :] == slot[:, None]
    owner_cont = jnp.sum(jnp.where(matches, continued[None, :], 0), axis=1)
    carried = owner_cont // half * R_DEV + half + owner_cont % half
    return jnp.where(position < half, rows, carried)


def pick_rows(order, rows):
    chosen = order[:, None] == jnp.arange(rows.shape[0], dtype=jnp.int32)[None, :]
    return jnp.dot(
        chosen.astype(jnp.bfloat16), rows, preferred_element_type=jnp.float32
    ).astype(jnp.bfloat16)


def exchange(parts):
    return lax.all_to_all(parts, "req", split_axis=0, concat_axis=0, tiled=True)


def over_lanes(parts):
    return lax.all_to_all(parts, "head", split_axis=0, concat_axis=0, tiled=True)


def whole_sum(partial):
    if lax.axis_size("req") > DIRECT:
        return lax.psum(partial, "req")
    groups = lax.axis_size("req")
    return jnp.sum(exchange(jnp.broadcast_to(partial[None], (groups,) + partial.shape)), axis=0)


def on_device(
    hidden_in,
    attention_gain,
    query_gain,
    key_gain,
    feedforward_gain,
    input_weight,
    output_weight,
    gate_weight,
    up_weight,
    down_weight,
    old_cache,
    keep_rows,
    drop_weights,
    dest_slots,
    lengths,
    page_table,
    source,
):
    groups = lax.axis_size("req")
    lanes = lax.axis_size("head")
    group = lax.axis_index("req")
    lane = lax.axis_index("head")
    requests = hidden_in.shape[0]
    half = R_DEV // 2
    split = KVH * HD
    ratio = HEADS // KVH
    scale = HD ** (-0.5)
    pages_here = old_cache.shape[0]
    everyone = jnp.arange(requests, dtype=jnp.int32)
    holders = held_request(everyone, source)
    held = lax.dynamic_slice_in_dim(holders, group * R_DEV, R_DEV, 0)
    held_len = lengths[held]
    positions = held_len * PAGE

    whole = lax.all_gather(hidden_in, "head", axis=1, tiled=True)
    normed = rms_rows(whole.astype(jnp.float32), attention_gain).astype(jnp.bfloat16)
    features = D // groups
    inputs = pick_rows(holders, lax.dynamic_slice_in_dim(normed, group * features, features, 1))
    partial_qkv = jnp.dot(inputs, input_weight, preferred_element_type=jnp.float32)
    sent = jnp.broadcast_to(
        partial_qkv.reshape(groups, 1, R_DEV, -1), (groups, lanes, R_DEV, partial_qkv.shape[1])
    ).reshape(groups * lanes, R_DEV, -1)
    got = lax.all_to_all(sent, both_axes, split_axis=0, concat_axis=0, tiled=True)
    mixed = jnp.sum(got.reshape(groups, lanes, R_DEV, -1), axis=0).astype(jnp.bfloat16)
    held_qkv = jnp.swapaxes(mixed, 0, 1).reshape(R_DEV, -1).astype(jnp.float32)

    share = groups // lanes
    piece = gate_weight.shape[1] // groups
    kept, means, bias = compact_pages(old_cache, keep_rows, drop_weights)
    output_weight, gate_weight, up_weight, means, _ = lax.optimization_barrier(
        (output_weight, gate_weight, up_weight, means, partial_qkv)
    )
    outputs = over_lanes(jnp.broadcast_to(output_weight[None], (lanes,) + output_weight.shape))
    outputs = jnp.swapaxes(outputs, 0, 1).reshape(output_weight.shape[0], -1)
    units = jnp.stack([gate_weight, up_weight]).reshape(2, features, share, lanes, piece)
    units = over_lanes(jnp.moveaxis(units, 3, 0))
    units = jnp.transpose(units, (2, 1, 0, 3, 4)).reshape(features, 2 * groups * piece)

    query = rotate(
        rms_rows(held_qkv[:, : HEADS * HD].reshape(R_DEV, HEADS, HD), query_gain), positions
    ).astype(jnp.bfloat16)
    key_new = rotate(
        rms_rows(held_qkv[:, HEADS * HD : (HEADS + KVH) * HD].reshape(R_DEV, KVH, HD), key_gain),
        positions,
    ).astype(jnp.bfloat16)
    value_new = held_qkv[:, (HEADS + KVH) * HD :].reshape(R_DEV, KVH, HD)
    destination = dest_slots[0]
    fresh_ids = jnp.arange(pages_here, dtype=jnp.int32)
    inverse = jnp.sum(
        jnp.where(destination[None, :] == fresh_ids[:, None], fresh_ids[None, :], 0), axis=1
    )
    compact = kept[inverse].reshape(pages_here // 2, PAGE, KVW)
    summaries = means[inverse]
    per_lane = NP // lanes
    table = page_table.reshape(R_DEV, per_lane, lanes)
    mine = lax.dynamic_slice_in_dim(table, lane, 1, 2)[:, :, 0]
    logical = jnp.arange(per_lane, dtype=jnp.int32) * lanes + lane
    live = logical[None, :] < held_len[:, None]
    owner = jnp.any((mine[:, :, None] == fresh_ids[None, None, :]) & live[:, :, None], axis=1)
    query_groups = query.reshape(R_DEV, KVH, ratio, HD)
    row_keys = kept[:, :, :split].reshape(pages_here, KEEP, KVH, HD)
    row_values = kept[:, :, split:].reshape(pages_here, KEEP, KVH, HD)
    row_live = keep_rows >= 0
    allowed = owner[:, None, None, :, None] & row_live[None, None, None, :, :]
    scores = (
        jnp.einsum("rngd,pmnd->rngpm", query_groups, row_keys, preferred_element_type=jnp.float32)
        * scale
    )
    scores = jnp.where(allowed, scores, negative)
    mean_keys = means[:, :split].reshape(pages_here, KVH, HD)
    mean_values = means[:, split:].reshape(pages_here, KVH, HD)
    mean_scores = (
        jnp.einsum("rngd,pnd->rngp", query_groups, mean_keys, preferred_element_type=jnp.float32)
        * scale
        + bias[None, None, None, :]
    )
    mean_allowed = owner[:, None, None, :]
    mean_scores = jnp.where(mean_allowed, mean_scores, negative)
    own_score = (
        jnp.einsum("rngd,rnd->rng", query_groups, key_new, preferred_element_type=jnp.float32)
        * scale
    )
    own_score = jnp.where(lane == 0, own_score, negative)
    top = jnp.maximum(jnp.max(scores, axis=(3, 4)), jnp.max(mean_scores, axis=3))
    top = jnp.maximum(top, own_score)
    row_weight = jnp.where(allowed, jnp.exp(scores - top[..., None, None]), 0.0)
    mean_weight = jnp.where(mean_allowed, jnp.exp(mean_scores - top[..., None]), 0.0)
    own_weight = jnp.where(lane == 0, jnp.exp(own_score - top), 0.0)
    mass = jnp.sum(row_weight, axis=(3, 4)) + jnp.sum(mean_weight, axis=3) + own_weight
    total = jnp.einsum(
        "rngpm,pmnd->rngd",
        row_weight,
        row_values.astype(jnp.float32),
        precision=lax.Precision.HIGHEST,
    )
    total = total + jnp.einsum(
        "rngp,pnd->rngd",
        mean_weight,
        mean_values.astype(jnp.float32),
        precision=lax.Precision.HIGHEST,
    )
    total = total + own_weight[..., None] * value_new[:, :, None, :]

    some = mass > 0.0
    level = jnp.where(some, top + jnp.log(jnp.where(some, mass, 1.0)), negative)
    means_out = total / jnp.where(some, mass, 1.0)[..., None]
    own = HEADS * HD // groups
    parts = jnp.stack([means_out, jnp.broadcast_to(level[..., None], total.shape)])
    parts = jnp.transpose(parts.reshape(2, R_DEV, groups, own), (2, 1, 0, 3))
    parts = jnp.broadcast_to(
        parts.reshape(groups, 1, R_DEV, 2 * own), (groups, lanes, R_DEV, 2 * own)
    ).reshape(groups * lanes, R_DEV, 2 * own)
    came = lax.all_to_all(parts, both_axes, 0, 0, tiled=True)
    came = came.reshape(groups, lanes, R_DEV, 2 * own)
    outs, levels = came[..., :own], came[..., own:]
    weights = jnp.exp(levels - jnp.max(levels, axis=1, keepdims=True))
    attention = jnp.sum(outs * weights, axis=1) / jnp.sum(weights, axis=1)
    attention = attention.reshape(requests, own).astype(jnp.bfloat16)
    back = jnp.sum(
        jnp.where(holders[None, :] == everyone[:, None], everyone[None, :], 0), axis=1
    )
    projected = jnp.dot(
        pick_rows(back, attention), outputs, preferred_element_type=jnp.float32
    )

    blocks = jnp.swapaxes(projected.reshape(requests, groups, features), 0, 1)
    hidden_here = lax.dynamic_slice_in_dim(whole, group * features, features, 1)
    mid = hidden_here.astype(jnp.float32) + jnp.sum(exchange(blocks), axis=0)
    mid = mid.astype(jnp.bfloat16).astype(jnp.float32)
    squares = jnp.sum(mid * mid, axis=1, keepdims=True)
    gain_here = lax.dynamic_slice_in_dim(feedforward_gain, group * features, features, 0)
    inputs_mid = (mid * gain_here).astype(jnp.bfloat16)
    both = jnp.dot(inputs_mid, units, preferred_element_type=jnp.float32)
    both = both.reshape(requests, 2, groups, piece)
    both = jnp.concatenate(
        [
            both[:, 0],
            both[:, 1],
            jnp.broadcast_to(squares[:, :, None], (requests, groups, 1)),
        ],
        axis=2,
    )
    sums = jnp.sum(exchange(jnp.swapaxes(both, 0, 1)), axis=0)
    factor = lax.rsqrt(sums[:, 2 * piece :] / D + epsilon)
    gate = sums[:, :piece] * factor
    active = (jax.nn.silu(gate) * (sums[:, piece : 2 * piece] * factor)).astype(jnp.bfloat16)
    active_here = lax.all_gather(active, "head", axis=1, tiled=True)
    down = jnp.dot(active_here, down_weight, preferred_element_type=jnp.float32)
    residual = [jnp.where(group == lane * share + k, mid, 0.0) for k in range(share)]
    down = down + jnp.concatenate(residual, axis=1)
    result = whole_sum(down).astype(jnp.bfloat16)
    return (compact, summaries, result)


def solution(mesh):
    placed = (
        P(None, "head"),
        P(),
        P(),
        P(),
        P(),
        P("req", "head"),
        P("req", "head"),
        P("req", "head"),
        P("req", "head"),
        P("req", "head"),
        P(("req", "head"), None, None),
        P(("req", "head"), None),
        P(("req", "head"), None),
        P(("req", "head"), None),
        P(),
        P("req", None),
        P(),
    )
    return jax.shard_map(
        on_device,
        mesh=mesh,
        in_specs=placed,
        out_specs=(P(("req", "head"), None, None), P(("req", "head"), None), P(None, "head")),
        check_vma=False,
    )
```

```python
import jax
import jax.numpy as jnp
from jax import lax
from jax.experimental import pallas as pl
from jax.experimental.pallas import tpu as pltpu
from jax.sharding import PartitionSpec as P

D = 2048
HEADS = 20
KVH = 5
HD = 64
FF = 5120
PAGE = 128
KEEP = 64
NP = 16
R_DEV = 2
KVW = 640

DIRECT = 8

epsilon = 1e-06
negative = -1e30
both_axes = ("req", "head")


def rms_scale(values):
    return lax.rsqrt(jnp.mean(values * values, axis=-1, keepdims=True) + epsilon)


def rms_rows(values, gain):
    return values * rms_scale(values) * gain


def rotate(vectors, positions):
    half = vectors.shape[-1] // 2
    frequency = 10000.0 ** (-jnp.arange(half, dtype=jnp.float32) / half)
    angles = positions.astype(jnp.float32)[:, None] * frequency[None, :]
    cosine = jnp.cos(angles)[:, None, :]
    sine = jnp.sin(angles)[:, None, :]
    first = vectors[..., :half]
    second = vectors[..., half:]
    return jnp.concatenate(
        [first * cosine - second * sine, second * cosine + first * sine], axis=-1
    )


def compact_pages(pages, keep, weights):
    rows = jnp.arange(pages.shape[1], dtype=jnp.int32)
    picks = keep[:, :, None] == rows[None, None, :]
    kept = jnp.einsum(
        "pkr,prc->pkc", picks.astype(jnp.bfloat16), pages, preferred_element_type=jnp.float32
    ).astype(jnp.bfloat16)
    dropped = weights * (1.0 - jnp.sum(picks.astype(jnp.float32), axis=1))
    total = jnp.sum(dropped, axis=1)
    means = (
        jnp.einsum(
            "pr,prc->pc", dropped, pages.astype(jnp.float32), precision=lax.Precision.HIGHEST
        )
        / total[:, None]
    )
    return (kept, means.astype(jnp.bfloat16), jnp.log(total))


def held_request(rows, source):
    half = R_DEV // 2
    position = rows % R_DEV
    slot = rows // R_DEV * half + position - half
    continued = jnp.arange(source.shape[0], dtype=jnp.int32)
    matches = source[None, :] == slot[:, None]
    owner_cont = jnp.sum(jnp.where(matches, continued[None, :], 0), axis=1)
    carried = owner_cont // half * R_DEV + half + owner_cont % half
    return jnp.where(position < half, rows, carried)


def pick_rows(order, rows):
    chosen = order[:, None] == jnp.arange(rows.shape[0], dtype=jnp.int32)[None, :]
    return jnp.dot(
        chosen.astype(jnp.bfloat16), rows, preferred_element_type=jnp.float32
    ).astype(jnp.bfloat16)


def exchange(parts):
    return lax.all_to_all(parts, "req", split_axis=0, concat_axis=0, tiled=True)


def to_block_owner(rows):
    groups = lax.axis_size("req")
    lanes = lax.axis_size("head")
    per_lane = groups // lanes
    pairs = [
        (g * lanes + h, (per_lane * h + g // lanes) * lanes + g % lanes)
        for g in range(groups)
        for h in range(lanes)
    ]
    return lax.ppermute(rows, both_axes, pairs)


def whole_sum(partial):
    if lax.axis_size("req") > DIRECT:
        return lax.psum(partial, "req")
    groups = lax.axis_size("req")
    return jnp.sum(exchange(jnp.broadcast_to(partial[None], (groups,) + partial.shape)), axis=0)


def on_device_wide(
    hidden_in,
    attention_gain,
    query_gain,
    key_gain,
    feedforward_gain,
    input_weight,
    output_weight,
    gate_weight,
    up_weight,
    down_weight,
    old_cache,
    keep_rows,
    drop_weights,
    dest_slots,
    lengths,
    page_table,
    source,
):
    groups = lax.axis_size("req")
    lanes = lax.axis_size("head")
    group = lax.axis_index("req")
    lane = lax.axis_index("head")
    requests = hidden_in.shape[0]
    half = R_DEV // 2
    split = KVH * HD
    ratio = HEADS // KVH
    scale = HD ** (-0.5)
    pages_here = old_cache.shape[0]
    everyone = jnp.arange(requests, dtype=jnp.int32)
    holders = held_request(everyone, source)
    held = lax.dynamic_slice_in_dim(holders, group * R_DEV, R_DEV, 0)
    held_len = lengths[held]
    positions = held_len * PAGE

    whole = lax.all_gather(hidden_in, "head", axis=1, tiled=True)
    normed = rms_rows(whole.astype(jnp.float32), attention_gain).astype(jnp.bfloat16)
    features = D // groups
    inputs = pick_rows(holders, lax.dynamic_slice_in_dim(normed, group * features, features, 1))
    partial_qkv = jnp.dot(inputs, input_weight, preferred_element_type=jnp.float32)
    sent = jnp.broadcast_to(
        partial_qkv.reshape(groups, 1, R_DEV, -1), (groups, lanes, R_DEV, partial_qkv.shape[1])
    ).reshape(groups * lanes, R_DEV, -1)
    got = lax.all_to_all(sent, both_axes, split_axis=0, concat_axis=0, tiled=True)
    mixed = jnp.sum(got.reshape(groups, lanes, R_DEV, -1), axis=0).astype(jnp.bfloat16)
    held_qkv = jnp.swapaxes(mixed, 0, 1).reshape(R_DEV, -1).astype(jnp.float32)

    query = rotate(
        rms_rows(held_qkv[:, : HEADS * HD].reshape(R_DEV, HEADS, HD), query_gain), positions
    ).astype(jnp.bfloat16)
    key_new = rotate(
        rms_rows(held_qkv[:, HEADS * HD : (HEADS + KVH) * HD].reshape(R_DEV, KVH, HD), key_gain),
        positions,
    ).astype(jnp.bfloat16)
    value_new = held_qkv[:, (HEADS + KVH) * HD :].reshape(R_DEV, KVH, HD)
    kept, means, bias = compact_pages(old_cache, keep_rows, drop_weights)
    destination = dest_slots[0]
    fresh_ids = jnp.arange(pages_here, dtype=jnp.int32)
    inverse = jnp.sum(
        jnp.where(destination[None, :] == fresh_ids[:, None], fresh_ids[None, :], 0), axis=1
    )
    compact = kept[inverse].reshape(pages_here // 2, PAGE, KVW)
    summaries = means[inverse]
    per_lane = NP // lanes
    table = page_table.reshape(R_DEV, per_lane, lanes)
    mine = lax.dynamic_slice_in_dim(table, lane, 1, 2)[:, :, 0]
    logical = jnp.arange(per_lane, dtype=jnp.int32) * lanes + lane
    live = logical[None, :] < held_len[:, None]
    owner = jnp.any((mine[:, :, None] == fresh_ids[None, None, :]) & live[:, :, None], axis=1)
    query_groups = query.reshape(R_DEV, KVH, ratio, HD)
    row_keys = kept[:, :, :split].reshape(pages_here, KEEP, KVH, HD)
    row_values = kept[:, :, split:].reshape(pages_here, KEEP, KVH, HD)
    row_live = keep_rows >= 0
    allowed = owner[:, None, None, :, None] & row_live[None, None, None, :, :]
    scores = (
        jnp.einsum("rngd,pmnd->rngpm", query_groups, row_keys, preferred_element_type=jnp.float32)
        * scale
    )
    scores = jnp.where(allowed, scores, negative)
    mean_keys = means[:, :split].reshape(pages_here, KVH, HD)
    mean_values = means[:, split:].reshape(pages_here, KVH, HD)
    mean_scores = (
        jnp.einsum("rngd,pnd->rngp", query_groups, mean_keys, preferred_element_type=jnp.float32)
        * scale
        + bias[None, None, None, :]
    )
    mean_allowed = owner[:, None, None, :]
    mean_scores = jnp.where(mean_allowed, mean_scores, negative)
    own_score = (
        jnp.einsum("rngd,rnd->rng", query_groups, key_new, preferred_element_type=jnp.float32)
        * scale
    )
    own_score = jnp.where(lane == 0, own_score, negative)
    top = jnp.maximum(jnp.max(scores, axis=(3, 4)), jnp.max(mean_scores, axis=3))
    top = jnp.maximum(top, own_score)
    row_weight = jnp.where(allowed, jnp.exp(scores - top[..., None, None]), 0.0)
    mean_weight = jnp.where(mean_allowed, jnp.exp(mean_scores - top[..., None]), 0.0)
    own_weight = jnp.where(lane == 0, jnp.exp(own_score - top), 0.0)
    mass = jnp.sum(row_weight, axis=(3, 4)) + jnp.sum(mean_weight, axis=3) + own_weight
    total = jnp.einsum(
        "rngpm,pmnd->rngd",
        row_weight,
        row_values.astype(jnp.float32),
        precision=lax.Precision.HIGHEST,
    )
    total = total + jnp.einsum(
        "rngp,pnd->rngd",
        mean_weight,
        mean_values.astype(jnp.float32),
        precision=lax.Precision.HIGHEST,
    )
    total = total + own_weight[..., None] * value_new[:, :, None, :]

    some = mass > 0.0
    level = jnp.where(some, top + jnp.log(jnp.where(some, mass, 1.0)), negative)
    means_out = total / jnp.where(some, mass, 1.0)[..., None]
    own = HEADS * HD // groups
    parts = jnp.stack([means_out, jnp.broadcast_to(level[..., None], total.shape)])
    parts = jnp.transpose(parts.reshape(2, R_DEV, groups, own), (2, 1, 0, 3))
    parts = jnp.broadcast_to(
        parts.reshape(groups, 1, R_DEV, 2 * own), (groups, lanes, R_DEV, 2 * own)
    ).reshape(groups * lanes, R_DEV, 2 * own)
    came = lax.all_to_all(parts, both_axes, 0, 0, tiled=True)
    came = came.reshape(groups, lanes, R_DEV, 2 * own)
    outs, levels = came[..., :own], came[..., own:]
    weights = jnp.exp(levels - jnp.max(levels, axis=1, keepdims=True))
    attention = jnp.sum(outs * weights, axis=1) / jnp.sum(weights, axis=1)
    attention = attention.reshape(requests, own).astype(jnp.bfloat16)
    back = jnp.sum(
        jnp.where(holders[None, :] == everyone[:, None], everyone[None, :], 0), axis=1
    )
    projected = jnp.dot(
        pick_rows(back, attention), output_weight, preferred_element_type=jnp.float32
    )
    projected = projected + jnp.where(group == 0, hidden_in.astype(jnp.float32), 0.0)

    share = groups // lanes
    blocks = jnp.moveaxis(projected.reshape(requests, share, 1, features), 0, 2)
    blocks = jnp.broadcast_to(blocks, (share, lanes, requests, features))
    mid = jnp.sum(exchange(blocks.reshape(groups, requests, features)), axis=0)
    mid = to_block_owner(mid.astype(jnp.bfloat16)).astype(jnp.float32)
    squares = jnp.sum(mid * mid, axis=1, keepdims=True)
    gain_here = lax.dynamic_slice_in_dim(feedforward_gain, group * features, features, 0)
    inputs_mid = (mid * gain_here).astype(jnp.bfloat16)
    local_units = gate_weight.shape[1]
    piece = local_units // groups
    gates = jnp.dot(inputs_mid, gate_weight, preferred_element_type=jnp.float32)
    ups = jnp.dot(inputs_mid, up_weight, preferred_element_type=jnp.float32)
    both = jnp.concatenate(
        [
            gates.reshape(requests, groups, piece),
            ups.reshape(requests, groups, piece),
            jnp.broadcast_to(squares[:, :, None], (requests, groups, 1)),
        ],
        axis=2,
    )
    sums = jnp.sum(exchange(jnp.swapaxes(both, 0, 1)), axis=0)
    factor = lax.rsqrt(sums[:, 2 * piece :] / D + epsilon)
    gate = sums[:, :piece] * factor
    active = (jax.nn.silu(gate) * (sums[:, piece : 2 * piece] * factor)).astype(jnp.bfloat16)
    active_here = lax.all_gather(to_block_owner(active), "head", axis=1, tiled=True)
    down = jnp.dot(active_here, down_weight, preferred_element_type=jnp.float32)
    residual = [jnp.where(group == lane * share + k, mid, 0.0) for k in range(share)]
    down = down + jnp.concatenate(residual, axis=1)
    result = whole_sum(down).astype(jnp.bfloat16)
    return (compact, summaries, result)


TILE = 128
bfloat = jnp.bfloat16
single = jnp.float32


def iota(shape, axis):
    return lax.broadcasted_iota(jnp.int32, shape, axis)


def run(kernel, outs, scalars, arrays, scratch=(), flops=0):
    in_specs = [pl.BlockSpec(memory_space=pltpu.SMEM) for _ in scalars]
    in_specs += [pl.BlockSpec(memory_space=pltpu.VMEM) for _ in arrays]
    moved = sum(a.size * a.dtype.itemsize for a in list(arrays) + list(outs))
    return pl.pallas_call(
        kernel,
        out_shape=list(outs),
        in_specs=in_specs,
        out_specs=[pl.BlockSpec(memory_space=pltpu.VMEM) for _ in outs],
        scratch_shapes=list(scratch),
        compiler_params=pltpu.CompilerParams(vmem_limit_bytes=16 * 2**20),
        cost_estimate=pl.CostEstimate(flops=flops, bytes_accessed=moved, transcendentals=0),
    )(*scalars, *arrays)


def shaped(shape, dtype):
    return jax.ShapeDtypeStruct(shape, dtype)


def first_kernel(ids, whole, gain, holders, weight, sent, wide):
    rows = whole.shape[0]
    groups = rows // R_DEV
    lanes = sent.shape[0] // groups
    features, columns = weight.shape
    values = whole[...].astype(single)
    factor = lax.rsqrt(jnp.mean(values * values, axis=1, keepdims=True) + epsilon)
    here = pl.ds(pl.multiple_of(ids[0] * features, features), features)
    normed = (whole[:, here].astype(single) * factor * gain[:, here]).astype(bfloat)
    order = (holders[...] == iota((rows, rows), 1)).astype(single).astype(bfloat)
    normed = jnp.dot(order, normed, preferred_element_type=single).astype(bfloat)
    wide[...] = jnp.zeros_like(wide)
    wide[:, :columns] = jnp.dot(normed, weight[...], preferred_element_type=single)
    for g in range(groups):
        tile = jnp.concatenate(
            [
                wide[R_DEV * g : R_DEV * (g + 1), TILE * j : TILE * (j + 1)]
                for j in range(wide.shape[1] // TILE)
            ],
            axis=0,
        )
        for k in range(lanes):
            sent[g * lanes + k] = tile


def compact_kernel(
    dest, pages, keep, weights, compact, summaries, kept, means, bias, ordered, plain
):
    count, rows, _ = pages.shape
    row = iota((rows, TILE), 0)
    column = iota((rows, TILE), 1)
    for p in range(count):
        picks = (keep[p : p + 1, :] == row).astype(single)
        dropped = weights[:, p : p + 1] * (1.0 - jnp.sum(picks, axis=1, keepdims=True))
        total = jnp.sum(dropped, axis=0, keepdims=True)
        high = dropped.astype(bfloat).astype(single)
        rest = dropped - high
        middle = rest.astype(bfloat).astype(single)
        low = rest - middle
        left = jnp.where(column == KEEP, high, picks)
        left = jnp.where(column == KEEP + 1, middle, left)
        left = jnp.where(column == KEEP + 2, low, left).astype(bfloat)
        both = lax.dot_general(
            left, pages[p], (((0,), (0,)), ((), ())), preferred_element_type=single
        )
        rows_kept = both[:KEEP].astype(bfloat)
        kept[KEEP * p : KEEP * (p + 1), :] = rows_kept
        slot = dest[p]
        start = pl.multiple_of((slot & 1) * KEEP, KEEP)
        compact[slot >> 1, pl.ds(start, KEEP), :] = rows_kept
        mean = both[KEEP : KEEP + 1] + both[KEEP + 1 : KEEP + 2] + both[KEEP + 2 : KEEP + 3]
        mean = mean / total
        plain[p : p + 1, :] = mean
        ordered[pl.ds(slot, 1), :] = mean
        bias[p : p + 1, :] = jnp.broadcast_to(jnp.log(total), (1, TILE))
    means[...] = plain[...].astype(bfloat)
    summaries[...] = ordered[...].astype(bfloat)


def deal_kernel(ids, gate, up, own, one, two, three, dealt):
    outs = (own, one, two, three)
    lanes = len(outs)
    piece = own.shape[1] // 4
    block = lanes * piece
    for k in range(lanes):
        for b in range(2):
            columns = slice(b * block + k * piece, b * block + (k + 1) * piece)
            start = 2 * b * piece
            dealt[k, :, start : start + piece] = gate[:, columns].astype(single)
            dealt[k, :, start + piece : start + 2 * piece] = up[:, columns].astype(single)
    for turn in range(lanes):
        outs[turn][...] = dealt[lax.rem(ids[1] + turn, lanes)].astype(bfloat)


def attend_kernel(
    came, cosine, sine, gain, kept, means, bias, mask, extra_mask, sent, x, extra_k, extra_v, out
):
    lanes = 4
    groups = came.shape[0] // lanes
    width = (HEADS + 2 * KVH) * HD // lanes
    span = -(-KVH * HD // TILE) * TILE
    key_cols = slice(0, span)
    value_cols = slice(KVW - span, KVW)
    first_key = HEADS * HD // TILE * R_DEV
    scale = HD ** (-0.5)
    x[...] = jnp.zeros_like(x)
    column = iota((8, TILE), 1)
    for k in range(lanes):
        tile = came[k]
        for g in range(1, groups):
            tile = tile + came[g * lanes + k]
        tile = tile.astype(bfloat).astype(single)
        base, shift = divmod(width * k, TILE)
        base = base * R_DEV
        if shift:
            tile = pltpu.roll(tile, shift, 1)
            x[base + 2 : base + 10, :] += jnp.where(column < shift, tile, 0.0)
        x[base : base + 8, :] += jnp.where(column >= shift, tile, 0.0)
    values = x[...]
    same_head = (iota((TILE, TILE), 0) // HD == iota((TILE, TILE), 1) // HD).astype(single)
    squares = jnp.dot(
        values * values, same_head, precision=lax.Precision.HIGHEST, preferred_element_type=single
    )
    normed = values * lax.rsqrt(squares / HD + epsilon) * gain[...]
    early = iota(values.shape, 1) % HD < HD // 2
    swapped = jnp.where(
        early, pltpu.roll(normed, TILE - HD // 2, 1), pltpu.roll(normed, HD // 2, 1)
    )
    turned = (normed * cosine[...] + swapped * sine[...]).astype(bfloat).astype(single)

    rows = 24
    row = iota((rows, TILE), 0)
    half = iota((rows, TILE), 1) // HD
    key_head = row >> 2
    query = jnp.where(row < first_key, turned[:rows], 0.0)
    other = pltpu.roll(query, HD, 1)
    queries = []
    for u in range(2):
        placed = jnp.where(
            half == (key_head & 1), jnp.where((key_head & 1) == u, query, other), 0.0
        )
        queries.append(
            jnp.concatenate(
                [jnp.where((key_head >> 1) == c, placed, 0.0) for c in range(span // TILE)], axis=1
            )
        )
    queries = jnp.concatenate(queries, axis=0).astype(bfloat)

    extra_k[...] = jnp.zeros_like(extra_k)
    extra_v[...] = jnp.zeros_like(extra_v)
    count = means.shape[0]
    extra_k[:count, :] = means[:, key_cols].astype(single)
    extra_v[:count, :] = means[:, value_cols].astype(single)
    first_value = first_key + KVH * HD // TILE * R_DEV
    for c in range(span // TILE):
        at = slice(c * TILE, (c + 1) * TILE)
        r = first_key + R_DEV * c
        extra_k[count : count + R_DEV, at] = turned[r : r + R_DEV]
        r = first_value + R_DEV * c
        extra_v[count : count + R_DEV, at] = values[r : r + R_DEV]

    def by_request(pair, size):
        odd = iota((2 * rows, size), 0) & 1
        return jnp.where(odd == 0, pair[0:1, :], pair[1:2, :])

    def dot_rows(left, right):
        return lax.dot_general(
            left, right, (((1,), (1,)), ((), ())), preferred_element_type=single
        )

    entries = kept.shape[0]
    extras = extra_k.shape[0]
    scores = dot_rows(queries, kept[:, key_cols]) * scale + by_request(mask, entries)
    diagonal = jnp.where(iota(bias.shape, 0) == iota(bias.shape, 1), bias[...], 0.0)
    bias_row = jnp.sum(diagonal, axis=0, keepdims=True)[:, :extras]
    extra = dot_rows(queries, extra_k[...].astype(bfloat)) * scale + bias_row
    extra = extra + by_request(extra_mask, extras)
    top = jnp.maximum(
        jnp.max(scores, axis=1, keepdims=True), jnp.max(extra, axis=1, keepdims=True)
    )
    weight = jnp.where(scores > 0.5 * negative, jnp.exp(scores - top), 0.0)
    extra_weight = jnp.where(extra > 0.5 * negative, jnp.exp(extra - top), 0.0)
    mass = jnp.sum(weight, axis=1, keepdims=True) + jnp.sum(extra_weight, axis=1, keepdims=True)

    def weighted(parts, right):
        high = parts.astype(bfloat)
        low = (parts - high.astype(single)).astype(bfloat)
        return jnp.dot(high, right, preferred_element_type=single) + jnp.dot(
            low, right, preferred_element_type=single
        )

    total = weighted(weight, kept[:, value_cols]) + weighted(
        extra_weight, extra_v[...].astype(bfloat)
    )
    some = mass > 0.0
    mass = jnp.where(some, mass, 1.0)
    total = total / mass
    level = jnp.where(some, top + jnp.log(mass), negative)

    lead = (KVW - span) % TILE + (KVW // 2 - (KVW - span)) // HD
    slot = key_head + lead
    results = []
    for u in range(2):
        mine = total[rows * u : rows * (u + 1)]
        picked = mine[:, :TILE]
        for c in range(1, span // TILE):
            picked = jnp.where((slot >> 1) == c, mine[:, c * TILE : (c + 1) * TILE], picked)
        results.append(jnp.where((slot & 1) == u, picked, pltpu.roll(picked, HD, 1)))
    out[:rows, :] = jnp.where(half == 0, results[0], results[1])
    out[rows:, :] = jnp.where(half == 0, level[:rows], level[rows:])
    own = HEADS * HD // groups
    for g in range(groups):
        r = own * g // TILE * R_DEV
        tile = jnp.concatenate([out[r : r + 4, :], out[rows + r : rows + r + 4, :]], axis=0)
        for k in range(lanes):
            sent[g * lanes + k] = tile


def project_kernel(ids, came, back, own, one, two, three, sent, rows):
    weights = (own, one, two, three)
    lanes = len(weights)
    groups = came.shape[0] // lanes
    features = own.shape[0]
    requests = rows.shape[0]
    for g in range(groups):
        tiles = [came[g * lanes + k] for k in range(lanes)]
        levels = [tile[4:8] for tile in tiles]
        top = jnp.maximum(
            jnp.maximum(levels[0], levels[1]), jnp.maximum(levels[2], levels[3])
        )
        shares = [jnp.exp(level - top) for level in levels]
        mixed = sum(share * tile[0:4] for share, tile in zip(shares, tiles)) / sum(shares)
        rows[R_DEV * g : R_DEV * (g + 1), :TILE] = mixed[:R_DEV]
        rows[R_DEV * g : R_DEV * (g + 1), TILE:] = mixed[R_DEV:]
    shift = lax.rem(2 * TILE - lax.rem(ids[0] * features, TILE), 2 * TILE)
    attention = pltpu.roll(rows[...].astype(bfloat).astype(single), shift, 1)
    order = (back[...] == iota((requests, requests), 1)).astype(single).astype(bfloat)
    attention = jnp.dot(order, attention.astype(bfloat), preferred_element_type=single)
    attention = attention[:, :features].astype(bfloat)
    width = sent.shape[2]
    for turn in range(lanes):
        projected = jnp.dot(attention, weights[turn][...], preferred_element_type=single)
        source = lax.rem(ids[1] + lanes - turn, lanes)
        for b in range(2):
            sent[2 * source + b] = projected[:, width * b : width * (b + 1)]


def units_kernel(ids, came, whole, gain, own, one, two, three, sent, mid_out):
    weights = (own, one, two, three)
    lanes = len(weights)
    groups, rows, features = came.shape
    here = pl.ds(pl.multiple_of(ids[0] * features, features), features)
    mid = came[0]
    for g in range(1, groups):
        mid = mid + came[g]
    mid = (mid + whole[:, here].astype(single)).astype(bfloat)
    mid_out[...] = mid
    mid = mid.astype(single)
    squares = jnp.sum(mid * mid, axis=1, keepdims=True)
    inputs = (mid * gain[:, here]).astype(bfloat)
    width = own.shape[1] // 2
    for turn in range(lanes):
        units = jnp.dot(inputs, weights[turn][...], preferred_element_type=single)
        source = lax.rem(ids[1] + lanes - turn, lanes)
        for b in range(2):
            sent[2 * source + b, :, :width] = units[:, width * b : width * (b + 1)]
            sent[2 * source + b, :, width:] = jnp.broadcast_to(
                squares, (rows, sent.shape[2] - width)
            )


def active_kernel(came, active):
    total = came[0]
    for g in range(1, came.shape[0]):
        total = total + came[g]
    piece = active.shape[1]
    factor = lax.rsqrt(total[:, 2 * piece : 2 * piece + 1] / D + epsilon)
    gate = total[:, :piece] * factor
    up = total[:, piece : 2 * piece] * factor
    active[...] = (gate / (1.0 + jnp.exp(-gate)) * up).astype(bfloat)


def down_kernel(ids, active, weight, mid, sent):
    groups, rows, width = sent.shape
    lanes, _, piece = active.shape
    half = mid.shape[1]
    down = jnp.dot(active[0], weight[:piece, :], preferred_element_type=single)
    for k in range(1, lanes):
        down = down + jnp.dot(
            active[k], weight[piece * k : piece * (k + 1), :], preferred_element_type=single
        )
    added = mid[...].astype(single)
    for b in range(width // half):
        columns = slice(half * b, half * (b + 1))
        mine = ids[0] == ids[1] * (width // half) + b
        total = down[:, columns] + jnp.where(mine, added, 0.0)
        for g in range(groups):
            sent[g, :, columns] = total


def result_kernel(came, result):
    total = came[0]
    for g in range(1, came.shape[0]):
        total = total + came[g]
    result[...] = total.astype(bfloat)


def turned_lanes(value, turn):
    lanes = lax.axis_size("head")
    return lax.ppermute(value, "head", [(k, (k + turn) % lanes) for k in range(lanes)])


def on_device(
    hidden_in,
    attention_gain,
    query_gain,
    key_gain,
    feedforward_gain,
    input_weight,
    output_weight,
    gate_weight,
    up_weight,
    down_weight,
    old_cache,
    keep_rows,
    drop_weights,
    dest_slots,
    lengths,
    page_table,
    source,
):
    groups = lax.axis_size("req")
    lanes = lax.axis_size("head")
    group = lax.axis_index("req")
    lane = lax.axis_index("head")
    requests = hidden_in.shape[0]
    pages_here = old_cache.shape[0]
    everyone = jnp.arange(requests, dtype=jnp.int32)
    ids = jnp.stack([group, lane]).astype(jnp.int32)
    holders = held_request(everyone, source)
    back = jnp.sum(
        jnp.where(holders[None, :] == everyone[:, None], everyone[None, :], 0), axis=1
    )
    held = lax.dynamic_slice_in_dim(holders, group * R_DEV, R_DEV, 0)
    chosen = held[:, None] == everyone[None, :]
    held_len = jnp.sum(jnp.where(chosen, lengths[None, :], 0), axis=1)
    devices = groups * lanes
    features = D // groups
    piece = gate_weight.shape[1] // groups

    whole = lax.all_gather(hidden_in, "head", axis=1, tiled=True)
    columns = input_weight.shape[1]
    padded = -(-columns // TILE) * TILE
    (sent,) = run(
        first_kernel,
        [shaped((devices, R_DEV * padded // TILE, TILE), single)],
        [ids],
        [whole, attention_gain[None, :], holders[:, None], input_weight],
        [pltpu.VMEM((requests, padded), single)],
        2 * requests * features * columns,
    )
    came = lax.all_to_all(sent, both_axes, 0, 0, tiled=True)

    compact, summaries, kept, means, bias = run(
        compact_kernel,
        [
            shaped((pages_here // 2, PAGE, KVW), bfloat),
            shaped((pages_here, KVW), bfloat),
            shaped((pages_here * KEEP, KVW), bfloat),
            shaped((pages_here, KVW), bfloat),
            shaped((pages_here, TILE), single),
        ],
        [dest_slots[0]],
        [
            old_cache,
            jnp.pad(keep_rows, ((0, 0), (0, TILE - KEEP)), constant_values=-1),
            drop_weights.T,
        ],
        [pltpu.VMEM((pages_here, KVW), single), pltpu.VMEM((pages_here, KVW), single)],
        2 * pages_here * TILE * PAGE * KVW,
    )
    own_units, *other_units = run(
        deal_kernel,
        [shaped((features, 4 * piece), bfloat)] * lanes,
        [ids],
        [gate_weight, up_weight],
        [pltpu.VMEM((lanes, features, 4 * piece), single)],
    )
    output_weights = [output_weight]
    unit_weights = [own_units]
    for turn in range(1, lanes):
        output_weights.append(turned_lanes(output_weight, turn))
    for turn in range(1, lanes):
        unit_weights.append(turned_lanes(other_units[turn - 1], turn))

    per_lane = NP // lanes
    slots = jnp.arange(pages_here, dtype=jnp.int32)
    logical = jnp.arange(NP, dtype=jnp.int32)
    live = (logical[None, :] < held_len[:, None]) & (logical % lanes == lane)[None, :]
    owner = jnp.any(
        (page_table[:, :, None] == slots[None, None, :]) & live[:, :, None], axis=1
    )
    mask = jnp.where(owner[:, :, None] & (keep_rows >= 0)[None], 0.0, negative)
    mask = mask.reshape(R_DEV, pages_here * KEEP)
    own_entry = (jnp.arange(R_DEV)[:, None] == jnp.arange(8)[None, :]) & (lane == 0)
    extra_mask = jnp.where(jnp.concatenate([owner, own_entry], axis=1), 0.0, negative)
    half = HD // 2
    frequency = 10000.0 ** (-jnp.arange(half, dtype=jnp.float32) / half)
    angles = (held_len * PAGE).astype(jnp.float32)[:, None] * frequency[None, :]
    cosine = jnp.tile(jnp.cos(angles), (16, TILE // half))
    sine = jnp.sin(angles)
    sine = jnp.tile(jnp.concatenate([-sine, sine], axis=1), (16, TILE // HD))
    query_rows = HEADS * HD // TILE * R_DEV
    gain_rows = jnp.concatenate(
        [
            jnp.broadcast_to(jnp.tile(query_gain, TILE // HD)[None], (query_rows, TILE)),
            jnp.broadcast_to(jnp.tile(key_gain, TILE // HD)[None], (32 - query_rows, TILE)),
        ]
    )
    span = -(-KVH * HD // TILE) * TILE
    (parts,) = run(
        attend_kernel,
        [shaped((devices, 8, TILE), single)],
        [],
        [came, cosine, sine, gain_rows, kept, means, bias, mask, extra_mask],
        [
            pltpu.VMEM((32, TILE), single),
            pltpu.VMEM((16, span), single),
            pltpu.VMEM((16, span), single),
            pltpu.VMEM((48, TILE), single),
        ],
        6 * 48 * pages_here * KEEP * span,
    )
    came = lax.all_to_all(parts, both_axes, 0, 0, tiled=True)
    (sent,) = run(
        project_kernel,
        [shaped((groups, requests, features), single)],
        [ids],
        [came, back[:, None], *output_weights],
        [pltpu.VMEM((requests, 2 * TILE), single)],
        2 * requests * output_weight.size * lanes,
    )
    came = exchange(sent)
    sent, mid = run(
        units_kernel,
        [shaped((groups, requests, 3 * TILE), single), shaped((requests, features), bfloat)],
        [ids],
        [came, whole, feedforward_gain[None, :], *unit_weights],
        [],
        4 * requests * gate_weight.size,
    )
    (active,) = run(active_kernel, [shaped((requests, piece), bfloat)], [], [exchange(sent)])
    active = lax.all_gather(active, "head")
    (sent,) = run(
        down_kernel,
        [shaped((groups, requests, down_weight.shape[1]), single)],
        [ids],
        [active, down_weight, mid],
        [],
        2 * requests * down_weight.size,
    )
    (result,) = run(
        result_kernel, [shaped((requests, down_weight.shape[1]), bfloat)], [], [exchange(sent)]
    )
    return (compact, summaries, result)


def solution(mesh):
    placed = (
        P(None, "head"),
        P(),
        P(),
        P(),
        P(),
        P("req", "head"),
        P("req", "head"),
        P("req", "head"),
        P("req", "head"),
        P("req", "head"),
        P(("req", "head"), None, None),
        P(("req", "head"), None),
        P(("req", "head"), None),
        P(("req", "head"), None),
        P(),
        P("req", None),
        P(),
    )
    return jax.shard_map(
        on_device if mesh.shape["req"] <= DIRECT else on_device_wide,
        mesh=mesh,
        in_specs=placed,
        out_specs=(P(("req", "head"), None, None), P(("req", "head"), None), P(None, "head")),
        check_vma=False,
    )
```

```python
import jax
import jax.numpy as jnp
import numpy as np
from jax import lax
from jax.experimental import pallas as pl
from jax.experimental.pallas import tpu as pltpu
from jax.sharding import PartitionSpec as P

D = 2048
HEADS = 20
KVH = 5
HD = 64
FF = 5120
PAGE = 128
KEEP = 64
NP = 16
R_DEV = 2
KVW = 640

DIRECT = 8

epsilon = 1e-06
negative = -1e30
both_axes = ("req", "head")


def rms_scale(values):
    return lax.rsqrt(jnp.mean(values * values, axis=-1, keepdims=True) + epsilon)


def rms_rows(values, gain):
    return values * rms_scale(values) * gain


def rotate(vectors, positions):
    half = vectors.shape[-1] // 2
    frequency = 10000.0 ** (-jnp.arange(half, dtype=jnp.float32) / half)
    angles = positions.astype(jnp.float32)[:, None] * frequency[None, :]
    cosine = jnp.cos(angles)[:, None, :]
    sine = jnp.sin(angles)[:, None, :]
    first = vectors[..., :half]
    second = vectors[..., half:]
    return jnp.concatenate(
        [first * cosine - second * sine, second * cosine + first * sine], axis=-1
    )


def compact_pages(pages, keep, weights):
    rows = jnp.arange(pages.shape[1], dtype=jnp.int32)
    picks = keep[:, :, None] == rows[None, None, :]
    kept = jnp.einsum(
        "pkr,prc->pkc", picks.astype(jnp.bfloat16), pages, preferred_element_type=jnp.float32
    ).astype(jnp.bfloat16)
    dropped = weights * (1.0 - jnp.sum(picks.astype(jnp.float32), axis=1))
    total = jnp.sum(dropped, axis=1)
    means = (
        jnp.einsum(
            "pr,prc->pc", dropped, pages.astype(jnp.float32), precision=lax.Precision.HIGHEST
        )
        / total[:, None]
    )
    return (kept, means.astype(jnp.bfloat16), jnp.log(total))


def held_request(rows, source):
    half = R_DEV // 2
    position = rows % R_DEV
    slot = rows // R_DEV * half + position - half
    continued = jnp.arange(source.shape[0], dtype=jnp.int32)
    matches = source[None, :] == slot[:, None]
    owner_cont = jnp.sum(jnp.where(matches, continued[None, :], 0), axis=1)
    carried = owner_cont // half * R_DEV + half + owner_cont % half
    return jnp.where(position < half, rows, carried)


def pick_rows(order, rows):
    chosen = order[:, None] == jnp.arange(rows.shape[0], dtype=jnp.int32)[None, :]
    return jnp.dot(
        chosen.astype(jnp.bfloat16), rows, preferred_element_type=jnp.float32
    ).astype(jnp.bfloat16)


def exchange(parts):
    return lax.all_to_all(parts, "req", split_axis=0, concat_axis=0, tiled=True)


def to_block_owner(rows):
    groups = lax.axis_size("req")
    lanes = lax.axis_size("head")
    per_lane = groups // lanes
    pairs = [
        (g * lanes + h, (per_lane * h + g // lanes) * lanes + g % lanes)
        for g in range(groups)
        for h in range(lanes)
    ]
    return lax.ppermute(rows, both_axes, pairs)


def whole_sum(partial):
    if lax.axis_size("req") > DIRECT:
        return lax.psum(partial, "req")
    groups = lax.axis_size("req")
    return jnp.sum(exchange(jnp.broadcast_to(partial[None], (groups,) + partial.shape)), axis=0)


def on_device_wide(
    hidden_in,
    attention_gain,
    query_gain,
    key_gain,
    feedforward_gain,
    input_weight,
    output_weight,
    gate_weight,
    up_weight,
    down_weight,
    old_cache,
    keep_rows,
    drop_weights,
    dest_slots,
    lengths,
    page_table,
    source,
):
    groups = lax.axis_size("req")
    lanes = lax.axis_size("head")
    group = lax.axis_index("req")
    lane = lax.axis_index("head")
    requests = hidden_in.shape[0]
    half = R_DEV // 2
    split = KVH * HD
    ratio = HEADS // KVH
    scale = HD ** (-0.5)
    pages_here = old_cache.shape[0]
    everyone = jnp.arange(requests, dtype=jnp.int32)
    holders = held_request(everyone, source)
    held = lax.dynamic_slice_in_dim(holders, group * R_DEV, R_DEV, 0)
    held_len = lengths[held]
    positions = held_len * PAGE

    whole = lax.all_gather(hidden_in, "head", axis=1, tiled=True)
    normed = rms_rows(whole.astype(jnp.float32), attention_gain).astype(jnp.bfloat16)
    features = D // groups
    inputs = pick_rows(holders, lax.dynamic_slice_in_dim(normed, group * features, features, 1))
    partial_qkv = jnp.dot(inputs, input_weight, preferred_element_type=jnp.float32)
    sent = jnp.broadcast_to(
        partial_qkv.reshape(groups, 1, R_DEV, -1), (groups, lanes, R_DEV, partial_qkv.shape[1])
    ).reshape(groups * lanes, R_DEV, -1)
    got = lax.all_to_all(sent, both_axes, split_axis=0, concat_axis=0, tiled=True)
    mixed = jnp.sum(got.reshape(groups, lanes, R_DEV, -1), axis=0).astype(jnp.bfloat16)
    held_qkv = jnp.swapaxes(mixed, 0, 1).reshape(R_DEV, -1).astype(jnp.float32)

    query = rotate(
        rms_rows(held_qkv[:, : HEADS * HD].reshape(R_DEV, HEADS, HD), query_gain), positions
    ).astype(jnp.bfloat16)
    key_new = rotate(
        rms_rows(held_qkv[:, HEADS * HD : (HEADS + KVH) * HD].reshape(R_DEV, KVH, HD), key_gain),
        positions,
    ).astype(jnp.bfloat16)
    value_new = held_qkv[:, (HEADS + KVH) * HD :].reshape(R_DEV, KVH, HD)
    kept, means, bias = compact_pages(old_cache, keep_rows, drop_weights)
    destination = dest_slots[0]
    fresh_ids = jnp.arange(pages_here, dtype=jnp.int32)
    inverse = jnp.sum(
        jnp.where(destination[None, :] == fresh_ids[:, None], fresh_ids[None, :], 0), axis=1
    )
    compact = kept[inverse].reshape(pages_here // 2, PAGE, KVW)
    summaries = means[inverse]
    per_lane = NP // lanes
    table = page_table.reshape(R_DEV, per_lane, lanes)
    mine = lax.dynamic_slice_in_dim(table, lane, 1, 2)[:, :, 0]
    logical = jnp.arange(per_lane, dtype=jnp.int32) * lanes + lane
    live = logical[None, :] < held_len[:, None]
    owner = jnp.any((mine[:, :, None] == fresh_ids[None, None, :]) & live[:, :, None], axis=1)
    query_groups = query.reshape(R_DEV, KVH, ratio, HD)
    row_keys = kept[:, :, :split].reshape(pages_here, KEEP, KVH, HD)
    row_values = kept[:, :, split:].reshape(pages_here, KEEP, KVH, HD)
    row_live = keep_rows >= 0
    allowed = owner[:, None, None, :, None] & row_live[None, None, None, :, :]
    scores = (
        jnp.einsum("rngd,pmnd->rngpm", query_groups, row_keys, preferred_element_type=jnp.float32)
        * scale
    )
    scores = jnp.where(allowed, scores, negative)
    mean_keys = means[:, :split].reshape(pages_here, KVH, HD)
    mean_values = means[:, split:].reshape(pages_here, KVH, HD)
    mean_scores = (
        jnp.einsum("rngd,pnd->rngp", query_groups, mean_keys, preferred_element_type=jnp.float32)
        * scale
        + bias[None, None, None, :]
    )
    mean_allowed = owner[:, None, None, :]
    mean_scores = jnp.where(mean_allowed, mean_scores, negative)
    own_score = (
        jnp.einsum("rngd,rnd->rng", query_groups, key_new, preferred_element_type=jnp.float32)
        * scale
    )
    own_score = jnp.where(lane == 0, own_score, negative)
    top = jnp.maximum(jnp.max(scores, axis=(3, 4)), jnp.max(mean_scores, axis=3))
    top = jnp.maximum(top, own_score)
    row_weight = jnp.where(allowed, jnp.exp(scores - top[..., None, None]), 0.0)
    mean_weight = jnp.where(mean_allowed, jnp.exp(mean_scores - top[..., None]), 0.0)
    own_weight = jnp.where(lane == 0, jnp.exp(own_score - top), 0.0)
    mass = jnp.sum(row_weight, axis=(3, 4)) + jnp.sum(mean_weight, axis=3) + own_weight
    total = jnp.einsum(
        "rngpm,pmnd->rngd",
        row_weight,
        row_values.astype(jnp.float32),
        precision=lax.Precision.HIGHEST,
    )
    total = total + jnp.einsum(
        "rngp,pnd->rngd",
        mean_weight,
        mean_values.astype(jnp.float32),
        precision=lax.Precision.HIGHEST,
    )
    total = total + own_weight[..., None] * value_new[:, :, None, :]

    some = mass > 0.0
    level = jnp.where(some, top + jnp.log(jnp.where(some, mass, 1.0)), negative)
    means_out = total / jnp.where(some, mass, 1.0)[..., None]
    own = HEADS * HD // groups
    parts = jnp.stack([means_out, jnp.broadcast_to(level[..., None], total.shape)])
    parts = jnp.transpose(parts.reshape(2, R_DEV, groups, own), (2, 1, 0, 3))
    parts = jnp.broadcast_to(
        parts.reshape(groups, 1, R_DEV, 2 * own), (groups, lanes, R_DEV, 2 * own)
    ).reshape(groups * lanes, R_DEV, 2 * own)
    came = lax.all_to_all(parts, both_axes, 0, 0, tiled=True)
    came = came.reshape(groups, lanes, R_DEV, 2 * own)
    outs, levels = came[..., :own], came[..., own:]
    weights = jnp.exp(levels - jnp.max(levels, axis=1, keepdims=True))
    attention = jnp.sum(outs * weights, axis=1) / jnp.sum(weights, axis=1)
    attention = attention.reshape(requests, own).astype(jnp.bfloat16)
    back = jnp.sum(
        jnp.where(holders[None, :] == everyone[:, None], everyone[None, :], 0), axis=1
    )
    projected = jnp.dot(
        pick_rows(back, attention), output_weight, preferred_element_type=jnp.float32
    )
    projected = projected + jnp.where(group == 0, hidden_in.astype(jnp.float32), 0.0)

    share = groups // lanes
    blocks = jnp.moveaxis(projected.reshape(requests, share, 1, features), 0, 2)
    blocks = jnp.broadcast_to(blocks, (share, lanes, requests, features))
    mid = jnp.sum(exchange(blocks.reshape(groups, requests, features)), axis=0)
    mid = to_block_owner(mid.astype(jnp.bfloat16)).astype(jnp.float32)
    squares = jnp.sum(mid * mid, axis=1, keepdims=True)
    gain_here = lax.dynamic_slice_in_dim(feedforward_gain, group * features, features, 0)
    inputs_mid = (mid * gain_here).astype(jnp.bfloat16)
    local_units = gate_weight.shape[1]
    piece = local_units // groups
    gates = jnp.dot(inputs_mid, gate_weight, preferred_element_type=jnp.float32)
    ups = jnp.dot(inputs_mid, up_weight, preferred_element_type=jnp.float32)
    both = jnp.concatenate(
        [
            gates.reshape(requests, groups, piece),
            ups.reshape(requests, groups, piece),
            jnp.broadcast_to(squares[:, :, None], (requests, groups, 1)),
        ],
        axis=2,
    )
    sums = jnp.sum(exchange(jnp.swapaxes(both, 0, 1)), axis=0)
    factor = lax.rsqrt(sums[:, 2 * piece :] / D + epsilon)
    gate = sums[:, :piece] * factor
    active = (jax.nn.silu(gate) * (sums[:, piece : 2 * piece] * factor)).astype(jnp.bfloat16)
    active_here = lax.all_gather(to_block_owner(active), "head", axis=1, tiled=True)
    down = jnp.dot(active_here, down_weight, preferred_element_type=jnp.float32)
    residual = [jnp.where(group == lane * share + k, mid, 0.0) for k in range(share)]
    down = down + jnp.concatenate(residual, axis=1)
    result = whole_sum(down).astype(jnp.bfloat16)
    return (compact, summaries, result)


TILE = 128
bfloat = jnp.bfloat16
single = jnp.float32


def iota(shape, axis):
    return lax.broadcasted_iota(jnp.int32, shape, axis)


def run(kernel, outs, far, near, scratch=(), flops=0):
    in_specs = [pl.BlockSpec(memory_space=pltpu.HBM) for _ in far]
    in_specs += [pl.BlockSpec(memory_space=pltpu.VMEM) for _ in near]
    moved = sum(a.size * a.dtype.itemsize for a in [*far, *near, *outs])
    return pl.pallas_call(
        kernel,
        out_shape=list(outs),
        in_specs=in_specs,
        out_specs=[pl.BlockSpec(memory_space=pltpu.VMEM) for _ in outs],
        scratch_shapes=list(scratch),
        compiler_params=pltpu.CompilerParams(vmem_limit_bytes=16 * 2**20),
        cost_estimate=pl.CostEstimate(flops=flops, bytes_accessed=moved, transcendentals=0),
    )(*far, *near)


def fetch(sources, targets, done):
    copies = [
        pltpu.make_async_copy(source, target, done.at[k])
        for k, (source, target) in enumerate(zip(sources, targets))
    ]
    for copy in copies:
        copy.start()
    return copies


def local_like(*arrays):
    return [pltpu.VMEM(a.shape, a.dtype) for a in arrays]


def scalar_like(*arrays):
    return [pltpu.SMEM(a.shape, a.dtype) for a in arrays]


def row_order(source, count, to_holder):
    first, second = iota((count, count), 0), iota((count, count), 1)
    if not to_holder:
        first, second = second, first
    order = (first == second) & (first % R_DEV == 0)
    for c in range(source.shape[1]):
        order = order | ((first == source[0, c] * R_DEV + 1) & (second == c * R_DEV + 1))
    return order.astype(single).astype(bfloat)


def shaped(shape, dtype):
    return jax.ShapeDtypeStruct(shape, dtype)


def first_kernel(
    source_far, gain_far, weight_far, whole, sent, source, gain, weight, wide, done
):
    copies = fetch((source_far, gain_far, weight_far), (source, gain, weight), done)
    rows = whole.shape[0]
    groups = rows // R_DEV
    lanes = sent.shape[0] // groups
    columns, features = weight.shape
    values = whole[...].astype(single)
    factor = lax.rsqrt(jnp.mean(values * values, axis=1, keepdims=True) + epsilon)
    here = pl.ds(pl.multiple_of(lax.axis_index("req") * features, features), features)
    wide[...] = jnp.zeros_like(wide)
    for copy in copies:
        copy.wait()
    normed = (whole[:, here].astype(single) * factor * gain[:, here]).astype(bfloat)
    order = row_order(source, rows, True)
    normed = jnp.dot(order, normed, preferred_element_type=single).astype(bfloat)
    wide[:, :columns] = dot_rows(normed, weight[...])
    for g in range(groups):
        tile = jnp.concatenate(
            [
                wide[R_DEV * g : R_DEV * (g + 1), TILE * j : TILE * (j + 1)]
                for j in range(wide.shape[1] // TILE)
            ],
            axis=0,
        )
        for k in range(lanes):
            sent[g * lanes + k] = tile


def dot_rows(left, right):
    return lax.dot_general(left, right, (((1,), (1,)), ((), ())), preferred_element_type=single)


def prepare_kernel(*refs):
    far, refs = refs[:12], refs[12:]
    (compact, summaries, kept, added, tables, own, one, two, three), refs = refs[:9], refs[9:]
    near, (ordered, plain, dealt, done) = refs[:12], refs[12:]
    copies = fetch(far, near, done)
    (dest, lengths, source, table, keep, weights, query_gain, key_gain, turns) = near[:9]
    pages, gate, up = near[9:]
    group = lax.axis_index("req")
    lane = lax.axis_index("head")
    lanes = lax.axis_size("head")
    for copy in copies[:9]:
        copy.wait()

    carried = 0
    for c in range(source.shape[1]):
        carried = carried + jnp.where(source[0, c] == group, c, 0)
    held_len = (lengths[0, group * R_DEV], lengths[0, carried * R_DEV + 1])
    count, rows, _ = pages.shape
    owned = []
    for r in range(R_DEV):
        slots = []
        for i in range(table.shape[1] // lanes):
            j = i * lanes + lane
            slots.append(jnp.where(j < held_len[r], table[r, j], -1))
        owned.append(slots)

    def owner(r, p):
        found = owned[r][0] == p
        for slot in owned[r][1:]:
            found = found | (slot == p)
        return found

    row = iota((32, TILE), 0)
    odd = (row & 1) == 1
    half_rows = turns.shape[0] // 2
    for part in range(2):
        pair = [turns[pl.ds(part * half_rows + held_len[r], 1), :] for r in range(R_DEV)]
        tables[32 * part : 32 * (part + 1), :] = jnp.where(odd, pair[1], pair[0])
    query_rows = HEADS * HD // TILE * R_DEV
    for c in range(TILE // HD):
        columns = slice(HD * c, HD * (c + 1))
        tables[64 : 64 + query_rows, columns] = jnp.broadcast_to(
            query_gain[...], (query_rows, HD)
        )
        tables[64 + query_rows : 96, columns] = jnp.broadcast_to(
            key_gain[...], (32 - query_rows, HD)
        )

    column = iota((1, TILE), 1)
    entries = count * KEEP
    added[...] = jnp.full_like(added, negative)
    extra = [
        jnp.where((column == count + r) & (lane == 0), 0.0, negative) for r in range(R_DEV)
    ]
    weight_columns = weights[...].T
    rows_of = iota((rows, KEEP), 0)
    place = iota((rows, KEEP), 1)
    copies[9].wait()
    for p in range(count):
        picks = (keep[p : p + 1, :] == rows_of).astype(single)
        dropped = weight_columns[:, p : p + 1] * (1.0 - jnp.sum(picks, axis=1, keepdims=True))
        total = jnp.sum(dropped, axis=0, keepdims=True)
        high = dropped.astype(bfloat).astype(single)
        rest = dropped - high
        middle = rest.astype(bfloat).astype(single)
        terms = jnp.where(place == 0, high, jnp.where(place == 1, middle, rest - middle))
        terms = jnp.where(place < 3, terms, 0.0)
        left = jnp.concatenate([picks, terms], axis=1).astype(bfloat)
        both = lax.dot_general(
            left, pages[p], (((0,), (0,)), ((), ())), preferred_element_type=single
        )
        rows_kept = both[:KEEP].astype(bfloat)
        kept[KEEP * p : KEEP * (p + 1), :] = rows_kept
        slot = dest[0, p]
        start = pl.multiple_of((slot & 1) * KEEP, KEEP)
        compact[slot >> 1, pl.ds(start, KEEP), :] = rows_kept
        mean = both[KEEP : KEEP + 1] + both[KEEP + 1 : KEEP + 2] + both[KEEP + 2 : KEEP + 3]
        mean = mean / total
        plain[p : p + 1, :] = mean
        ordered[pl.ds(slot, 1), :] = mean
        live = jnp.where(keep[p : p + 1, :] >= 0, 0.0, negative)
        for r in range(R_DEV):
            here = owner(r, p)
            added[r : r + 1, KEEP * p : KEEP * (p + 1)] = jnp.where(here, live, negative)
            level = jnp.where(here, jnp.log(total), negative)
            extra[r] = jnp.where(column == p, level, extra[r])
    for r in range(R_DEV):
        added[r : r + 1, entries : entries + TILE] = extra[r]
    plain[count:, :] = jnp.zeros_like(plain[count:, :])
    kept[entries:, :] = plain[...].astype(bfloat)
    summaries[...] = ordered[...].astype(bfloat)

    outs = (own, one, two, three)
    piece = own.shape[1] // 4
    block = lanes * piece
    for copy in copies[10:]:
        copy.wait()
    for k in range(lanes):
        for b in range(2):
            columns = slice(b * block + k * piece, b * block + (k + 1) * piece)
            start = 2 * b * piece
            dealt[k, :, start : start + piece] = gate[:, columns].astype(single)
            dealt[k, :, start + piece : start + 2 * piece] = up[:, columns].astype(single)
    for turn in range(lanes):
        outs[turn][...] = dealt[lax.rem(lane + turn, lanes)].astype(bfloat)


def attend_kernel(came, kept, added, tables, sent, x, extra_k, extra_v, out):
    lanes = lax.axis_size("head")
    groups = came.shape[0] // lanes
    width = (HEADS + 2 * KVH) * HD // lanes
    span = -(-KVH * HD // TILE) * TILE
    key_cols = slice(0, span)
    value_cols = slice(KVW - span, KVW)
    first_key = HEADS * HD // TILE * R_DEV
    scale = HD ** (-0.5)
    x[...] = jnp.zeros_like(x)
    column = iota((8, TILE), 1)
    for k in range(lanes):
        tile = came[k]
        for g in range(1, groups):
            tile = tile + came[g * lanes + k]
        tile = tile.astype(bfloat).astype(single)
        base, shift = divmod(width * k, TILE)
        base = base * R_DEV
        if shift:
            tile = pltpu.roll(tile, shift, 1)
            x[base + 2 : base + 10, :] += jnp.where(column < shift, tile, 0.0)
        x[base : base + 8, :] += jnp.where(column >= shift, tile, 0.0)
    values = x[...]
    same_head = (iota((TILE, TILE), 0) // HD == iota((TILE, TILE), 1) // HD).astype(single)
    squares = jnp.dot(
        values * values, same_head, precision=lax.Precision.HIGHEST, preferred_element_type=single
    )
    normed = values * lax.rsqrt(squares / HD + epsilon) * tables[64:96, :]
    early = iota(values.shape, 1) % HD < HD // 2
    swapped = jnp.where(
        early, pltpu.roll(normed, TILE - HD // 2, 1), pltpu.roll(normed, HD // 2, 1)
    )
    turned = normed * tables[0:32, :] + swapped * tables[32:64, :]
    turned = turned.astype(bfloat).astype(single)

    rows = 24
    row = iota((rows, TILE), 0)
    half = iota((rows, TILE), 1) // HD
    key_head = row >> 2
    query = jnp.where(row < first_key, turned[:rows], 0.0)
    other = pltpu.roll(query, HD, 1)
    queries = []
    for u in range(2):
        placed = jnp.where(
            half == (key_head & 1), jnp.where((key_head & 1) == u, query, other), 0.0
        )
        queries.append(
            jnp.concatenate(
                [jnp.where((key_head >> 1) == c, placed, 0.0) for c in range(span // TILE)], axis=1
            )
        )
    queries = jnp.concatenate(queries, axis=0).astype(bfloat)

    extras = extra_k.shape[0]
    entries = kept.shape[0] - extras
    count = entries // KEEP
    extra_k[...] = kept[entries:, key_cols].astype(single)
    extra_v[...] = kept[entries:, value_cols].astype(single)
    first_value = first_key + KVH * HD // TILE * R_DEV
    for c in range(span // TILE):
        at = slice(c * TILE, (c + 1) * TILE)
        r = first_key + R_DEV * c
        extra_k[count : count + R_DEV, at] = turned[r : r + R_DEV]
        r = first_value + R_DEV * c
        extra_v[count : count + R_DEV, at] = values[r : r + R_DEV]

    def by_request(columns, size):
        odd = (iota((2 * rows, size), 0) & 1) == 1
        return jnp.where(odd, added[1:2, columns], added[0:1, columns])

    scores = dot_rows(queries, kept[:entries, key_cols]) * scale
    scores = scores + by_request(slice(0, entries), entries)
    extra = dot_rows(queries, extra_k[...].astype(bfloat)) * scale
    extra = extra + by_request(slice(entries, entries + extras), extras)
    top = jnp.maximum(
        jnp.max(scores, axis=1, keepdims=True), jnp.max(extra, axis=1, keepdims=True)
    )
    weight = jnp.where(scores > 0.5 * negative, jnp.exp(scores - top), 0.0)
    extra_weight = jnp.where(extra > 0.5 * negative, jnp.exp(extra - top), 0.0)
    mass = jnp.sum(weight, axis=1, keepdims=True) + jnp.sum(extra_weight, axis=1, keepdims=True)

    def weighted(parts, right):
        high = parts.astype(bfloat)
        low = (parts - high.astype(single)).astype(bfloat)
        return jnp.dot(high, right, preferred_element_type=single) + jnp.dot(
            low, right, preferred_element_type=single
        )

    total = weighted(weight, kept[:entries, value_cols]) + weighted(
        extra_weight, extra_v[...].astype(bfloat)
    )
    some = mass > 0.0
    mass = jnp.where(some, mass, 1.0)
    total = total / mass
    level = jnp.where(some, top + jnp.log(mass), negative)

    slot = key_head + (KVW // 2 - (KVW - span)) // HD
    results = []
    for u in range(2):
        mine = total[rows * u : rows * (u + 1)]
        picked = mine[:, :TILE]
        for c in range(1, span // TILE):
            picked = jnp.where((slot >> 1) == c, mine[:, c * TILE : (c + 1) * TILE], picked)
        results.append(jnp.where((slot & 1) == u, picked, pltpu.roll(picked, HD, 1)))
    out[:rows, :] = jnp.where(half == 0, results[0], results[1])
    out[rows:, :] = jnp.where(half == 0, level[:rows], level[rows:])
    own = HEADS * HD // groups
    for g in range(groups):
        r = own * g // TILE * R_DEV
        tile = jnp.concatenate([out[r : r + 4, :], out[rows + r : rows + r + 4, :]], axis=0)
        for k in range(lanes):
            sent[g * lanes + k] = tile


def project_kernel(source_far, weight_far, came, sent, source, weight, rows, done):
    copies = fetch((source_far, weight_far), (source, weight), done)
    lanes = lax.axis_size("head")
    groups = came.shape[0] // lanes
    features = weight.shape[0]
    requests = rows.shape[0]
    for g in range(groups):
        tiles = [came[g * lanes + k] for k in range(lanes)]
        levels = [tile[4:8] for tile in tiles]
        top = jnp.maximum(
            jnp.maximum(levels[0], levels[1]), jnp.maximum(levels[2], levels[3])
        )
        shares = [jnp.exp(level - top) for level in levels]
        mixed = sum(share * tile[0:4] for share, tile in zip(shares, tiles)) / sum(shares)
        rows[R_DEV * g : R_DEV * (g + 1), :TILE] = mixed[:R_DEV]
        rows[R_DEV * g : R_DEV * (g + 1), TILE:] = mixed[R_DEV:]
    shift = lax.rem(2 * TILE - lax.rem(lax.axis_index("req") * features, TILE), 2 * TILE)
    attention = pltpu.roll(rows[...].astype(bfloat).astype(single), shift, 1)
    for copy in copies:
        copy.wait()
    order = row_order(source, requests, False)
    attention = jnp.dot(order, attention.astype(bfloat), preferred_element_type=single)
    attention = attention[:, :features].astype(bfloat)
    projected = jnp.dot(attention, weight[...], preferred_element_type=single).astype(bfloat)
    width = sent.shape[2]
    share = groups // lanes
    for g in range(groups):
        b = g % share
        for k in range(lanes):
            sent[g * lanes + k] = projected[:, width * b : width * (b + 1)]


def units_kernel(gain_far, came, whole, own, one, two, three, sent, mid_out, gain, done):
    (copy,) = fetch((gain_far,), (gain,), done)
    weights = (own, one, two, three)
    lanes = len(weights)
    devices, rows, features = came.shape
    groups = devices // lanes
    share = groups // lanes
    group = lax.axis_index("req")
    lane = lax.axis_index("head")
    here = pl.ds(pl.multiple_of(group * features, features), features)
    mid = whole[:, here].astype(single)
    for g in range(groups):
        mid = mid + came[g * lanes + group // share].astype(single)
    mid = mid.astype(bfloat)
    mid_out[...] = mid
    mid = mid.astype(single)
    squares = jnp.sum(mid * mid, axis=1, keepdims=True)
    width = own.shape[1] // 2
    place = iota((rows, sent.shape[2] - width), 1)
    high = squares.astype(bfloat).astype(single)
    rest = squares - high
    middle = rest.astype(bfloat).astype(single)
    terms = jnp.where(place == 0, high, jnp.where(place == 1, middle, rest - middle))
    terms = jnp.where(place < 3, terms, 0.0).astype(bfloat)
    copy.wait()
    inputs = (mid * gain[:, here]).astype(bfloat)
    for turn in range(lanes):
        units = jnp.dot(inputs, weights[turn][...], preferred_element_type=single)
        target = lax.rem(lane + lanes - turn, lanes) * share
        for b in range(share):
            sent[target + b, :, :width] = units[:, width * b : width * (b + 1)].astype(bfloat)
            sent[target + b, :, width:] = terms


def summed(came):
    total = came[0].astype(single)
    for g in range(1, came.shape[0]):
        total = total + came[g].astype(single)
    return total


def active_kernel(came, active):
    total = summed(came)
    piece = active.shape[1]
    squares = total[:, 2 * piece : 2 * piece + 1] + total[:, 2 * piece + 1 : 2 * piece + 2]
    squares = squares + total[:, 2 * piece + 2 : 2 * piece + 3]
    factor = lax.rsqrt(squares / D + epsilon)
    gate = total[:, :piece] * factor
    up = total[:, piece : 2 * piece] * factor
    active[...] = (gate / (1.0 + jnp.exp(-gate)) * up).astype(bfloat)


def down_kernel(active, weight, mid, sent):
    groups, rows, width = sent.shape
    lanes, _, piece = active.shape
    half = mid.shape[1]
    share = width // half
    down = jnp.dot(active[0], weight[:piece, :], preferred_element_type=single)
    for k in range(1, lanes):
        down = down + jnp.dot(
            active[k], weight[piece * k : piece * (k + 1), :], preferred_element_type=single
        )
    residual = mid[...].astype(single)
    group = lax.axis_index("req")
    lane = lax.axis_index("head")
    for b in range(share):
        columns = slice(half * b, half * (b + 1))
        mine = group == lane * share + b
        total = (down[:, columns] + jnp.where(mine, residual, 0.0)).astype(bfloat)
        for g in range(groups):
            sent[g, :, columns] = total


def result_kernel(came, result):
    result[...] = summed(came).astype(bfloat)


def rotation_table():
    half = HD // 2
    size = -(-(NP + 1) // 8) * 8
    frequency = 10000.0 ** (-np.arange(half) / half)
    angles = PAGE * np.arange(size)[:, None] * frequency[None, :]
    cosine, sine = np.cos(angles), np.sin(angles)
    wide = [np.tile(np.concatenate(pair, axis=1), (1, TILE // HD)) for pair in
            ((cosine, cosine), (-sine, sine))]
    return jnp.asarray(np.concatenate(wide), dtype=single)


def turned_lanes(value, turn):
    lanes = lax.axis_size("head")
    return lax.ppermute(value, "head", [(k, (k + turn) % lanes) for k in range(lanes)])


def on_device(
    hidden_in,
    attention_gain,
    query_gain,
    key_gain,
    feedforward_gain,
    input_weight,
    output_weight,
    gate_weight,
    up_weight,
    down_weight,
    old_cache,
    keep_rows,
    drop_weights,
    dest_slots,
    lengths,
    page_table,
    source,
):
    groups = lax.axis_size("req")
    lanes = lax.axis_size("head")
    requests = hidden_in.shape[0]
    pages_here = old_cache.shape[0]
    devices = groups * lanes
    features = D // groups
    piece = gate_weight.shape[1] // groups
    copies = pltpu.SemaphoreType.DMA

    whole = lax.all_gather(hidden_in, "head", axis=1, tiled=True)
    columns = input_weight.shape[1]
    padded = -(-columns // TILE) * TILE
    holds = source[None, :]
    gain = attention_gain[None, :]
    weight = input_weight.T
    (sent,) = run(
        first_kernel,
        [shaped((devices, R_DEV * padded // TILE, TILE), single)],
        [holds, gain, weight],
        [whole],
        [
            *scalar_like(holds),
            *local_like(gain, weight),
            pltpu.VMEM((requests, padded), single),
            copies((3,)),
        ],
        2 * requests * features * columns,
    )
    came = lax.all_to_all(sent, both_axes, 0, 0, tiled=True)

    scalars = [dest_slots, lengths[None, :], holds, page_table]
    arrays = [
        keep_rows,
        drop_weights,
        query_gain[None, :],
        key_gain[None, :],
        rotation_table(),
        old_cache,
        gate_weight,
        up_weight,
    ]
    entries = pages_here * KEEP
    extras = 16
    compact, summaries, kept, added, tables, own_units, *other_units = run(
        prepare_kernel,
        [
            shaped((pages_here // 2, PAGE, KVW), bfloat),
            shaped((pages_here, KVW), bfloat),
            shaped((entries + extras, KVW), bfloat),
            shaped((8, entries + TILE), single),
            shaped((96, TILE), single),
        ]
        + [shaped((features, 4 * piece), bfloat)] * lanes,
        scalars + arrays,
        [],
        [
            *scalar_like(*scalars),
            *local_like(*arrays),
            pltpu.VMEM((pages_here, KVW), single),
            pltpu.VMEM((extras, KVW), single),
            pltpu.VMEM((lanes, features, 4 * piece), single),
            copies((len(scalars + arrays),)),
        ],
        2 * pages_here * TILE * PAGE * KVW,
    )
    span = -(-KVH * HD // TILE) * TILE
    (parts,) = run(
        attend_kernel,
        [shaped((devices, 8, TILE), single)],
        [],
        [came, kept, added, tables],
        [
            pltpu.VMEM((32, TILE), single),
            pltpu.VMEM((extras, span), single),
            pltpu.VMEM((extras, span), single),
            pltpu.VMEM((48, TILE), single),
        ],
        6 * 48 * entries * span,
    )
    *other_units, _ = lax.optimization_barrier((*other_units, parts))
    units = [own_units]
    for turn in range(1, lanes):
        units.append(turned_lanes(other_units[turn - 1], turn))
    came = lax.all_to_all(parts, both_axes, 0, 0, tiled=True)
    (sent,) = run(
        project_kernel,
        [shaped((devices, requests, features), bfloat)],
        [holds, output_weight],
        [came],
        [
            *scalar_like(holds),
            *local_like(output_weight),
            pltpu.VMEM((requests, 2 * TILE), single),
            copies((2,)),
        ],
        2 * requests * output_weight.size,
    )
    came = lax.all_to_all(sent, both_axes, 0, 0, tiled=True)
    gain = feedforward_gain[None, :]
    sent, mid = run(
        units_kernel,
        [shaped((groups, requests, 3 * TILE), bfloat), shaped((requests, features), bfloat)],
        [gain],
        [came, whole, *units],
        [*local_like(gain), copies((1,))],
        4 * requests * gate_weight.size,
    )
    (active,) = run(active_kernel, [shaped((requests, piece), bfloat)], [], [exchange(sent)])
    active = lax.all_gather(active, "head")
    (sent,) = run(
        down_kernel,
        [shaped((groups, requests, down_weight.shape[1]), bfloat)],
        [],
        [active, down_weight, mid],
        [],
        2 * requests * down_weight.size,
    )
    (result,) = run(
        result_kernel, [shaped((requests, down_weight.shape[1]), bfloat)], [], [exchange(sent)]
    )
    return (compact, summaries, result)


def solution(mesh):
    placed = (
        P(None, "head"),
        P(),
        P(),
        P(),
        P(),
        P("req", "head"),
        P("req", "head"),
        P("req", "head"),
        P("req", "head"),
        P("req", "head"),
        P(("req", "head"), None, None),
        P(("req", "head"), None),
        P(("req", "head"), None),
        P(("req", "head"), None),
        P(),
        P("req", None),
        P(),
    )
    return jax.shard_map(
        on_device if mesh.shape["req"] <= DIRECT else on_device_wide,
        mesh=mesh,
        in_specs=placed,
        out_specs=(P(("req", "head"), None, None), P(("req", "head"), None), P(None, "head")),
        check_vma=False,
    )
```

```python
import jax
import jax.numpy as jnp
import numpy as np
from jax import lax
from jax.experimental import pallas as pl
from jax.experimental.pallas import tpu as pltpu
from jax.sharding import PartitionSpec as P

D = 2048
HEADS = 20
KVH = 5
HD = 64
FF = 5120
PAGE = 128
KEEP = 64
NP = 16
R_DEV = 2
KVW = 640

DIRECT = 8

epsilon = 1e-06
negative = -1e30
both_axes = ("req", "head")


def rms_scale(values):
    return lax.rsqrt(jnp.mean(values * values, axis=-1, keepdims=True) + epsilon)


def rms_rows(values, gain):
    return values * rms_scale(values) * gain


def rotate(vectors, positions):
    half = vectors.shape[-1] // 2
    frequency = 10000.0 ** (-jnp.arange(half, dtype=jnp.float32) / half)
    angles = positions.astype(jnp.float32)[:, None] * frequency[None, :]
    cosine = jnp.cos(angles)[:, None, :]
    sine = jnp.sin(angles)[:, None, :]
    first = vectors[..., :half]
    second = vectors[..., half:]
    return jnp.concatenate(
        [first * cosine - second * sine, second * cosine + first * sine], axis=-1
    )


def compact_pages(pages, keep, weights):
    rows = jnp.arange(pages.shape[1], dtype=jnp.int32)
    picks = keep[:, :, None] == rows[None, None, :]
    kept = jnp.einsum(
        "pkr,prc->pkc", picks.astype(jnp.bfloat16), pages, preferred_element_type=jnp.float32
    ).astype(jnp.bfloat16)
    dropped = weights * (1.0 - jnp.sum(picks.astype(jnp.float32), axis=1))
    total = jnp.sum(dropped, axis=1)
    means = (
        jnp.einsum(
            "pr,prc->pc", dropped, pages.astype(jnp.float32), precision=lax.Precision.HIGHEST
        )
        / total[:, None]
    )
    return (kept, means.astype(jnp.bfloat16), jnp.log(total))


def held_request(rows, source):
    half = R_DEV // 2
    position = rows % R_DEV
    slot = rows // R_DEV * half + position - half
    continued = jnp.arange(source.shape[0], dtype=jnp.int32)
    matches = source[None, :] == slot[:, None]
    owner_cont = jnp.sum(jnp.where(matches, continued[None, :], 0), axis=1)
    carried = owner_cont // half * R_DEV + half + owner_cont % half
    return jnp.where(position < half, rows, carried)


def pick_rows(order, rows):
    chosen = order[:, None] == jnp.arange(rows.shape[0], dtype=jnp.int32)[None, :]
    return jnp.dot(
        chosen.astype(jnp.bfloat16), rows, preferred_element_type=jnp.float32
    ).astype(jnp.bfloat16)


def exchange(parts):
    return lax.all_to_all(parts, "req", split_axis=0, concat_axis=0, tiled=True)


def to_block_owner(rows):
    groups = lax.axis_size("req")
    lanes = lax.axis_size("head")
    per_lane = groups // lanes
    pairs = [
        (g * lanes + h, (per_lane * h + g // lanes) * lanes + g % lanes)
        for g in range(groups)
        for h in range(lanes)
    ]
    return lax.ppermute(rows, both_axes, pairs)


def whole_sum(partial):
    if lax.axis_size("req") > DIRECT:
        return lax.psum(partial, "req")
    groups = lax.axis_size("req")
    return jnp.sum(exchange(jnp.broadcast_to(partial[None], (groups,) + partial.shape)), axis=0)


def on_device_wide(
    hidden_in,
    attention_gain,
    query_gain,
    key_gain,
    feedforward_gain,
    input_weight,
    output_weight,
    gate_weight,
    up_weight,
    down_weight,
    old_cache,
    keep_rows,
    drop_weights,
    dest_slots,
    lengths,
    page_table,
    source,
):
    groups = lax.axis_size("req")
    lanes = lax.axis_size("head")
    group = lax.axis_index("req")
    lane = lax.axis_index("head")
    requests = hidden_in.shape[0]
    half = R_DEV // 2
    split = KVH * HD
    ratio = HEADS // KVH
    scale = HD ** (-0.5)
    pages_here = old_cache.shape[0]
    everyone = jnp.arange(requests, dtype=jnp.int32)
    holders = held_request(everyone, source)
    held = lax.dynamic_slice_in_dim(holders, group * R_DEV, R_DEV, 0)
    held_len = lengths[held]
    positions = held_len * PAGE

    whole = lax.all_gather(hidden_in, "head", axis=1, tiled=True)
    normed = rms_rows(whole.astype(jnp.float32), attention_gain).astype(jnp.bfloat16)
    features = D // groups
    inputs = pick_rows(holders, lax.dynamic_slice_in_dim(normed, group * features, features, 1))
    partial_qkv = jnp.dot(inputs, input_weight, preferred_element_type=jnp.float32)
    sent = jnp.broadcast_to(
        partial_qkv.reshape(groups, 1, R_DEV, -1), (groups, lanes, R_DEV, partial_qkv.shape[1])
    ).reshape(groups * lanes, R_DEV, -1)
    got = lax.all_to_all(sent, both_axes, split_axis=0, concat_axis=0, tiled=True)
    mixed = jnp.sum(got.reshape(groups, lanes, R_DEV, -1), axis=0).astype(jnp.bfloat16)
    held_qkv = jnp.swapaxes(mixed, 0, 1).reshape(R_DEV, -1).astype(jnp.float32)

    query = rotate(
        rms_rows(held_qkv[:, : HEADS * HD].reshape(R_DEV, HEADS, HD), query_gain), positions
    ).astype(jnp.bfloat16)
    key_new = rotate(
        rms_rows(held_qkv[:, HEADS * HD : (HEADS + KVH) * HD].reshape(R_DEV, KVH, HD), key_gain),
        positions,
    ).astype(jnp.bfloat16)
    value_new = held_qkv[:, (HEADS + KVH) * HD :].reshape(R_DEV, KVH, HD)
    kept, means, bias = compact_pages(old_cache, keep_rows, drop_weights)
    destination = dest_slots[0]
    fresh_ids = jnp.arange(pages_here, dtype=jnp.int32)
    inverse = jnp.sum(
        jnp.where(destination[None, :] == fresh_ids[:, None], fresh_ids[None, :], 0), axis=1
    )
    compact = kept[inverse].reshape(pages_here // 2, PAGE, KVW)
    summaries = means[inverse]
    per_lane = NP // lanes
    table = page_table.reshape(R_DEV, per_lane, lanes)
    mine = lax.dynamic_slice_in_dim(table, lane, 1, 2)[:, :, 0]
    logical = jnp.arange(per_lane, dtype=jnp.int32) * lanes + lane
    live = logical[None, :] < held_len[:, None]
    owner = jnp.any((mine[:, :, None] == fresh_ids[None, None, :]) & live[:, :, None], axis=1)
    query_groups = query.reshape(R_DEV, KVH, ratio, HD)
    row_keys = kept[:, :, :split].reshape(pages_here, KEEP, KVH, HD)
    row_values = kept[:, :, split:].reshape(pages_here, KEEP, KVH, HD)
    row_live = keep_rows >= 0
    allowed = owner[:, None, None, :, None] & row_live[None, None, None, :, :]
    scores = (
        jnp.einsum("rngd,pmnd->rngpm", query_groups, row_keys, preferred_element_type=jnp.float32)
        * scale
    )
    scores = jnp.where(allowed, scores, negative)
    mean_keys = means[:, :split].reshape(pages_here, KVH, HD)
    mean_values = means[:, split:].reshape(pages_here, KVH, HD)
    mean_scores = (
        jnp.einsum("rngd,pnd->rngp", query_groups, mean_keys, preferred_element_type=jnp.float32)
        * scale
        + bias[None, None, None, :]
    )
    mean_allowed = owner[:, None, None, :]
    mean_scores = jnp.where(mean_allowed, mean_scores, negative)
    own_score = (
        jnp.einsum("rngd,rnd->rng", query_groups, key_new, preferred_element_type=jnp.float32)
        * scale
    )
    own_score = jnp.where(lane == 0, own_score, negative)
    top = jnp.maximum(jnp.max(scores, axis=(3, 4)), jnp.max(mean_scores, axis=3))
    top = jnp.maximum(top, own_score)
    row_weight = jnp.where(allowed, jnp.exp(scores - top[..., None, None]), 0.0)
    mean_weight = jnp.where(mean_allowed, jnp.exp(mean_scores - top[..., None]), 0.0)
    own_weight = jnp.where(lane == 0, jnp.exp(own_score - top), 0.0)
    mass = jnp.sum(row_weight, axis=(3, 4)) + jnp.sum(mean_weight, axis=3) + own_weight
    total = jnp.einsum(
        "rngpm,pmnd->rngd",
        row_weight,
        row_values.astype(jnp.float32),
        precision=lax.Precision.HIGHEST,
    )
    total = total + jnp.einsum(
        "rngp,pnd->rngd",
        mean_weight,
        mean_values.astype(jnp.float32),
        precision=lax.Precision.HIGHEST,
    )
    total = total + own_weight[..., None] * value_new[:, :, None, :]

    some = mass > 0.0
    level = jnp.where(some, top + jnp.log(jnp.where(some, mass, 1.0)), negative)
    means_out = total / jnp.where(some, mass, 1.0)[..., None]
    own = HEADS * HD // groups
    parts = jnp.stack([means_out, jnp.broadcast_to(level[..., None], total.shape)])
    parts = jnp.transpose(parts.reshape(2, R_DEV, groups, own), (2, 1, 0, 3))
    parts = jnp.broadcast_to(
        parts.reshape(groups, 1, R_DEV, 2 * own), (groups, lanes, R_DEV, 2 * own)
    ).reshape(groups * lanes, R_DEV, 2 * own)
    came = lax.all_to_all(parts, both_axes, 0, 0, tiled=True)
    came = came.reshape(groups, lanes, R_DEV, 2 * own)
    outs, levels = came[..., :own], came[..., own:]
    weights = jnp.exp(levels - jnp.max(levels, axis=1, keepdims=True))
    attention = jnp.sum(outs * weights, axis=1) / jnp.sum(weights, axis=1)
    attention = attention.reshape(requests, own).astype(jnp.bfloat16)
    back = jnp.sum(
        jnp.where(holders[None, :] == everyone[:, None], everyone[None, :], 0), axis=1
    )
    projected = jnp.dot(
        pick_rows(back, attention), output_weight, preferred_element_type=jnp.float32
    )
    projected = projected + jnp.where(group == 0, hidden_in.astype(jnp.float32), 0.0)

    share = groups // lanes
    blocks = jnp.moveaxis(projected.reshape(requests, share, 1, features), 0, 2)
    blocks = jnp.broadcast_to(blocks, (share, lanes, requests, features))
    mid = jnp.sum(exchange(blocks.reshape(groups, requests, features)), axis=0)
    mid = to_block_owner(mid.astype(jnp.bfloat16)).astype(jnp.float32)
    squares = jnp.sum(mid * mid, axis=1, keepdims=True)
    gain_here = lax.dynamic_slice_in_dim(feedforward_gain, group * features, features, 0)
    inputs_mid = (mid * gain_here).astype(jnp.bfloat16)
    local_units = gate_weight.shape[1]
    piece = local_units // groups
    gates = jnp.dot(inputs_mid, gate_weight, preferred_element_type=jnp.float32)
    ups = jnp.dot(inputs_mid, up_weight, preferred_element_type=jnp.float32)
    both = jnp.concatenate(
        [
            gates.reshape(requests, groups, piece),
            ups.reshape(requests, groups, piece),
            jnp.broadcast_to(squares[:, :, None], (requests, groups, 1)),
        ],
        axis=2,
    )
    sums = jnp.sum(exchange(jnp.swapaxes(both, 0, 1)), axis=0)
    factor = lax.rsqrt(sums[:, 2 * piece :] / D + epsilon)
    gate = sums[:, :piece] * factor
    active = (jax.nn.silu(gate) * (sums[:, piece : 2 * piece] * factor)).astype(jnp.bfloat16)
    active_here = lax.all_gather(to_block_owner(active), "head", axis=1, tiled=True)
    down = jnp.dot(active_here, down_weight, preferred_element_type=jnp.float32)
    residual = [jnp.where(group == lane * share + k, mid, 0.0) for k in range(share)]
    down = down + jnp.concatenate(residual, axis=1)
    result = whole_sum(down).astype(jnp.bfloat16)
    return (compact, summaries, result)


TILE = 128
bfloat = jnp.bfloat16
single = jnp.float32


def iota(shape, axis):
    return lax.broadcasted_iota(jnp.int32, shape, axis)


def run(kernel, outs, far, near, scratch=(), flops=0):
    in_specs = [pl.BlockSpec(memory_space=pltpu.HBM) for _ in far]
    in_specs += [pl.BlockSpec(memory_space=pltpu.VMEM) for _ in near]
    moved = sum(a.size * a.dtype.itemsize for a in [*far, *near, *outs])
    return pl.pallas_call(
        kernel,
        out_shape=list(outs),
        in_specs=in_specs,
        out_specs=[pl.BlockSpec(memory_space=pltpu.VMEM) for _ in outs],
        scratch_shapes=list(scratch),
        compiler_params=pltpu.CompilerParams(vmem_limit_bytes=16 * 2**20),
        cost_estimate=pl.CostEstimate(flops=flops, bytes_accessed=moved, transcendentals=0),
    )(*[pltpu.with_memory_space_constraint(a, pltpu.HBM) for a in far], *near)


def fetch(sources, targets, done):
    copies = [
        pltpu.make_async_copy(source, target, done.at[k])
        for k, (source, target) in enumerate(zip(sources, targets))
    ]
    for copy in copies:
        copy.start()
    return copies


def local_like(*arrays):
    return [pltpu.VMEM(a.shape, a.dtype) for a in arrays]


def scalar_like(*arrays):
    return [pltpu.SMEM(a.shape, a.dtype) for a in arrays]


def row_order(source, count, to_holder):
    first, second = iota((count, count), 0), iota((count, count), 1)
    if not to_holder:
        first, second = second, first
    order = (first == second) & (first % R_DEV == 0)
    for c in range(source.shape[1]):
        order = order | ((first == source[0, c] * R_DEV + 1) & (second == c * R_DEV + 1))
    return order.astype(single).astype(bfloat)


def shaped(shape, dtype):
    return jax.ShapeDtypeStruct(shape, dtype)


def first_kernel(
    source_far, gain_far, weight_far, whole, sent, source, gain, weight, wide, done
):
    copies = fetch((source_far, gain_far, weight_far), (source, gain, weight), done)
    rows = whole.shape[0]
    groups = rows // R_DEV
    lanes = sent.shape[0] // groups
    columns, features = weight.shape
    values = whole[...].astype(single)
    factor = lax.rsqrt(jnp.mean(values * values, axis=1, keepdims=True) + epsilon)
    here = pl.ds(pl.multiple_of(lax.axis_index("req") * features, features), features)
    wide[...] = jnp.zeros_like(wide)
    for copy in copies:
        copy.wait()
    normed = (whole[:, here].astype(single) * factor * gain[:, here]).astype(bfloat)
    order = row_order(source, rows, True)
    normed = jnp.dot(order, normed, preferred_element_type=single).astype(bfloat)
    wide[:, :columns] = dot_rows(normed, weight[...])
    for g in range(groups):
        tile = jnp.concatenate(
            [
                wide[R_DEV * g : R_DEV * (g + 1), TILE * j : TILE * (j + 1)]
                for j in range(wide.shape[1] // TILE)
            ],
            axis=0,
        )
        for k in range(lanes):
            sent[g * lanes + k] = tile


def dot_rows(left, right):
    return lax.dot_general(left, right, (((1,), (1,)), ((), ())), preferred_element_type=single)


def prepare_kernel(*refs):
    far, refs = refs[:12], refs[12:]
    (compact, summaries, kept, added, tables, own, one, two, three), refs = refs[:9], refs[9:]
    near, (ordered, plain, dealt, done) = refs[:12], refs[12:]
    copies = fetch(far, near, done)
    (dest, lengths, source, table, keep, weights, query_gain, key_gain, turns) = near[:9]
    pages, gate, up = near[9:]
    group = lax.axis_index("req")
    lane = lax.axis_index("head")
    lanes = lax.axis_size("head")
    for copy in copies[:9]:
        copy.wait()

    carried = 0
    for c in range(source.shape[1]):
        carried = carried + jnp.where(source[0, c] == group, c, 0)
    held_len = (lengths[0, group * R_DEV], lengths[0, carried * R_DEV + 1])
    count, rows, _ = pages.shape
    owned = []
    for r in range(R_DEV):
        slots = []
        for i in range(table.shape[1] // lanes):
            j = i * lanes + lane
            slots.append(jnp.where(j < held_len[r], table[r, j], -1))
        owned.append(slots)

    def owner(r, p):
        found = owned[r][0] == p
        for slot in owned[r][1:]:
            found = found | (slot == p)
        return found

    row = iota((32, TILE), 0)
    odd = (row & 1) == 1
    half_rows = turns.shape[0] // 2
    for part in range(2):
        pair = [turns[pl.ds(part * half_rows + held_len[r], 1), :] for r in range(R_DEV)]
        tables[32 * part : 32 * (part + 1), :] = jnp.where(odd, pair[1], pair[0])
    query_rows = HEADS * HD // TILE * R_DEV
    for c in range(TILE // HD):
        columns = slice(HD * c, HD * (c + 1))
        tables[64 : 64 + query_rows, columns] = jnp.broadcast_to(
            query_gain[...], (query_rows, HD)
        )
        tables[64 + query_rows : 96, columns] = jnp.broadcast_to(
            key_gain[...], (32 - query_rows, HD)
        )

    column = iota((1, TILE), 1)
    entries = count * KEEP
    added[...] = jnp.full_like(added, negative)
    extra = [
        jnp.where((column == count + r) & (lane == 0), 0.0, negative) for r in range(R_DEV)
    ]
    weight_columns = weights[...].T
    rows_of = iota((rows, KEEP), 0)
    place = iota((rows, KEEP), 1)
    copies[9].wait()
    for p in range(count):
        picks = (keep[p : p + 1, :] == rows_of).astype(single)
        dropped = weight_columns[:, p : p + 1] * (1.0 - jnp.sum(picks, axis=1, keepdims=True))
        total = jnp.sum(dropped, axis=0, keepdims=True)
        high = dropped.astype(bfloat).astype(single)
        rest = dropped - high
        middle = rest.astype(bfloat).astype(single)
        terms = jnp.where(place == 0, high, jnp.where(place == 1, middle, rest - middle))
        terms = jnp.where(place < 3, terms, 0.0)
        left = jnp.concatenate([picks, terms], axis=1).astype(bfloat)
        both = lax.dot_general(
            left, pages[p], (((0,), (0,)), ((), ())), preferred_element_type=single
        )
        rows_kept = both[:KEEP].astype(bfloat)
        kept[KEEP * p : KEEP * (p + 1), :] = rows_kept
        slot = dest[0, p]
        start = pl.multiple_of((slot & 1) * KEEP, KEEP)
        compact[slot >> 1, pl.ds(start, KEEP), :] = rows_kept
        mean = both[KEEP : KEEP + 1] + both[KEEP + 1 : KEEP + 2] + both[KEEP + 2 : KEEP + 3]
        mean = mean / total
        plain[p : p + 1, :] = mean
        ordered[pl.ds(slot, 1), :] = mean
        live = jnp.where(keep[p : p + 1, :] >= 0, 0.0, negative)
        for r in range(R_DEV):
            here = owner(r, p)
            added[r : r + 1, KEEP * p : KEEP * (p + 1)] = jnp.where(here, live, negative)
            level = jnp.where(here, jnp.log(total), negative)
            extra[r] = jnp.where(column == p, level, extra[r])
    for r in range(R_DEV):
        added[r : r + 1, entries : entries + TILE] = extra[r]
    plain[count:, :] = jnp.zeros_like(plain[count:, :])
    kept[entries:, :] = plain[...].astype(bfloat)
    summaries[...] = ordered[...].astype(bfloat)

    outs = (own, one, two, three)
    piece = own.shape[1] // 4
    block = lanes * piece
    for copy in copies[10:]:
        copy.wait()
    for k in range(lanes):
        for b in range(2):
            columns = slice(b * block + k * piece, b * block + (k + 1) * piece)
            start = 2 * b * piece
            dealt[k, :, start : start + piece] = gate[:, columns].astype(single)
            dealt[k, :, start + piece : start + 2 * piece] = up[:, columns].astype(single)
    for turn in range(lanes):
        outs[turn][...] = dealt[lane ^ turn].astype(bfloat)


def attend_kernel(came, kept, added, tables, sent, x, extra_k, extra_v, out):
    lanes = lax.axis_size("head")
    groups = came.shape[0] // lanes
    width = (HEADS + 2 * KVH) * HD // lanes
    span = -(-KVH * HD // TILE) * TILE
    key_cols = slice(0, span)
    value_cols = slice(KVW - span, KVW)
    first_key = HEADS * HD // TILE * R_DEV
    scale = HD ** (-0.5)
    x[...] = jnp.zeros_like(x)
    column = iota((8, TILE), 1)
    for k in range(lanes):
        tile = came[k]
        for g in range(1, groups):
            tile = tile + came[g * lanes + k]
        tile = tile.astype(bfloat).astype(single)
        base, shift = divmod(width * k, TILE)
        base = base * R_DEV
        if shift:
            tile = pltpu.roll(tile, shift, 1)
            x[base + 2 : base + 10, :] += jnp.where(column < shift, tile, 0.0)
        x[base : base + 8, :] += jnp.where(column >= shift, tile, 0.0)
    values = x[...]
    same_head = (iota((TILE, TILE), 0) // HD == iota((TILE, TILE), 1) // HD).astype(single)
    squares = jnp.dot(
        values * values, same_head, precision=lax.Precision.HIGHEST, preferred_element_type=single
    )
    normed = values * lax.rsqrt(squares / HD + epsilon) * tables[64:96, :]
    early = iota(values.shape, 1) % HD < HD // 2
    swapped = jnp.where(
        early, pltpu.roll(normed, TILE - HD // 2, 1), pltpu.roll(normed, HD // 2, 1)
    )
    turned = normed * tables[0:32, :] + swapped * tables[32:64, :]
    turned = turned.astype(bfloat).astype(single)

    rows = 24
    row = iota((rows, TILE), 0)
    half = iota((rows, TILE), 1) // HD
    key_head = row >> 2
    query = jnp.where(row < first_key, turned[:rows], 0.0)
    other = pltpu.roll(query, HD, 1)
    queries = []
    for u in range(2):
        placed = jnp.where(
            half == (key_head & 1), jnp.where((key_head & 1) == u, query, other), 0.0
        )
        queries.append(
            jnp.concatenate(
                [jnp.where((key_head >> 1) == c, placed, 0.0) for c in range(span // TILE)], axis=1
            )
        )
    queries = jnp.concatenate(queries, axis=0).astype(bfloat)

    extras = extra_k.shape[0]
    entries = kept.shape[0] - extras
    count = entries // KEEP
    extra_k[...] = kept[entries:, key_cols].astype(single)
    extra_v[...] = kept[entries:, value_cols].astype(single)
    first_value = first_key + KVH * HD // TILE * R_DEV
    for c in range(span // TILE):
        at = slice(c * TILE, (c + 1) * TILE)
        r = first_key + R_DEV * c
        extra_k[count : count + R_DEV, at] = turned[r : r + R_DEV]
        r = first_value + R_DEV * c
        extra_v[count : count + R_DEV, at] = values[r : r + R_DEV]

    def by_request(columns, size):
        odd = (iota((2 * rows, size), 0) & 1) == 1
        return jnp.where(odd, added[1:2, columns], added[0:1, columns])

    scores = dot_rows(queries, kept[:entries, key_cols]) * scale
    scores = scores + by_request(slice(0, entries), entries)
    extra = dot_rows(queries, extra_k[...].astype(bfloat)) * scale
    extra = extra + by_request(slice(entries, entries + extras), extras)
    top = jnp.maximum(
        jnp.max(scores, axis=1, keepdims=True), jnp.max(extra, axis=1, keepdims=True)
    )
    weight = jnp.where(scores > 0.5 * negative, jnp.exp(scores - top), 0.0)
    extra_weight = jnp.where(extra > 0.5 * negative, jnp.exp(extra - top), 0.0)
    mass = jnp.sum(weight, axis=1, keepdims=True) + jnp.sum(extra_weight, axis=1, keepdims=True)

    def weighted(parts, right):
        high = parts.astype(bfloat)
        low = (parts - high.astype(single)).astype(bfloat)
        return jnp.dot(high, right, preferred_element_type=single) + jnp.dot(
            low, right, preferred_element_type=single
        )

    total = weighted(weight, kept[:entries, value_cols]) + weighted(
        extra_weight, extra_v[...].astype(bfloat)
    )
    some = mass > 0.0
    mass = jnp.where(some, mass, 1.0)
    total = total / mass
    level = jnp.where(some, top + jnp.log(mass), negative)

    slot = key_head + (KVW // 2 - (KVW - span)) // HD
    results = []
    for u in range(2):
        mine = total[rows * u : rows * (u + 1)]
        picked = mine[:, :TILE]
        for c in range(1, span // TILE):
            picked = jnp.where((slot >> 1) == c, mine[:, c * TILE : (c + 1) * TILE], picked)
        results.append(jnp.where((slot & 1) == u, picked, pltpu.roll(picked, HD, 1)))
    out[:rows, :] = jnp.where(half == 0, results[0], results[1])
    out[rows:, :] = jnp.where(half == 0, level[:rows], level[rows:])
    own = HEADS * HD // groups
    for g in range(groups):
        r = own * g // TILE * R_DEV
        tile = jnp.concatenate([out[r : r + 4, :], out[rows + r : rows + r + 4, :]], axis=0)
        for k in range(lanes):
            sent[g * lanes + k] = tile


def project_kernel(source_far, weight_far, came, sent, source, weight, rows, done):
    copies = fetch((source_far, weight_far), (source, weight), done)
    lanes = lax.axis_size("head")
    groups = came.shape[0] // lanes
    features = weight.shape[0]
    requests = rows.shape[0]
    for g in range(groups):
        tiles = [came[g * lanes + k] for k in range(lanes)]
        levels = [tile[4:8] for tile in tiles]
        top = jnp.maximum(
            jnp.maximum(levels[0], levels[1]), jnp.maximum(levels[2], levels[3])
        )
        shares = [jnp.exp(level - top) for level in levels]
        mixed = sum(share * tile[0:4] for share, tile in zip(shares, tiles)) / sum(shares)
        rows[R_DEV * g : R_DEV * (g + 1), :TILE] = mixed[:R_DEV]
        rows[R_DEV * g : R_DEV * (g + 1), TILE:] = mixed[R_DEV:]
    shift = lax.rem(2 * TILE - lax.rem(lax.axis_index("req") * features, TILE), 2 * TILE)
    attention = pltpu.roll(rows[...].astype(bfloat).astype(single), shift, 1)
    for copy in copies:
        copy.wait()
    order = row_order(source, requests, False)
    attention = jnp.dot(order, attention.astype(bfloat), preferred_element_type=single)
    attention = attention[:, :features].astype(bfloat)
    projected = jnp.dot(attention, weight[...], preferred_element_type=single).astype(bfloat)
    width = sent.shape[2]
    share = groups // lanes
    for g in range(groups):
        b = g % share
        for k in range(lanes):
            sent[g * lanes + k] = projected[:, width * b : width * (b + 1)]


def units_kernel(gain_far, came, whole, own, one, two, three, sent, mid_out, gain, done):
    (copy,) = fetch((gain_far,), (gain,), done)
    weights = (own, one, two, three)
    lanes = len(weights)
    devices, rows, features = came.shape
    groups = devices // lanes
    share = groups // lanes
    group = lax.axis_index("req")
    lane = lax.axis_index("head")
    here = pl.ds(pl.multiple_of(group * features, features), features)
    mid = whole[:, here].astype(single)
    for g in range(groups):
        mid = mid + came[g * lanes + group // share].astype(single)
    mid = mid.astype(bfloat)
    mid_out[...] = mid
    mid = mid.astype(single)
    squares = jnp.sum(mid * mid, axis=1, keepdims=True)
    width = own.shape[1] // 2
    place = iota((rows, sent.shape[2] - width), 1)
    high = squares.astype(bfloat).astype(single)
    rest = squares - high
    middle = rest.astype(bfloat).astype(single)
    terms = jnp.where(place == 0, high, jnp.where(place == 1, middle, rest - middle))
    terms = jnp.where(place < 3, terms, 0.0).astype(bfloat)
    copy.wait()
    inputs = (mid * gain[:, here]).astype(bfloat)
    for turn in range(lanes):
        units = jnp.dot(inputs, weights[turn][...], preferred_element_type=single)
        target = (lane ^ turn) * share
        for b in range(share):
            sent[target + b, :, :width] = units[:, width * b : width * (b + 1)].astype(bfloat)
            sent[target + b, :, width:] = terms


def summed(came):
    total = came[0].astype(single)
    for g in range(1, came.shape[0]):
        total = total + came[g].astype(single)
    return total


def active_kernel(came, active):
    total = summed(came)
    piece = active.shape[1]
    squares = total[:, 2 * piece : 2 * piece + 1] + total[:, 2 * piece + 1 : 2 * piece + 2]
    squares = squares + total[:, 2 * piece + 2 : 2 * piece + 3]
    factor = lax.rsqrt(squares / D + epsilon)
    gate = total[:, :piece] * factor
    up = total[:, piece : 2 * piece] * factor
    active[...] = (gate / (1.0 + jnp.exp(-gate)) * up).astype(bfloat)


def down_kernel(active, weight, mid, sent):
    groups, rows, width = sent.shape
    lanes, _, piece = active.shape
    half = mid.shape[1]
    share = width // half
    down = jnp.dot(active[0], weight[:piece, :], preferred_element_type=single)
    for k in range(1, lanes):
        down = down + jnp.dot(
            active[k], weight[piece * k : piece * (k + 1), :], preferred_element_type=single
        )
    residual = mid[...].astype(single)
    group = lax.axis_index("req")
    lane = lax.axis_index("head")
    for b in range(share):
        columns = slice(half * b, half * (b + 1))
        mine = group == lane * share + b
        total = (down[:, columns] + jnp.where(mine, residual, 0.0)).astype(bfloat)
        for g in range(groups):
            sent[g, :, columns] = total


def result_kernel(came, result):
    result[...] = summed(came).astype(bfloat)


def rotation_table():
    half = HD // 2
    size = -(-(NP + 1) // 8) * 8
    frequency = 10000.0 ** (-np.arange(half) / half)
    angles = PAGE * np.arange(size)[:, None] * frequency[None, :]
    cosine, sine = np.cos(angles), np.sin(angles)
    wide = [np.tile(np.concatenate(pair, axis=1), (1, TILE // HD)) for pair in
            ((cosine, cosine), (-sine, sine))]
    return jnp.asarray(np.concatenate(wide), dtype=single)


def swapped_lanes(value, turn):
    lanes = lax.axis_size("head")
    return lax.ppermute(value, "head", [(k, k ^ turn) for k in range(lanes)])


def on_device(
    hidden_in,
    attention_gain,
    query_gain,
    key_gain,
    feedforward_gain,
    input_weight,
    output_weight,
    gate_weight,
    up_weight,
    down_weight,
    old_cache,
    keep_rows,
    drop_weights,
    dest_slots,
    lengths,
    page_table,
    source,
):
    groups = lax.axis_size("req")
    lanes = lax.axis_size("head")
    requests = hidden_in.shape[0]
    pages_here = old_cache.shape[0]
    devices = groups * lanes
    features = D // groups
    piece = gate_weight.shape[1] // groups
    copies = pltpu.SemaphoreType.DMA

    whole = lax.all_gather(hidden_in, "head", axis=1, tiled=True)
    columns = input_weight.shape[1]
    padded = -(-columns // TILE) * TILE
    holds = source[None, :]
    gain = attention_gain[None, :]
    weight = input_weight.T
    (sent,) = run(
        first_kernel,
        [shaped((devices, R_DEV * padded // TILE, TILE), single)],
        [holds, gain, weight],
        [whole],
        [
            *scalar_like(holds),
            *local_like(gain, weight),
            pltpu.VMEM((requests, padded), single),
            copies((3,)),
        ],
        2 * requests * features * columns,
    )
    came = lax.all_to_all(sent, both_axes, 0, 0, tiled=True)

    scalars = [dest_slots, lengths[None, :], holds, page_table]
    arrays = [
        keep_rows,
        drop_weights,
        query_gain[None, :],
        key_gain[None, :],
        rotation_table(),
        old_cache,
        gate_weight,
        up_weight,
    ]
    entries = pages_here * KEEP
    extras = 16
    compact, summaries, kept, added, tables, own_units, *other_units = run(
        prepare_kernel,
        [
            shaped((pages_here // 2, PAGE, KVW), bfloat),
            shaped((pages_here, KVW), bfloat),
            shaped((entries + extras, KVW), bfloat),
            shaped((8, entries + TILE), single),
            shaped((96, TILE), single),
        ]
        + [shaped((features, 4 * piece), bfloat)] * lanes,
        scalars + arrays,
        [],
        [
            *scalar_like(*scalars),
            *local_like(*arrays),
            pltpu.VMEM((pages_here, KVW), single),
            pltpu.VMEM((extras, KVW), single),
            pltpu.VMEM((lanes, features, 4 * piece), single),
            copies((len(scalars + arrays),)),
        ],
        2 * pages_here * TILE * PAGE * KVW,
    )
    span = -(-KVH * HD // TILE) * TILE
    (parts,) = run(
        attend_kernel,
        [shaped((devices, 8, TILE), single)],
        [],
        [came, kept, added, tables],
        [
            pltpu.VMEM((32, TILE), single),
            pltpu.VMEM((extras, span), single),
            pltpu.VMEM((extras, span), single),
            pltpu.VMEM((48, TILE), single),
        ],
        6 * 48 * entries * span,
    )
    *other_units, _ = lax.optimization_barrier((*other_units, parts))
    units = [swapped_lanes(other_units[turn - 1], turn) for turn in range(1, lanes)]
    came = lax.all_to_all(parts, both_axes, 0, 0, tiled=True)
    came, *units[:2] = lax.optimization_barrier((came, *units[:2]))
    units = [own_units, *units]
    (sent,) = run(
        project_kernel,
        [shaped((devices, requests, features), bfloat)],
        [holds, output_weight],
        [came],
        [
            *scalar_like(holds),
            *local_like(output_weight),
            pltpu.VMEM((requests, 2 * TILE), single),
            copies((2,)),
        ],
        2 * requests * output_weight.size,
    )
    came = lax.all_to_all(sent, both_axes, 0, 0, tiled=True)
    gain = feedforward_gain[None, :]
    sent, mid = run(
        units_kernel,
        [shaped((groups, requests, 3 * TILE), bfloat), shaped((requests, features), bfloat)],
        [gain],
        [came, whole, *units],
        [*local_like(gain), copies((1,))],
        4 * requests * gate_weight.size,
    )
    (active,) = run(active_kernel, [shaped((requests, piece), bfloat)], [], [exchange(sent)])
    active = lax.all_gather(active, "head")
    (sent,) = run(
        down_kernel,
        [shaped((groups, requests, down_weight.shape[1]), bfloat)],
        [],
        [active, down_weight, mid],
        [],
        2 * requests * down_weight.size,
    )
    (result,) = run(
        result_kernel, [shaped((requests, down_weight.shape[1]), bfloat)], [], [exchange(sent)]
    )
    return (compact, summaries, result)


def solution(mesh):
    placed = (
        P(None, "head"),
        P(),
        P(),
        P(),
        P(),
        P("req", "head"),
        P("req", "head"),
        P("req", "head"),
        P("req", "head"),
        P("req", "head"),
        P(("req", "head"), None, None),
        P(("req", "head"), None),
        P(("req", "head"), None),
        P(("req", "head"), None),
        P(),
        P("req", None),
        P(),
    )
    return jax.shard_map(
        on_device if mesh.shape["req"] <= DIRECT else on_device_wide,
        mesh=mesh,
        in_specs=placed,
        out_specs=(P(("req", "head"), None, None), P(("req", "head"), None), P(None, "head")),
        check_vma=False,
    )
```

```python
import jax
import jax.numpy as jnp
import numpy as np
from jax import lax
from jax.experimental import pallas as pl
from jax.experimental.pallas import tpu as pltpu
from jax.sharding import PartitionSpec as P

D = 2048
HEADS = 20
KVH = 5
HD = 64
FF = 5120
PAGE = 128
KEEP = 64
NP = 16
R_DEV = 2
KVW = 640

DIRECT = 8

epsilon = 1e-06
negative = -1e30
both_axes = ("req", "head")


def rms_scale(values):
    return lax.rsqrt(jnp.mean(values * values, axis=-1, keepdims=True) + epsilon)


def rms_rows(values, gain):
    return values * rms_scale(values) * gain


def rotate(vectors, positions):
    half = vectors.shape[-1] // 2
    frequency = 10000.0 ** (-jnp.arange(half, dtype=jnp.float32) / half)
    angles = positions.astype(jnp.float32)[:, None] * frequency[None, :]
    cosine = jnp.cos(angles)[:, None, :]
    sine = jnp.sin(angles)[:, None, :]
    first = vectors[..., :half]
    second = vectors[..., half:]
    return jnp.concatenate(
        [first * cosine - second * sine, second * cosine + first * sine], axis=-1
    )


def compact_pages(pages, keep, weights):
    rows = jnp.arange(pages.shape[1], dtype=jnp.int32)
    picks = keep[:, :, None] == rows[None, None, :]
    kept = jnp.einsum(
        "pkr,prc->pkc", picks.astype(jnp.bfloat16), pages, preferred_element_type=jnp.float32
    ).astype(jnp.bfloat16)
    dropped = weights * (1.0 - jnp.sum(picks.astype(jnp.float32), axis=1))
    total = jnp.sum(dropped, axis=1)
    means = (
        jnp.einsum(
            "pr,prc->pc", dropped, pages.astype(jnp.float32), precision=lax.Precision.HIGHEST
        )
        / total[:, None]
    )
    return (kept, means.astype(jnp.bfloat16), jnp.log(total))


def held_request(rows, source):
    half = R_DEV // 2
    position = rows % R_DEV
    slot = rows // R_DEV * half + position - half
    continued = jnp.arange(source.shape[0], dtype=jnp.int32)
    matches = source[None, :] == slot[:, None]
    owner_cont = jnp.sum(jnp.where(matches, continued[None, :], 0), axis=1)
    carried = owner_cont // half * R_DEV + half + owner_cont % half
    return jnp.where(position < half, rows, carried)


def pick_rows(order, rows):
    chosen = order[:, None] == jnp.arange(rows.shape[0], dtype=jnp.int32)[None, :]
    return jnp.dot(
        chosen.astype(jnp.bfloat16), rows, preferred_element_type=jnp.float32
    ).astype(jnp.bfloat16)


def exchange(parts):
    return lax.all_to_all(parts, "req", split_axis=0, concat_axis=0, tiled=True)


def to_block_owner(rows):
    groups = lax.axis_size("req")
    lanes = lax.axis_size("head")
    per_lane = groups // lanes
    pairs = [
        (g * lanes + h, (per_lane * h + g // lanes) * lanes + g % lanes)
        for g in range(groups)
        for h in range(lanes)
    ]
    return lax.ppermute(rows, both_axes, pairs)


def whole_sum(partial):
    if lax.axis_size("req") > DIRECT:
        return lax.psum(partial, "req")
    groups = lax.axis_size("req")
    return jnp.sum(exchange(jnp.broadcast_to(partial[None], (groups,) + partial.shape)), axis=0)


def on_device_wide(
    hidden_in,
    attention_gain,
    query_gain,
    key_gain,
    feedforward_gain,
    input_weight,
    output_weight,
    gate_weight,
    up_weight,
    down_weight,
    old_cache,
    keep_rows,
    drop_weights,
    dest_slots,
    lengths,
    page_table,
    source,
):
    groups = lax.axis_size("req")
    lanes = lax.axis_size("head")
    group = lax.axis_index("req")
    lane = lax.axis_index("head")
    requests = hidden_in.shape[0]
    half = R_DEV // 2
    split = KVH * HD
    ratio = HEADS // KVH
    scale = HD ** (-0.5)
    pages_here = old_cache.shape[0]
    everyone = jnp.arange(requests, dtype=jnp.int32)
    holders = held_request(everyone, source)
    held = lax.dynamic_slice_in_dim(holders, group * R_DEV, R_DEV, 0)
    held_len = lengths[held]
    positions = held_len * PAGE

    whole = lax.all_gather(hidden_in, "head", axis=1, tiled=True)
    normed = rms_rows(whole.astype(jnp.float32), attention_gain).astype(jnp.bfloat16)
    features = D // groups
    inputs = pick_rows(holders, lax.dynamic_slice_in_dim(normed, group * features, features, 1))
    partial_qkv = jnp.dot(inputs, input_weight, preferred_element_type=jnp.float32)
    sent = jnp.broadcast_to(
        partial_qkv.reshape(groups, 1, R_DEV, -1), (groups, lanes, R_DEV, partial_qkv.shape[1])
    ).reshape(groups * lanes, R_DEV, -1)
    got = lax.all_to_all(sent, both_axes, split_axis=0, concat_axis=0, tiled=True)
    mixed = jnp.sum(got.reshape(groups, lanes, R_DEV, -1), axis=0).astype(jnp.bfloat16)
    held_qkv = jnp.swapaxes(mixed, 0, 1).reshape(R_DEV, -1).astype(jnp.float32)

    query = rotate(
        rms_rows(held_qkv[:, : HEADS * HD].reshape(R_DEV, HEADS, HD), query_gain), positions
    ).astype(jnp.bfloat16)
    key_new = rotate(
        rms_rows(held_qkv[:, HEADS * HD : (HEADS + KVH) * HD].reshape(R_DEV, KVH, HD), key_gain),
        positions,
    ).astype(jnp.bfloat16)
    value_new = held_qkv[:, (HEADS + KVH) * HD :].reshape(R_DEV, KVH, HD)
    kept, means, bias = compact_pages(old_cache, keep_rows, drop_weights)
    destination = dest_slots[0]
    fresh_ids = jnp.arange(pages_here, dtype=jnp.int32)
    inverse = jnp.sum(
        jnp.where(destination[None, :] == fresh_ids[:, None], fresh_ids[None, :], 0), axis=1
    )
    compact = kept[inverse].reshape(pages_here // 2, PAGE, KVW)
    summaries = means[inverse]
    per_lane = NP // lanes
    table = page_table.reshape(R_DEV, per_lane, lanes)
    mine = lax.dynamic_slice_in_dim(table, lane, 1, 2)[:, :, 0]
    logical = jnp.arange(per_lane, dtype=jnp.int32) * lanes + lane
    live = logical[None, :] < held_len[:, None]
    owner = jnp.any((mine[:, :, None] == fresh_ids[None, None, :]) & live[:, :, None], axis=1)
    query_groups = query.reshape(R_DEV, KVH, ratio, HD)
    row_keys = kept[:, :, :split].reshape(pages_here, KEEP, KVH, HD)
    row_values = kept[:, :, split:].reshape(pages_here, KEEP, KVH, HD)
    row_live = keep_rows >= 0
    allowed = owner[:, None, None, :, None] & row_live[None, None, None, :, :]
    scores = (
        jnp.einsum("rngd,pmnd->rngpm", query_groups, row_keys, preferred_element_type=jnp.float32)
        * scale
    )
    scores = jnp.where(allowed, scores, negative)
    mean_keys = means[:, :split].reshape(pages_here, KVH, HD)
    mean_values = means[:, split:].reshape(pages_here, KVH, HD)
    mean_scores = (
        jnp.einsum("rngd,pnd->rngp", query_groups, mean_keys, preferred_element_type=jnp.float32)
        * scale
        + bias[None, None, None, :]
    )
    mean_allowed = owner[:, None, None, :]
    mean_scores = jnp.where(mean_allowed, mean_scores, negative)
    own_score = (
        jnp.einsum("rngd,rnd->rng", query_groups, key_new, preferred_element_type=jnp.float32)
        * scale
    )
    own_score = jnp.where(lane == 0, own_score, negative)
    top = jnp.maximum(jnp.max(scores, axis=(3, 4)), jnp.max(mean_scores, axis=3))
    top = jnp.maximum(top, own_score)
    row_weight = jnp.where(allowed, jnp.exp(scores - top[..., None, None]), 0.0)
    mean_weight = jnp.where(mean_allowed, jnp.exp(mean_scores - top[..., None]), 0.0)
    own_weight = jnp.where(lane == 0, jnp.exp(own_score - top), 0.0)
    mass = jnp.sum(row_weight, axis=(3, 4)) + jnp.sum(mean_weight, axis=3) + own_weight
    total = jnp.einsum(
        "rngpm,pmnd->rngd",
        row_weight,
        row_values.astype(jnp.float32),
        precision=lax.Precision.HIGHEST,
    )
    total = total + jnp.einsum(
        "rngp,pnd->rngd",
        mean_weight,
        mean_values.astype(jnp.float32),
        precision=lax.Precision.HIGHEST,
    )
    total = total + own_weight[..., None] * value_new[:, :, None, :]

    some = mass > 0.0
    level = jnp.where(some, top + jnp.log(jnp.where(some, mass, 1.0)), negative)
    means_out = total / jnp.where(some, mass, 1.0)[..., None]
    own = HEADS * HD // groups
    parts = jnp.stack([means_out, jnp.broadcast_to(level[..., None], total.shape)])
    parts = jnp.transpose(parts.reshape(2, R_DEV, groups, own), (2, 1, 0, 3))
    parts = jnp.broadcast_to(
        parts.reshape(groups, 1, R_DEV, 2 * own), (groups, lanes, R_DEV, 2 * own)
    ).reshape(groups * lanes, R_DEV, 2 * own)
    came = lax.all_to_all(parts, both_axes, 0, 0, tiled=True)
    came = came.reshape(groups, lanes, R_DEV, 2 * own)
    outs, levels = came[..., :own], came[..., own:]
    weights = jnp.exp(levels - jnp.max(levels, axis=1, keepdims=True))
    attention = jnp.sum(outs * weights, axis=1) / jnp.sum(weights, axis=1)
    attention = attention.reshape(requests, own).astype(jnp.bfloat16)
    back = jnp.sum(
        jnp.where(holders[None, :] == everyone[:, None], everyone[None, :], 0), axis=1
    )
    projected = jnp.dot(
        pick_rows(back, attention), output_weight, preferred_element_type=jnp.float32
    )
    projected = projected + jnp.where(group == 0, hidden_in.astype(jnp.float32), 0.0)

    share = groups // lanes
    blocks = jnp.moveaxis(projected.reshape(requests, share, 1, features), 0, 2)
    blocks = jnp.broadcast_to(blocks, (share, lanes, requests, features))
    mid = jnp.sum(exchange(blocks.reshape(groups, requests, features)), axis=0)
    mid = to_block_owner(mid.astype(jnp.bfloat16)).astype(jnp.float32)
    squares = jnp.sum(mid * mid, axis=1, keepdims=True)
    gain_here = lax.dynamic_slice_in_dim(feedforward_gain, group * features, features, 0)
    inputs_mid = (mid * gain_here).astype(jnp.bfloat16)
    local_units = gate_weight.shape[1]
    piece = local_units // groups
    gates = jnp.dot(inputs_mid, gate_weight, preferred_element_type=jnp.float32)
    ups = jnp.dot(inputs_mid, up_weight, preferred_element_type=jnp.float32)
    both = jnp.concatenate(
        [
            gates.reshape(requests, groups, piece),
            ups.reshape(requests, groups, piece),
            jnp.broadcast_to(squares[:, :, None], (requests, groups, 1)),
        ],
        axis=2,
    )
    sums = jnp.sum(exchange(jnp.swapaxes(both, 0, 1)), axis=0)
    factor = lax.rsqrt(sums[:, 2 * piece :] / D + epsilon)
    gate = sums[:, :piece] * factor
    active = (jax.nn.silu(gate) * (sums[:, piece : 2 * piece] * factor)).astype(jnp.bfloat16)
    active_here = lax.all_gather(to_block_owner(active), "head", axis=1, tiled=True)
    down = jnp.dot(active_here, down_weight, preferred_element_type=jnp.float32)
    residual = [jnp.where(group == lane * share + k, mid, 0.0) for k in range(share)]
    down = down + jnp.concatenate(residual, axis=1)
    result = whole_sum(down).astype(jnp.bfloat16)
    return (compact, summaries, result)


TILE = 128
bfloat = jnp.bfloat16
single = jnp.float32


def iota(shape, axis):
    return lax.broadcasted_iota(jnp.int32, shape, axis)


def run(kernel, outs, far, near, scratch=(), flops=0):
    in_specs = [pl.BlockSpec(memory_space=pltpu.HBM) for _ in far]
    in_specs += [pl.BlockSpec(memory_space=pltpu.VMEM) for _ in near]
    moved = sum(a.size * a.dtype.itemsize for a in [*far, *near, *outs])
    return pl.pallas_call(
        kernel,
        out_shape=list(outs),
        in_specs=in_specs,
        out_specs=[pl.BlockSpec(memory_space=pltpu.VMEM) for _ in outs],
        scratch_shapes=list(scratch),
        compiler_params=pltpu.CompilerParams(vmem_limit_bytes=16 * 2**20),
        cost_estimate=pl.CostEstimate(flops=flops, bytes_accessed=moved, transcendentals=0),
    )(*[pltpu.with_memory_space_constraint(a, pltpu.HBM) for a in far], *near)


def fetch(sources, targets, done):
    copies = [
        pltpu.make_async_copy(source, target, done.at[k])
        for k, (source, target) in enumerate(zip(sources, targets))
    ]
    for copy in copies:
        copy.start()
    return copies


def local_like(*arrays):
    return [pltpu.VMEM(a.shape, a.dtype) for a in arrays]


def scalar_like(*arrays):
    return [pltpu.SMEM(a.shape, a.dtype) for a in arrays]


def row_order(source, count, to_holder):
    first, second = iota((count, count), 0), iota((count, count), 1)
    if not to_holder:
        first, second = second, first
    order = (first == second) & (first % R_DEV == 0)
    for c in range(source.shape[1]):
        order = order | ((first == source[0, c] * R_DEV + 1) & (second == c * R_DEV + 1))
    return order.astype(single).astype(bfloat)


def shaped(shape, dtype):
    return jax.ShapeDtypeStruct(shape, dtype)


def first_kernel(
    source_far, gain_far, weight_far, whole, sent, source, gain, weight, wide, done
):
    copies = fetch((source_far, gain_far, weight_far), (source, gain, weight), done)
    rows = whole.shape[0]
    groups = rows // R_DEV
    lanes = sent.shape[0] // groups
    columns, features = weight.shape
    values = whole[...].astype(single)
    factor = lax.rsqrt(jnp.mean(values * values, axis=1, keepdims=True) + epsilon)
    here = pl.ds(pl.multiple_of(lax.axis_index("req") * features, features), features)
    wide[...] = jnp.zeros_like(wide)
    for copy in copies:
        copy.wait()
    normed = (whole[:, here].astype(single) * factor * gain[:, here]).astype(bfloat)
    order = row_order(source, rows, True)
    normed = jnp.dot(order, normed, preferred_element_type=single).astype(bfloat)
    wide[:, :columns] = dot_rows(normed, weight[...])
    for g in range(groups):
        tile = jnp.concatenate(
            [
                wide[R_DEV * g : R_DEV * (g + 1), TILE * j : TILE * (j + 1)]
                for j in range(wide.shape[1] // TILE)
            ],
            axis=0,
        )
        for k in range(lanes):
            sent[g * lanes + k] = tile


def dot_rows(left, right):
    return lax.dot_general(left, right, (((1,), (1,)), ((), ())), preferred_element_type=single)


def prepare_kernel(*refs):
    far, refs = refs[:10], refs[10:]
    (compact, summaries, kept, added, tables), refs = refs[:5], refs[5:]
    near, (ordered, plain, done) = refs[:10], refs[10:]
    copies = fetch(far, near, done)
    (dest, lengths, source, table, keep, weights, query_gain, key_gain, turns) = near[:9]
    pages = near[9]
    group = lax.axis_index("req")
    lane = lax.axis_index("head")
    lanes = lax.axis_size("head")
    for copy in copies[:9]:
        copy.wait()

    carried = 0
    for c in range(source.shape[1]):
        carried = carried + jnp.where(source[0, c] == group, c, 0)
    held_len = (lengths[0, group * R_DEV], lengths[0, carried * R_DEV + 1])
    count, rows, _ = pages.shape
    owned = []
    for r in range(R_DEV):
        slots = []
        for i in range(table.shape[1] // lanes):
            j = i * lanes + lane
            slots.append(jnp.where(j < held_len[r], table[r, j], -1))
        owned.append(slots)

    def owner(r, p):
        found = owned[r][0] == p
        for slot in owned[r][1:]:
            found = found | (slot == p)
        return found

    row = iota((32, TILE), 0)
    odd = (row & 1) == 1
    half_rows = turns.shape[0] // 2
    for part in range(2):
        pair = [turns[pl.ds(part * half_rows + held_len[r], 1), :] for r in range(R_DEV)]
        tables[32 * part : 32 * (part + 1), :] = jnp.where(odd, pair[1], pair[0])
    query_rows = HEADS * HD // TILE * R_DEV
    for c in range(TILE // HD):
        columns = slice(HD * c, HD * (c + 1))
        tables[64 : 64 + query_rows, columns] = jnp.broadcast_to(
            query_gain[...], (query_rows, HD)
        )
        tables[64 + query_rows : 96, columns] = jnp.broadcast_to(
            key_gain[...], (32 - query_rows, HD)
        )

    column = iota((1, TILE), 1)
    entries = count * KEEP
    added[...] = jnp.full_like(added, negative)
    extra = [
        jnp.where((column == count + r) & (lane == 0), 0.0, negative) for r in range(R_DEV)
    ]
    weight_columns = weights[...].T
    rows_of = iota((rows, KEEP), 0)
    place = iota((rows, KEEP), 1)
    copies[9].wait()
    for p in range(count):
        picks = (keep[p : p + 1, :] == rows_of).astype(single)
        dropped = weight_columns[:, p : p + 1] * (1.0 - jnp.sum(picks, axis=1, keepdims=True))
        total = jnp.sum(dropped, axis=0, keepdims=True)
        high = dropped.astype(bfloat).astype(single)
        rest = dropped - high
        middle = rest.astype(bfloat).astype(single)
        terms = jnp.where(place == 0, high, jnp.where(place == 1, middle, rest - middle))
        terms = jnp.where(place < 3, terms, 0.0)
        left = jnp.concatenate([picks, terms], axis=1).astype(bfloat)
        both = lax.dot_general(
            left, pages[p], (((0,), (0,)), ((), ())), preferred_element_type=single
        )
        rows_kept = both[:KEEP].astype(bfloat)
        kept[KEEP * p : KEEP * (p + 1), :] = rows_kept
        slot = dest[0, p]
        start = pl.multiple_of((slot & 1) * KEEP, KEEP)
        compact[slot >> 1, pl.ds(start, KEEP), :] = rows_kept
        mean = both[KEEP : KEEP + 1] + both[KEEP + 1 : KEEP + 2] + both[KEEP + 2 : KEEP + 3]
        mean = mean / total
        plain[p : p + 1, :] = mean
        ordered[pl.ds(slot, 1), :] = mean
        live = jnp.where(keep[p : p + 1, :] >= 0, 0.0, negative)
        for r in range(R_DEV):
            here = owner(r, p)
            added[r : r + 1, KEEP * p : KEEP * (p + 1)] = jnp.where(here, live, negative)
            level = jnp.where(here, jnp.log(total), negative)
            extra[r] = jnp.where(column == p, level, extra[r])
    for r in range(R_DEV):
        added[r : r + 1, entries : entries + TILE] = extra[r]
    plain[count:, :] = jnp.zeros_like(plain[count:, :])
    kept[entries:, :] = plain[...].astype(bfloat)
    summaries[...] = ordered[...].astype(bfloat)


def attend_kernel(came, kept, added, tables, sent, x, extra_k, extra_v, out):
    lanes = lax.axis_size("head")
    groups = came.shape[0] // lanes
    width = (HEADS + 2 * KVH) * HD // lanes
    span = -(-KVH * HD // TILE) * TILE
    key_cols = slice(0, span)
    value_cols = slice(KVW - span, KVW)
    first_key = HEADS * HD // TILE * R_DEV
    scale = HD ** (-0.5)
    x[...] = jnp.zeros_like(x)
    column = iota((8, TILE), 1)
    for k in range(lanes):
        tile = came[k]
        for g in range(1, groups):
            tile = tile + came[g * lanes + k]
        tile = tile.astype(bfloat).astype(single)
        base, shift = divmod(width * k, TILE)
        base = base * R_DEV
        if shift:
            tile = pltpu.roll(tile, shift, 1)
            x[base + 2 : base + 10, :] += jnp.where(column < shift, tile, 0.0)
        x[base : base + 8, :] += jnp.where(column >= shift, tile, 0.0)
    values = x[...]
    same_head = (iota((TILE, TILE), 0) // HD == iota((TILE, TILE), 1) // HD).astype(single)
    squares = jnp.dot(
        values * values, same_head, precision=lax.Precision.HIGHEST, preferred_element_type=single
    )
    normed = values * lax.rsqrt(squares / HD + epsilon) * tables[64:96, :]
    early = iota(values.shape, 1) % HD < HD // 2
    swapped = jnp.where(
        early, pltpu.roll(normed, TILE - HD // 2, 1), pltpu.roll(normed, HD // 2, 1)
    )
    turned = normed * tables[0:32, :] + swapped * tables[32:64, :]
    turned = turned.astype(bfloat).astype(single)

    rows = 24
    row = iota((rows, TILE), 0)
    half = iota((rows, TILE), 1) // HD
    key_head = row >> 2
    query = jnp.where(row < first_key, turned[:rows], 0.0)
    other = pltpu.roll(query, HD, 1)
    queries = []
    for u in range(2):
        placed = jnp.where(
            half == (key_head & 1), jnp.where((key_head & 1) == u, query, other), 0.0
        )
        queries.append(
            jnp.concatenate(
                [jnp.where((key_head >> 1) == c, placed, 0.0) for c in range(span // TILE)], axis=1
            )
        )
    queries = jnp.concatenate(queries, axis=0).astype(bfloat)

    extras = extra_k.shape[0]
    entries = kept.shape[0] - extras
    count = entries // KEEP
    extra_k[...] = kept[entries:, key_cols].astype(single)
    extra_v[...] = kept[entries:, value_cols].astype(single)
    first_value = first_key + KVH * HD // TILE * R_DEV
    for c in range(span // TILE):
        at = slice(c * TILE, (c + 1) * TILE)
        r = first_key + R_DEV * c
        extra_k[count : count + R_DEV, at] = turned[r : r + R_DEV]
        r = first_value + R_DEV * c
        extra_v[count : count + R_DEV, at] = values[r : r + R_DEV]

    def by_request(columns, size):
        odd = (iota((2 * rows, size), 0) & 1) == 1
        return jnp.where(odd, added[1:2, columns], added[0:1, columns])

    scores = dot_rows(queries, kept[:entries, key_cols]) * scale
    scores = scores + by_request(slice(0, entries), entries)
    extra = dot_rows(queries, extra_k[...].astype(bfloat)) * scale
    extra = extra + by_request(slice(entries, entries + extras), extras)
    top = jnp.maximum(
        jnp.max(scores, axis=1, keepdims=True), jnp.max(extra, axis=1, keepdims=True)
    )
    weight = jnp.where(scores > 0.5 * negative, jnp.exp(scores - top), 0.0)
    extra_weight = jnp.where(extra > 0.5 * negative, jnp.exp(extra - top), 0.0)
    mass = jnp.sum(weight, axis=1, keepdims=True) + jnp.sum(extra_weight, axis=1, keepdims=True)

    def weighted(parts, right):
        high = parts.astype(bfloat)
        low = (parts - high.astype(single)).astype(bfloat)
        return jnp.dot(high, right, preferred_element_type=single) + jnp.dot(
            low, right, preferred_element_type=single
        )

    total = weighted(weight, kept[:entries, value_cols]) + weighted(
        extra_weight, extra_v[...].astype(bfloat)
    )
    some = mass > 0.0
    mass = jnp.where(some, mass, 1.0)
    total = total / mass
    level = jnp.where(some, top + jnp.log(mass), negative)

    slot = key_head + (KVW // 2 - (KVW - span)) // HD
    results = []
    for u in range(2):
        mine = total[rows * u : rows * (u + 1)]
        picked = mine[:, :TILE]
        for c in range(1, span // TILE):
            picked = jnp.where((slot >> 1) == c, mine[:, c * TILE : (c + 1) * TILE], picked)
        results.append(jnp.where((slot & 1) == u, picked, pltpu.roll(picked, HD, 1)))
    out[:rows, :] = jnp.where(half == 0, results[0], results[1])
    out[rows:, :] = jnp.where(half == 0, level[:rows], level[rows:])
    own = HEADS * HD // groups
    for g in range(groups):
        r = own * g // TILE * R_DEV
        tile = jnp.concatenate([out[r : r + 4, :], out[rows + r : rows + r + 4, :]], axis=0)
        for k in range(lanes):
            sent[g * lanes + k] = tile


def project_kernel(source_far, weight_far, came, sent, source, weight, rows, done):
    copies = fetch((source_far, weight_far), (source, weight), done)
    lanes = lax.axis_size("head")
    groups = came.shape[0] // lanes
    features = weight.shape[0]
    requests = rows.shape[0]
    for g in range(groups):
        tiles = [came[g * lanes + k] for k in range(lanes)]
        levels = [tile[4:8] for tile in tiles]
        top = jnp.maximum(
            jnp.maximum(levels[0], levels[1]), jnp.maximum(levels[2], levels[3])
        )
        shares = [jnp.exp(level - top) for level in levels]
        mixed = sum(share * tile[0:4] for share, tile in zip(shares, tiles)) / sum(shares)
        rows[R_DEV * g : R_DEV * (g + 1), :TILE] = mixed[:R_DEV]
        rows[R_DEV * g : R_DEV * (g + 1), TILE:] = mixed[R_DEV:]
    shift = lax.rem(2 * TILE - lax.rem(lax.axis_index("req") * features, TILE), 2 * TILE)
    attention = pltpu.roll(rows[...].astype(bfloat).astype(single), shift, 1)
    for copy in copies:
        copy.wait()
    order = row_order(source, requests, False)
    attention = jnp.dot(order, attention.astype(bfloat), preferred_element_type=single)
    attention = attention[:, :features].astype(bfloat)
    projected = jnp.dot(attention, weight[...], preferred_element_type=single).astype(bfloat)
    width = sent.shape[2]
    share = groups // lanes
    for g in range(groups):
        b = g % share
        for k in range(lanes):
            sent[g * lanes + k] = projected[:, width * b : width * (b + 1)]


def units_kernel(gain_far, came, whole, gate, up, sent, mid_out, gain, done):
    (copy,) = fetch((gain_far,), (gain,), done)
    lanes = lax.axis_size("head")
    devices, rows, features = came.shape
    groups = devices // lanes
    share = groups // lanes
    group = lax.axis_index("req")
    here = pl.ds(pl.multiple_of(group * features, features), features)
    mid = whole[:, here].astype(single)
    for g in range(groups):
        mid = mid + came[g * lanes + group // share].astype(single)
    mid = mid.astype(bfloat)
    mid_out[...] = mid
    mid = mid.astype(single)
    squares = jnp.sum(mid * mid, axis=1, keepdims=True)
    piece = gate.shape[1] // groups
    place = iota((rows, sent.shape[2] - 2 * piece), 1)
    high = squares.astype(bfloat).astype(single)
    rest = squares - high
    middle = rest.astype(bfloat).astype(single)
    terms = jnp.where(place == 0, high, jnp.where(place == 1, middle, rest - middle))
    terms = jnp.where(place < 3, terms, 0.0).astype(bfloat)
    copy.wait()
    inputs = (mid * gain[:, here]).astype(bfloat)
    gates = jnp.dot(inputs, gate[...], preferred_element_type=single).astype(bfloat)
    ups = jnp.dot(inputs, up[...], preferred_element_type=single).astype(bfloat)
    for b in range(share):
        for k in range(lanes):
            columns = slice((b * lanes + k) * piece, (b * lanes + k + 1) * piece)
            for g in range(b, groups, share):
                sent[g * lanes + k, :, :piece] = gates[:, columns]
                sent[g * lanes + k, :, piece : 2 * piece] = ups[:, columns]
                sent[g * lanes + k, :, 2 * piece :] = terms


def active_kernel(came, active):
    lanes = lax.axis_size("head")
    groups = came.shape[0] // lanes
    source = lax.axis_index("req") // (groups // lanes)
    total = came[source].astype(single)
    for g in range(1, groups):
        total = total + came[g * lanes + source].astype(single)
    piece = active.shape[1]
    squares = total[:, 2 * piece : 2 * piece + 1] + total[:, 2 * piece + 1 : 2 * piece + 2]
    squares = squares + total[:, 2 * piece + 2 : 2 * piece + 3]
    factor = lax.rsqrt(squares / D + epsilon)
    gate = total[:, :piece] * factor
    up = total[:, piece : 2 * piece] * factor
    active[...] = (gate / (1.0 + jnp.exp(-gate)) * up).astype(bfloat)


def down_kernel(active, weight, mid, sent):
    groups, rows, width = sent.shape
    lanes, _, piece = active.shape
    half = mid.shape[1]
    share = width // half
    down = jnp.dot(active[0], weight[:piece, :], preferred_element_type=single)
    for k in range(1, lanes):
        down = down + jnp.dot(
            active[k], weight[piece * k : piece * (k + 1), :], preferred_element_type=single
        )
    residual = mid[...].astype(single)
    group = lax.axis_index("req")
    lane = lax.axis_index("head")
    for b in range(share):
        columns = slice(half * b, half * (b + 1))
        mine = group == lane * share + b
        total = (down[:, columns] + jnp.where(mine, residual, 0.0)).astype(bfloat)
        for g in range(groups):
            sent[g, :, columns] = total


def result_kernel(came, result):
    total = came[0].astype(single)
    for g in range(1, came.shape[0]):
        total = total + came[g].astype(single)
    result[...] = total.astype(bfloat)


def rotation_table():
    half = HD // 2
    size = -(-(NP + 1) // 8) * 8
    frequency = 10000.0 ** (-np.arange(half) / half)
    angles = PAGE * np.arange(size)[:, None] * frequency[None, :]
    cosine, sine = np.cos(angles), np.sin(angles)
    wide = [np.tile(np.concatenate(pair, axis=1), (1, TILE // HD)) for pair in
            ((cosine, cosine), (-sine, sine))]
    return jnp.asarray(np.concatenate(wide), dtype=single)


def on_device(
    hidden_in,
    attention_gain,
    query_gain,
    key_gain,
    feedforward_gain,
    input_weight,
    output_weight,
    gate_weight,
    up_weight,
    down_weight,
    old_cache,
    keep_rows,
    drop_weights,
    dest_slots,
    lengths,
    page_table,
    source,
):
    groups = lax.axis_size("req")
    lanes = lax.axis_size("head")
    requests = hidden_in.shape[0]
    pages_here = old_cache.shape[0]
    devices = groups * lanes
    features = D // groups
    piece = gate_weight.shape[1] // groups
    copies = pltpu.SemaphoreType.DMA

    whole = lax.all_gather(hidden_in, "head", axis=1, tiled=True)
    columns = input_weight.shape[1]
    padded = -(-columns // TILE) * TILE
    holds = source[None, :]
    gain = attention_gain[None, :]
    weight = input_weight.T
    (sent,) = run(
        first_kernel,
        [shaped((devices, R_DEV * padded // TILE, TILE), single)],
        [holds, gain, weight],
        [whole],
        [
            *scalar_like(holds),
            *local_like(gain, weight),
            pltpu.VMEM((requests, padded), single),
            copies((3,)),
        ],
        2 * requests * features * columns,
    )
    came = lax.all_to_all(sent, both_axes, 0, 0, tiled=True)

    scalars = [dest_slots, lengths[None, :], holds, page_table]
    arrays = [
        keep_rows,
        drop_weights,
        query_gain[None, :],
        key_gain[None, :],
        rotation_table(),
        old_cache,
    ]
    entries = pages_here * KEEP
    extras = 16
    compact, summaries, kept, added, tables = run(
        prepare_kernel,
        [
            shaped((pages_here // 2, PAGE, KVW), bfloat),
            shaped((pages_here, KVW), bfloat),
            shaped((entries + extras, KVW), bfloat),
            shaped((8, entries + TILE), single),
            shaped((96, TILE), single),
        ],
        scalars + arrays,
        [],
        [
            *scalar_like(*scalars),
            *local_like(*arrays),
            pltpu.VMEM((pages_here, KVW), single),
            pltpu.VMEM((extras, KVW), single),
            copies((len(scalars + arrays),)),
        ],
        2 * pages_here * TILE * PAGE * KVW,
    )
    span = -(-KVH * HD // TILE) * TILE
    (parts,) = run(
        attend_kernel,
        [shaped((devices, 8, TILE), single)],
        [],
        [came, kept, added, tables],
        [
            pltpu.VMEM((32, TILE), single),
            pltpu.VMEM((extras, span), single),
            pltpu.VMEM((extras, span), single),
            pltpu.VMEM((48, TILE), single),
        ],
        6 * 48 * entries * span,
    )
    came = lax.all_to_all(parts, both_axes, 0, 0, tiled=True)
    (sent,) = run(
        project_kernel,
        [shaped((devices, requests, features), bfloat)],
        [holds, output_weight],
        [came],
        [
            *scalar_like(holds),
            *local_like(output_weight),
            pltpu.VMEM((requests, 2 * TILE), single),
            copies((2,)),
        ],
        2 * requests * output_weight.size,
    )
    came = lax.all_to_all(sent, both_axes, 0, 0, tiled=True)
    gain = feedforward_gain[None, :]
    sent, mid = run(
        units_kernel,
        [shaped((devices, requests, 3 * TILE), bfloat), shaped((requests, features), bfloat)],
        [gain],
        [came, whole, gate_weight, up_weight],
        [*local_like(gain), copies((1,))],
        4 * requests * gate_weight.size,
    )
    came = lax.all_to_all(sent, both_axes, 0, 0, tiled=True)
    (active,) = run(active_kernel, [shaped((requests, piece), bfloat)], [], [came])
    active = lax.all_gather(active, "head")
    (sent,) = run(
        down_kernel,
        [shaped((groups, requests, down_weight.shape[1]), bfloat)],
        [],
        [active, down_weight, mid],
        [],
        2 * requests * down_weight.size,
    )
    (result,) = run(
        result_kernel, [shaped((requests, down_weight.shape[1]), bfloat)], [], [exchange(sent)]
    )
    return (compact, summaries, result)


def solution(mesh):
    placed = (
        P(None, "head"),
        P(),
        P(),
        P(),
        P(),
        P("req", "head"),
        P("req", "head"),
        P("req", "head"),
        P("req", "head"),
        P("req", "head"),
        P(("req", "head"), None, None),
        P(("req", "head"), None),
        P(("req", "head"), None),
        P(("req", "head"), None),
        P(),
        P("req", None),
        P(),
    )
    return jax.shard_map(
        on_device if mesh.shape["req"] <= DIRECT else on_device_wide,
        mesh=mesh,
        in_specs=placed,
        out_specs=(P(("req", "head"), None, None), P(("req", "head"), None), P(None, "head")),
        check_vma=False,
    )
```

```python
import jax
import jax.numpy as jnp
import numpy as np
from jax import lax
from jax.experimental import pallas as pl
from jax.experimental.pallas import tpu as pltpu
from jax.sharding import PartitionSpec as P

D = 2048
HEADS = 20
KVH = 5
HD = 64
FF = 5120
PAGE = 128
KEEP = 64
NP = 16
R_DEV = 2
KVW = 640

DIRECT = 8

epsilon = 1e-06
negative = -1e30
both_axes = ("req", "head")


def rms_scale(values):
    return lax.rsqrt(jnp.mean(values * values, axis=-1, keepdims=True) + epsilon)


def rms_rows(values, gain):
    return values * rms_scale(values) * gain


def rotate(vectors, positions):
    half = vectors.shape[-1] // 2
    frequency = 10000.0 ** (-jnp.arange(half, dtype=jnp.float32) / half)
    angles = positions.astype(jnp.float32)[:, None] * frequency[None, :]
    cosine = jnp.cos(angles)[:, None, :]
    sine = jnp.sin(angles)[:, None, :]
    first = vectors[..., :half]
    second = vectors[..., half:]
    return jnp.concatenate(
        [first * cosine - second * sine, second * cosine + first * sine], axis=-1
    )


def compact_pages(pages, keep, weights):
    rows = jnp.arange(pages.shape[1], dtype=jnp.int32)
    picks = keep[:, :, None] == rows[None, None, :]
    kept = jnp.einsum(
        "pkr,prc->pkc", picks.astype(jnp.bfloat16), pages, preferred_element_type=jnp.float32
    ).astype(jnp.bfloat16)
    dropped = weights * (1.0 - jnp.sum(picks.astype(jnp.float32), axis=1))
    total = jnp.sum(dropped, axis=1)
    means = (
        jnp.einsum(
            "pr,prc->pc", dropped, pages.astype(jnp.float32), precision=lax.Precision.HIGHEST
        )
        / total[:, None]
    )
    return (kept, means.astype(jnp.bfloat16), jnp.log(total))


def held_request(rows, source):
    half = R_DEV // 2
    position = rows % R_DEV
    slot = rows // R_DEV * half + position - half
    continued = jnp.arange(source.shape[0], dtype=jnp.int32)
    matches = source[None, :] == slot[:, None]
    owner_cont = jnp.sum(jnp.where(matches, continued[None, :], 0), axis=1)
    carried = owner_cont // half * R_DEV + half + owner_cont % half
    return jnp.where(position < half, rows, carried)


def pick_rows(order, rows):
    chosen = order[:, None] == jnp.arange(rows.shape[0], dtype=jnp.int32)[None, :]
    return jnp.dot(
        chosen.astype(jnp.bfloat16), rows, preferred_element_type=jnp.float32
    ).astype(jnp.bfloat16)


def exchange(parts):
    return lax.all_to_all(parts, "req", split_axis=0, concat_axis=0, tiled=True)


def to_block_owner(rows):
    groups = lax.axis_size("req")
    lanes = lax.axis_size("head")
    per_lane = groups // lanes
    pairs = [
        (g * lanes + h, (per_lane * h + g // lanes) * lanes + g % lanes)
        for g in range(groups)
        for h in range(lanes)
    ]
    return lax.ppermute(rows, both_axes, pairs)


def whole_sum(partial):
    if lax.axis_size("req") > DIRECT:
        return lax.psum(partial, "req")
    groups = lax.axis_size("req")
    return jnp.sum(exchange(jnp.broadcast_to(partial[None], (groups,) + partial.shape)), axis=0)


def on_device_wide(
    hidden_in,
    attention_gain,
    query_gain,
    key_gain,
    feedforward_gain,
    input_weight,
    output_weight,
    gate_weight,
    up_weight,
    down_weight,
    old_cache,
    keep_rows,
    drop_weights,
    dest_slots,
    lengths,
    page_table,
    source,
):
    groups = lax.axis_size("req")
    lanes = lax.axis_size("head")
    group = lax.axis_index("req")
    lane = lax.axis_index("head")
    requests = hidden_in.shape[0]
    half = R_DEV // 2
    split = KVH * HD
    ratio = HEADS // KVH
    scale = HD ** (-0.5)
    pages_here = old_cache.shape[0]
    everyone = jnp.arange(requests, dtype=jnp.int32)
    holders = held_request(everyone, source)
    held = lax.dynamic_slice_in_dim(holders, group * R_DEV, R_DEV, 0)
    held_len = lengths[held]
    positions = held_len * PAGE

    whole = lax.all_gather(hidden_in, "head", axis=1, tiled=True)
    normed = rms_rows(whole.astype(jnp.float32), attention_gain).astype(jnp.bfloat16)
    features = D // groups
    inputs = pick_rows(holders, lax.dynamic_slice_in_dim(normed, group * features, features, 1))
    partial_qkv = jnp.dot(inputs, input_weight, preferred_element_type=jnp.float32)
    sent = jnp.broadcast_to(
        partial_qkv.reshape(groups, 1, R_DEV, -1), (groups, lanes, R_DEV, partial_qkv.shape[1])
    ).reshape(groups * lanes, R_DEV, -1)
    got = lax.all_to_all(sent, both_axes, split_axis=0, concat_axis=0, tiled=True)
    mixed = jnp.sum(got.reshape(groups, lanes, R_DEV, -1), axis=0).astype(jnp.bfloat16)
    held_qkv = jnp.swapaxes(mixed, 0, 1).reshape(R_DEV, -1).astype(jnp.float32)

    query = rotate(
        rms_rows(held_qkv[:, : HEADS * HD].reshape(R_DEV, HEADS, HD), query_gain), positions
    ).astype(jnp.bfloat16)
    key_new = rotate(
        rms_rows(held_qkv[:, HEADS * HD : (HEADS + KVH) * HD].reshape(R_DEV, KVH, HD), key_gain),
        positions,
    ).astype(jnp.bfloat16)
    value_new = held_qkv[:, (HEADS + KVH) * HD :].reshape(R_DEV, KVH, HD)
    kept, means, bias = compact_pages(old_cache, keep_rows, drop_weights)
    destination = dest_slots[0]
    fresh_ids = jnp.arange(pages_here, dtype=jnp.int32)
    inverse = jnp.sum(
        jnp.where(destination[None, :] == fresh_ids[:, None], fresh_ids[None, :], 0), axis=1
    )
    compact = kept[inverse].reshape(pages_here // 2, PAGE, KVW)
    summaries = means[inverse]
    per_lane = NP // lanes
    table = page_table.reshape(R_DEV, per_lane, lanes)
    mine = lax.dynamic_slice_in_dim(table, lane, 1, 2)[:, :, 0]
    logical = jnp.arange(per_lane, dtype=jnp.int32) * lanes + lane
    live = logical[None, :] < held_len[:, None]
    owner = jnp.any((mine[:, :, None] == fresh_ids[None, None, :]) & live[:, :, None], axis=1)
    query_groups = query.reshape(R_DEV, KVH, ratio, HD)
    row_keys = kept[:, :, :split].reshape(pages_here, KEEP, KVH, HD)
    row_values = kept[:, :, split:].reshape(pages_here, KEEP, KVH, HD)
    row_live = keep_rows >= 0
    allowed = owner[:, None, None, :, None] & row_live[None, None, None, :, :]
    scores = (
        jnp.einsum("rngd,pmnd->rngpm", query_groups, row_keys, preferred_element_type=jnp.float32)
        * scale
    )
    scores = jnp.where(allowed, scores, negative)
    mean_keys = means[:, :split].reshape(pages_here, KVH, HD)
    mean_values = means[:, split:].reshape(pages_here, KVH, HD)
    mean_scores = (
        jnp.einsum("rngd,pnd->rngp", query_groups, mean_keys, preferred_element_type=jnp.float32)
        * scale
        + bias[None, None, None, :]
    )
    mean_allowed = owner[:, None, None, :]
    mean_scores = jnp.where(mean_allowed, mean_scores, negative)
    own_score = (
        jnp.einsum("rngd,rnd->rng", query_groups, key_new, preferred_element_type=jnp.float32)
        * scale
    )
    own_score = jnp.where(lane == 0, own_score, negative)
    top = jnp.maximum(jnp.max(scores, axis=(3, 4)), jnp.max(mean_scores, axis=3))
    top = jnp.maximum(top, own_score)
    row_weight = jnp.where(allowed, jnp.exp(scores - top[..., None, None]), 0.0)
    mean_weight = jnp.where(mean_allowed, jnp.exp(mean_scores - top[..., None]), 0.0)
    own_weight = jnp.where(lane == 0, jnp.exp(own_score - top), 0.0)
    mass = jnp.sum(row_weight, axis=(3, 4)) + jnp.sum(mean_weight, axis=3) + own_weight
    total = jnp.einsum(
        "rngpm,pmnd->rngd",
        row_weight,
        row_values.astype(jnp.float32),
        precision=lax.Precision.HIGHEST,
    )
    total = total + jnp.einsum(
        "rngp,pnd->rngd",
        mean_weight,
        mean_values.astype(jnp.float32),
        precision=lax.Precision.HIGHEST,
    )
    total = total + own_weight[..., None] * value_new[:, :, None, :]

    some = mass > 0.0
    level = jnp.where(some, top + jnp.log(jnp.where(some, mass, 1.0)), negative)
    means_out = total / jnp.where(some, mass, 1.0)[..., None]
    own = HEADS * HD // groups
    parts = jnp.stack([means_out, jnp.broadcast_to(level[..., None], total.shape)])
    parts = jnp.transpose(parts.reshape(2, R_DEV, groups, own), (2, 1, 0, 3))
    parts = jnp.broadcast_to(
        parts.reshape(groups, 1, R_DEV, 2 * own), (groups, lanes, R_DEV, 2 * own)
    ).reshape(groups * lanes, R_DEV, 2 * own)
    came = lax.all_to_all(parts, both_axes, 0, 0, tiled=True)
    came = came.reshape(groups, lanes, R_DEV, 2 * own)
    outs, levels = came[..., :own], came[..., own:]
    weights = jnp.exp(levels - jnp.max(levels, axis=1, keepdims=True))
    attention = jnp.sum(outs * weights, axis=1) / jnp.sum(weights, axis=1)
    attention = attention.reshape(requests, own).astype(jnp.bfloat16)
    back = jnp.sum(
        jnp.where(holders[None, :] == everyone[:, None], everyone[None, :], 0), axis=1
    )
    projected = jnp.dot(
        pick_rows(back, attention), output_weight, preferred_element_type=jnp.float32
    )
    projected = projected + jnp.where(group == 0, hidden_in.astype(jnp.float32), 0.0)

    share = groups // lanes
    blocks = jnp.moveaxis(projected.reshape(requests, share, 1, features), 0, 2)
    blocks = jnp.broadcast_to(blocks, (share, lanes, requests, features))
    mid = jnp.sum(exchange(blocks.reshape(groups, requests, features)), axis=0)
    mid = to_block_owner(mid.astype(jnp.bfloat16)).astype(jnp.float32)
    squares = jnp.sum(mid * mid, axis=1, keepdims=True)
    gain_here = lax.dynamic_slice_in_dim(feedforward_gain, group * features, features, 0)
    inputs_mid = (mid * gain_here).astype(jnp.bfloat16)
    local_units = gate_weight.shape[1]
    piece = local_units // groups
    gates = jnp.dot(inputs_mid, gate_weight, preferred_element_type=jnp.float32)
    ups = jnp.dot(inputs_mid, up_weight, preferred_element_type=jnp.float32)
    both = jnp.concatenate(
        [
            gates.reshape(requests, groups, piece),
            ups.reshape(requests, groups, piece),
            jnp.broadcast_to(squares[:, :, None], (requests, groups, 1)),
        ],
        axis=2,
    )
    sums = jnp.sum(exchange(jnp.swapaxes(both, 0, 1)), axis=0)
    factor = lax.rsqrt(sums[:, 2 * piece :] / D + epsilon)
    gate = sums[:, :piece] * factor
    active = (jax.nn.silu(gate) * (sums[:, piece : 2 * piece] * factor)).astype(jnp.bfloat16)
    active_here = lax.all_gather(to_block_owner(active), "head", axis=1, tiled=True)
    down = jnp.dot(active_here, down_weight, preferred_element_type=jnp.float32)
    residual = [jnp.where(group == lane * share + k, mid, 0.0) for k in range(share)]
    down = down + jnp.concatenate(residual, axis=1)
    result = whole_sum(down).astype(jnp.bfloat16)
    return (compact, summaries, result)


TILE = 128
bfloat = jnp.bfloat16
single = jnp.float32


TERMS = 4


def three_terms(value, place):
    high = value.astype(bfloat).astype(single)
    rest = value - high
    middle = rest.astype(bfloat).astype(single)
    low = jnp.where(place == 2, rest - middle, 0.0)
    return jnp.where(place == 0, high, jnp.where(place == 1, middle, low))


def iota(shape, axis):
    return lax.broadcasted_iota(jnp.int32, shape, axis)


def run(kernel, outs, far, near, scratch=(), flops=0):
    in_specs = [pl.BlockSpec(memory_space=pltpu.HBM) for _ in far]
    in_specs += [pl.BlockSpec(memory_space=pltpu.VMEM) for _ in near]
    moved = sum(a.size * a.dtype.itemsize for a in [*far, *near, *outs])
    return pl.pallas_call(
        kernel,
        out_shape=list(outs),
        in_specs=in_specs,
        out_specs=[pl.BlockSpec(memory_space=pltpu.VMEM) for _ in outs],
        scratch_shapes=list(scratch),
        compiler_params=pltpu.CompilerParams(vmem_limit_bytes=16 * 2**20),
        cost_estimate=pl.CostEstimate(flops=flops, bytes_accessed=moved, transcendentals=0),
    )(*[pltpu.with_memory_space_constraint(a, pltpu.HBM) for a in far], *near)


def fetch(sources, targets, done):
    copies = [
        pltpu.make_async_copy(source, target, done.at[k])
        for k, (source, target) in enumerate(zip(sources, targets))
    ]
    for copy in copies:
        copy.start()
    return copies


def local_like(*arrays):
    return [pltpu.VMEM(a.shape, a.dtype) for a in arrays]


def scalar_like(*arrays):
    return [pltpu.SMEM(a.shape, a.dtype) for a in arrays]


def row_order(source, count, to_holder):
    first, second = iota((count, count), 0), iota((count, count), 1)
    if not to_holder:
        first, second = second, first
    order = (first == second) & (first % R_DEV == 0)
    for c in range(source.shape[1]):
        order = order | ((first == source[0, c] * R_DEV + 1) & (second == c * R_DEV + 1))
    return order.astype(single).astype(bfloat)


def shaped(shape, dtype):
    return jax.ShapeDtypeStruct(shape, dtype)


def first_kernel(
    source_far, gain_far, weight_far, whole, sent, source, gain, weight, wide, done
):
    copies = fetch((source_far, gain_far, weight_far), (source, gain, weight), done)
    rows = whole.shape[0]
    groups = rows // R_DEV
    lanes = sent.shape[0] // groups
    columns, features = weight.shape
    values = whole[...].astype(single)
    factor = lax.rsqrt(jnp.mean(values * values, axis=1, keepdims=True) + epsilon)
    here = pl.ds(pl.multiple_of(lax.axis_index("req") * features, features), features)
    wide[...] = jnp.zeros_like(wide)
    for copy in copies:
        copy.wait()
    normed = (whole[:, here].astype(single) * factor * gain[:, here]).astype(bfloat)
    order = row_order(source, rows, True)
    normed = jnp.dot(order, normed, preferred_element_type=single).astype(bfloat)
    wide[:, :columns] = dot_rows(normed, weight[...])
    for g in range(groups):
        tile = jnp.concatenate(
            [
                wide[R_DEV * g : R_DEV * (g + 1), TILE * j : TILE * (j + 1)]
                for j in range(wide.shape[1] // TILE)
            ],
            axis=0,
        )
        for k in range(lanes):
            sent[g * lanes + k] = tile


def dot_rows(left, right):
    return lax.dot_general(left, right, (((1,), (1,)), ((), ())), preferred_element_type=single)


def prepare_kernel(*refs):
    far, refs = refs[:12], refs[12:]
    (compact, summaries, kept, added, tables, mine, theirs), refs = refs[:7], refs[7:]
    near, (ordered, plain, dealt, done) = refs[:12], refs[12:]
    copies = fetch(far, near, done)
    (dest, lengths, source, table, keep, weights, query_gain, key_gain, turns) = near[:9]
    pages, gate, up = near[9:]
    group = lax.axis_index("req")
    lane = lax.axis_index("head")
    lanes = lax.axis_size("head")
    for copy in copies[:9]:
        copy.wait()

    carried = 0
    for c in range(source.shape[1]):
        carried = carried + jnp.where(source[0, c] == group, c, 0)
    held_len = (lengths[0, group * R_DEV], lengths[0, carried * R_DEV + 1])
    count, rows, _ = pages.shape
    owned = []
    for r in range(R_DEV):
        slots = []
        for i in range(table.shape[1] // lanes):
            j = i * lanes + lane
            slots.append(jnp.where(j < held_len[r], table[r, j], -1))
        owned.append(slots)

    def owner(r, p):
        found = owned[r][0] == p
        for slot in owned[r][1:]:
            found = found | (slot == p)
        return found

    row = iota((32, TILE), 0)
    odd = (row & 1) == 1
    half_rows = turns.shape[0] // 2
    for part in range(2):
        pair = [turns[pl.ds(part * half_rows + held_len[r], 1), :] for r in range(R_DEV)]
        tables[32 * part : 32 * (part + 1), :] = jnp.where(odd, pair[1], pair[0])
    query_rows = HEADS * HD // TILE * R_DEV
    for c in range(TILE // HD):
        columns = slice(HD * c, HD * (c + 1))
        tables[64 : 64 + query_rows, columns] = jnp.broadcast_to(
            query_gain[...], (query_rows, HD)
        )
        tables[64 + query_rows : 96, columns] = jnp.broadcast_to(
            key_gain[...], (32 - query_rows, HD)
        )

    column = iota((1, TILE), 1)
    entries = count * KEEP
    added[...] = jnp.full_like(added, negative)
    extra = [
        jnp.where((column == count + r) & (lane == 0), 0.0, negative) for r in range(R_DEV)
    ]
    weight_columns = weights[...].T
    rows_of = iota((rows, KEEP), 0)
    place = iota((rows, KEEP), 1)
    copies[9].wait()
    for p in range(count):
        picks = (keep[p : p + 1, :] == rows_of).astype(single)
        dropped = weight_columns[:, p : p + 1] * (1.0 - jnp.sum(picks, axis=1, keepdims=True))
        total = jnp.sum(dropped, axis=0, keepdims=True)
        left = jnp.concatenate([picks, three_terms(dropped, place)], axis=1).astype(bfloat)
        both = lax.dot_general(
            left, pages[p], (((0,), (0,)), ((), ())), preferred_element_type=single
        )
        rows_kept = both[:KEEP].astype(bfloat)
        kept[KEEP * p : KEEP * (p + 1), :] = rows_kept
        slot = dest[0, p]
        start = pl.multiple_of((slot & 1) * KEEP, KEEP)
        compact[slot >> 1, pl.ds(start, KEEP), :] = rows_kept
        mean = both[KEEP : KEEP + 1] + both[KEEP + 1 : KEEP + 2] + both[KEEP + 2 : KEEP + 3]
        mean = mean / total
        plain[p : p + 1, :] = mean
        ordered[pl.ds(slot, 1), :] = mean
        live = jnp.where(keep[p : p + 1, :] >= 0, 0.0, negative)
        for r in range(R_DEV):
            here = owner(r, p)
            added[r : r + 1, KEEP * p : KEEP * (p + 1)] = jnp.where(here, live, negative)
            level = jnp.where(here, jnp.log(total), negative)
            extra[r] = jnp.where(column == p, level, extra[r])
    for r in range(R_DEV):
        added[r : r + 1, entries : entries + TILE] = extra[r]
    plain[count:, :] = jnp.zeros_like(plain[count:, :])
    kept[entries:, :] = plain[...].astype(bfloat)
    summaries[...] = ordered[...].astype(bfloat)

    for copy in copies[10:]:
        copy.wait()
    block = gate.shape[1] // 2
    piece = block // 2
    for k in range(2):
        for b in range(2):
            columns = slice(b * block + k * piece, b * block + (k + 1) * piece)
            start = b * block
            dealt[k, :, start : start + piece] = gate[:, columns].astype(single)
            dealt[k, :, start + piece : start + block] = up[:, columns].astype(single)
    mine[...] = dealt[lane & 1].astype(bfloat)
    theirs[...] = dealt[1 - (lane & 1)].astype(bfloat)


def attend_kernel(came, kept, added, tables, sent, x, extra_k, extra_v, out):
    lanes = lax.axis_size("head")
    groups = came.shape[0] // lanes
    width = (HEADS + 2 * KVH) * HD // lanes
    span = -(-KVH * HD // TILE) * TILE
    key_cols = slice(0, span)
    value_cols = slice(KVW - span, KVW)
    first_key = HEADS * HD // TILE * R_DEV
    scale = HD ** (-0.5)
    x[...] = jnp.zeros_like(x)
    column = iota((8, TILE), 1)
    for k in range(lanes):
        tile = came[k]
        for g in range(1, groups):
            tile = tile + came[g * lanes + k]
        tile = tile.astype(bfloat).astype(single)
        base, shift = divmod(width * k, TILE)
        base = base * R_DEV
        if shift:
            tile = pltpu.roll(tile, shift, 1)
            x[base + 2 : base + 10, :] += jnp.where(column < shift, tile, 0.0)
        x[base : base + 8, :] += jnp.where(column >= shift, tile, 0.0)
    values = x[...]
    same_head = (iota((TILE, TILE), 0) // HD == iota((TILE, TILE), 1) // HD).astype(single)
    squares = jnp.dot(
        values * values, same_head, precision=lax.Precision.HIGHEST, preferred_element_type=single
    )
    normed = values * lax.rsqrt(squares / HD + epsilon) * tables[64:96, :]
    early = iota(values.shape, 1) % HD < HD // 2
    swapped = jnp.where(
        early, pltpu.roll(normed, TILE - HD // 2, 1), pltpu.roll(normed, HD // 2, 1)
    )
    turned = normed * tables[0:32, :] + swapped * tables[32:64, :]
    turned = turned.astype(bfloat).astype(single)

    rows = 24
    row = iota((rows, TILE), 0)
    half = iota((rows, TILE), 1) // HD
    key_head = row >> 2
    query = jnp.where(row < first_key, turned[:rows], 0.0)
    other = pltpu.roll(query, HD, 1)
    queries = []
    for u in range(2):
        placed = jnp.where(
            half == (key_head & 1), jnp.where((key_head & 1) == u, query, other), 0.0
        )
        queries.append(
            jnp.concatenate(
                [jnp.where((key_head >> 1) == c, placed, 0.0) for c in range(span // TILE)], axis=1
            )
        )
    queries = jnp.concatenate(queries, axis=0).astype(bfloat)

    extras = extra_k.shape[0]
    entries = kept.shape[0] - extras
    count = entries // KEEP
    extra_k[...] = kept[entries:, key_cols].astype(single)
    extra_v[...] = kept[entries:, value_cols].astype(single)
    first_value = first_key + KVH * HD // TILE * R_DEV
    for c in range(span // TILE):
        at = slice(c * TILE, (c + 1) * TILE)
        r = first_key + R_DEV * c
        extra_k[count : count + R_DEV, at] = turned[r : r + R_DEV]
        r = first_value + R_DEV * c
        extra_v[count : count + R_DEV, at] = values[r : r + R_DEV]

    def by_request(columns, size):
        odd = (iota((2 * rows, size), 0) & 1) == 1
        return jnp.where(odd, added[1:2, columns], added[0:1, columns])

    scores = dot_rows(queries, kept[:entries, key_cols]) * scale
    scores = scores + by_request(slice(0, entries), entries)
    extra = dot_rows(queries, extra_k[...].astype(bfloat)) * scale
    extra = extra + by_request(slice(entries, entries + extras), extras)
    top = jnp.maximum(
        jnp.max(scores, axis=1, keepdims=True), jnp.max(extra, axis=1, keepdims=True)
    )
    weight = jnp.where(scores > 0.5 * negative, jnp.exp(scores - top), 0.0)
    extra_weight = jnp.where(extra > 0.5 * negative, jnp.exp(extra - top), 0.0)
    mass = jnp.sum(weight, axis=1, keepdims=True) + jnp.sum(extra_weight, axis=1, keepdims=True)

    def weighted(parts, right):
        high = parts.astype(bfloat)
        low = (parts - high.astype(single)).astype(bfloat)
        return jnp.dot(high, right, preferred_element_type=single) + jnp.dot(
            low, right, preferred_element_type=single
        )

    total = weighted(weight, kept[:entries, value_cols]) + weighted(
        extra_weight, extra_v[...].astype(bfloat)
    )
    some = mass > 0.0
    mass = jnp.where(some, mass, 1.0)
    total = total / mass
    level = jnp.where(some, top + jnp.log(mass), negative)

    slot = key_head + (KVW // 2 - (KVW - span)) // HD
    results = []
    for u in range(2):
        mine = total[rows * u : rows * (u + 1)]
        picked = mine[:, :TILE]
        for c in range(1, span // TILE):
            picked = jnp.where((slot >> 1) == c, mine[:, c * TILE : (c + 1) * TILE], picked)
        results.append(jnp.where((slot & 1) == u, picked, pltpu.roll(picked, HD, 1)))
    out[:rows, :] = jnp.where(half == 0, results[0], results[1])
    level = jnp.where(half == 0, level[:rows], level[rows:])
    out[rows:, :] = three_terms(level, iota(level.shape, 1) % TERMS)
    own = HEADS * HD // groups
    for g in range(groups):
        r = own * g // TILE * R_DEV
        tile = jnp.concatenate([out[r : r + 4, :], out[rows + r : rows + r + 4, :]], axis=0)
        for k in range(lanes):
            sent[g * lanes + k] = tile.astype(bfloat)


def project_kernel(
    source_far, own_far, came, one, two, three, sent, source, own, rows, done
):
    copies = fetch((source_far, own_far), (source, own), done)
    lanes = lax.axis_size("head")
    groups = came.shape[0] // lanes
    features = own.shape[0]
    requests = rows.shape[0]
    near = (iota((TILE, TILE), 0) // TERMS == iota((TILE, TILE), 1) // TERMS).astype(single)
    tiles = came[...].reshape(groups * lanes * 8, TILE)
    levels = jnp.dot(tiles, near.astype(bfloat), preferred_element_type=single)
    tiles = tiles.astype(single).reshape(groups, lanes, 8, TILE)
    levels = levels.reshape(groups, lanes, 8, TILE)
    for g in range(groups):
        mine = [levels[g, k, 4:8] for k in range(lanes)]
        top = jnp.maximum(jnp.maximum(mine[0], mine[1]), jnp.maximum(mine[2], mine[3]))
        shares = [jnp.exp(level - top) for level in mine]
        mixed = sum(share * tiles[g, k, 0:4] for k, share in enumerate(shares)) / sum(shares)
        rows[R_DEV * g : R_DEV * (g + 1), :TILE] = mixed[:R_DEV]
        rows[R_DEV * g : R_DEV * (g + 1), TILE:] = mixed[R_DEV:]
    shift = lax.rem(2 * TILE - lax.rem(lax.axis_index("req") * features, TILE), 2 * TILE)
    attention = pltpu.roll(rows[...].astype(bfloat).astype(single), shift, 1)
    for copy in copies:
        copy.wait()
    order = row_order(source, requests, False)
    attention = jnp.dot(order, attention.astype(bfloat), preferred_element_type=single)
    attention = attention[:, :features].astype(bfloat)
    width = sent.shape[2]
    share = groups // lanes
    for turn, weight in enumerate((own, one, two, three)):
        projected = jnp.dot(attention, weight[...], preferred_element_type=single)
        target = (lax.axis_index("head") ^ turn) * share
        for b in range(share):
            sent[target + b] = projected[:, width * b : width * (b + 1)].astype(bfloat)


def units_kernel(gain_far, came, whole, mine, theirs, sent, mid_out, gain, done):
    (copy,) = fetch((gain_far,), (gain,), done)
    groups, rows, features = came.shape
    share = groups // lax.axis_size("head")
    group = lax.axis_index("req")
    lane = lax.axis_index("head")
    here = pl.ds(pl.multiple_of(group * features, features), features)
    mid = whole[:, here].astype(single)
    for g in range(groups):
        mid = mid + came[g].astype(single)
    mid = mid.astype(bfloat)
    mid_out[...] = mid
    mid = mid.astype(single)
    squares = jnp.sum(mid * mid, axis=1, keepdims=True)
    block = mine.shape[1] // share
    terms = three_terms(squares, iota((rows, sent.shape[2] - block), 1)).astype(bfloat)
    copy.wait()
    inputs = (mid * gain[:, here]).astype(bfloat)
    for turn, weight in enumerate((mine, theirs)):
        units = jnp.dot(inputs, weight[...], preferred_element_type=single).astype(bfloat)
        target = (lane ^ turn) * share
        for b in range(share):
            sent[target + b, :, :block] = units[:, block * b : block * (b + 1)]
            sent[target + b, :, block:] = terms


def active_kernel(came, active):
    total = came[0].astype(single)
    for g in range(1, came.shape[0]):
        total = total + came[g].astype(single)
    piece = active.shape[1]
    squares = jnp.sum(total[:, 2 * piece : 2 * piece + 3], axis=1, keepdims=True)
    factor = lax.rsqrt(squares / D + epsilon)
    gate = total[:, :piece] * factor
    up = total[:, piece : 2 * piece] * factor
    active[...] = (gate / (1.0 + jnp.exp(-gate)) * up).astype(bfloat)


def down_kernel(active, weight, mid, sent):
    groups, rows, width = sent.shape
    lanes, _, piece = active.shape
    half = mid.shape[1]
    share = width // half
    group = lax.axis_index("req")
    lane = lax.axis_index("head")
    first = group // (2 * share) * 2
    down = jnp.dot(active[first], weight[:piece, :], preferred_element_type=single)
    down = down + jnp.dot(active[first + 1], weight[piece:, :], preferred_element_type=single)
    residual = mid[...].astype(single)
    for b in range(share):
        columns = slice(half * b, half * (b + 1))
        mine = group == lane * share + b
        total = (down[:, columns] + jnp.where(mine, residual, 0.0)).astype(bfloat)
        for g in range(groups):
            sent[g, :, columns] = total


def result_kernel(came, result):
    total = came[0].astype(single)
    for g in range(1, came.shape[0]):
        total = total + came[g].astype(single)
    result[...] = total.astype(bfloat)


def rotation_table():
    half = HD // 2
    size = -(-(NP + 1) // 8) * 8
    frequency = 10000.0 ** (-np.arange(half) / half)
    angles = PAGE * np.arange(size)[:, None] * frequency[None, :]
    cosine, sine = np.cos(angles), np.sin(angles)
    wide = [np.tile(np.concatenate(pair, axis=1), (1, TILE // HD)) for pair in
            ((cosine, cosine), (-sine, sine))]
    return jnp.asarray(np.concatenate(wide), dtype=single)


def swapped_lanes(value, turn):
    lanes = lax.axis_size("head")
    return lax.ppermute(value, "head", [(k, k ^ turn) for k in range(lanes)])


def on_device(
    hidden_in,
    attention_gain,
    query_gain,
    key_gain,
    feedforward_gain,
    input_weight,
    output_weight,
    gate_weight,
    up_weight,
    down_weight,
    old_cache,
    keep_rows,
    drop_weights,
    dest_slots,
    lengths,
    page_table,
    source,
):
    groups = lax.axis_size("req")
    lanes = lax.axis_size("head")
    requests = hidden_in.shape[0]
    pages_here = old_cache.shape[0]
    devices = groups * lanes
    features = D // groups
    copies = pltpu.SemaphoreType.DMA

    whole = lax.all_gather(hidden_in, "head", axis=1, tiled=True)
    columns = input_weight.shape[1]
    padded = -(-columns // TILE) * TILE
    holds = source[None, :]
    gain = attention_gain[None, :]
    weight = input_weight.T
    (sent,) = run(
        first_kernel,
        [shaped((devices, R_DEV * padded // TILE, TILE), single)],
        [holds, gain, weight],
        [whole],
        [
            *scalar_like(holds),
            *local_like(gain, weight),
            pltpu.VMEM((requests, padded), single),
            copies((3,)),
        ],
        2 * requests * features * columns,
    )
    came = lax.all_to_all(sent, both_axes, 0, 0, tiled=True)

    scalars = [dest_slots, lengths[None, :], holds, page_table]
    arrays = [
        keep_rows,
        drop_weights,
        query_gain[None, :],
        key_gain[None, :],
        rotation_table(),
        old_cache,
        gate_weight,
        up_weight,
    ]
    entries = pages_here * KEEP
    extras = 16
    compact, summaries, kept, added, tables, mine, theirs = run(
        prepare_kernel,
        [
            shaped((pages_here // 2, PAGE, KVW), bfloat),
            shaped((pages_here, KVW), bfloat),
            shaped((entries + extras, KVW), bfloat),
            shaped((8, entries + TILE), single),
            shaped((96, TILE), single),
            shaped(gate_weight.shape, bfloat),
            shaped(gate_weight.shape, bfloat),
        ],
        scalars + arrays,
        [],
        [
            *scalar_like(*scalars),
            *local_like(*arrays),
            pltpu.VMEM((pages_here, KVW), single),
            pltpu.VMEM((extras, KVW), single),
            pltpu.VMEM((2,) + gate_weight.shape, single),
            copies((len(scalars + arrays),)),
        ],
        2 * pages_here * TILE * PAGE * KVW,
    )
    span = -(-KVH * HD // TILE) * TILE
    (parts,) = run(
        attend_kernel,
        [shaped((devices, 8, TILE), bfloat)],
        [],
        [came, kept, added, tables],
        [
            pltpu.VMEM((32, TILE), single),
            pltpu.VMEM((extras, span), single),
            pltpu.VMEM((extras, span), single),
            pltpu.VMEM((48, TILE), single),
        ],
        6 * 48 * entries * span,
    )
    output_weights, theirs, _ = lax.optimization_barrier((output_weight, theirs, parts))
    others = [swapped_lanes(output_weights, turn) for turn in range(1, lanes)]
    theirs = swapped_lanes(theirs, 1)
    came = lax.all_to_all(parts, both_axes, 0, 0, tiled=True)
    came, theirs, *others = lax.optimization_barrier((came, theirs, *others))
    (sent,) = run(
        project_kernel,
        [shaped((groups, requests, features), bfloat)],
        [holds, output_weight],
        [came, *others],
        [
            *scalar_like(holds),
            *local_like(output_weight),
            pltpu.VMEM((requests, 2 * TILE), single),
            copies((2,)),
        ],
        2 * requests * output_weight.size * lanes,
    )
    gain = feedforward_gain[None, :]
    block = gate_weight.shape[1] // 2
    sent, mid = run(
        units_kernel,
        [
            shaped((groups, requests, block + TILE), bfloat),
            shaped((requests, features), bfloat),
        ],
        [gain],
        [exchange(sent), whole, mine, theirs],
        [*local_like(gain), copies((1,))],
        4 * requests * gate_weight.size,
    )
    (active,) = run(
        active_kernel, [shaped((requests, block // 2), bfloat)], [], [exchange(sent)]
    )
    active = lax.all_gather(active, "head")
    (sent,) = run(
        down_kernel,
        [shaped((groups, requests, down_weight.shape[1]), bfloat)],
        [],
        [active, down_weight, mid],
        [],
        2 * requests * down_weight.size,
    )
    (result,) = run(
        result_kernel, [shaped((requests, down_weight.shape[1]), bfloat)], [], [exchange(sent)]
    )
    return (compact, summaries, result)


def solution(mesh):
    placed = (
        P(None, "head"),
        P(),
        P(),
        P(),
        P(),
        P("req", "head"),
        P("req", "head"),
        P("req", "head"),
        P("req", "head"),
        P("req", "head"),
        P(("req", "head"), None, None),
        P(("req", "head"), None),
        P(("req", "head"), None),
        P(("req", "head"), None),
        P(),
        P("req", None),
        P(),
    )
    return jax.shard_map(
        on_device if mesh.shape["req"] <= DIRECT else on_device_wide,
        mesh=mesh,
        in_specs=placed,
        out_specs=(P(("req", "head"), None, None), P(("req", "head"), None), P(None, "head")),
        check_vma=False,
    )
```

```python
import jax
import jax.numpy as jnp
import numpy as np
from jax import lax
from jax.experimental import pallas as pl
from jax.experimental.pallas import tpu as pltpu
from jax.sharding import PartitionSpec as P

D = 2048
HEADS = 20
KVH = 5
HD = 64
FF = 5120
PAGE = 128
KEEP = 64
NP = 16
R_DEV = 2
KVW = 640

DIRECT = 8

epsilon = 1e-06
negative = -1e30
both_axes = ("req", "head")


def rms_scale(values):
    return lax.rsqrt(jnp.mean(values * values, axis=-1, keepdims=True) + epsilon)


def rms_rows(values, gain):
    return values * rms_scale(values) * gain


def rotate(vectors, positions):
    half = vectors.shape[-1] // 2
    frequency = 10000.0 ** (-jnp.arange(half, dtype=jnp.float32) / half)
    angles = positions.astype(jnp.float32)[:, None] * frequency[None, :]
    cosine = jnp.cos(angles)[:, None, :]
    sine = jnp.sin(angles)[:, None, :]
    first = vectors[..., :half]
    second = vectors[..., half:]
    return jnp.concatenate(
        [first * cosine - second * sine, second * cosine + first * sine], axis=-1
    )


def compact_pages(pages, keep, weights):
    rows = jnp.arange(pages.shape[1], dtype=jnp.int32)
    picks = keep[:, :, None] == rows[None, None, :]
    kept = jnp.einsum(
        "pkr,prc->pkc", picks.astype(jnp.bfloat16), pages, preferred_element_type=jnp.float32
    ).astype(jnp.bfloat16)
    dropped = weights * (1.0 - jnp.sum(picks.astype(jnp.float32), axis=1))
    total = jnp.sum(dropped, axis=1)
    means = (
        jnp.einsum(
            "pr,prc->pc", dropped, pages.astype(jnp.float32), precision=lax.Precision.HIGHEST
        )
        / total[:, None]
    )
    return (kept, means.astype(jnp.bfloat16), jnp.log(total))


def held_request(rows, source):
    half = R_DEV // 2
    position = rows % R_DEV
    slot = rows // R_DEV * half + position - half
    continued = jnp.arange(source.shape[0], dtype=jnp.int32)
    matches = source[None, :] == slot[:, None]
    owner_cont = jnp.sum(jnp.where(matches, continued[None, :], 0), axis=1)
    carried = owner_cont // half * R_DEV + half + owner_cont % half
    return jnp.where(position < half, rows, carried)


def pick_rows(order, rows):
    chosen = order[:, None] == jnp.arange(rows.shape[0], dtype=jnp.int32)[None, :]
    return jnp.dot(
        chosen.astype(jnp.bfloat16), rows, preferred_element_type=jnp.float32
    ).astype(jnp.bfloat16)


def exchange(parts):
    return lax.all_to_all(parts, "req", split_axis=0, concat_axis=0, tiled=True)


def to_block_owner(rows):
    groups = lax.axis_size("req")
    lanes = lax.axis_size("head")
    per_lane = groups // lanes
    pairs = [
        (g * lanes + h, (per_lane * h + g // lanes) * lanes + g % lanes)
        for g in range(groups)
        for h in range(lanes)
    ]
    return lax.ppermute(rows, both_axes, pairs)


def whole_sum(partial):
    if lax.axis_size("req") > DIRECT:
        return lax.psum(partial, "req")
    groups = lax.axis_size("req")
    return jnp.sum(exchange(jnp.broadcast_to(partial[None], (groups,) + partial.shape)), axis=0)


def on_device_wide(
    hidden_in,
    attention_gain,
    query_gain,
    key_gain,
    feedforward_gain,
    input_weight,
    output_weight,
    gate_weight,
    up_weight,
    down_weight,
    old_cache,
    keep_rows,
    drop_weights,
    dest_slots,
    lengths,
    page_table,
    source,
):
    groups = lax.axis_size("req")
    lanes = lax.axis_size("head")
    group = lax.axis_index("req")
    lane = lax.axis_index("head")
    requests = hidden_in.shape[0]
    half = R_DEV // 2
    split = KVH * HD
    ratio = HEADS // KVH
    scale = HD ** (-0.5)
    pages_here = old_cache.shape[0]
    everyone = jnp.arange(requests, dtype=jnp.int32)
    holders = held_request(everyone, source)
    held = lax.dynamic_slice_in_dim(holders, group * R_DEV, R_DEV, 0)
    held_len = lengths[held]
    positions = held_len * PAGE

    whole = lax.all_gather(hidden_in, "head", axis=1, tiled=True)
    normed = rms_rows(whole.astype(jnp.float32), attention_gain).astype(jnp.bfloat16)
    features = D // groups
    inputs = pick_rows(holders, lax.dynamic_slice_in_dim(normed, group * features, features, 1))
    partial_qkv = jnp.dot(inputs, input_weight, preferred_element_type=jnp.float32)
    sent = jnp.broadcast_to(
        partial_qkv.reshape(groups, 1, R_DEV, -1), (groups, lanes, R_DEV, partial_qkv.shape[1])
    ).reshape(groups * lanes, R_DEV, -1)
    got = lax.all_to_all(sent, both_axes, split_axis=0, concat_axis=0, tiled=True)
    mixed = jnp.sum(got.reshape(groups, lanes, R_DEV, -1), axis=0).astype(jnp.bfloat16)
    held_qkv = jnp.swapaxes(mixed, 0, 1).reshape(R_DEV, -1).astype(jnp.float32)

    query = rotate(
        rms_rows(held_qkv[:, : HEADS * HD].reshape(R_DEV, HEADS, HD), query_gain), positions
    ).astype(jnp.bfloat16)
    key_new = rotate(
        rms_rows(held_qkv[:, HEADS * HD : (HEADS + KVH) * HD].reshape(R_DEV, KVH, HD), key_gain),
        positions,
    ).astype(jnp.bfloat16)
    value_new = held_qkv[:, (HEADS + KVH) * HD :].reshape(R_DEV, KVH, HD)
    kept, means, bias = compact_pages(old_cache, keep_rows, drop_weights)
    destination = dest_slots[0]
    fresh_ids = jnp.arange(pages_here, dtype=jnp.int32)
    inverse = jnp.sum(
        jnp.where(destination[None, :] == fresh_ids[:, None], fresh_ids[None, :], 0), axis=1
    )
    compact = kept[inverse].reshape(pages_here // 2, PAGE, KVW)
    summaries = means[inverse]
    per_lane = NP // lanes
    table = page_table.reshape(R_DEV, per_lane, lanes)
    mine = lax.dynamic_slice_in_dim(table, lane, 1, 2)[:, :, 0]
    logical = jnp.arange(per_lane, dtype=jnp.int32) * lanes + lane
    live = logical[None, :] < held_len[:, None]
    owner = jnp.any((mine[:, :, None] == fresh_ids[None, None, :]) & live[:, :, None], axis=1)
    query_groups = query.reshape(R_DEV, KVH, ratio, HD)
    row_keys = kept[:, :, :split].reshape(pages_here, KEEP, KVH, HD)
    row_values = kept[:, :, split:].reshape(pages_here, KEEP, KVH, HD)
    row_live = keep_rows >= 0
    allowed = owner[:, None, None, :, None] & row_live[None, None, None, :, :]
    scores = (
        jnp.einsum("rngd,pmnd->rngpm", query_groups, row_keys, preferred_element_type=jnp.float32)
        * scale
    )
    scores = jnp.where(allowed, scores, negative)
    mean_keys = means[:, :split].reshape(pages_here, KVH, HD)
    mean_values = means[:, split:].reshape(pages_here, KVH, HD)
    mean_scores = (
        jnp.einsum("rngd,pnd->rngp", query_groups, mean_keys, preferred_element_type=jnp.float32)
        * scale
        + bias[None, None, None, :]
    )
    mean_allowed = owner[:, None, None, :]
    mean_scores = jnp.where(mean_allowed, mean_scores, negative)
    own_score = (
        jnp.einsum("rngd,rnd->rng", query_groups, key_new, preferred_element_type=jnp.float32)
        * scale
    )
    own_score = jnp.where(lane == 0, own_score, negative)
    top = jnp.maximum(jnp.max(scores, axis=(3, 4)), jnp.max(mean_scores, axis=3))
    top = jnp.maximum(top, own_score)
    row_weight = jnp.where(allowed, jnp.exp(scores - top[..., None, None]), 0.0)
    mean_weight = jnp.where(mean_allowed, jnp.exp(mean_scores - top[..., None]), 0.0)
    own_weight = jnp.where(lane == 0, jnp.exp(own_score - top), 0.0)
    mass = jnp.sum(row_weight, axis=(3, 4)) + jnp.sum(mean_weight, axis=3) + own_weight
    total = jnp.einsum(
        "rngpm,pmnd->rngd",
        row_weight,
        row_values.astype(jnp.float32),
        precision=lax.Precision.HIGHEST,
    )
    total = total + jnp.einsum(
        "rngp,pnd->rngd",
        mean_weight,
        mean_values.astype(jnp.float32),
        precision=lax.Precision.HIGHEST,
    )
    total = total + own_weight[..., None] * value_new[:, :, None, :]

    some = mass > 0.0
    level = jnp.where(some, top + jnp.log(jnp.where(some, mass, 1.0)), negative)
    means_out = total / jnp.where(some, mass, 1.0)[..., None]
    own = HEADS * HD // groups
    parts = jnp.stack([means_out, jnp.broadcast_to(level[..., None], total.shape)])
    parts = jnp.transpose(parts.reshape(2, R_DEV, groups, own), (2, 1, 0, 3))
    parts = jnp.broadcast_to(
        parts.reshape(groups, 1, R_DEV, 2 * own), (groups, lanes, R_DEV, 2 * own)
    ).reshape(groups * lanes, R_DEV, 2 * own)
    came = lax.all_to_all(parts, both_axes, 0, 0, tiled=True)
    came = came.reshape(groups, lanes, R_DEV, 2 * own)
    outs, levels = came[..., :own], came[..., own:]
    weights = jnp.exp(levels - jnp.max(levels, axis=1, keepdims=True))
    attention = jnp.sum(outs * weights, axis=1) / jnp.sum(weights, axis=1)
    attention = attention.reshape(requests, own).astype(jnp.bfloat16)
    back = jnp.sum(
        jnp.where(holders[None, :] == everyone[:, None], everyone[None, :], 0), axis=1
    )
    projected = jnp.dot(
        pick_rows(back, attention), output_weight, preferred_element_type=jnp.float32
    )
    projected = projected + jnp.where(group == 0, hidden_in.astype(jnp.float32), 0.0)

    share = groups // lanes
    blocks = jnp.moveaxis(projected.reshape(requests, share, 1, features), 0, 2)
    blocks = jnp.broadcast_to(blocks, (share, lanes, requests, features))
    mid = jnp.sum(exchange(blocks.reshape(groups, requests, features)), axis=0)
    mid = to_block_owner(mid.astype(jnp.bfloat16)).astype(jnp.float32)
    squares = jnp.sum(mid * mid, axis=1, keepdims=True)
    gain_here = lax.dynamic_slice_in_dim(feedforward_gain, group * features, features, 0)
    inputs_mid = (mid * gain_here).astype(jnp.bfloat16)
    local_units = gate_weight.shape[1]
    piece = local_units // groups
    gates = jnp.dot(inputs_mid, gate_weight, preferred_element_type=jnp.float32)
    ups = jnp.dot(inputs_mid, up_weight, preferred_element_type=jnp.float32)
    both = jnp.concatenate(
        [
            gates.reshape(requests, groups, piece),
            ups.reshape(requests, groups, piece),
            jnp.broadcast_to(squares[:, :, None], (requests, groups, 1)),
        ],
        axis=2,
    )
    sums = jnp.sum(exchange(jnp.swapaxes(both, 0, 1)), axis=0)
    factor = lax.rsqrt(sums[:, 2 * piece :] / D + epsilon)
    gate = sums[:, :piece] * factor
    active = (jax.nn.silu(gate) * (sums[:, piece : 2 * piece] * factor)).astype(jnp.bfloat16)
    active_here = lax.all_gather(to_block_owner(active), "head", axis=1, tiled=True)
    down = jnp.dot(active_here, down_weight, preferred_element_type=jnp.float32)
    residual = [jnp.where(group == lane * share + k, mid, 0.0) for k in range(share)]
    down = down + jnp.concatenate(residual, axis=1)
    result = whole_sum(down).astype(jnp.bfloat16)
    return (compact, summaries, result)


TILE = 128
bfloat = jnp.bfloat16
single = jnp.float32


TERMS = 4


def three_terms(value, place):
    high = value.astype(bfloat).astype(single)
    rest = value - high
    middle = rest.astype(bfloat).astype(single)
    low = jnp.where(place == 2, rest - middle, 0.0)
    return jnp.where(place == 0, high, jnp.where(place == 1, middle, low))


def iota(shape, axis):
    return lax.broadcasted_iota(jnp.int32, shape, axis)


def run(kernel, outs, far, near, scratch=(), flops=0):
    in_specs = [pl.BlockSpec(memory_space=pltpu.HBM) for _ in far]
    in_specs += [pl.BlockSpec(memory_space=pltpu.VMEM) for _ in near]
    moved = sum(a.size * a.dtype.itemsize for a in [*far, *near, *outs])
    return pl.pallas_call(
        kernel,
        out_shape=list(outs),
        in_specs=in_specs,
        out_specs=[pl.BlockSpec(memory_space=pltpu.VMEM) for _ in outs],
        scratch_shapes=list(scratch),
        compiler_params=pltpu.CompilerParams(vmem_limit_bytes=16 * 2**20),
        cost_estimate=pl.CostEstimate(flops=flops, bytes_accessed=moved, transcendentals=0),
    )(*[pltpu.with_memory_space_constraint(a, pltpu.HBM) for a in far], *near)


def fetch(sources, targets, done):
    copies = [
        pltpu.make_async_copy(source, target, done.at[k])
        for k, (source, target) in enumerate(zip(sources, targets))
    ]
    for copy in copies:
        copy.start()
    return copies


def local_like(*arrays):
    return [pltpu.VMEM(a.shape, a.dtype) for a in arrays]


def scalar_like(*arrays):
    return [pltpu.SMEM(a.shape, a.dtype) for a in arrays]


def row_order(source, count, to_holder):
    first, second = iota((count, count), 0), iota((count, count), 1)
    if not to_holder:
        first, second = second, first
    order = (first == second) & (first % R_DEV == 0)
    for c in range(source.shape[1]):
        order = order | ((first == source[0, c] * R_DEV + 1) & (second == c * R_DEV + 1))
    return order.astype(single).astype(bfloat)


def shaped(shape, dtype):
    return jax.ShapeDtypeStruct(shape, dtype)


def first_kernel(
    source_far, gain_far, weight_far, whole, sent, source, gain, weight, wide, done
):
    copies = fetch((source_far, gain_far, weight_far), (source, gain, weight), done)
    rows = whole.shape[0]
    groups = rows // R_DEV
    lanes = sent.shape[0] // groups
    columns, features = weight.shape
    values = whole[...].astype(single)
    factor = lax.rsqrt(jnp.mean(values * values, axis=1, keepdims=True) + epsilon)
    here = pl.ds(pl.multiple_of(lax.axis_index("req") * features, features), features)
    wide[...] = jnp.zeros_like(wide)
    for copy in copies:
        copy.wait()
    normed = (whole[:, here].astype(single) * factor * gain[:, here]).astype(bfloat)
    order = row_order(source, rows, True)
    normed = jnp.dot(order, normed, preferred_element_type=single).astype(bfloat)
    wide[:, :columns] = dot_rows(normed, weight[...])
    for g in range(groups):
        tile = jnp.concatenate(
            [
                wide[R_DEV * g : R_DEV * (g + 1), TILE * j : TILE * (j + 1)]
                for j in range(wide.shape[1] // TILE)
            ],
            axis=0,
        )
        for k in range(lanes):
            sent[g * lanes + k] = tile


def dot_rows(left, right):
    return lax.dot_general(left, right, (((1,), (1,)), ((), ())), preferred_element_type=single)


def prepare_kernel(*refs):
    far, refs = refs[:13], refs[13:]
    (compact, summaries, kept, added, tables, mine, theirs, *handed), refs = refs[:9], refs[9:]
    near, (ordered, plain, dealt, done) = refs[:13], refs[13:]
    copies = fetch(far, near, done)
    (dest, lengths, source, table, keep, weights, query_gain, key_gain, turns) = near[:9]
    pages, gate, up, output = near[9:]
    group = lax.axis_index("req")
    lane = lax.axis_index("head")
    lanes = lax.axis_size("head")
    for copy in copies[:9]:
        copy.wait()

    carried = 0
    for c in range(source.shape[1]):
        carried = carried + jnp.where(source[0, c] == group, c, 0)
    held_len = (lengths[0, group * R_DEV], lengths[0, carried * R_DEV + 1])
    count, rows, _ = pages.shape
    owned = []
    for r in range(R_DEV):
        slots = []
        for i in range(table.shape[1] // lanes):
            j = i * lanes + lane
            slots.append(jnp.where(j < held_len[r], table[r, j], -1))
        owned.append(slots)

    def owner(r, p):
        found = owned[r][0] == p
        for slot in owned[r][1:]:
            found = found | (slot == p)
        return found

    row = iota((32, TILE), 0)
    odd = (row & 1) == 1
    half_rows = turns.shape[0] // 2
    for part in range(2):
        pair = [turns[pl.ds(part * half_rows + held_len[r], 1), :] for r in range(R_DEV)]
        tables[32 * part : 32 * (part + 1), :] = jnp.where(odd, pair[1], pair[0])
    query_rows = HEADS * HD // TILE * R_DEV
    for c in range(TILE // HD):
        columns = slice(HD * c, HD * (c + 1))
        tables[64 : 64 + query_rows, columns] = jnp.broadcast_to(
            query_gain[...], (query_rows, HD)
        )
        tables[64 + query_rows : 96, columns] = jnp.broadcast_to(
            key_gain[...], (32 - query_rows, HD)
        )

    column = iota((1, TILE), 1)
    entries = count * KEEP
    added[...] = jnp.full_like(added, negative)
    extra = [
        jnp.where((column == count + r) & (lane == 0), 0.0, negative) for r in range(R_DEV)
    ]
    weight_columns = weights[...].T
    rows_of = iota((rows, KEEP), 0)
    place = iota((rows, KEEP), 1)
    copies[9].wait()
    for p in range(count):
        picks = (keep[p : p + 1, :] == rows_of).astype(single)
        dropped = weight_columns[:, p : p + 1] * (1.0 - jnp.sum(picks, axis=1, keepdims=True))
        total = jnp.sum(dropped, axis=0, keepdims=True)
        left = jnp.concatenate([picks, three_terms(dropped, place)], axis=1).astype(bfloat)
        both = lax.dot_general(
            left, pages[p], (((0,), (0,)), ((), ())), preferred_element_type=single
        )
        rows_kept = both[:KEEP].astype(bfloat)
        kept[KEEP * p : KEEP * (p + 1), :] = rows_kept
        slot = dest[0, p]
        start = pl.multiple_of((slot & 1) * KEEP, KEEP)
        compact[slot >> 1, pl.ds(start, KEEP), :] = rows_kept
        mean = both[KEEP : KEEP + 1] + both[KEEP + 1 : KEEP + 2] + both[KEEP + 2 : KEEP + 3]
        mean = mean / total
        plain[p : p + 1, :] = mean
        ordered[pl.ds(slot, 1), :] = mean
        live = jnp.where(keep[p : p + 1, :] >= 0, 0.0, negative)
        for r in range(R_DEV):
            here = owner(r, p)
            added[r : r + 1, KEEP * p : KEEP * (p + 1)] = jnp.where(here, live, negative)
            level = jnp.where(here, jnp.log(total), negative)
            extra[r] = jnp.where(column == p, level, extra[r])
    for r in range(R_DEV):
        added[r : r + 1, entries : entries + TILE] = extra[r]
    plain[count:, :] = jnp.zeros_like(plain[count:, :])
    kept[entries:, :] = plain[...].astype(bfloat)
    summaries[...] = ordered[...].astype(bfloat)

    for copy in copies[10:]:
        copy.wait()
    block = gate.shape[1] // 2
    piece = block // 2
    for k in range(2):
        for b in range(2):
            columns = slice(b * block + k * piece, b * block + (k + 1) * piece)
            start = b * block
            dealt[k, :, start : start + piece] = gate[:, columns].astype(single)
            dealt[k, :, start + piece : start + block] = up[:, columns].astype(single)
    mine[...] = dealt[lane & 1].astype(bfloat)
    theirs[...] = dealt[1 - (lane & 1)].astype(bfloat)
    width = handed[0].shape[1]
    for turn, block in enumerate(handed):
        start = pl.multiple_of(((group & 1) ^ turn) * width, width)
        block[...] = output[:, pl.ds(start, width)]


def attend_kernel(came, kept, added, tables, sent, x, extra_k, extra_v, out, logs):
    lanes = lax.axis_size("head")
    groups = came.shape[0] // lanes
    width = (HEADS + 2 * KVH) * HD // lanes
    span = -(-KVH * HD // TILE) * TILE
    key_cols = slice(0, span)
    value_cols = slice(KVW - span, KVW)
    first_key = HEADS * HD // TILE * R_DEV
    scale = HD ** (-0.5)
    x[...] = jnp.zeros_like(x)
    column = iota((8, TILE), 1)
    for k in range(lanes):
        tile = came[k].astype(single)
        for g in range(1, groups):
            tile = tile + came[g * lanes + k].astype(single)
        tile = tile.astype(bfloat).astype(single)
        base, shift = divmod(width * k, TILE)
        base = base * R_DEV
        if shift:
            tile = pltpu.roll(tile, shift, 1)
            x[base + 2 : base + 10, :] += jnp.where(column < shift, tile, 0.0)
        x[base : base + 8, :] += jnp.where(column >= shift, tile, 0.0)
    values = x[...]
    same_head = (iota((TILE, TILE), 0) // HD == iota((TILE, TILE), 1) // HD).astype(single)
    squares = jnp.dot(
        values * values, same_head, precision=lax.Precision.HIGHEST, preferred_element_type=single
    )
    normed = values * lax.rsqrt(squares / HD + epsilon) * tables[64:96, :]
    early = iota(values.shape, 1) % HD < HD // 2
    swapped = jnp.where(
        early, pltpu.roll(normed, TILE - HD // 2, 1), pltpu.roll(normed, HD // 2, 1)
    )
    turned = normed * tables[0:32, :] + swapped * tables[32:64, :]
    turned = turned.astype(bfloat).astype(single)

    rows = 24
    row = iota((rows, TILE), 0)
    half = iota((rows, TILE), 1) // HD
    key_head = row >> 2
    query = jnp.where(row < first_key, turned[:rows], 0.0)
    other = pltpu.roll(query, HD, 1)
    queries = []
    for u in range(2):
        placed = jnp.where(
            half == (key_head & 1), jnp.where((key_head & 1) == u, query, other), 0.0
        )
        queries.append(
            jnp.concatenate(
                [jnp.where((key_head >> 1) == c, placed, 0.0) for c in range(span // TILE)], axis=1
            )
        )
    queries = jnp.concatenate(queries, axis=0).astype(bfloat)

    extras = extra_k.shape[0]
    entries = kept.shape[0] - extras
    count = entries // KEEP
    extra_k[...] = kept[entries:, key_cols].astype(single)
    extra_v[...] = kept[entries:, value_cols].astype(single)
    first_value = first_key + KVH * HD // TILE * R_DEV
    for c in range(span // TILE):
        at = slice(c * TILE, (c + 1) * TILE)
        r = first_key + R_DEV * c
        extra_k[count : count + R_DEV, at] = turned[r : r + R_DEV]
        r = first_value + R_DEV * c
        extra_v[count : count + R_DEV, at] = values[r : r + R_DEV]

    def by_request(columns, size):
        odd = (iota((2 * rows, size), 0) & 1) == 1
        return jnp.where(odd, added[1:2, columns], added[0:1, columns])

    scores = dot_rows(queries, kept[:entries, key_cols]) * scale
    scores = scores + by_request(slice(0, entries), entries)
    extra = dot_rows(queries, extra_k[...].astype(bfloat)) * scale
    extra = extra + by_request(slice(entries, entries + extras), extras)
    top = jnp.maximum(
        jnp.max(scores, axis=1, keepdims=True), jnp.max(extra, axis=1, keepdims=True)
    )
    weight = jnp.where(scores > 0.5 * negative, jnp.exp(scores - top), 0.0)
    extra_weight = jnp.where(extra > 0.5 * negative, jnp.exp(extra - top), 0.0)
    mass = jnp.sum(weight, axis=1, keepdims=True) + jnp.sum(extra_weight, axis=1, keepdims=True)

    def weighted(parts, right):
        high = parts.astype(bfloat)
        low = (parts - high.astype(single)).astype(bfloat)
        return jnp.dot(high, right, preferred_element_type=single) + jnp.dot(
            low, right, preferred_element_type=single
        )

    total = weighted(weight, kept[:entries, value_cols]) + weighted(
        extra_weight, extra_v[...].astype(bfloat)
    )
    some = mass > 0.0
    mass = jnp.where(some, mass, 1.0)
    total = total / mass
    level = jnp.where(some, top + jnp.log(mass), negative)

    slot = key_head + (KVW // 2 - (KVW - span)) // HD
    results = []
    for u in range(2):
        mine = total[rows * u : rows * (u + 1)]
        picked = mine[:, :TILE]
        for c in range(1, span // TILE):
            picked = jnp.where((slot >> 1) == c, mine[:, c * TILE : (c + 1) * TILE], picked)
        results.append(jnp.where((slot & 1) == u, picked, pltpu.roll(picked, HD, 1)))
    out[...] = jnp.where(half == 0, results[0], results[1])
    logs[...] = jnp.broadcast_to(level, logs.shape)
    own = HEADS * HD // lanes
    size = 6
    column = iota((size, TILE), 1)
    here = column // TERMS == iota((size, TILE), 0)
    for k in range(lanes):
        r = own * k // TILE * R_DEV
        tile = [out[r : r + size, :]]
        for u in range(2):
            coded = three_terms(logs[rows * u + r : rows * u + r + size, :], column % TERMS)
            tile.append(jnp.sum(jnp.where(here, coded, 0.0), axis=0, keepdims=True))
        tile = jnp.concatenate(tile, axis=0).astype(bfloat)
        for g in range(groups):
            sent[g * lanes + k] = tile


def project_kernel(source_far, came, first, second, sent, source, logs, rows, pieces, done):
    (copy,) = fetch((source_far,), (source,), done)
    lanes = lax.axis_size("head")
    groups = came.shape[0] // lanes
    group = lax.axis_index("req")
    features = first.shape[0]
    requests = rows.shape[0]
    size = 6
    tiles = [came[d].astype(single) for d in range(groups * lanes)]
    for g in range(groups):
        for k in range(lanes):
            logs[k, 2 * g : 2 * g + 2, :] = tiles[g * lanes + k][size:]
    spread = (iota((8, TILE), 1) // TERMS == iota((8, TILE), 0)).astype(single).astype(bfloat)
    levels = [dot_rows(spread, logs[k].astype(bfloat)) for k in range(lanes)]
    top = jnp.maximum(jnp.maximum(levels[0], levels[1]), jnp.maximum(levels[2], levels[3]))
    shares = [jnp.exp(level - top) for level in levels]
    mass = sum(shares)
    shares = [share / mass for share in shares]
    lower = iota((8, TILE), 1) < HD
    for g in range(groups):
        mixed = 0.0
        for k in range(lanes):
            share = shares[k]
            share = jnp.where(lower, share[:, 2 * g : 2 * g + 1], share[:, 2 * g + 1 : 2 * g + 2])
            mixed = mixed + share * tiles[g * lanes + k]
        for j in range(size // R_DEV):
            rows[R_DEV * g : R_DEV * (g + 1), TILE * j : TILE * (j + 1)] = mixed[
                R_DEV * j : R_DEV * (j + 1)
            ]
    width = rows.shape[1]
    shift = lax.rem(lax.axis_index("head") * (2 * features), TILE)
    attention = rows[...].astype(bfloat).astype(single)
    attention = pltpu.roll(attention, lax.rem(width - shift, width), 1)
    copy.wait()
    order = row_order(source, requests, False)
    attention = jnp.dot(order, attention.astype(bfloat), preferred_element_type=single)
    for b in range(2):
        pieces[b] = attention[:, features * b : features * (b + 1)]
    total = 0.0
    for turn, weight in enumerate((first, second)):
        piece = pieces[(group & 1) ^ turn].astype(bfloat)
        total = total + jnp.dot(piece, weight[...], preferred_element_type=single)
    sent[...] = total


def units_kernel(gain_far, came, whole, mine, theirs, sent, mid_out, gain, done):
    (copy,) = fetch((gain_far,), (gain,), done)
    lanes, rows, features = came.shape
    share = sent.shape[0] // lanes
    group = lax.axis_index("req")
    lane = lax.axis_index("head")
    here = pl.ds(pl.multiple_of(group * features, features), features)
    mid = came[0]
    for k in range(1, lanes):
        mid = mid + came[k]
    mid = (whole[:, here].astype(single) + mid).astype(bfloat)
    mid_out[...] = mid
    mid = mid.astype(single)
    squares = jnp.sum(mid * mid, axis=1, keepdims=True)
    block = mine.shape[1] // share
    terms = three_terms(squares, iota((rows, sent.shape[2] - block), 1)).astype(bfloat)
    copy.wait()
    inputs = (mid * gain[:, here]).astype(bfloat)
    for turn, weight in enumerate((mine, theirs)):
        units = jnp.dot(inputs, weight[...], preferred_element_type=single).astype(bfloat)
        target = (lane ^ turn) * share
        for b in range(share):
            sent[target + b, :, :block] = units[:, block * b : block * (b + 1)]
            sent[target + b, :, block:] = terms


def active_kernel(came, active):
    total = came[0].astype(single)
    for g in range(1, came.shape[0]):
        total = total + came[g].astype(single)
    piece = active.shape[1]
    squares = jnp.sum(total[:, 2 * piece : 2 * piece + 3], axis=1, keepdims=True)
    factor = lax.rsqrt(squares / D + epsilon)
    gate = total[:, :piece] * factor
    up = total[:, piece : 2 * piece] * factor
    active[...] = (gate / (1.0 + jnp.exp(-gate)) * up).astype(bfloat)


def down_kernel(active, weight, mid, sent):
    groups, rows, width = sent.shape
    lanes, _, piece = active.shape
    half = mid.shape[1]
    share = width // half
    group = lax.axis_index("req")
    lane = lax.axis_index("head")
    first = group // (2 * share) * 2
    down = jnp.dot(active[first], weight[:piece, :], preferred_element_type=single)
    down = down + jnp.dot(active[first + 1], weight[piece:, :], preferred_element_type=single)
    residual = mid[...].astype(single)
    for b in range(share):
        columns = slice(half * b, half * (b + 1))
        mine = group == lane * share + b
        total = (down[:, columns] + jnp.where(mine, residual, 0.0)).astype(bfloat)
        for g in range(groups):
            sent[g, :, columns] = total


def result_kernel(came, result):
    total = came[0].astype(single)
    for g in range(1, came.shape[0]):
        total = total + came[g].astype(single)
    result[...] = total.astype(bfloat)


def rotation_table():
    half = HD // 2
    size = -(-(NP + 1) // 8) * 8
    frequency = 10000.0 ** (-np.arange(half) / half)
    angles = PAGE * np.arange(size)[:, None] * frequency[None, :]
    cosine, sine = np.cos(angles), np.sin(angles)
    wide = [np.tile(np.concatenate(pair, axis=1), (1, TILE // HD)) for pair in
            ((cosine, cosine), (-sine, sine))]
    return jnp.asarray(np.concatenate(wide), dtype=single)


def swapped_lanes(value, turn):
    lanes = lax.axis_size("head")
    return lax.ppermute(value, "head", [(k, k ^ turn) for k in range(lanes)])


def handed_over(value, turn):
    groups = lax.axis_size("req")
    lanes = lax.axis_size("head")
    share = groups // lanes
    pairs = [
        (g * lanes + h, (share * h + ((g & 1) ^ turn)) * lanes + g // share)
        for g in range(groups)
        for h in range(lanes)
    ]
    return lax.ppermute(value, both_axes, pairs)


def on_device(
    hidden_in,
    attention_gain,
    query_gain,
    key_gain,
    feedforward_gain,
    input_weight,
    output_weight,
    gate_weight,
    up_weight,
    down_weight,
    old_cache,
    keep_rows,
    drop_weights,
    dest_slots,
    lengths,
    page_table,
    source,
):
    groups = lax.axis_size("req")
    lanes = lax.axis_size("head")
    requests = hidden_in.shape[0]
    pages_here = old_cache.shape[0]
    devices = groups * lanes
    features = D // groups
    copies = pltpu.SemaphoreType.DMA

    whole = lax.all_gather(hidden_in, "head", axis=1, tiled=True)
    columns = input_weight.shape[1]
    padded = -(-columns // TILE) * TILE
    holds = source[None, :]
    gain = attention_gain[None, :]
    weight = input_weight.T
    (sent,) = run(
        first_kernel,
        [shaped((devices, R_DEV * padded // TILE, TILE), single)],
        [holds, gain, weight],
        [whole],
        [
            *scalar_like(holds),
            *local_like(gain, weight),
            pltpu.VMEM((requests, padded), single),
            copies((3,)),
        ],
        2 * requests * features * columns,
    )
    came = lax.all_to_all(sent, both_axes, 0, 0, tiled=True)

    scalars = [dest_slots, lengths[None, :], holds, page_table]
    arrays = [
        keep_rows,
        drop_weights,
        query_gain[None, :],
        key_gain[None, :],
        rotation_table(),
        old_cache,
        gate_weight,
        up_weight,
        output_weight,
    ]
    entries = pages_here * KEEP
    extras = 16
    compact, summaries, kept, added, tables, mine, theirs, *handed = run(
        prepare_kernel,
        [
            shaped((pages_here // 2, PAGE, KVW), bfloat),
            shaped((pages_here, KVW), bfloat),
            shaped((entries + extras, KVW), bfloat),
            shaped((8, entries + TILE), single),
            shaped((96, TILE), single),
            shaped(gate_weight.shape, bfloat),
            shaped(gate_weight.shape, bfloat),
            shaped((output_weight.shape[0], features), bfloat),
            shaped((output_weight.shape[0], features), bfloat),
        ],
        scalars + arrays,
        [],
        [
            *scalar_like(*scalars),
            *local_like(*arrays),
            pltpu.VMEM((pages_here, KVW), single),
            pltpu.VMEM((extras, KVW), single),
            pltpu.VMEM((2,) + gate_weight.shape, single),
            copies((len(scalars + arrays),)),
        ],
        2 * pages_here * TILE * PAGE * KVW,
    )
    span = -(-KVH * HD // TILE) * TILE
    (parts,) = run(
        attend_kernel,
        [shaped((devices, 8, TILE), bfloat)],
        [],
        [came, kept, added, tables],
        [
            pltpu.VMEM((32, TILE), single),
            pltpu.VMEM((extras, span), single),
            pltpu.VMEM((extras, span), single),
            pltpu.VMEM((24, TILE), single),
            pltpu.VMEM((48, TILE), single),
        ],
        6 * 48 * entries * span,
    )
    theirs, *handed, _ = lax.optimization_barrier((theirs, *handed, parts))
    theirs = swapped_lanes(theirs, 1)
    handed = [handed_over(value, turn) for turn, value in enumerate(handed)]
    came = lax.all_to_all(parts, both_axes, 0, 0, tiled=True)
    came, theirs, *handed = lax.optimization_barrier((came, theirs, *handed))
    (sent,) = run(
        project_kernel,
        [shaped((requests, features), single)],
        [holds],
        [came, *handed],
        [
            *scalar_like(holds),
            pltpu.VMEM((lanes, 2 * groups, TILE), single),
            pltpu.VMEM((requests, 3 * TILE), single),
            pltpu.VMEM((2, requests, output_weight.shape[0]), single),
            copies((1,)),
        ],
        2 * requests * output_weight.size,
    )
    gain = feedforward_gain[None, :]
    block = gate_weight.shape[1] // 2
    sent, mid = run(
        units_kernel,
        [
            shaped((groups, requests, block + TILE), bfloat),
            shaped((requests, features), bfloat),
        ],
        [gain],
        [lax.all_gather(sent, "head"), whole, mine, theirs],
        [*local_like(gain), copies((1,))],
        4 * requests * gate_weight.size,
    )
    (active,) = run(
        active_kernel, [shaped((requests, block // 2), bfloat)], [], [exchange(sent)]
    )
    active = lax.all_gather(active, "head")
    (sent,) = run(
        down_kernel,
        [shaped((groups, requests, down_weight.shape[1]), bfloat)],
        [],
        [active, down_weight, mid],
        [],
        2 * requests * down_weight.size,
    )
    (result,) = run(
        result_kernel, [shaped((requests, down_weight.shape[1]), bfloat)], [], [exchange(sent)]
    )
    return (compact, summaries, result)


def solution(mesh):
    placed = (
        P(None, "head"),
        P(),
        P(),
        P(),
        P(),
        P("req", "head"),
        P("req", "head"),
        P("req", "head"),
        P("req", "head"),
        P("req", "head"),
        P(("req", "head"), None, None),
        P(("req", "head"), None),
        P(("req", "head"), None),
        P(("req", "head"), None),
        P(),
        P("req", None),
        P(),
    )
    return jax.shard_map(
        on_device if mesh.shape["req"] <= DIRECT else on_device_wide,
        mesh=mesh,
        in_specs=placed,
        out_specs=(P(("req", "head"), None, None), P(("req", "head"), None), P(None, "head")),
        check_vma=False,
    )
```

```python
import jax
import jax.numpy as jnp
import numpy as np
from jax import lax
from jax.experimental import pallas as pl
from jax.experimental.pallas import tpu as pltpu
from jax.sharding import PartitionSpec as P

D = 2048
HEADS = 20
KVH = 5
HD = 64
FF = 5120
PAGE = 128
KEEP = 64
NP = 16
R_DEV = 2
KVW = 640

DIRECT = 8

epsilon = 1e-06
negative = -1e30
both_axes = ("req", "head")


def rms_scale(values):
    return lax.rsqrt(jnp.mean(values * values, axis=-1, keepdims=True) + epsilon)


def rms_rows(values, gain):
    return values * rms_scale(values) * gain


def rotate(vectors, positions):
    half = vectors.shape[-1] // 2
    frequency = 10000.0 ** (-jnp.arange(half, dtype=jnp.float32) / half)
    angles = positions.astype(jnp.float32)[:, None] * frequency[None, :]
    cosine = jnp.cos(angles)[:, None, :]
    sine = jnp.sin(angles)[:, None, :]
    first = vectors[..., :half]
    second = vectors[..., half:]
    return jnp.concatenate(
        [first * cosine - second * sine, second * cosine + first * sine], axis=-1
    )


def compact_pages(pages, keep, weights):
    rows = jnp.arange(pages.shape[1], dtype=jnp.int32)
    picks = keep[:, :, None] == rows[None, None, :]
    kept = jnp.einsum(
        "pkr,prc->pkc", picks.astype(jnp.bfloat16), pages, preferred_element_type=jnp.float32
    ).astype(jnp.bfloat16)
    dropped = weights * (1.0 - jnp.sum(picks.astype(jnp.float32), axis=1))
    total = jnp.sum(dropped, axis=1)
    means = (
        jnp.einsum(
            "pr,prc->pc", dropped, pages.astype(jnp.float32), precision=lax.Precision.HIGHEST
        )
        / total[:, None]
    )
    return (kept, means.astype(jnp.bfloat16), jnp.log(total))


def held_request(rows, source):
    half = R_DEV // 2
    position = rows % R_DEV
    slot = rows // R_DEV * half + position - half
    continued = jnp.arange(source.shape[0], dtype=jnp.int32)
    matches = source[None, :] == slot[:, None]
    owner_cont = jnp.sum(jnp.where(matches, continued[None, :], 0), axis=1)
    carried = owner_cont // half * R_DEV + half + owner_cont % half
    return jnp.where(position < half, rows, carried)


def pick_rows(order, rows):
    chosen = order[:, None] == jnp.arange(rows.shape[0], dtype=jnp.int32)[None, :]
    return jnp.dot(
        chosen.astype(jnp.bfloat16), rows, preferred_element_type=jnp.float32
    ).astype(jnp.bfloat16)


def exchange(parts):
    return lax.all_to_all(parts, "req", split_axis=0, concat_axis=0, tiled=True)


def to_block_owner(rows):
    groups = lax.axis_size("req")
    lanes = lax.axis_size("head")
    per_lane = groups // lanes
    pairs = [
        (g * lanes + h, (per_lane * h + g // lanes) * lanes + g % lanes)
        for g in range(groups)
        for h in range(lanes)
    ]
    return lax.ppermute(rows, both_axes, pairs)


def whole_sum(partial):
    if lax.axis_size("req") > DIRECT:
        return lax.psum(partial, "req")
    groups = lax.axis_size("req")
    return jnp.sum(exchange(jnp.broadcast_to(partial[None], (groups,) + partial.shape)), axis=0)


def on_device_wide(
    hidden_in,
    attention_gain,
    query_gain,
    key_gain,
    feedforward_gain,
    input_weight,
    output_weight,
    gate_weight,
    up_weight,
    down_weight,
    old_cache,
    keep_rows,
    drop_weights,
    dest_slots,
    lengths,
    page_table,
    source,
):
    groups = lax.axis_size("req")
    lanes = lax.axis_size("head")
    group = lax.axis_index("req")
    lane = lax.axis_index("head")
    requests = hidden_in.shape[0]
    half = R_DEV // 2
    split = KVH * HD
    ratio = HEADS // KVH
    scale = HD ** (-0.5)
    pages_here = old_cache.shape[0]
    everyone = jnp.arange(requests, dtype=jnp.int32)
    holders = held_request(everyone, source)
    held = lax.dynamic_slice_in_dim(holders, group * R_DEV, R_DEV, 0)
    held_len = lengths[held]
    positions = held_len * PAGE

    whole = lax.all_gather(hidden_in, "head", axis=1, tiled=True)
    normed = rms_rows(whole.astype(jnp.float32), attention_gain).astype(jnp.bfloat16)
    features = D // groups
    inputs = pick_rows(holders, lax.dynamic_slice_in_dim(normed, group * features, features, 1))
    partial_qkv = jnp.dot(inputs, input_weight, preferred_element_type=jnp.float32)
    sent = jnp.broadcast_to(
        partial_qkv.reshape(groups, 1, R_DEV, -1), (groups, lanes, R_DEV, partial_qkv.shape[1])
    ).reshape(groups * lanes, R_DEV, -1)
    got = lax.all_to_all(sent, both_axes, split_axis=0, concat_axis=0, tiled=True)
    mixed = jnp.sum(got.reshape(groups, lanes, R_DEV, -1), axis=0).astype(jnp.bfloat16)
    held_qkv = jnp.swapaxes(mixed, 0, 1).reshape(R_DEV, -1).astype(jnp.float32)

    query = rotate(
        rms_rows(held_qkv[:, : HEADS * HD].reshape(R_DEV, HEADS, HD), query_gain), positions
    ).astype(jnp.bfloat16)
    key_new = rotate(
        rms_rows(held_qkv[:, HEADS * HD : (HEADS + KVH) * HD].reshape(R_DEV, KVH, HD), key_gain),
        positions,
    ).astype(jnp.bfloat16)
    value_new = held_qkv[:, (HEADS + KVH) * HD :].reshape(R_DEV, KVH, HD)
    kept, means, bias = compact_pages(old_cache, keep_rows, drop_weights)
    destination = dest_slots[0]
    fresh_ids = jnp.arange(pages_here, dtype=jnp.int32)
    inverse = jnp.sum(
        jnp.where(destination[None, :] == fresh_ids[:, None], fresh_ids[None, :], 0), axis=1
    )
    compact = kept[inverse].reshape(pages_here // 2, PAGE, KVW)
    summaries = means[inverse]
    per_lane = NP // lanes
    table = page_table.reshape(R_DEV, per_lane, lanes)
    mine = lax.dynamic_slice_in_dim(table, lane, 1, 2)[:, :, 0]
    logical = jnp.arange(per_lane, dtype=jnp.int32) * lanes + lane
    live = logical[None, :] < held_len[:, None]
    owner = jnp.any((mine[:, :, None] == fresh_ids[None, None, :]) & live[:, :, None], axis=1)
    query_groups = query.reshape(R_DEV, KVH, ratio, HD)
    row_keys = kept[:, :, :split].reshape(pages_here, KEEP, KVH, HD)
    row_values = kept[:, :, split:].reshape(pages_here, KEEP, KVH, HD)
    row_live = keep_rows >= 0
    allowed = owner[:, None, None, :, None] & row_live[None, None, None, :, :]
    scores = (
        jnp.einsum("rngd,pmnd->rngpm", query_groups, row_keys, preferred_element_type=jnp.float32)
        * scale
    )
    scores = jnp.where(allowed, scores, negative)
    mean_keys = means[:, :split].reshape(pages_here, KVH, HD)
    mean_values = means[:, split:].reshape(pages_here, KVH, HD)
    mean_scores = (
        jnp.einsum("rngd,pnd->rngp", query_groups, mean_keys, preferred_element_type=jnp.float32)
        * scale
        + bias[None, None, None, :]
    )
    mean_allowed = owner[:, None, None, :]
    mean_scores = jnp.where(mean_allowed, mean_scores, negative)
    own_score = (
        jnp.einsum("rngd,rnd->rng", query_groups, key_new, preferred_element_type=jnp.float32)
        * scale
    )
    own_score = jnp.where(lane == 0, own_score, negative)
    top = jnp.maximum(jnp.max(scores, axis=(3, 4)), jnp.max(mean_scores, axis=3))
    top = jnp.maximum(top, own_score)
    row_weight = jnp.where(allowed, jnp.exp(scores - top[..., None, None]), 0.0)
    mean_weight = jnp.where(mean_allowed, jnp.exp(mean_scores - top[..., None]), 0.0)
    own_weight = jnp.where(lane == 0, jnp.exp(own_score - top), 0.0)
    mass = jnp.sum(row_weight, axis=(3, 4)) + jnp.sum(mean_weight, axis=3) + own_weight
    total = jnp.einsum(
        "rngpm,pmnd->rngd",
        row_weight,
        row_values.astype(jnp.float32),
        precision=lax.Precision.HIGHEST,
    )
    total = total + jnp.einsum(
        "rngp,pnd->rngd",
        mean_weight,
        mean_values.astype(jnp.float32),
        precision=lax.Precision.HIGHEST,
    )
    total = total + own_weight[..., None] * value_new[:, :, None, :]

    some = mass > 0.0
    level = jnp.where(some, top + jnp.log(jnp.where(some, mass, 1.0)), negative)
    means_out = total / jnp.where(some, mass, 1.0)[..., None]
    own = HEADS * HD // groups
    parts = jnp.stack([means_out, jnp.broadcast_to(level[..., None], total.shape)])
    parts = jnp.transpose(parts.reshape(2, R_DEV, groups, own), (2, 1, 0, 3))
    parts = jnp.broadcast_to(
        parts.reshape(groups, 1, R_DEV, 2 * own), (groups, lanes, R_DEV, 2 * own)
    ).reshape(groups * lanes, R_DEV, 2 * own)
    came = lax.all_to_all(parts, both_axes, 0, 0, tiled=True)
    came = came.reshape(groups, lanes, R_DEV, 2 * own)
    outs, levels = came[..., :own], came[..., own:]
    weights = jnp.exp(levels - jnp.max(levels, axis=1, keepdims=True))
    attention = jnp.sum(outs * weights, axis=1) / jnp.sum(weights, axis=1)
    attention = attention.reshape(requests, own).astype(jnp.bfloat16)
    back = jnp.sum(
        jnp.where(holders[None, :] == everyone[:, None], everyone[None, :], 0), axis=1
    )
    projected = jnp.dot(
        pick_rows(back, attention), output_weight, preferred_element_type=jnp.float32
    )
    projected = projected + jnp.where(group == 0, hidden_in.astype(jnp.float32), 0.0)

    share = groups // lanes
    blocks = jnp.moveaxis(projected.reshape(requests, share, 1, features), 0, 2)
    blocks = jnp.broadcast_to(blocks, (share, lanes, requests, features))
    mid = jnp.sum(exchange(blocks.reshape(groups, requests, features)), axis=0)
    mid = to_block_owner(mid.astype(jnp.bfloat16)).astype(jnp.float32)
    squares = jnp.sum(mid * mid, axis=1, keepdims=True)
    gain_here = lax.dynamic_slice_in_dim(feedforward_gain, group * features, features, 0)
    inputs_mid = (mid * gain_here).astype(jnp.bfloat16)
    local_units = gate_weight.shape[1]
    piece = local_units // groups
    gates = jnp.dot(inputs_mid, gate_weight, preferred_element_type=jnp.float32)
    ups = jnp.dot(inputs_mid, up_weight, preferred_element_type=jnp.float32)
    both = jnp.concatenate(
        [
            gates.reshape(requests, groups, piece),
            ups.reshape(requests, groups, piece),
            jnp.broadcast_to(squares[:, :, None], (requests, groups, 1)),
        ],
        axis=2,
    )
    sums = jnp.sum(exchange(jnp.swapaxes(both, 0, 1)), axis=0)
    factor = lax.rsqrt(sums[:, 2 * piece :] / D + epsilon)
    gate = sums[:, :piece] * factor
    active = (jax.nn.silu(gate) * (sums[:, piece : 2 * piece] * factor)).astype(jnp.bfloat16)
    active_here = lax.all_gather(to_block_owner(active), "head", axis=1, tiled=True)
    down = jnp.dot(active_here, down_weight, preferred_element_type=jnp.float32)
    residual = [jnp.where(group == lane * share + k, mid, 0.0) for k in range(share)]
    down = down + jnp.concatenate(residual, axis=1)
    result = whole_sum(down).astype(jnp.bfloat16)
    return (compact, summaries, result)


TILE = 128
bfloat = jnp.bfloat16
single = jnp.float32


TERMS = 4


def three_terms(value, place):
    high = value.astype(bfloat).astype(single)
    rest = value - high
    middle = rest.astype(bfloat).astype(single)
    low = jnp.where(place == 2, rest - middle, 0.0)
    return jnp.where(place == 0, high, jnp.where(place == 1, middle, low))


def iota(shape, axis):
    return lax.broadcasted_iota(jnp.int32, shape, axis)


def run(kernel, outs, far, near, scratch=(), flops=0):
    in_specs = [pl.BlockSpec(memory_space=pltpu.HBM) for _ in far]
    in_specs += [pl.BlockSpec(memory_space=pltpu.VMEM) for _ in near]
    moved = sum(a.size * a.dtype.itemsize for a in [*far, *near, *outs])
    return pl.pallas_call(
        kernel,
        out_shape=list(outs),
        in_specs=in_specs,
        out_specs=[pl.BlockSpec(memory_space=pltpu.VMEM) for _ in outs],
        scratch_shapes=list(scratch),
        compiler_params=pltpu.CompilerParams(vmem_limit_bytes=16 * 2**20),
        cost_estimate=pl.CostEstimate(flops=flops, bytes_accessed=moved, transcendentals=0),
    )(*[pltpu.with_memory_space_constraint(a, pltpu.HBM) for a in far], *near)


def fetch(sources, targets, done):
    copies = [
        pltpu.make_async_copy(source, target, done.at[k])
        for k, (source, target) in enumerate(zip(sources, targets))
    ]
    for copy in copies:
        copy.start()
    return copies


def local_like(*arrays):
    return [pltpu.VMEM(a.shape, a.dtype) for a in arrays]


def scalar_like(*arrays):
    return [pltpu.SMEM(a.shape, a.dtype) for a in arrays]


def row_order(source, count, to_holder):
    first, second = iota((count, count), 0), iota((count, count), 1)
    if not to_holder:
        first, second = second, first
    order = (first == second) & (first % R_DEV == 0)
    for c in range(source.shape[1]):
        order = order | ((first == source[0, c] * R_DEV + 1) & (second == c * R_DEV + 1))
    return order.astype(single).astype(bfloat)


def shaped(shape, dtype):
    return jax.ShapeDtypeStruct(shape, dtype)


def first_kernel(
    source_far, gain_far, weight_far, hidden_far, one, two, three, sent, block, source, gain,
    weight, hidden, lanes_of, wide, done
):
    copies = fetch(
        (source_far, gain_far, weight_far, hidden_far), (source, gain, weight, hidden), done
    )
    rows = hidden.shape[0]
    groups = rows // R_DEV
    lanes = sent.shape[0] // groups
    columns, features = weight.shape
    group = lax.axis_index("req")
    share = groups // lanes
    squares = 0.0
    for turn, values in enumerate((one, two, three)):
        values = values[...].astype(single)
        lanes_of[turn + 1] = values
        squares = squares + jnp.sum(values * values, axis=1, keepdims=True)
    copies[3].wait()
    values = hidden[...].astype(single)
    lanes_of[0] = values
    squares = squares + jnp.sum(values * values, axis=1, keepdims=True)
    factor = lax.rsqrt(squares / D + epsilon)
    here = pl.ds(pl.multiple_of(group * features, features), features)
    within = pl.ds(pl.multiple_of(group % share * features, features), features)
    mine = lanes_of[group // share ^ lax.axis_index("head"), :, within]
    block[...] = mine.astype(bfloat)
    wide[...] = jnp.zeros_like(wide)
    for copy in copies[:3]:
        copy.wait()
    normed = (mine * factor * gain[:, here]).astype(bfloat)
    order = row_order(source, rows, True)
    normed = jnp.dot(order, normed, preferred_element_type=single).astype(bfloat)
    wide[:, :columns] = dot_rows(normed, weight[...])
    for g in range(groups):
        tile = jnp.concatenate(
            [
                wide[R_DEV * g : R_DEV * (g + 1), TILE * j : TILE * (j + 1)]
                for j in range(wide.shape[1] // TILE)
            ],
            axis=0,
        )
        for k in range(lanes):
            sent[g * lanes + k] = tile


def dot_rows(left, right):
    return lax.dot_general(left, right, (((1,), (1,)), ((), ())), preferred_element_type=single)


def prepare_kernel(*refs):
    far, refs = refs[:12], refs[12:]
    (compact, summaries, kept, added, tables, mine, theirs), refs = refs[:7], refs[7:]
    near, (ordered, plain, dealt, done) = refs[:12], refs[12:]
    copies = fetch(far, near, done)
    (dest, lengths, source, table, keep, weights, query_gain, key_gain, turns) = near[:9]
    pages, gate, up = near[9:]
    group = lax.axis_index("req")
    lane = lax.axis_index("head")
    lanes = lax.axis_size("head")
    for copy in copies[:9]:
        copy.wait()

    carried = 0
    for c in range(source.shape[1]):
        carried = carried + jnp.where(source[0, c] == group, c, 0)
    held_len = (lengths[0, group * R_DEV], lengths[0, carried * R_DEV + 1])
    count, rows, _ = pages.shape
    owned = []
    for r in range(R_DEV):
        slots = []
        for i in range(table.shape[1] // lanes):
            j = i * lanes + lane
            slots.append(jnp.where(j < held_len[r], table[r, j], -1))
        owned.append(slots)

    def owner(r, p):
        found = owned[r][0] == p
        for slot in owned[r][1:]:
            found = found | (slot == p)
        return found

    row = iota((32, TILE), 0)
    odd = (row & 1) == 1
    half_rows = turns.shape[0] // 2
    for part in range(2):
        pair = [turns[pl.ds(part * half_rows + held_len[r], 1), :] for r in range(R_DEV)]
        tables[32 * part : 32 * (part + 1), :] = jnp.where(odd, pair[1], pair[0])
    query_rows = HEADS * HD // TILE * R_DEV
    for c in range(TILE // HD):
        columns = slice(HD * c, HD * (c + 1))
        tables[64 : 64 + query_rows, columns] = jnp.broadcast_to(
            query_gain[...], (query_rows, HD)
        )
        tables[64 + query_rows : 96, columns] = jnp.broadcast_to(
            key_gain[...], (32 - query_rows, HD)
        )

    column = iota((1, TILE), 1)
    entries = count * KEEP
    added[...] = jnp.full_like(added, negative)
    extra = [
        jnp.where((column == count + r) & (lane == 0), 0.0, negative) for r in range(R_DEV)
    ]
    weight_columns = weights[...].T
    rows_of = iota((rows, KEEP), 0)
    place = iota((rows, KEEP), 1)
    copies[9].wait()
    for p in range(count):
        picks = (keep[p : p + 1, :] == rows_of).astype(single)
        dropped = weight_columns[:, p : p + 1] * (1.0 - jnp.sum(picks, axis=1, keepdims=True))
        total = jnp.sum(dropped, axis=0, keepdims=True)
        left = jnp.concatenate([picks, three_terms(dropped, place)], axis=1).astype(bfloat)
        both = lax.dot_general(
            left, pages[p], (((0,), (0,)), ((), ())), preferred_element_type=single
        )
        rows_kept = both[:KEEP].astype(bfloat)
        kept[KEEP * p : KEEP * (p + 1), :] = rows_kept
        slot = dest[0, p]
        start = pl.multiple_of((slot & 1) * KEEP, KEEP)
        compact[slot >> 1, pl.ds(start, KEEP), :] = rows_kept
        mean = both[KEEP : KEEP + 1] + both[KEEP + 1 : KEEP + 2] + both[KEEP + 2 : KEEP + 3]
        mean = mean / total
        plain[p : p + 1, :] = mean
        ordered[pl.ds(slot, 1), :] = mean
        live = jnp.where(keep[p : p + 1, :] >= 0, 0.0, negative)
        for r in range(R_DEV):
            here = owner(r, p)
            added[r : r + 1, KEEP * p : KEEP * (p + 1)] = jnp.where(here, live, negative)
            level = jnp.where(here, jnp.log(total), negative)
            extra[r] = jnp.where(column == p, level, extra[r])
    for r in range(R_DEV):
        added[r : r + 1, entries : entries + TILE] = extra[r]
    plain[count:, :] = jnp.zeros_like(plain[count:, :])
    kept[entries:, :] = plain[...].astype(bfloat)
    summaries[...] = ordered[...].astype(bfloat)

    for copy in copies[10:]:
        copy.wait()
    block = gate.shape[1] // 2
    piece = block // 2
    for k in range(2):
        for b in range(2):
            columns = slice(b * block + k * piece, b * block + (k + 1) * piece)
            start = b * block
            dealt[k, :, start : start + piece] = gate[:, columns].astype(single)
            dealt[k, :, start + piece : start + block] = up[:, columns].astype(single)
    mine[...] = dealt[lane & 1].astype(bfloat)
    theirs[...] = dealt[1 - (lane & 1)].astype(bfloat)


def attend_kernel(came, kept, added, tables, sent, x, extra_k, extra_v, out, logs):
    lanes = lax.axis_size("head")
    groups = came.shape[0] // lanes
    width = (HEADS + 2 * KVH) * HD // lanes
    span = -(-KVH * HD // TILE) * TILE
    key_cols = slice(0, span)
    value_cols = slice(KVW - span, KVW)
    first_key = HEADS * HD // TILE * R_DEV
    scale = HD ** (-0.5)
    x[...] = jnp.zeros_like(x)
    column = iota((8, TILE), 1)
    for k in range(lanes):
        tile = came[k].astype(single)
        for g in range(1, groups):
            tile = tile + came[g * lanes + k].astype(single)
        tile = tile.astype(bfloat).astype(single)
        base, shift = divmod(width * k, TILE)
        base = base * R_DEV
        if shift:
            tile = pltpu.roll(tile, shift, 1)
            x[base + 2 : base + 10, :] += jnp.where(column < shift, tile, 0.0)
        x[base : base + 8, :] += jnp.where(column >= shift, tile, 0.0)
    values = x[...]
    same_head = (iota((TILE, TILE), 0) // HD == iota((TILE, TILE), 1) // HD).astype(single)
    squares = jnp.dot(
        values * values, same_head, precision=lax.Precision.HIGHEST, preferred_element_type=single
    )
    normed = values * lax.rsqrt(squares / HD + epsilon) * tables[64:96, :]
    early = iota(values.shape, 1) % HD < HD // 2
    swapped = jnp.where(
        early, pltpu.roll(normed, TILE - HD // 2, 1), pltpu.roll(normed, HD // 2, 1)
    )
    turned = normed * tables[0:32, :] + swapped * tables[32:64, :]
    turned = turned.astype(bfloat).astype(single)

    rows = 24
    row = iota((rows, TILE), 0)
    half = iota((rows, TILE), 1) // HD
    key_head = row >> 2
    query = jnp.where(row < first_key, turned[:rows], 0.0)
    other = pltpu.roll(query, HD, 1)
    queries = []
    for u in range(2):
        placed = jnp.where(
            half == (key_head & 1), jnp.where((key_head & 1) == u, query, other), 0.0
        )
        queries.append(
            jnp.concatenate(
                [jnp.where((key_head >> 1) == c, placed, 0.0) for c in range(span // TILE)], axis=1
            )
        )
    queries = jnp.concatenate(queries, axis=0).astype(bfloat)

    extras = extra_k.shape[0]
    entries = kept.shape[0] - extras
    count = entries // KEEP
    extra_k[...] = kept[entries:, key_cols].astype(single)
    extra_v[...] = kept[entries:, value_cols].astype(single)
    first_value = first_key + KVH * HD // TILE * R_DEV
    for c in range(span // TILE):
        at = slice(c * TILE, (c + 1) * TILE)
        r = first_key + R_DEV * c
        extra_k[count : count + R_DEV, at] = turned[r : r + R_DEV]
        r = first_value + R_DEV * c
        extra_v[count : count + R_DEV, at] = values[r : r + R_DEV]

    def by_request(columns, size):
        odd = (iota((2 * rows, size), 0) & 1) == 1
        return jnp.where(odd, added[1:2, columns], added[0:1, columns])

    scores = dot_rows(queries, kept[:entries, key_cols]) * scale
    scores = scores + by_request(slice(0, entries), entries)
    extra = dot_rows(queries, extra_k[...].astype(bfloat)) * scale
    extra = extra + by_request(slice(entries, entries + extras), extras)
    top = jnp.maximum(
        jnp.max(scores, axis=1, keepdims=True), jnp.max(extra, axis=1, keepdims=True)
    )
    weight = jnp.where(scores > 0.5 * negative, jnp.exp(scores - top), 0.0)
    extra_weight = jnp.where(extra > 0.5 * negative, jnp.exp(extra - top), 0.0)
    mass = jnp.sum(weight, axis=1, keepdims=True) + jnp.sum(extra_weight, axis=1, keepdims=True)

    def weighted(parts, right):
        high = parts.astype(bfloat)
        low = (parts - high.astype(single)).astype(bfloat)
        return jnp.dot(high, right, preferred_element_type=single) + jnp.dot(
            low, right, preferred_element_type=single
        )

    total = weighted(weight, kept[:entries, value_cols]) + weighted(
        extra_weight, extra_v[...].astype(bfloat)
    )
    some = mass > 0.0
    mass = jnp.where(some, mass, 1.0)
    total = total / mass
    level = jnp.where(some, top + jnp.log(mass), negative)

    slot = key_head + (KVW // 2 - (KVW - span)) // HD
    results = []
    for u in range(2):
        mine = total[rows * u : rows * (u + 1)]
        picked = mine[:, :TILE]
        for c in range(1, span // TILE):
            picked = jnp.where((slot >> 1) == c, mine[:, c * TILE : (c + 1) * TILE], picked)
        results.append(jnp.where((slot & 1) == u, picked, pltpu.roll(picked, HD, 1)))
    out[...] = jnp.where(half == 0, results[0], results[1])
    logs[...] = jnp.broadcast_to(level, logs.shape)
    own = HEADS * HD // lanes
    size = 6
    column = iota((size, TILE), 1)
    here = column // TERMS == iota((size, TILE), 0)
    for k in range(lanes):
        r = own * k // TILE * R_DEV
        tile = [out[r : r + size, :]]
        for u in range(2):
            coded = three_terms(logs[rows * u + r : rows * u + r + size, :], column % TERMS)
            tile.append(jnp.sum(jnp.where(here, coded, 0.0), axis=0, keepdims=True))
        tile = jnp.concatenate(tile, axis=0).astype(bfloat)
        for g in range(groups):
            sent[g * lanes + k] = tile


def project_kernel(source_far, came, first, second, sent, source, logs, rows, pieces, done):
    (copy,) = fetch((source_far,), (source,), done)
    lanes = lax.axis_size("head")
    groups = came.shape[0] // lanes
    group = lax.axis_index("req")
    features = first.shape[0]
    requests = rows.shape[0]
    size = 6
    tiles = [came[d].astype(single) for d in range(groups * lanes)]
    for g in range(groups):
        for k in range(lanes):
            logs[k, 2 * g : 2 * g + 2, :] = tiles[g * lanes + k][size:]
    spread = (iota((8, TILE), 1) // TERMS == iota((8, TILE), 0)).astype(single).astype(bfloat)
    levels = [dot_rows(spread, logs[k].astype(bfloat)) for k in range(lanes)]
    top = jnp.maximum(jnp.maximum(levels[0], levels[1]), jnp.maximum(levels[2], levels[3]))
    shares = [jnp.exp(level - top) for level in levels]
    mass = sum(shares)
    shares = [share / mass for share in shares]
    lower = iota((8, TILE), 1) < HD
    for g in range(groups):
        mixed = 0.0
        for k in range(lanes):
            share = shares[k]
            share = jnp.where(lower, share[:, 2 * g : 2 * g + 1], share[:, 2 * g + 1 : 2 * g + 2])
            mixed = mixed + share * tiles[g * lanes + k]
        for j in range(size // R_DEV):
            rows[R_DEV * g : R_DEV * (g + 1), TILE * j : TILE * (j + 1)] = mixed[
                R_DEV * j : R_DEV * (j + 1)
            ]
    width = rows.shape[1]
    shift = lax.rem(lax.axis_index("head") * (2 * features), TILE)
    attention = rows[...].astype(bfloat).astype(single)
    attention = pltpu.roll(attention, lax.rem(width - shift, width), 1)
    copy.wait()
    order = row_order(source, requests, False)
    attention = jnp.dot(order, attention.astype(bfloat), preferred_element_type=single)
    for b in range(2):
        pieces[b] = attention[:, features * b : features * (b + 1)]
    total = 0.0
    width = sent.shape[1]
    columns = pl.ds(pl.multiple_of((group & 1) * width, width), width)
    for turn, weight in enumerate((first, second)):
        piece = pieces[(group & 1) ^ turn].astype(bfloat)
        total = total + jnp.dot(piece, weight[:, columns], preferred_element_type=single)
    sent[...] = total


def units_kernel(
    gain_far, own, one, two, three, hidden, mine, theirs, sent, mid_out, gain, done
):
    (copy,) = fetch((gain_far,), (gain,), done)
    rows, features = own.shape
    share = sent.shape[0] // lax.axis_size("head")
    group = lax.axis_index("req")
    lane = lax.axis_index("head")
    here = pl.ds(pl.multiple_of(group * features, features), features)
    mid = (own[...] + one[...]) + (two[...] + three[...])
    mid = (hidden[...].astype(single) + mid).astype(bfloat)
    mid_out[...] = mid
    mid = mid.astype(single)
    squares = jnp.sum(mid * mid, axis=1, keepdims=True)
    block = mine.shape[1] // share
    terms = three_terms(squares, iota((rows, sent.shape[2] - block), 1)).astype(bfloat)
    copy.wait()
    inputs = (mid * gain[:, here]).astype(bfloat)
    for turn, weight in enumerate((mine, theirs)):
        units = jnp.dot(inputs, weight[...], preferred_element_type=single).astype(bfloat)
        target = (lane ^ turn) * share
        for b in range(share):
            sent[target + b, :, :block] = units[:, block * b : block * (b + 1)]
            sent[target + b, :, block:] = terms


def active_kernel(came, active):
    total = came[0].astype(single)
    for g in range(1, came.shape[0]):
        total = total + came[g].astype(single)
    piece = active.shape[1]
    squares = jnp.sum(total[:, 2 * piece : 2 * piece + 3], axis=1, keepdims=True)
    factor = lax.rsqrt(squares / D + epsilon)
    gate = total[:, :piece] * factor
    up = total[:, piece : 2 * piece] * factor
    active[...] = (gate / (1.0 + jnp.exp(-gate)) * up).astype(bfloat)


def down_kernel(own, one, two, three, weight, mid, sent, active):
    groups, rows, width = sent.shape
    piece = own.shape[1]
    half = mid.shape[1]
    for turn, values in enumerate((own, one, two, three)):
        active[turn] = values[...]
    share = width // half
    group = lax.axis_index("req")
    lane = lax.axis_index("head")
    first = group // (2 * share) * 2 ^ lane
    down = jnp.dot(active[first], weight[:piece, :], preferred_element_type=single)
    down = down + jnp.dot(active[first ^ 1], weight[piece:, :], preferred_element_type=single)
    residual = mid[...].astype(single)
    for b in range(share):
        columns = slice(half * b, half * (b + 1))
        mine = group == lane * share + b
        total = (down[:, columns] + jnp.where(mine, residual, 0.0)).astype(bfloat)
        for g in range(groups):
            sent[g, :, columns] = total


def result_kernel(came, result):
    total = came[0].astype(single)
    for g in range(1, came.shape[0]):
        total = total + came[g].astype(single)
    result[...] = total.astype(bfloat)


def rotation_table():
    half = HD // 2
    size = -(-(NP + 1) // 8) * 8
    frequency = 10000.0 ** (-np.arange(half) / half)
    angles = PAGE * np.arange(size)[:, None] * frequency[None, :]
    cosine, sine = np.cos(angles), np.sin(angles)
    wide = [np.tile(np.concatenate(pair, axis=1), (1, TILE // HD)) for pair in
            ((cosine, cosine), (-sine, sine))]
    return jnp.asarray(np.concatenate(wide), dtype=single)


def swapped_lanes(value, turn):
    lanes = lax.axis_size("head")
    return lax.ppermute(value, "head", [(k, k ^ turn) for k in range(lanes)])


def from_lanes(value):
    return [value] + [swapped_lanes(value, turn) for turn in range(1, lax.axis_size("head"))]


def handed_over(value, turn):
    groups = lax.axis_size("req")
    lanes = lax.axis_size("head")
    share = groups // lanes
    pairs = [
        (g * lanes + h, (share * h + ((g & 1) ^ turn)) * lanes + g // share)
        for g in range(groups)
        for h in range(lanes)
    ]
    return lax.ppermute(value, both_axes, pairs)


def on_device(
    hidden_in,
    attention_gain,
    query_gain,
    key_gain,
    feedforward_gain,
    input_weight,
    output_weight,
    gate_weight,
    up_weight,
    down_weight,
    old_cache,
    keep_rows,
    drop_weights,
    dest_slots,
    lengths,
    page_table,
    source,
):
    groups = lax.axis_size("req")
    lanes = lax.axis_size("head")
    requests = hidden_in.shape[0]
    pages_here = old_cache.shape[0]
    devices = groups * lanes
    features = D // groups
    copies = pltpu.SemaphoreType.DMA

    columns = input_weight.shape[1]
    padded = -(-columns // TILE) * TILE
    holds = source[None, :]
    gain = attention_gain[None, :]
    weight = input_weight.T
    far = [holds, gain, weight, hidden_in]
    sent, hidden_block = run(
        first_kernel,
        [
            shaped((devices, R_DEV * padded // TILE, TILE), single),
            shaped((requests, features), bfloat),
        ],
        far,
        from_lanes(hidden_in)[1:],
        [
            *scalar_like(holds),
            *local_like(*far[1:]),
            pltpu.VMEM((lanes,) + hidden_in.shape, single),
            pltpu.VMEM((requests, padded), single),
            copies((len(far),)),
        ],
        2 * requests * features * columns,
    )
    came = lax.all_to_all(sent, both_axes, 0, 0, tiled=True)
    output_weights, _ = lax.optimization_barrier((output_weight, sent))
    handed = [handed_over(output_weights, turn) for turn in range(2)]

    scalars = [dest_slots, lengths[None, :], holds, page_table]
    arrays = [
        keep_rows,
        drop_weights,
        query_gain[None, :],
        key_gain[None, :],
        rotation_table(),
        old_cache,
        gate_weight,
        up_weight,
    ]
    entries = pages_here * KEEP
    extras = 16
    compact, summaries, kept, added, tables, mine, theirs = run(
        prepare_kernel,
        [
            shaped((pages_here // 2, PAGE, KVW), bfloat),
            shaped((pages_here, KVW), bfloat),
            shaped((entries + extras, KVW), bfloat),
            shaped((8, entries + TILE), single),
            shaped((96, TILE), single),
            shaped(gate_weight.shape, bfloat),
            shaped(gate_weight.shape, bfloat),
        ],
        scalars + arrays,
        [],
        [
            *scalar_like(*scalars),
            *local_like(*arrays),
            pltpu.VMEM((pages_here, KVW), single),
            pltpu.VMEM((extras, KVW), single),
            pltpu.VMEM((2,) + gate_weight.shape, single),
            copies((len(scalars + arrays),)),
        ],
        2 * pages_here * TILE * PAGE * KVW,
    )
    came, *handed = lax.optimization_barrier((came, *handed))
    span = -(-KVH * HD // TILE) * TILE
    (parts,) = run(
        attend_kernel,
        [shaped((devices, 8, TILE), bfloat)],
        [],
        [came, kept, added, tables],
        [
            pltpu.VMEM((32, TILE), single),
            pltpu.VMEM((extras, span), single),
            pltpu.VMEM((extras, span), single),
            pltpu.VMEM((24, TILE), single),
            pltpu.VMEM((48, TILE), single),
        ],
        6 * 48 * entries * span,
    )
    theirs, _ = lax.optimization_barrier((theirs, parts))
    theirs = swapped_lanes(theirs, 1)
    came = lax.all_to_all(parts, both_axes, 0, 0, tiled=True)
    came, theirs = lax.optimization_barrier((came, theirs))
    (sent,) = run(
        project_kernel,
        [shaped((requests, features), single)],
        [holds],
        [came, *handed],
        [
            *scalar_like(holds),
            pltpu.VMEM((lanes, 2 * groups, TILE), single),
            pltpu.VMEM((requests, 3 * TILE), single),
            pltpu.VMEM((2, requests, output_weight.shape[0]), single),
            copies((1,)),
        ],
        2 * requests * output_weight.size,
    )
    gain = feedforward_gain[None, :]
    block = gate_weight.shape[1] // 2
    sent, mid = run(
        units_kernel,
        [
            shaped((groups, requests, block + TILE), bfloat),
            shaped((requests, features), bfloat),
        ],
        [gain],
        [*from_lanes(sent), hidden_block, mine, theirs],
        [*local_like(gain), copies((1,))],
        4 * requests * gate_weight.size,
    )
    (active,) = run(
        active_kernel, [shaped((requests, block // 2), bfloat)], [], [exchange(sent)]
    )
    (sent,) = run(
        down_kernel,
        [shaped((groups, requests, down_weight.shape[1]), bfloat)],
        [],
        [*from_lanes(active), down_weight, mid],
        [pltpu.VMEM((lanes,) + active.shape, bfloat)],
        2 * requests * down_weight.size,
    )
    (result,) = run(
        result_kernel, [shaped((requests, down_weight.shape[1]), bfloat)], [], [exchange(sent)]
    )
    return (compact, summaries, result)


def solution(mesh):
    placed = (
        P(None, "head"),
        P(),
        P(),
        P(),
        P(),
        P("req", "head"),
        P("req", "head"),
        P("req", "head"),
        P("req", "head"),
        P("req", "head"),
        P(("req", "head"), None, None),
        P(("req", "head"), None),
        P(("req", "head"), None),
        P(("req", "head"), None),
        P(),
        P("req", None),
        P(),
    )
    return jax.shard_map(
        on_device if mesh.shape["req"] <= DIRECT else on_device_wide,
        mesh=mesh,
        in_specs=placed,
        out_specs=(P(("req", "head"), None, None), P(("req", "head"), None), P(None, "head")),
        check_vma=False,
    )
```

```python
import jax
import jax.numpy as jnp
import numpy as np
from jax import lax
from jax.experimental import pallas as pl
from jax.experimental.pallas import tpu as pltpu
from jax.sharding import PartitionSpec as P

D = 2048
HEADS = 20
KVH = 5
HD = 64
FF = 5120
PAGE = 128
KEEP = 64
NP = 16
R_DEV = 2
KVW = 640

DIRECT = 8

epsilon = 1e-06
negative = -1e30
both_axes = ("req", "head")


def rms_scale(values):
    return lax.rsqrt(jnp.mean(values * values, axis=-1, keepdims=True) + epsilon)


def rms_rows(values, gain):
    return values * rms_scale(values) * gain


def rotate(vectors, positions):
    half = vectors.shape[-1] // 2
    frequency = 10000.0 ** (-jnp.arange(half, dtype=jnp.float32) / half)
    angles = positions.astype(jnp.float32)[:, None] * frequency[None, :]
    cosine = jnp.cos(angles)[:, None, :]
    sine = jnp.sin(angles)[:, None, :]
    first = vectors[..., :half]
    second = vectors[..., half:]
    return jnp.concatenate(
        [first * cosine - second * sine, second * cosine + first * sine], axis=-1
    )


def compact_pages(pages, keep, weights):
    rows = jnp.arange(pages.shape[1], dtype=jnp.int32)
    picks = keep[:, :, None] == rows[None, None, :]
    kept = jnp.einsum(
        "pkr,prc->pkc", picks.astype(jnp.bfloat16), pages, preferred_element_type=jnp.float32
    ).astype(jnp.bfloat16)
    dropped = weights * (1.0 - jnp.sum(picks.astype(jnp.float32), axis=1))
    total = jnp.sum(dropped, axis=1)
    means = (
        jnp.einsum(
            "pr,prc->pc", dropped, pages.astype(jnp.float32), precision=lax.Precision.HIGHEST
        )
        / total[:, None]
    )
    return (kept, means.astype(jnp.bfloat16), jnp.log(total))


def held_request(rows, source):
    half = R_DEV // 2
    position = rows % R_DEV
    slot = rows // R_DEV * half + position - half
    continued = jnp.arange(source.shape[0], dtype=jnp.int32)
    matches = source[None, :] == slot[:, None]
    owner_cont = jnp.sum(jnp.where(matches, continued[None, :], 0), axis=1)
    carried = owner_cont // half * R_DEV + half + owner_cont % half
    return jnp.where(position < half, rows, carried)


def pick_rows(order, rows):
    chosen = order[:, None] == jnp.arange(rows.shape[0], dtype=jnp.int32)[None, :]
    return jnp.dot(
        chosen.astype(jnp.bfloat16), rows, preferred_element_type=jnp.float32
    ).astype(jnp.bfloat16)


def exchange(parts):
    return lax.all_to_all(parts, "req", split_axis=0, concat_axis=0, tiled=True)


def to_block_owner(rows):
    groups = lax.axis_size("req")
    lanes = lax.axis_size("head")
    per_lane = groups // lanes
    pairs = [
        (g * lanes + h, (per_lane * h + g // lanes) * lanes + g % lanes)
        for g in range(groups)
        for h in range(lanes)
    ]
    return lax.ppermute(rows, both_axes, pairs)


def whole_sum(partial):
    if lax.axis_size("req") > DIRECT:
        return lax.psum(partial, "req")
    groups = lax.axis_size("req")
    return jnp.sum(exchange(jnp.broadcast_to(partial[None], (groups,) + partial.shape)), axis=0)


def on_device_wide(
    hidden_in,
    attention_gain,
    query_gain,
    key_gain,
    feedforward_gain,
    input_weight,
    output_weight,
    gate_weight,
    up_weight,
    down_weight,
    old_cache,
    keep_rows,
    drop_weights,
    dest_slots,
    lengths,
    page_table,
    source,
):
    groups = lax.axis_size("req")
    lanes = lax.axis_size("head")
    group = lax.axis_index("req")
    lane = lax.axis_index("head")
    requests = hidden_in.shape[0]
    half = R_DEV // 2
    split = KVH * HD
    ratio = HEADS // KVH
    scale = HD ** (-0.5)
    pages_here = old_cache.shape[0]
    everyone = jnp.arange(requests, dtype=jnp.int32)
    holders = held_request(everyone, source)
    held = lax.dynamic_slice_in_dim(holders, group * R_DEV, R_DEV, 0)
    held_len = lengths[held]
    positions = held_len * PAGE

    whole = lax.all_gather(hidden_in, "head", axis=1, tiled=True)
    normed = rms_rows(whole.astype(jnp.float32), attention_gain).astype(jnp.bfloat16)
    features = D // groups
    inputs = pick_rows(holders, lax.dynamic_slice_in_dim(normed, group * features, features, 1))
    partial_qkv = jnp.dot(inputs, input_weight, preferred_element_type=jnp.float32)
    sent = jnp.broadcast_to(
        partial_qkv.reshape(groups, 1, R_DEV, -1), (groups, lanes, R_DEV, partial_qkv.shape[1])
    ).reshape(groups * lanes, R_DEV, -1)
    got = lax.all_to_all(sent, both_axes, split_axis=0, concat_axis=0, tiled=True)
    mixed = jnp.sum(got.reshape(groups, lanes, R_DEV, -1), axis=0).astype(jnp.bfloat16)
    held_qkv = jnp.swapaxes(mixed, 0, 1).reshape(R_DEV, -1).astype(jnp.float32)

    query = rotate(
        rms_rows(held_qkv[:, : HEADS * HD].reshape(R_DEV, HEADS, HD), query_gain), positions
    ).astype(jnp.bfloat16)
    key_new = rotate(
        rms_rows(held_qkv[:, HEADS * HD : (HEADS + KVH) * HD].reshape(R_DEV, KVH, HD), key_gain),
        positions,
    ).astype(jnp.bfloat16)
    value_new = held_qkv[:, (HEADS + KVH) * HD :].reshape(R_DEV, KVH, HD)
    kept, means, bias = compact_pages(old_cache, keep_rows, drop_weights)
    destination = dest_slots[0]
    fresh_ids = jnp.arange(pages_here, dtype=jnp.int32)
    inverse = jnp.sum(
        jnp.where(destination[None, :] == fresh_ids[:, None], fresh_ids[None, :], 0), axis=1
    )
    compact = kept[inverse].reshape(pages_here // 2, PAGE, KVW)
    summaries = means[inverse]
    per_lane = NP // lanes
    table = page_table.reshape(R_DEV, per_lane, lanes)
    mine = lax.dynamic_slice_in_dim(table, lane, 1, 2)[:, :, 0]
    logical = jnp.arange(per_lane, dtype=jnp.int32) * lanes + lane
    live = logical[None, :] < held_len[:, None]
    owner = jnp.any((mine[:, :, None] == fresh_ids[None, None, :]) & live[:, :, None], axis=1)
    query_groups = query.reshape(R_DEV, KVH, ratio, HD)
    row_keys = kept[:, :, :split].reshape(pages_here, KEEP, KVH, HD)
    row_values = kept[:, :, split:].reshape(pages_here, KEEP, KVH, HD)
    row_live = keep_rows >= 0
    allowed = owner[:, None, None, :, None] & row_live[None, None, None, :, :]
    scores = (
        jnp.einsum("rngd,pmnd->rngpm", query_groups, row_keys, preferred_element_type=jnp.float32)
        * scale
    )
    scores = jnp.where(allowed, scores, negative)
    mean_keys = means[:, :split].reshape(pages_here, KVH, HD)
    mean_values = means[:, split:].reshape(pages_here, KVH, HD)
    mean_scores = (
        jnp.einsum("rngd,pnd->rngp", query_groups, mean_keys, preferred_element_type=jnp.float32)
        * scale
        + bias[None, None, None, :]
    )
    mean_allowed = owner[:, None, None, :]
    mean_scores = jnp.where(mean_allowed, mean_scores, negative)
    own_score = (
        jnp.einsum("rngd,rnd->rng", query_groups, key_new, preferred_element_type=jnp.float32)
        * scale
    )
    own_score = jnp.where(lane == 0, own_score, negative)
    top = jnp.maximum(jnp.max(scores, axis=(3, 4)), jnp.max(mean_scores, axis=3))
    top = jnp.maximum(top, own_score)
    row_weight = jnp.where(allowed, jnp.exp(scores - top[..., None, None]), 0.0)
    mean_weight = jnp.where(mean_allowed, jnp.exp(mean_scores - top[..., None]), 0.0)
    own_weight = jnp.where(lane == 0, jnp.exp(own_score - top), 0.0)
    mass = jnp.sum(row_weight, axis=(3, 4)) + jnp.sum(mean_weight, axis=3) + own_weight
    total = jnp.einsum(
        "rngpm,pmnd->rngd",
        row_weight,
        row_values.astype(jnp.float32),
        precision=lax.Precision.HIGHEST,
    )
    total = total + jnp.einsum(
        "rngp,pnd->rngd",
        mean_weight,
        mean_values.astype(jnp.float32),
        precision=lax.Precision.HIGHEST,
    )
    total = total + own_weight[..., None] * value_new[:, :, None, :]

    some = mass > 0.0
    level = jnp.where(some, top + jnp.log(jnp.where(some, mass, 1.0)), negative)
    means_out = total / jnp.where(some, mass, 1.0)[..., None]
    own = HEADS * HD // groups
    parts = jnp.stack([means_out, jnp.broadcast_to(level[..., None], total.shape)])
    parts = jnp.transpose(parts.reshape(2, R_DEV, groups, own), (2, 1, 0, 3))
    parts = jnp.broadcast_to(
        parts.reshape(groups, 1, R_DEV, 2 * own), (groups, lanes, R_DEV, 2 * own)
    ).reshape(groups * lanes, R_DEV, 2 * own)
    came = lax.all_to_all(parts, both_axes, 0, 0, tiled=True)
    came = came.reshape(groups, lanes, R_DEV, 2 * own)
    outs, levels = came[..., :own], came[..., own:]
    weights = jnp.exp(levels - jnp.max(levels, axis=1, keepdims=True))
    attention = jnp.sum(outs * weights, axis=1) / jnp.sum(weights, axis=1)
    attention = attention.reshape(requests, own).astype(jnp.bfloat16)
    back = jnp.sum(
        jnp.where(holders[None, :] == everyone[:, None], everyone[None, :], 0), axis=1
    )
    projected = jnp.dot(
        pick_rows(back, attention), output_weight, preferred_element_type=jnp.float32
    )
    projected = projected + jnp.where(group == 0, hidden_in.astype(jnp.float32), 0.0)

    share = groups // lanes
    blocks = jnp.moveaxis(projected.reshape(requests, share, 1, features), 0, 2)
    blocks = jnp.broadcast_to(blocks, (share, lanes, requests, features))
    mid = jnp.sum(exchange(blocks.reshape(groups, requests, features)), axis=0)
    mid = to_block_owner(mid.astype(jnp.bfloat16)).astype(jnp.float32)
    squares = jnp.sum(mid * mid, axis=1, keepdims=True)
    gain_here = lax.dynamic_slice_in_dim(feedforward_gain, group * features, features, 0)
    inputs_mid = (mid * gain_here).astype(jnp.bfloat16)
    local_units = gate_weight.shape[1]
    piece = local_units // groups
    gates = jnp.dot(inputs_mid, gate_weight, preferred_element_type=jnp.float32)
    ups = jnp.dot(inputs_mid, up_weight, preferred_element_type=jnp.float32)
    both = jnp.concatenate(
        [
            gates.reshape(requests, groups, piece),
            ups.reshape(requests, groups, piece),
            jnp.broadcast_to(squares[:, :, None], (requests, groups, 1)),
        ],
        axis=2,
    )
    sums = jnp.sum(exchange(jnp.swapaxes(both, 0, 1)), axis=0)
    factor = lax.rsqrt(sums[:, 2 * piece :] / D + epsilon)
    gate = sums[:, :piece] * factor
    active = (jax.nn.silu(gate) * (sums[:, piece : 2 * piece] * factor)).astype(jnp.bfloat16)
    active_here = lax.all_gather(to_block_owner(active), "head", axis=1, tiled=True)
    down = jnp.dot(active_here, down_weight, preferred_element_type=jnp.float32)
    residual = [jnp.where(group == lane * share + k, mid, 0.0) for k in range(share)]
    down = down + jnp.concatenate(residual, axis=1)
    result = whole_sum(down).astype(jnp.bfloat16)
    return (compact, summaries, result)


TILE = 128
bfloat = jnp.bfloat16
single = jnp.float32


TERMS = 4


def three_terms(value, place):
    high = value.astype(bfloat).astype(single)
    rest = value - high
    middle = rest.astype(bfloat).astype(single)
    low = jnp.where(place == 2, rest - middle, 0.0)
    return jnp.where(place == 0, high, jnp.where(place == 1, middle, low))


def iota(shape, axis):
    return lax.broadcasted_iota(jnp.int32, shape, axis)


def run(kernel, outs, far, near, scratch=(), flops=0):
    in_specs = [pl.BlockSpec(memory_space=pltpu.HBM) for _ in far]
    in_specs += [pl.BlockSpec(memory_space=pltpu.VMEM) for _ in near]
    moved = sum(a.size * a.dtype.itemsize for a in [*far, *near, *outs])
    return pl.pallas_call(
        kernel,
        out_shape=list(outs),
        in_specs=in_specs,
        out_specs=[pl.BlockSpec(memory_space=pltpu.VMEM) for _ in outs],
        scratch_shapes=list(scratch),
        compiler_params=pltpu.CompilerParams(vmem_limit_bytes=16 * 2**20),
        cost_estimate=pl.CostEstimate(flops=flops, bytes_accessed=moved, transcendentals=0),
    )(*[pltpu.with_memory_space_constraint(a, pltpu.HBM) for a in far], *near)


def fetch(sources, targets, done):
    copies = [
        pltpu.make_async_copy(source, target, done.at[k])
        for k, (source, target) in enumerate(zip(sources, targets))
    ]
    for copy in copies:
        copy.start()
    return copies


def local_like(*arrays):
    return [pltpu.VMEM(a.shape, a.dtype) for a in arrays]


def scalar_like(*arrays):
    return [pltpu.SMEM(a.shape, a.dtype) for a in arrays]


def row_order(source, count, to_holder):
    first, second = iota((count, count), 0), iota((count, count), 1)
    if not to_holder:
        first, second = second, first
    order = (first == second) & (first % R_DEV == 0)
    for c in range(source.shape[1]):
        order = order | ((first == source[0, c] * R_DEV + 1) & (second == c * R_DEV + 1))
    return order.astype(single).astype(bfloat)


def shaped(shape, dtype):
    return jax.ShapeDtypeStruct(shape, dtype)


def first_kernel(
    source_far, gain_far, weight_far, hidden_far, one, two, three, sent, block, source, gain,
    weight, hidden, lanes_of, wide, done
):
    copies = fetch(
        (source_far, gain_far, weight_far, hidden_far), (source, gain, weight, hidden), done
    )
    rows = hidden.shape[0]
    groups = rows // R_DEV
    lanes = sent.shape[0] // groups
    columns, features = weight.shape
    group = lax.axis_index("req")
    share = groups // lanes
    squares = 0.0
    for turn, values in enumerate((one, two, three)):
        values = values[...].astype(single)
        lanes_of[turn + 1] = values
        squares = squares + jnp.sum(values * values, axis=1, keepdims=True)
    copies[3].wait()
    values = hidden[...].astype(single)
    lanes_of[0] = values
    squares = squares + jnp.sum(values * values, axis=1, keepdims=True)
    factor = lax.rsqrt(squares / D + epsilon)
    here = pl.ds(pl.multiple_of(group * features, features), features)
    within = pl.ds(pl.multiple_of(group % share * features, features), features)
    mine = lanes_of[group // share ^ lax.axis_index("head"), :, within]
    block[...] = mine.astype(bfloat)
    wide[...] = jnp.zeros_like(wide)
    for copy in copies[:3]:
        copy.wait()
    normed = (mine * factor * gain[:, here]).astype(bfloat)
    order = row_order(source, rows, True)
    normed = jnp.dot(order, normed, preferred_element_type=single).astype(bfloat)
    wide[:, :columns] = dot_rows(normed, weight[...])
    for g in range(groups):
        tile = jnp.concatenate(
            [
                wide[R_DEV * g : R_DEV * (g + 1), TILE * j : TILE * (j + 1)]
                for j in range(wide.shape[1] // TILE)
            ],
            axis=0,
        )
        for k in range(lanes):
            sent[g * lanes + k] = tile


def dot_rows(left, right):
    return lax.dot_general(left, right, (((1,), (1,)), ((), ())), preferred_element_type=single)


def prepare_kernel(*refs):
    far, refs = refs[:12], refs[12:]
    (compact, summaries, kept, added, tables, mine, theirs), refs = refs[:7], refs[7:]
    near, (ordered, plain, dealt, done) = refs[:12], refs[12:]
    copies = fetch(far, near, done)
    (dest, lengths, source, table, keep, weights, query_gain, key_gain, turns) = near[:9]
    pages, gate, up = near[9:]
    group = lax.axis_index("req")
    lane = lax.axis_index("head")
    lanes = lax.axis_size("head")
    for copy in copies[:9]:
        copy.wait()

    carried = 0
    for c in range(source.shape[1]):
        carried = carried + jnp.where(source[0, c] == group, c, 0)
    held_len = (lengths[0, group * R_DEV], lengths[0, carried * R_DEV + 1])
    count, rows, _ = pages.shape
    owned = []
    for r in range(R_DEV):
        slots = []
        for i in range(table.shape[1] // lanes):
            j = i * lanes + lane
            slots.append(jnp.where(j < held_len[r], table[r, j], -1))
        owned.append(slots)

    def owner(r, p):
        found = owned[r][0] == p
        for slot in owned[r][1:]:
            found = found | (slot == p)
        return found

    row = iota((32, TILE), 0)
    odd = (row & 1) == 1
    half_rows = turns.shape[0] // 2
    for part in range(2):
        pair = [turns[pl.ds(part * half_rows + held_len[r], 1), :] for r in range(R_DEV)]
        tables[32 * part : 32 * (part + 1), :] = jnp.where(odd, pair[1], pair[0])
    query_rows = HEADS * HD // TILE * R_DEV
    for c in range(TILE // HD):
        columns = slice(HD * c, HD * (c + 1))
        tables[64 : 64 + query_rows, columns] = jnp.broadcast_to(
            query_gain[...], (query_rows, HD)
        )
        tables[64 + query_rows : 96, columns] = jnp.broadcast_to(
            key_gain[...], (32 - query_rows, HD)
        )

    column = iota((1, TILE), 1)
    entries = count * KEEP
    added[...] = jnp.full_like(added, negative)
    extra = [
        jnp.where((column == count + r) & (lane == 0), 0.0, negative) for r in range(R_DEV)
    ]
    weight_columns = weights[...].T
    rows_of = iota((rows, KEEP), 0)
    place = iota((rows, KEEP), 1)
    copies[9].wait()
    for p in range(count):
        picks = (keep[p : p + 1, :] == rows_of).astype(single)
        dropped = weight_columns[:, p : p + 1] * (1.0 - jnp.sum(picks, axis=1, keepdims=True))
        total = jnp.sum(dropped, axis=0, keepdims=True)
        left = jnp.concatenate([picks, three_terms(dropped, place)], axis=1).astype(bfloat)
        both = lax.dot_general(
            left, pages[p], (((0,), (0,)), ((), ())), preferred_element_type=single
        )
        rows_kept = both[:KEEP].astype(bfloat)
        kept[KEEP * p : KEEP * (p + 1), :] = rows_kept
        slot = dest[0, p]
        start = pl.multiple_of((slot & 1) * KEEP, KEEP)
        compact[slot >> 1, pl.ds(start, KEEP), :] = rows_kept
        mean = both[KEEP : KEEP + 1] + both[KEEP + 1 : KEEP + 2] + both[KEEP + 2 : KEEP + 3]
        mean = mean / total
        plain[p : p + 1, :] = mean
        ordered[pl.ds(slot, 1), :] = mean
        live = jnp.where(keep[p : p + 1, :] >= 0, 0.0, negative)
        for r in range(R_DEV):
            here = owner(r, p)
            added[r : r + 1, KEEP * p : KEEP * (p + 1)] = jnp.where(here, live, negative)
            level = jnp.where(here, jnp.log(total), negative)
            extra[r] = jnp.where(column == p, level, extra[r])
    for r in range(R_DEV):
        added[r : r + 1, entries : entries + TILE] = extra[r]
    plain[count:, :] = jnp.zeros_like(plain[count:, :])
    kept[entries:, :] = plain[...].astype(bfloat)
    summaries[...] = ordered[...].astype(bfloat)

    for copy in copies[10:]:
        copy.wait()
    block = gate.shape[1] // 2
    piece = block // 2
    for k in range(2):
        for b in range(2):
            columns = slice(b * block + k * piece, b * block + (k + 1) * piece)
            start = b * block
            dealt[k, :, start : start + piece] = gate[:, columns].astype(single)
            dealt[k, :, start + piece : start + block] = up[:, columns].astype(single)
    mine[...] = dealt[lane & 1].astype(bfloat)
    theirs[...] = dealt[1 - (lane & 1)].astype(bfloat)


def attend_kernel(came, kept, added, tables, sent, x, extra_k, extra_v, out):
    lanes = lax.axis_size("head")
    groups = came.shape[0] // lanes
    width = (HEADS + 2 * KVH) * HD // lanes
    span = -(-KVH * HD // TILE) * TILE
    key_cols = slice(0, span)
    value_cols = slice(KVW - span, KVW)
    first_key = HEADS * HD // TILE * R_DEV
    scale = HD ** (-0.5)
    x[...] = jnp.zeros_like(x)
    column = iota((8, TILE), 1)
    for k in range(lanes):
        tile = came[k]
        for g in range(1, groups):
            tile = tile + came[g * lanes + k]
        tile = tile.astype(bfloat).astype(single)
        base, shift = divmod(width * k, TILE)
        base = base * R_DEV
        if shift:
            tile = pltpu.roll(tile, shift, 1)
            x[base + 2 : base + 10, :] += jnp.where(column < shift, tile, 0.0)
        x[base : base + 8, :] += jnp.where(column >= shift, tile, 0.0)
    values = x[...]
    same_head = (iota((TILE, TILE), 0) // HD == iota((TILE, TILE), 1) // HD).astype(single)
    squares = jnp.dot(
        values * values, same_head, precision=lax.Precision.HIGHEST, preferred_element_type=single
    )
    normed = values * lax.rsqrt(squares / HD + epsilon) * tables[64:96, :]
    early = iota(values.shape, 1) % HD < HD // 2
    swapped = jnp.where(
        early, pltpu.roll(normed, TILE - HD // 2, 1), pltpu.roll(normed, HD // 2, 1)
    )
    turned = normed * tables[0:32, :] + swapped * tables[32:64, :]
    turned = turned.astype(bfloat).astype(single)

    rows = 24
    row = iota((rows, TILE), 0)
    half = iota((rows, TILE), 1) // HD
    key_head = row >> 2
    query = jnp.where(row < first_key, turned[:rows], 0.0)
    other = pltpu.roll(query, HD, 1)
    queries = []
    for u in range(2):
        placed = jnp.where(
            half == (key_head & 1), jnp.where((key_head & 1) == u, query, other), 0.0
        )
        queries.append(
            jnp.concatenate(
                [jnp.where((key_head >> 1) == c, placed, 0.0) for c in range(span // TILE)], axis=1
            )
        )
    queries = jnp.concatenate(queries, axis=0).astype(bfloat)

    extras = extra_k.shape[0]
    entries = kept.shape[0] - extras
    count = entries // KEEP
    extra_k[...] = kept[entries:, key_cols].astype(single)
    extra_v[...] = kept[entries:, value_cols].astype(single)
    first_value = first_key + KVH * HD // TILE * R_DEV
    for c in range(span // TILE):
        at = slice(c * TILE, (c + 1) * TILE)
        r = first_key + R_DEV * c
        extra_k[count : count + R_DEV, at] = turned[r : r + R_DEV]
        r = first_value + R_DEV * c
        extra_v[count : count + R_DEV, at] = values[r : r + R_DEV]

    def by_request(columns, size):
        odd = (iota((2 * rows, size), 0) & 1) == 1
        return jnp.where(odd, added[1:2, columns], added[0:1, columns])

    scores = dot_rows(queries, kept[:entries, key_cols]) * scale
    scores = scores + by_request(slice(0, entries), entries)
    extra = dot_rows(queries, extra_k[...].astype(bfloat)) * scale
    extra = extra + by_request(slice(entries, entries + extras), extras)
    top = jnp.maximum(
        jnp.max(scores, axis=1, keepdims=True), jnp.max(extra, axis=1, keepdims=True)
    )
    weight = jnp.where(scores > 0.5 * negative, jnp.exp(scores - top), 0.0)
    extra_weight = jnp.where(extra > 0.5 * negative, jnp.exp(extra - top), 0.0)
    mass = jnp.sum(weight, axis=1, keepdims=True) + jnp.sum(extra_weight, axis=1, keepdims=True)

    def weighted(parts, right):
        high = parts.astype(bfloat)
        low = (parts - high.astype(single)).astype(bfloat)
        return jnp.dot(high, right, preferred_element_type=single) + jnp.dot(
            low, right, preferred_element_type=single
        )

    total = weighted(weight, kept[:entries, value_cols]) + weighted(
        extra_weight, extra_v[...].astype(bfloat)
    )
    some = mass > 0.0
    mass = jnp.where(some, mass, 1.0)
    total = total / mass
    level = jnp.where(some, top + jnp.log(mass), negative)

    slot = key_head + (KVW // 2 - (KVW - span)) // HD
    results = []
    for u in range(2):
        mine = total[rows * u : rows * (u + 1)]
        picked = mine[:, :TILE]
        for c in range(1, span // TILE):
            picked = jnp.where((slot >> 1) == c, mine[:, c * TILE : (c + 1) * TILE], picked)
        results.append(jnp.where((slot & 1) == u, picked, pltpu.roll(picked, HD, 1)))
    out[:rows, :] = jnp.where(half == 0, results[0], results[1])
    level = jnp.where(half == 0, level[:rows], level[rows:])
    out[rows:, :] = three_terms(level, iota(level.shape, 1) % TERMS)
    own = HEADS * HD // groups
    for g in range(groups):
        r = own * g // TILE * R_DEV
        tile = jnp.concatenate([out[r : r + 4, :], out[rows + r : rows + r + 4, :]], axis=0)
        for k in range(lanes):
            sent[g * lanes + k] = tile.astype(bfloat)


def project_kernel(
    source_far, own_far, came, one, two, three, kept, given, source, own, rows, blocks, done
):
    copies = fetch((source_far, own_far), (source, own), done)
    lanes = lax.axis_size("head")
    groups = came.shape[0] // lanes
    features = own.shape[0]
    requests = rows.shape[0]
    near = (iota((TILE, TILE), 0) // TERMS == iota((TILE, TILE), 1) // TERMS).astype(single)
    tiles = came[...].reshape(groups * lanes * 8, TILE)
    levels = jnp.dot(tiles, near.astype(bfloat), preferred_element_type=single)
    tiles = tiles.astype(single).reshape(groups, lanes, 8, TILE)
    levels = levels.reshape(groups, lanes, 8, TILE)
    for g in range(groups):
        mine = [levels[g, k, 4:8] for k in range(lanes)]
        top = jnp.maximum(jnp.maximum(mine[0], mine[1]), jnp.maximum(mine[2], mine[3]))
        shares = [jnp.exp(level - top) for level in mine]
        mixed = sum(share * tiles[g, k, 0:4] for k, share in enumerate(shares)) / sum(shares)
        rows[R_DEV * g : R_DEV * (g + 1), :TILE] = mixed[:R_DEV]
        rows[R_DEV * g : R_DEV * (g + 1), TILE:] = mixed[R_DEV:]
    shift = lax.rem(2 * TILE - lax.rem(lax.axis_index("req") * features, TILE), 2 * TILE)
    attention = pltpu.roll(rows[...].astype(bfloat).astype(single), shift, 1)
    for copy in copies:
        copy.wait()
    order = row_order(source, requests, False)
    attention = jnp.dot(order, attention.astype(bfloat), preferred_element_type=single)
    attention = attention[:, :features].astype(bfloat)
    width = kept.shape[2]
    group = lax.axis_index("req")
    for turn, weight in enumerate((own, one, two, three)):
        projected = jnp.dot(attention, weight[...], preferred_element_type=single)
        for b in range(2):
            blocks[b, lax.axis_index("head") ^ turn] = projected[:, width * b : width * (b + 1)]
    kept[...] = blocks[group & 1]
    given[...] = blocks[1 - (group & 1)].astype(bfloat)


def spread_kernel(kept, came, own, one, two, three, total):
    total[...] = kept[...] + came[...].astype(single)
    place = lax.axis_index("req") >> 1
    own[...] = total[place]
    for turn, block in enumerate((one, two, three)):
        block[...] = total[place ^ (turn + 1)].astype(bfloat)


def units_kernel(
    gain_far, own, one, two, three, hidden, mine, theirs, kept, given, mid_out, gain, chunks, done
):
    (copy,) = fetch((gain_far,), (gain,), done)
    rows, features = own.shape
    group = lax.axis_index("req")
    here = pl.ds(pl.multiple_of(group * features, features), features)
    mid = own[...] + one[...].astype(single) + two[...].astype(single)
    mid = mid + three[...].astype(single) + hidden[...].astype(single)
    mid = mid.astype(bfloat)
    mid_out[...] = mid
    mid = mid.astype(single)
    squares = jnp.sum(mid * mid, axis=1, keepdims=True)
    block = mine.shape[1] // 2
    terms = three_terms(squares, iota((rows, chunks.shape[3] - block), 1))
    copy.wait()
    inputs = (mid * gain[:, here]).astype(bfloat)
    for turn, weight in enumerate((mine, theirs)):
        units = jnp.dot(inputs, weight[...], preferred_element_type=single)
        for b in range(2):
            chunks[b, turn, :, :block] = units[:, block * b : block * (b + 1)]
            chunks[b, turn, :, block:] = terms
    kept[...] = chunks[group & 1]
    given[...] = chunks[1 - (group & 1)].astype(bfloat)


def halves_kernel(kept, came, own, one, two, three, total):
    total[...] = kept[...] + came[...].astype(single)
    place = lax.axis_index("req") >> 1 ^ lax.axis_index("head")
    own[...] = total[place & 1]
    for turn, block in enumerate((one, two, three)):
        block[...] = total[(place ^ (turn + 1)) & 1].astype(bfloat)


def active_kernel(own, one, two, three, active):
    total = own[...] + one[...].astype(single)
    total = total + two[...].astype(single) + three[...].astype(single)
    piece = active.shape[1]
    squares = jnp.sum(total[:, 2 * piece : 2 * piece + 3], axis=1, keepdims=True)
    factor = lax.rsqrt(squares / D + epsilon)
    gate = total[:, :piece] * factor
    up = total[:, piece : 2 * piece] * factor
    active[...] = (gate / (1.0 + jnp.exp(-gate)) * up).astype(bfloat)


def down_kernel(own, one, two, three, weight, mid, sent, active):
    width = sent.shape[1]
    piece = own.shape[1]
    half = mid.shape[1]
    for turn, values in enumerate((own, one, two, three)):
        active[turn] = values[...]
    share = width // half
    group = lax.axis_index("req")
    lane = lax.axis_index("head")
    first = group // (2 * share) * 2 ^ lane
    down = jnp.dot(active[first], weight[:piece, :], preferred_element_type=single)
    down = down + jnp.dot(active[first ^ 1], weight[piece:, :], preferred_element_type=single)
    residual = mid[...].astype(single)
    for b in range(share):
        columns = slice(half * b, half * (b + 1))
        mine = group == lane * share + b
        total = down[:, columns] + jnp.where(mine, residual, 0.0)
        sent[:, columns] = total.astype(bfloat)


def pair_kernel(own, came, total):
    total[...] = (own[...].astype(single) + came[...].astype(single)).astype(bfloat)


def result_kernel(own, one, two, three, result, terms):
    place = lax.axis_index("req") >> 1
    for turn, values in enumerate((own, one, two, three)):
        terms[place ^ turn] = values[...].astype(single)
    result[...] = ((terms[0] + terms[1]) + (terms[2] + terms[3])).astype(bfloat)


def rotation_table():
    half = HD // 2
    size = -(-(NP + 1) // 8) * 8
    frequency = 10000.0 ** (-np.arange(half) / half)
    angles = PAGE * np.arange(size)[:, None] * frequency[None, :]
    cosine, sine = np.cos(angles), np.sin(angles)
    wide = [np.tile(np.concatenate(pair, axis=1), (1, TILE // HD)) for pair in
            ((cosine, cosine), (-sine, sine))]
    return jnp.asarray(np.concatenate(wide), dtype=single)


def swapped_lanes(value, turn):
    lanes = lax.axis_size("head")
    return lax.ppermute(value, "head", [(k, k ^ turn) for k in range(lanes)])


def from_lanes(value):
    return [value] + [swapped_lanes(value, turn) for turn in range(1, lax.axis_size("head"))]


def swapped_y(value):
    return lax.ppermute(value, "req", [(g, g ^ 1) for g in range(lax.axis_size("req"))])


def swapped_z(values):
    groups = lax.axis_size("req")
    return [
        lax.ppermute(value, "req", [(g, g ^ 2 * (k + 1)) for g in range(groups)])
        for k, value in enumerate(values)
    ]


def on_device(
    hidden_in,
    attention_gain,
    query_gain,
    key_gain,
    feedforward_gain,
    input_weight,
    output_weight,
    gate_weight,
    up_weight,
    down_weight,
    old_cache,
    keep_rows,
    drop_weights,
    dest_slots,
    lengths,
    page_table,
    source,
):
    groups = lax.axis_size("req")
    lanes = lax.axis_size("head")
    requests = hidden_in.shape[0]
    pages_here = old_cache.shape[0]
    devices = groups * lanes
    features = D // groups
    copies = pltpu.SemaphoreType.DMA

    columns = input_weight.shape[1]
    padded = -(-columns // TILE) * TILE
    holds = source[None, :]
    gain = attention_gain[None, :]
    weight = input_weight.T
    far = [holds, gain, weight, hidden_in]
    sent, hidden_block = run(
        first_kernel,
        [
            shaped((devices, R_DEV * padded // TILE, TILE), single),
            shaped((requests, features), bfloat),
        ],
        far,
        from_lanes(hidden_in)[1:],
        [
            *scalar_like(holds),
            *local_like(*far[1:]),
            pltpu.VMEM((lanes,) + hidden_in.shape, single),
            pltpu.VMEM((requests, padded), single),
            copies((len(far),)),
        ],
        2 * requests * features * columns,
    )
    came = lax.all_to_all(sent, both_axes, 0, 0, tiled=True)

    scalars = [dest_slots, lengths[None, :], holds, page_table]
    arrays = [
        keep_rows,
        drop_weights,
        query_gain[None, :],
        key_gain[None, :],
        rotation_table(),
        old_cache,
        gate_weight,
        up_weight,
    ]
    entries = pages_here * KEEP
    extras = 16
    compact, summaries, kept, added, tables, mine, theirs = run(
        prepare_kernel,
        [
            shaped((pages_here // 2, PAGE, KVW), bfloat),
            shaped((pages_here, KVW), bfloat),
            shaped((entries + extras, KVW), bfloat),
            shaped((8, entries + TILE), single),
            shaped((96, TILE), single),
            shaped(gate_weight.shape, bfloat),
            shaped(gate_weight.shape, bfloat),
        ],
        scalars + arrays,
        [],
        [
            *scalar_like(*scalars),
            *local_like(*arrays),
            pltpu.VMEM((pages_here, KVW), single),
            pltpu.VMEM((extras, KVW), single),
            pltpu.VMEM((2,) + gate_weight.shape, single),
            copies((len(scalars + arrays),)),
        ],
        2 * pages_here * TILE * PAGE * KVW,
    )
    span = -(-KVH * HD // TILE) * TILE
    (parts,) = run(
        attend_kernel,
        [shaped((devices, 8, TILE), bfloat)],
        [],
        [came, kept, added, tables],
        [
            pltpu.VMEM((32, TILE), single),
            pltpu.VMEM((extras, span), single),
            pltpu.VMEM((extras, span), single),
            pltpu.VMEM((48, TILE), single),
        ],
        6 * 48 * entries * span,
    )
    output_weights, theirs, _ = lax.optimization_barrier((output_weight, theirs, parts))
    others = [swapped_lanes(output_weights, turn) for turn in range(1, lanes)]
    theirs = swapped_lanes(theirs, 1)
    came = lax.all_to_all(parts, both_axes, 0, 0, tiled=True)
    came, theirs, *others = lax.optimization_barrier((came, theirs, *others))
    places = groups // 2
    block = shaped((requests, features), single)
    kept, given = run(
        project_kernel,
        [
            shaped((places, requests, features), single),
            shaped((places, requests, features), bfloat),
        ],
        [holds, output_weight],
        [came, *others],
        [
            *scalar_like(holds),
            *local_like(output_weight),
            pltpu.VMEM((requests, 2 * TILE), single),
            pltpu.VMEM((2, places, requests, features), single),
            copies((2,)),
        ],
        2 * requests * output_weight.size * lanes,
    )
    own, *sends = run(
        spread_kernel,
        [block] + [shaped((requests, features), bfloat)] * 3,
        [],
        [kept, swapped_y(given)],
        local_like(kept),
    )
    gain = feedforward_gain[None, :]
    width = gate_weight.shape[1] // 2 + TILE
    kept, given, mid = run(
        units_kernel,
        [
            shaped((2, requests, width), single),
            shaped((2, requests, width), bfloat),
            shaped((requests, features), bfloat),
        ],
        [gain],
        [own, *swapped_z(sends), hidden_block, mine, theirs],
        [*local_like(gain), pltpu.VMEM((2, 2, requests, width), single), copies((1,))],
        4 * requests * gate_weight.size,
    )
    own, *sends = run(
        halves_kernel,
        [shaped((requests, width), single)] + [shaped((requests, width), bfloat)] * 3,
        [],
        [kept, swapped_y(given)],
        local_like(kept),
    )
    (active,) = run(
        active_kernel,
        [shaped((requests, gate_weight.shape[1] // 4), bfloat)],
        [],
        [own, *swapped_z(sends)],
    )
    (sent,) = run(
        down_kernel,
        [shaped((requests, down_weight.shape[1]), bfloat)],
        [],
        [*from_lanes(active), down_weight, mid],
        [pltpu.VMEM((lanes,) + active.shape, bfloat)],
        2 * requests * down_weight.size,
    )
    (own,) = run(pair_kernel, [shaped(sent.shape, bfloat)], [], [sent, swapped_y(sent)])
    (result,) = run(
        result_kernel,
        [shaped(sent.shape, bfloat)],
        [],
        [own, *swapped_z([own] * 3)],
        [pltpu.VMEM((places,) + sent.shape, single)],
    )
    return (compact, summaries, result)


def solution(mesh):
    placed = (
        P(None, "head"),
        P(),
        P(),
        P(),
        P(),
        P("req", "head"),
        P("req", "head"),
        P("req", "head"),
        P("req", "head"),
        P("req", "head"),
        P(("req", "head"), None, None),
        P(("req", "head"), None),
        P(("req", "head"), None),
        P(("req", "head"), None),
        P(),
        P("req", None),
        P(),
    )
    return jax.shard_map(
        on_device if mesh.shape["req"] <= DIRECT else on_device_wide,
        mesh=mesh,
        in_specs=placed,
        out_specs=(P(("req", "head"), None, None), P(("req", "head"), None), P(None, "head")),
        check_vma=False,
    )
```

```python
import jax
import jax.numpy as jnp
import numpy as np
from jax import lax
from jax.experimental import pallas as pl
from jax.experimental.pallas import tpu as pltpu
from jax.sharding import PartitionSpec as P

D = 2048
HEADS = 20
KVH = 5
HD = 64
FF = 5120
PAGE = 128
KEEP = 64
NP = 16
R_DEV = 2
KVW = 640

DIRECT = 8

epsilon = 1e-06
negative = -1e30
both_axes = ("req", "head")


def rms_scale(values):
    return lax.rsqrt(jnp.mean(values * values, axis=-1, keepdims=True) + epsilon)


def rms_rows(values, gain):
    return values * rms_scale(values) * gain


def rotate(vectors, positions):
    half = vectors.shape[-1] // 2
    frequency = 10000.0 ** (-jnp.arange(half, dtype=jnp.float32) / half)
    angles = positions.astype(jnp.float32)[:, None] * frequency[None, :]
    cosine = jnp.cos(angles)[:, None, :]
    sine = jnp.sin(angles)[:, None, :]
    first = vectors[..., :half]
    second = vectors[..., half:]
    return jnp.concatenate(
        [first * cosine - second * sine, second * cosine + first * sine], axis=-1
    )


def compact_pages(pages, keep, weights):
    rows = jnp.arange(pages.shape[1], dtype=jnp.int32)
    picks = keep[:, :, None] == rows[None, None, :]
    kept = jnp.einsum(
        "pkr,prc->pkc", picks.astype(jnp.bfloat16), pages, preferred_element_type=jnp.float32
    ).astype(jnp.bfloat16)
    dropped = weights * (1.0 - jnp.sum(picks.astype(jnp.float32), axis=1))
    total = jnp.sum(dropped, axis=1)
    means = (
        jnp.einsum(
            "pr,prc->pc", dropped, pages.astype(jnp.float32), precision=lax.Precision.HIGHEST
        )
        / total[:, None]
    )
    return (kept, means.astype(jnp.bfloat16), jnp.log(total))


def held_request(rows, source):
    half = R_DEV // 2
    position = rows % R_DEV
    slot = rows // R_DEV * half + position - half
    continued = jnp.arange(source.shape[0], dtype=jnp.int32)
    matches = source[None, :] == slot[:, None]
    owner_cont = jnp.sum(jnp.where(matches, continued[None, :], 0), axis=1)
    carried = owner_cont // half * R_DEV + half + owner_cont % half
    return jnp.where(position < half, rows, carried)


def pick_rows(order, rows):
    chosen = order[:, None] == jnp.arange(rows.shape[0], dtype=jnp.int32)[None, :]
    return jnp.dot(
        chosen.astype(jnp.bfloat16), rows, preferred_element_type=jnp.float32
    ).astype(jnp.bfloat16)


def exchange(parts):
    return lax.all_to_all(parts, "req", split_axis=0, concat_axis=0, tiled=True)


def to_block_owner(rows):
    groups = lax.axis_size("req")
    lanes = lax.axis_size("head")
    per_lane = groups // lanes
    pairs = [
        (g * lanes + h, (per_lane * h + g // lanes) * lanes + g % lanes)
        for g in range(groups)
        for h in range(lanes)
    ]
    return lax.ppermute(rows, both_axes, pairs)


def whole_sum(partial):
    if lax.axis_size("req") > DIRECT:
        return lax.psum(partial, "req")
    groups = lax.axis_size("req")
    return jnp.sum(exchange(jnp.broadcast_to(partial[None], (groups,) + partial.shape)), axis=0)


def on_device_wide(
    hidden_in,
    attention_gain,
    query_gain,
    key_gain,
    feedforward_gain,
    input_weight,
    output_weight,
    gate_weight,
    up_weight,
    down_weight,
    old_cache,
    keep_rows,
    drop_weights,
    dest_slots,
    lengths,
    page_table,
    source,
):
    groups = lax.axis_size("req")
    lanes = lax.axis_size("head")
    group = lax.axis_index("req")
    lane = lax.axis_index("head")
    requests = hidden_in.shape[0]
    half = R_DEV // 2
    split = KVH * HD
    ratio = HEADS // KVH
    scale = HD ** (-0.5)
    pages_here = old_cache.shape[0]
    everyone = jnp.arange(requests, dtype=jnp.int32)
    holders = held_request(everyone, source)
    held = lax.dynamic_slice_in_dim(holders, group * R_DEV, R_DEV, 0)
    held_len = lengths[held]
    positions = held_len * PAGE

    whole = lax.all_gather(hidden_in, "head", axis=1, tiled=True)
    normed = rms_rows(whole.astype(jnp.float32), attention_gain).astype(jnp.bfloat16)
    features = D // groups
    inputs = pick_rows(holders, lax.dynamic_slice_in_dim(normed, group * features, features, 1))
    partial_qkv = jnp.dot(inputs, input_weight, preferred_element_type=jnp.float32)
    sent = jnp.broadcast_to(
        partial_qkv.reshape(groups, 1, R_DEV, -1), (groups, lanes, R_DEV, partial_qkv.shape[1])
    ).reshape(groups * lanes, R_DEV, -1)
    got = lax.all_to_all(sent, both_axes, split_axis=0, concat_axis=0, tiled=True)
    mixed = jnp.sum(got.reshape(groups, lanes, R_DEV, -1), axis=0).astype(jnp.bfloat16)
    held_qkv = jnp.swapaxes(mixed, 0, 1).reshape(R_DEV, -1).astype(jnp.float32)

    query = rotate(
        rms_rows(held_qkv[:, : HEADS * HD].reshape(R_DEV, HEADS, HD), query_gain), positions
    ).astype(jnp.bfloat16)
    key_new = rotate(
        rms_rows(held_qkv[:, HEADS * HD : (HEADS + KVH) * HD].reshape(R_DEV, KVH, HD), key_gain),
        positions,
    ).astype(jnp.bfloat16)
    value_new = held_qkv[:, (HEADS + KVH) * HD :].reshape(R_DEV, KVH, HD)
    kept, means, bias = compact_pages(old_cache, keep_rows, drop_weights)
    destination = dest_slots[0]
    fresh_ids = jnp.arange(pages_here, dtype=jnp.int32)
    inverse = jnp.sum(
        jnp.where(destination[None, :] == fresh_ids[:, None], fresh_ids[None, :], 0), axis=1
    )
    compact = kept[inverse].reshape(pages_here // 2, PAGE, KVW)
    summaries = means[inverse]
    per_lane = NP // lanes
    table = page_table.reshape(R_DEV, per_lane, lanes)
    mine = lax.dynamic_slice_in_dim(table, lane, 1, 2)[:, :, 0]
    logical = jnp.arange(per_lane, dtype=jnp.int32) * lanes + lane
    live = logical[None, :] < held_len[:, None]
    owner = jnp.any((mine[:, :, None] == fresh_ids[None, None, :]) & live[:, :, None], axis=1)
    query_groups = query.reshape(R_DEV, KVH, ratio, HD)
    row_keys = kept[:, :, :split].reshape(pages_here, KEEP, KVH, HD)
    row_values = kept[:, :, split:].reshape(pages_here, KEEP, KVH, HD)
    row_live = keep_rows >= 0
    allowed = owner[:, None, None, :, None] & row_live[None, None, None, :, :]
    scores = (
        jnp.einsum("rngd,pmnd->rngpm", query_groups, row_keys, preferred_element_type=jnp.float32)
        * scale
    )
    scores = jnp.where(allowed, scores, negative)
    mean_keys = means[:, :split].reshape(pages_here, KVH, HD)
    mean_values = means[:, split:].reshape(pages_here, KVH, HD)
    mean_scores = (
        jnp.einsum("rngd,pnd->rngp", query_groups, mean_keys, preferred_element_type=jnp.float32)
        * scale
        + bias[None, None, None, :]
    )
    mean_allowed = owner[:, None, None, :]
    mean_scores = jnp.where(mean_allowed, mean_scores, negative)
    own_score = (
        jnp.einsum("rngd,rnd->rng", query_groups, key_new, preferred_element_type=jnp.float32)
        * scale
    )
    own_score = jnp.where(lane == 0, own_score, negative)
    top = jnp.maximum(jnp.max(scores, axis=(3, 4)), jnp.max(mean_scores, axis=3))
    top = jnp.maximum(top, own_score)
    row_weight = jnp.where(allowed, jnp.exp(scores - top[..., None, None]), 0.0)
    mean_weight = jnp.where(mean_allowed, jnp.exp(mean_scores - top[..., None]), 0.0)
    own_weight = jnp.where(lane == 0, jnp.exp(own_score - top), 0.0)
    mass = jnp.sum(row_weight, axis=(3, 4)) + jnp.sum(mean_weight, axis=3) + own_weight
    total = jnp.einsum(
        "rngpm,pmnd->rngd",
        row_weight,
        row_values.astype(jnp.float32),
        precision=lax.Precision.HIGHEST,
    )
    total = total + jnp.einsum(
        "rngp,pnd->rngd",
        mean_weight,
        mean_values.astype(jnp.float32),
        precision=lax.Precision.HIGHEST,
    )
    total = total + own_weight[..., None] * value_new[:, :, None, :]

    some = mass > 0.0
    level = jnp.where(some, top + jnp.log(jnp.where(some, mass, 1.0)), negative)
    means_out = total / jnp.where(some, mass, 1.0)[..., None]
    own = HEADS * HD // groups
    parts = jnp.stack([means_out, jnp.broadcast_to(level[..., None], total.shape)])
    parts = jnp.transpose(parts.reshape(2, R_DEV, groups, own), (2, 1, 0, 3))
    parts = jnp.broadcast_to(
        parts.reshape(groups, 1, R_DEV, 2 * own), (groups, lanes, R_DEV, 2 * own)
    ).reshape(groups * lanes, R_DEV, 2 * own)
    came = lax.all_to_all(parts, both_axes, 0, 0, tiled=True)
    came = came.reshape(groups, lanes, R_DEV, 2 * own)
    outs, levels = came[..., :own], came[..., own:]
    weights = jnp.exp(levels - jnp.max(levels, axis=1, keepdims=True))
    attention = jnp.sum(outs * weights, axis=1) / jnp.sum(weights, axis=1)
    attention = attention.reshape(requests, own).astype(jnp.bfloat16)
    back = jnp.sum(
        jnp.where(holders[None, :] == everyone[:, None], everyone[None, :], 0), axis=1
    )
    projected = jnp.dot(
        pick_rows(back, attention), output_weight, preferred_element_type=jnp.float32
    )
    projected = projected + jnp.where(group == 0, hidden_in.astype(jnp.float32), 0.0)

    share = groups // lanes
    blocks = jnp.moveaxis(projected.reshape(requests, share, 1, features), 0, 2)
    blocks = jnp.broadcast_to(blocks, (share, lanes, requests, features))
    mid = jnp.sum(exchange(blocks.reshape(groups, requests, features)), axis=0)
    mid = to_block_owner(mid.astype(jnp.bfloat16)).astype(jnp.float32)
    squares = jnp.sum(mid * mid, axis=1, keepdims=True)
    gain_here = lax.dynamic_slice_in_dim(feedforward_gain, group * features, features, 0)
    inputs_mid = (mid * gain_here).astype(jnp.bfloat16)
    local_units = gate_weight.shape[1]
    piece = local_units // groups
    gates = jnp.dot(inputs_mid, gate_weight, preferred_element_type=jnp.float32)
    ups = jnp.dot(inputs_mid, up_weight, preferred_element_type=jnp.float32)
    both = jnp.concatenate(
        [
            gates.reshape(requests, groups, piece),
            ups.reshape(requests, groups, piece),
            jnp.broadcast_to(squares[:, :, None], (requests, groups, 1)),
        ],
        axis=2,
    )
    sums = jnp.sum(exchange(jnp.swapaxes(both, 0, 1)), axis=0)
    factor = lax.rsqrt(sums[:, 2 * piece :] / D + epsilon)
    gate = sums[:, :piece] * factor
    active = (jax.nn.silu(gate) * (sums[:, piece : 2 * piece] * factor)).astype(jnp.bfloat16)
    active_here = lax.all_gather(to_block_owner(active), "head", axis=1, tiled=True)
    down = jnp.dot(active_here, down_weight, preferred_element_type=jnp.float32)
    residual = [jnp.where(group == lane * share + k, mid, 0.0) for k in range(share)]
    down = down + jnp.concatenate(residual, axis=1)
    result = whole_sum(down).astype(jnp.bfloat16)
    return (compact, summaries, result)


TILE = 128
bfloat = jnp.bfloat16
single = jnp.float32


TERMS = 4


def three_terms(value, place):
    high = value.astype(bfloat).astype(single)
    rest = value - high
    middle = rest.astype(bfloat).astype(single)
    low = jnp.where(place == 2, rest - middle, 0.0)
    return jnp.where(place == 0, high, jnp.where(place == 1, middle, low))


def iota(shape, axis):
    return lax.broadcasted_iota(jnp.int32, shape, axis)


def run(kernel, outs, far, near, scratch=(), flops=0):
    in_specs = [pl.BlockSpec(memory_space=pltpu.HBM) for _ in far]
    in_specs += [pl.BlockSpec(memory_space=pltpu.VMEM) for _ in near]
    moved = sum(a.size * a.dtype.itemsize for a in [*far, *near, *outs])
    return pl.pallas_call(
        kernel,
        out_shape=list(outs),
        in_specs=in_specs,
        out_specs=[pl.BlockSpec(memory_space=pltpu.VMEM) for _ in outs],
        scratch_shapes=list(scratch),
        compiler_params=pltpu.CompilerParams(vmem_limit_bytes=16 * 2**20),
        cost_estimate=pl.CostEstimate(flops=flops, bytes_accessed=moved, transcendentals=0),
    )(*[pltpu.with_memory_space_constraint(a, pltpu.HBM) for a in far], *near)


def fetch(sources, targets, done):
    copies = [
        pltpu.make_async_copy(source, target, done.at[k])
        for k, (source, target) in enumerate(zip(sources, targets))
    ]
    for copy in copies:
        copy.start()
    return copies


def local_like(*arrays):
    return [pltpu.VMEM(a.shape, a.dtype) for a in arrays]


def scalar_like(*arrays):
    return [pltpu.SMEM(a.shape, a.dtype) for a in arrays]


def row_order(source, count, to_holder):
    first, second = iota((count, count), 0), iota((count, count), 1)
    if not to_holder:
        first, second = second, first
    order = (first == second) & (first % R_DEV == 0)
    for c in range(source.shape[1]):
        order = order | ((first == source[0, c] * R_DEV + 1) & (second == c * R_DEV + 1))
    return order.astype(single).astype(bfloat)


def shaped(shape, dtype):
    return jax.ShapeDtypeStruct(shape, dtype)


def first_kernel(
    source_far, gain_far, weight_far, hidden_far, one, two, three, sent, block, source, gain,
    weight, hidden, lanes_of, wide, done
):
    copies = fetch(
        (source_far, gain_far, weight_far, hidden_far), (source, gain, weight, hidden), done
    )
    rows = hidden.shape[0]
    groups = rows // R_DEV
    lanes = sent.shape[0] // groups
    columns, features = weight.shape
    group = lax.axis_index("req")
    share = groups // lanes
    squares = 0.0
    for turn, values in enumerate((one, two, three)):
        values = values[...].astype(single)
        lanes_of[turn + 1] = values
        squares = squares + jnp.sum(values * values, axis=1, keepdims=True)
    copies[3].wait()
    values = hidden[...].astype(single)
    lanes_of[0] = values
    squares = squares + jnp.sum(values * values, axis=1, keepdims=True)
    factor = lax.rsqrt(squares / D + epsilon)
    here = pl.ds(pl.multiple_of(group * features, features), features)
    within = pl.ds(pl.multiple_of(group % share * features, features), features)
    mine = lanes_of[group // share ^ lax.axis_index("head"), :, within]
    block[...] = mine.astype(bfloat)
    wide[...] = jnp.zeros_like(wide)
    for copy in copies[:3]:
        copy.wait()
    normed = (mine * factor * gain[:, here]).astype(bfloat)
    order = row_order(source, rows, True)
    normed = jnp.dot(order, normed, preferred_element_type=single).astype(bfloat)
    wide[:, :columns] = dot_rows(normed, weight[...])
    for g in range(groups):
        tile = jnp.concatenate(
            [
                wide[R_DEV * g : R_DEV * (g + 1), TILE * j : TILE * (j + 1)]
                for j in range(wide.shape[1] // TILE)
            ],
            axis=0,
        )
        for k in range(lanes):
            sent[g * lanes + k] = tile


def dot_rows(left, right):
    return lax.dot_general(left, right, (((1,), (1,)), ((), ())), preferred_element_type=single)


def prepare_kernel(*refs):
    far, refs = refs[:12], refs[12:]
    (compact, summaries, kept, added, tables, mine, theirs), refs = refs[:7], refs[7:]
    near, (ordered, plain, dealt, done) = refs[:12], refs[12:]
    copies = fetch(far, near, done)
    (dest, lengths, source, table, keep, weights, query_gain, key_gain, turns) = near[:9]
    pages, gate, up = near[9:]
    group = lax.axis_index("req")
    lane = lax.axis_index("head")
    lanes = lax.axis_size("head")
    for copy in copies[:9]:
        copy.wait()

    carried = 0
    for c in range(source.shape[1]):
        carried = carried + jnp.where(source[0, c] == group, c, 0)
    held_len = (lengths[0, group * R_DEV], lengths[0, carried * R_DEV + 1])
    count, rows, _ = pages.shape
    owned = []
    for r in range(R_DEV):
        slots = []
        for i in range(table.shape[1] // lanes):
            j = i * lanes + lane
            slots.append(jnp.where(j < held_len[r], table[r, j], -1))
        owned.append(slots)

    def owner(r, p):
        found = owned[r][0] == p
        for slot in owned[r][1:]:
            found = found | (slot == p)
        return found

    row = iota((32, TILE), 0)
    odd = (row & 1) == 1
    half_rows = turns.shape[0] // 2
    for part in range(2):
        pair = [turns[pl.ds(part * half_rows + held_len[r], 1), :] for r in range(R_DEV)]
        tables[32 * part : 32 * (part + 1), :] = jnp.where(odd, pair[1], pair[0])
    query_rows = HEADS * HD // TILE * R_DEV
    for c in range(TILE // HD):
        columns = slice(HD * c, HD * (c + 1))
        tables[64 : 64 + query_rows, columns] = jnp.broadcast_to(
            query_gain[...], (query_rows, HD)
        )
        tables[64 + query_rows : 96, columns] = jnp.broadcast_to(
            key_gain[...], (32 - query_rows, HD)
        )

    column = iota((1, TILE), 1)
    entries = count * KEEP
    added[...] = jnp.full_like(added, negative)
    extra = [
        jnp.where((column == count + r) & (lane == 0), 0.0, negative) for r in range(R_DEV)
    ]
    weight_columns = weights[...].T
    rows_of = iota((rows, KEEP), 0)
    place = iota((rows, KEEP), 1)
    copies[9].wait()
    for p in range(count):
        picks = (keep[p : p + 1, :] == rows_of).astype(single)
        dropped = weight_columns[:, p : p + 1] * (1.0 - jnp.sum(picks, axis=1, keepdims=True))
        total = jnp.sum(dropped, axis=0, keepdims=True)
        left = jnp.concatenate([picks, three_terms(dropped, place)], axis=1).astype(bfloat)
        both = lax.dot_general(
            left, pages[p], (((0,), (0,)), ((), ())), preferred_element_type=single
        )
        rows_kept = both[:KEEP].astype(bfloat)
        kept[KEEP * p : KEEP * (p + 1), :] = rows_kept
        slot = dest[0, p]
        start = pl.multiple_of((slot & 1) * KEEP, KEEP)
        compact[slot >> 1, pl.ds(start, KEEP), :] = rows_kept
        mean = both[KEEP : KEEP + 1] + both[KEEP + 1 : KEEP + 2] + both[KEEP + 2 : KEEP + 3]
        mean = mean / total
        plain[p : p + 1, :] = mean
        ordered[pl.ds(slot, 1), :] = mean
        live = jnp.where(keep[p : p + 1, :] >= 0, 0.0, negative)
        for r in range(R_DEV):
            here = owner(r, p)
            added[r : r + 1, KEEP * p : KEEP * (p + 1)] = jnp.where(here, live, negative)
            level = jnp.where(here, jnp.log(total), negative)
            extra[r] = jnp.where(column == p, level, extra[r])
    for r in range(R_DEV):
        added[r : r + 1, entries : entries + TILE] = extra[r]
    plain[count:, :] = jnp.zeros_like(plain[count:, :])
    kept[entries:, :] = plain[...].astype(bfloat)
    summaries[...] = ordered[...].astype(bfloat)

    for copy in copies[10:]:
        copy.wait()
    block = gate.shape[1] // 2
    piece = block // 2
    for k in range(2):
        for b in range(2):
            columns = slice(b * block + k * piece, b * block + (k + 1) * piece)
            start = b * block
            dealt[k, :, start : start + piece] = gate[:, columns].astype(single)
            dealt[k, :, start + piece : start + block] = up[:, columns].astype(single)
    mine[...] = dealt[lane & 1].astype(bfloat)
    theirs[...] = dealt[1 - (lane & 1)].astype(bfloat)


def attend_kernel(came, kept, added, tables, sent, x, extra_k, extra_v, out, logs):
    lanes = lax.axis_size("head")
    groups = came.shape[0] // lanes
    width = (HEADS + 2 * KVH) * HD // lanes
    span = -(-KVH * HD // TILE) * TILE
    key_cols = slice(0, span)
    value_cols = slice(KVW - span, KVW)
    first_key = HEADS * HD // TILE * R_DEV
    scale = HD ** (-0.5)
    x[...] = jnp.zeros_like(x)
    column = iota((8, TILE), 1)
    for k in range(lanes):
        tile = came[k].astype(single)
        for g in range(1, groups):
            tile = tile + came[g * lanes + k].astype(single)
        tile = tile.astype(bfloat).astype(single)
        base, shift = divmod(width * k, TILE)
        base = base * R_DEV
        if shift:
            tile = pltpu.roll(tile, shift, 1)
            x[base + 2 : base + 10, :] += jnp.where(column < shift, tile, 0.0)
        x[base : base + 8, :] += jnp.where(column >= shift, tile, 0.0)
    values = x[...]
    same_head = (iota((TILE, TILE), 0) // HD == iota((TILE, TILE), 1) // HD).astype(single)
    squares = jnp.dot(
        values * values, same_head, precision=lax.Precision.HIGHEST, preferred_element_type=single
    )
    normed = values * lax.rsqrt(squares / HD + epsilon) * tables[64:96, :]
    early = iota(values.shape, 1) % HD < HD // 2
    swapped = jnp.where(
        early, pltpu.roll(normed, TILE - HD // 2, 1), pltpu.roll(normed, HD // 2, 1)
    )
    turned = normed * tables[0:32, :] + swapped * tables[32:64, :]
    turned = turned.astype(bfloat).astype(single)

    rows = 24
    row = iota((rows, TILE), 0)
    half = iota((rows, TILE), 1) // HD
    key_head = row >> 2
    query = jnp.where(row < first_key, turned[:rows], 0.0)
    other = pltpu.roll(query, HD, 1)
    queries = []
    for u in range(2):
        placed = jnp.where(
            half == (key_head & 1), jnp.where((key_head & 1) == u, query, other), 0.0
        )
        queries.append(
            jnp.concatenate(
                [jnp.where((key_head >> 1) == c, placed, 0.0) for c in range(span // TILE)], axis=1
            )
        )
    queries = jnp.concatenate(queries, axis=0).astype(bfloat)

    extras = extra_k.shape[0]
    entries = kept.shape[0] - extras
    count = entries // KEEP
    extra_k[...] = kept[entries:, key_cols].astype(single)
    extra_v[...] = kept[entries:, value_cols].astype(single)
    first_value = first_key + KVH * HD // TILE * R_DEV
    for c in range(span // TILE):
        at = slice(c * TILE, (c + 1) * TILE)
        r = first_key + R_DEV * c
        extra_k[count : count + R_DEV, at] = turned[r : r + R_DEV]
        r = first_value + R_DEV * c
        extra_v[count : count + R_DEV, at] = values[r : r + R_DEV]

    def by_request(columns, size):
        odd = (iota((2 * rows, size), 0) & 1) == 1
        return jnp.where(odd, added[1:2, columns], added[0:1, columns])

    scores = dot_rows(queries, kept[:entries, key_cols]) * scale
    scores = scores + by_request(slice(0, entries), entries)
    extra = dot_rows(queries, extra_k[...].astype(bfloat)) * scale
    extra = extra + by_request(slice(entries, entries + extras), extras)
    top = jnp.maximum(
        jnp.max(scores, axis=1, keepdims=True), jnp.max(extra, axis=1, keepdims=True)
    )
    weight = jnp.where(scores > 0.5 * negative, jnp.exp(scores - top), 0.0)
    extra_weight = jnp.where(extra > 0.5 * negative, jnp.exp(extra - top), 0.0)
    mass = jnp.sum(weight, axis=1, keepdims=True) + jnp.sum(extra_weight, axis=1, keepdims=True)

    def weighted(parts, right):
        high = parts.astype(bfloat)
        low = (parts - high.astype(single)).astype(bfloat)
        return jnp.dot(high, right, preferred_element_type=single) + jnp.dot(
            low, right, preferred_element_type=single
        )

    total = weighted(weight, kept[:entries, value_cols]) + weighted(
        extra_weight, extra_v[...].astype(bfloat)
    )
    some = mass > 0.0
    mass = jnp.where(some, mass, 1.0)
    total = total / mass
    level = jnp.where(some, top + jnp.log(mass), negative)

    slot = key_head + (KVW // 2 - (KVW - span)) // HD
    results = []
    for u in range(2):
        mine = total[rows * u : rows * (u + 1)]
        picked = mine[:, :TILE]
        for c in range(1, span // TILE):
            picked = jnp.where((slot >> 1) == c, mine[:, c * TILE : (c + 1) * TILE], picked)
        results.append(jnp.where((slot & 1) == u, picked, pltpu.roll(picked, HD, 1)))
    out[...] = jnp.where(half == 0, results[0], results[1])
    logs[...] = jnp.broadcast_to(level, logs.shape)
    own = HEADS * HD // lanes
    size = 6
    column = iota((size, TILE), 1)
    here = column // TERMS == iota((size, TILE), 0)
    for k in range(lanes):
        r = own * k // TILE * R_DEV
        tile = [out[r : r + size, :]]
        for u in range(2):
            coded = three_terms(logs[rows * u + r : rows * u + r + size, :], column % TERMS)
            tile.append(jnp.sum(jnp.where(here, coded, 0.0), axis=0, keepdims=True))
        tile = jnp.concatenate(tile, axis=0).astype(bfloat)
        for g in range(groups):
            sent[g * lanes + k] = tile


def blocks_kernel(weight_far, same, other, done):
    width = same.shape[1]
    group = lax.axis_index("req")
    starts = [pl.multiple_of(((group & 1) ^ turn) * width, width) for turn in range(2)]
    parts = [weight_far.at[:, pl.ds(start, width)] for start in starts]
    for copy in fetch(parts, (same, other), done):
        copy.wait()


def project_kernel(source_far, came, first, second, sent, source, logs, rows, pieces, done):
    (copy,) = fetch((source_far,), (source,), done)
    lanes = lax.axis_size("head")
    groups = came.shape[0] // lanes
    group = lax.axis_index("req")
    features = first.shape[0]
    requests = rows.shape[0]
    size = 6
    tiles = [came[d].astype(single) for d in range(groups * lanes)]
    for g in range(groups):
        for k in range(lanes):
            logs[k, 2 * g : 2 * g + 2, :] = tiles[g * lanes + k][size:]
    spread = (iota((8, TILE), 1) // TERMS == iota((8, TILE), 0)).astype(single).astype(bfloat)
    levels = [dot_rows(spread, logs[k].astype(bfloat)) for k in range(lanes)]
    top = jnp.maximum(jnp.maximum(levels[0], levels[1]), jnp.maximum(levels[2], levels[3]))
    shares = [jnp.exp(level - top) for level in levels]
    mass = sum(shares)
    shares = [share / mass for share in shares]
    lower = iota((8, TILE), 1) < HD
    for g in range(groups):
        mixed = 0.0
        for k in range(lanes):
            share = shares[k]
            share = jnp.where(lower, share[:, 2 * g : 2 * g + 1], share[:, 2 * g + 1 : 2 * g + 2])
            mixed = mixed + share * tiles[g * lanes + k]
        for j in range(size // R_DEV):
            rows[R_DEV * g : R_DEV * (g + 1), TILE * j : TILE * (j + 1)] = mixed[
                R_DEV * j : R_DEV * (j + 1)
            ]
    width = rows.shape[1]
    shift = lax.rem(lax.axis_index("head") * (2 * features), TILE)
    attention = rows[...].astype(bfloat).astype(single)
    attention = pltpu.roll(attention, lax.rem(width - shift, width), 1)
    copy.wait()
    order = row_order(source, requests, False)
    attention = jnp.dot(order, attention.astype(bfloat), preferred_element_type=single)
    for b in range(2):
        pieces[b] = attention[:, features * b : features * (b + 1)]
    total = 0.0
    for turn, weight in enumerate((first, second)):
        piece = pieces[(group & 1) ^ turn].astype(bfloat)
        total = total + jnp.dot(piece, weight[...], preferred_element_type=single)
    sent[...] = total


def units_kernel(
    gain_far, own, one, two, three, hidden, mine, theirs, sent, mid_out, gain, done
):
    (copy,) = fetch((gain_far,), (gain,), done)
    rows, features = own.shape
    share = sent.shape[0] // lax.axis_size("head")
    group = lax.axis_index("req")
    lane = lax.axis_index("head")
    here = pl.ds(pl.multiple_of(group * features, features), features)
    mid = (own[...] + one[...]) + (two[...] + three[...])
    mid = (hidden[...].astype(single) + mid).astype(bfloat)
    mid_out[...] = mid
    mid = mid.astype(single)
    squares = jnp.sum(mid * mid, axis=1, keepdims=True)
    block = mine.shape[1] // share
    terms = three_terms(squares, iota((rows, sent.shape[2] - block), 1)).astype(bfloat)
    copy.wait()
    inputs = (mid * gain[:, here]).astype(bfloat)
    for turn, weight in enumerate((mine, theirs)):
        units = jnp.dot(inputs, weight[...], preferred_element_type=single).astype(bfloat)
        target = (lane ^ turn) * share
        for b in range(share):
            sent[target + b, :, :block] = units[:, block * b : block * (b + 1)]
            sent[target + b, :, block:] = terms


def active_kernel(came, active):
    total = came[0].astype(single)
    for g in range(1, came.shape[0]):
        total = total + came[g].astype(single)
    piece = active.shape[1]
    squares = jnp.sum(total[:, 2 * piece : 2 * piece + 3], axis=1, keepdims=True)
    factor = lax.rsqrt(squares / D + epsilon)
    gate = total[:, :piece] * factor
    up = total[:, piece : 2 * piece] * factor
    active[...] = (gate / (1.0 + jnp.exp(-gate)) * up).astype(bfloat)


def down_kernel(own, one, two, three, weight, mid, sent, active):
    groups, rows, width = sent.shape
    piece = own.shape[1]
    half = mid.shape[1]
    for turn, values in enumerate((own, one, two, three)):
        active[turn] = values[...]
    share = width // half
    group = lax.axis_index("req")
    lane = lax.axis_index("head")
    first = group // (2 * share) * 2 ^ lane
    down = jnp.dot(active[first], weight[:piece, :], preferred_element_type=single)
    down = down + jnp.dot(active[first ^ 1], weight[piece:, :], preferred_element_type=single)
    residual = mid[...].astype(single)
    for b in range(share):
        columns = slice(half * b, half * (b + 1))
        mine = group == lane * share + b
        total = (down[:, columns] + jnp.where(mine, residual, 0.0)).astype(bfloat)
        for g in range(groups):
            sent[g, :, columns] = total


def result_kernel(came, result):
    total = came[0].astype(single)
    for g in range(1, came.shape[0]):
        total = total + came[g].astype(single)
    result[...] = total.astype(bfloat)


def rotation_table():
    half = HD // 2
    size = -(-(NP + 1) // 8) * 8
    frequency = 10000.0 ** (-np.arange(half) / half)
    angles = PAGE * np.arange(size)[:, None] * frequency[None, :]
    cosine, sine = np.cos(angles), np.sin(angles)
    wide = [np.tile(np.concatenate(pair, axis=1), (1, TILE // HD)) for pair in
            ((cosine, cosine), (-sine, sine))]
    return jnp.asarray(np.concatenate(wide), dtype=single)


def swapped_lanes(value, turn):
    lanes = lax.axis_size("head")
    return lax.ppermute(value, "head", [(k, k ^ turn) for k in range(lanes)])


def from_lanes(value):
    return [value] + [swapped_lanes(value, turn) for turn in range(1, lax.axis_size("head"))]


def handed_over(value, turn):
    groups = lax.axis_size("req")
    lanes = lax.axis_size("head")
    share = groups // lanes
    pairs = [
        (g * lanes + h, (share * h + ((g & 1) ^ turn)) * lanes + g // share)
        for g in range(groups)
        for h in range(lanes)
    ]
    return lax.ppermute(value, both_axes, pairs)


def on_device(
    hidden_in,
    attention_gain,
    query_gain,
    key_gain,
    feedforward_gain,
    input_weight,
    output_weight,
    gate_weight,
    up_weight,
    down_weight,
    old_cache,
    keep_rows,
    drop_weights,
    dest_slots,
    lengths,
    page_table,
    source,
):
    groups = lax.axis_size("req")
    lanes = lax.axis_size("head")
    requests = hidden_in.shape[0]
    pages_here = old_cache.shape[0]
    devices = groups * lanes
    features = D // groups
    copies = pltpu.SemaphoreType.DMA

    columns = input_weight.shape[1]
    padded = -(-columns // TILE) * TILE
    holds = source[None, :]
    gain = attention_gain[None, :]
    weight = input_weight.T
    far = [holds, gain, weight, hidden_in]
    sent, hidden_block = run(
        first_kernel,
        [
            shaped((devices, R_DEV * padded // TILE, TILE), single),
            shaped((requests, features), bfloat),
        ],
        far,
        from_lanes(hidden_in)[1:],
        [
            *scalar_like(holds),
            *local_like(*far[1:]),
            pltpu.VMEM((lanes,) + hidden_in.shape, single),
            pltpu.VMEM((requests, padded), single),
            copies((len(far),)),
        ],
        2 * requests * features * columns,
    )
    came = lax.all_to_all(sent, both_axes, 0, 0, tiled=True)
    blocks = run(
        blocks_kernel,
        [shaped((output_weight.shape[0], features), bfloat)] * 2,
        [output_weight],
        [],
        [copies((2,))],
    )
    handed = [handed_over(block, turn) for turn, block in enumerate(blocks)]

    scalars = [dest_slots, lengths[None, :], holds, page_table]
    arrays = [
        keep_rows,
        drop_weights,
        query_gain[None, :],
        key_gain[None, :],
        rotation_table(),
        old_cache,
        gate_weight,
        up_weight,
    ]
    entries = pages_here * KEEP
    extras = 16
    compact, summaries, kept, added, tables, mine, theirs = run(
        prepare_kernel,
        [
            shaped((pages_here // 2, PAGE, KVW), bfloat),
            shaped((pages_here, KVW), bfloat),
            shaped((entries + extras, KVW), bfloat),
            shaped((8, entries + TILE), single),
            shaped((96, TILE), single),
            shaped(gate_weight.shape, bfloat),
            shaped(gate_weight.shape, bfloat),
        ],
        scalars + arrays,
        [],
        [
            *scalar_like(*scalars),
            *local_like(*arrays),
            pltpu.VMEM((pages_here, KVW), single),
            pltpu.VMEM((extras, KVW), single),
            pltpu.VMEM((2,) + gate_weight.shape, single),
            copies((len(scalars + arrays),)),
        ],
        2 * pages_here * TILE * PAGE * KVW,
    )
    came, *handed = lax.optimization_barrier((came, *handed))
    span = -(-KVH * HD // TILE) * TILE
    (parts,) = run(
        attend_kernel,
        [shaped((devices, 8, TILE), bfloat)],
        [],
        [came, kept, added, tables],
        [
            pltpu.VMEM((32, TILE), single),
            pltpu.VMEM((extras, span), single),
            pltpu.VMEM((extras, span), single),
            pltpu.VMEM((24, TILE), single),
            pltpu.VMEM((48, TILE), single),
        ],
        6 * 48 * entries * span,
    )
    theirs, _ = lax.optimization_barrier((theirs, parts))
    theirs = swapped_lanes(theirs, 1)
    came = lax.all_to_all(parts, both_axes, 0, 0, tiled=True)
    came, theirs = lax.optimization_barrier((came, theirs))
    (sent,) = run(
        project_kernel,
        [shaped((requests, features), single)],
        [holds],
        [came, *handed],
        [
            *scalar_like(holds),
            pltpu.VMEM((lanes, 2 * groups, TILE), single),
            pltpu.VMEM((requests, 3 * TILE), single),
            pltpu.VMEM((2, requests, output_weight.shape[0]), single),
            copies((1,)),
        ],
        2 * requests * output_weight.size,
    )
    gain = feedforward_gain[None, :]
    block = gate_weight.shape[1] // 2
    sent, mid = run(
        units_kernel,
        [
            shaped((groups, requests, block + TILE), bfloat),
            shaped((requests, features), bfloat),
        ],
        [gain],
        [*from_lanes(sent), hidden_block, mine, theirs],
        [*local_like(gain), copies((1,))],
        4 * requests * gate_weight.size,
    )
    (active,) = run(
        active_kernel, [shaped((requests, block // 2), bfloat)], [], [exchange(sent)]
    )
    (sent,) = run(
        down_kernel,
        [shaped((groups, requests, down_weight.shape[1]), bfloat)],
        [],
        [*from_lanes(active), down_weight, mid],
        [pltpu.VMEM((lanes,) + active.shape, bfloat)],
        2 * requests * down_weight.size,
    )
    (result,) = run(
        result_kernel, [shaped((requests, down_weight.shape[1]), bfloat)], [], [exchange(sent)]
    )
    return (compact, summaries, result)


def solution(mesh):
    placed = (
        P(None, "head"),
        P(),
        P(),
        P(),
        P(),
        P("req", "head"),
        P("req", "head"),
        P("req", "head"),
        P("req", "head"),
        P("req", "head"),
        P(("req", "head"), None, None),
        P(("req", "head"), None),
        P(("req", "head"), None),
        P(("req", "head"), None),
        P(),
        P("req", None),
        P(),
    )
    return jax.shard_map(
        on_device if mesh.shape["req"] <= DIRECT else on_device_wide,
        mesh=mesh,
        in_specs=placed,
        out_specs=(P(("req", "head"), None, None), P(("req", "head"), None), P(None, "head")),
        check_vma=False,
    )
```

```python
import jax
import jax.numpy as jnp
import numpy as np
from jax import lax
from jax.experimental import pallas as pl
from jax.experimental.pallas import tpu as pltpu
from jax.sharding import PartitionSpec as P

D = 2048
HEADS = 20
KVH = 5
HD = 64
FF = 5120
PAGE = 128
KEEP = 64
NP = 16
R_DEV = 2
KVW = 640

DIRECT = 8

epsilon = 1e-06
negative = -1e30
both_axes = ("req", "head")


def rms_scale(values):
    return lax.rsqrt(jnp.mean(values * values, axis=-1, keepdims=True) + epsilon)


def rms_rows(values, gain):
    return values * rms_scale(values) * gain


def rotate(vectors, positions):
    half = vectors.shape[-1] // 2
    frequency = 10000.0 ** (-jnp.arange(half, dtype=jnp.float32) / half)
    angles = positions.astype(jnp.float32)[:, None] * frequency[None, :]
    cosine = jnp.cos(angles)[:, None, :]
    sine = jnp.sin(angles)[:, None, :]
    first = vectors[..., :half]
    second = vectors[..., half:]
    return jnp.concatenate(
        [first * cosine - second * sine, second * cosine + first * sine], axis=-1
    )


def compact_pages(pages, keep, weights):
    rows = jnp.arange(pages.shape[1], dtype=jnp.int32)
    picks = keep[:, :, None] == rows[None, None, :]
    kept = jnp.einsum(
        "pkr,prc->pkc", picks.astype(jnp.bfloat16), pages, preferred_element_type=jnp.float32
    ).astype(jnp.bfloat16)
    dropped = weights * (1.0 - jnp.sum(picks.astype(jnp.float32), axis=1))
    total = jnp.sum(dropped, axis=1)
    means = (
        jnp.einsum(
            "pr,prc->pc", dropped, pages.astype(jnp.float32), precision=lax.Precision.HIGHEST
        )
        / total[:, None]
    )
    return (kept, means.astype(jnp.bfloat16), jnp.log(total))


def held_request(rows, source):
    half = R_DEV // 2
    position = rows % R_DEV
    slot = rows // R_DEV * half + position - half
    continued = jnp.arange(source.shape[0], dtype=jnp.int32)
    matches = source[None, :] == slot[:, None]
    owner_cont = jnp.sum(jnp.where(matches, continued[None, :], 0), axis=1)
    carried = owner_cont // half * R_DEV + half + owner_cont % half
    return jnp.where(position < half, rows, carried)


def pick_rows(order, rows):
    chosen = order[:, None] == jnp.arange(rows.shape[0], dtype=jnp.int32)[None, :]
    return jnp.dot(
        chosen.astype(jnp.bfloat16), rows, preferred_element_type=jnp.float32
    ).astype(jnp.bfloat16)


def exchange(parts):
    return lax.all_to_all(parts, "req", split_axis=0, concat_axis=0, tiled=True)


def to_block_owner(rows):
    groups = lax.axis_size("req")
    lanes = lax.axis_size("head")
    per_lane = groups // lanes
    pairs = [
        (g * lanes + h, (per_lane * h + g // lanes) * lanes + g % lanes)
        for g in range(groups)
        for h in range(lanes)
    ]
    return lax.ppermute(rows, both_axes, pairs)


def whole_sum(partial):
    if lax.axis_size("req") > DIRECT:
        return lax.psum(partial, "req")
    groups = lax.axis_size("req")
    return jnp.sum(exchange(jnp.broadcast_to(partial[None], (groups,) + partial.shape)), axis=0)


def on_device_wide(
    hidden_in,
    attention_gain,
    query_gain,
    key_gain,
    feedforward_gain,
    input_weight,
    output_weight,
    gate_weight,
    up_weight,
    down_weight,
    old_cache,
    keep_rows,
    drop_weights,
    dest_slots,
    lengths,
    page_table,
    source,
):
    groups = lax.axis_size("req")
    lanes = lax.axis_size("head")
    group = lax.axis_index("req")
    lane = lax.axis_index("head")
    requests = hidden_in.shape[0]
    half = R_DEV // 2
    split = KVH * HD
    ratio = HEADS // KVH
    scale = HD ** (-0.5)
    pages_here = old_cache.shape[0]
    everyone = jnp.arange(requests, dtype=jnp.int32)
    holders = held_request(everyone, source)
    held = lax.dynamic_slice_in_dim(holders, group * R_DEV, R_DEV, 0)
    held_len = lengths[held]
    positions = held_len * PAGE

    whole = lax.all_gather(hidden_in, "head", axis=1, tiled=True)
    normed = rms_rows(whole.astype(jnp.float32), attention_gain).astype(jnp.bfloat16)
    features = D // groups
    inputs = pick_rows(holders, lax.dynamic_slice_in_dim(normed, group * features, features, 1))
    partial_qkv = jnp.dot(inputs, input_weight, preferred_element_type=jnp.float32)
    sent = jnp.broadcast_to(
        partial_qkv.reshape(groups, 1, R_DEV, -1), (groups, lanes, R_DEV, partial_qkv.shape[1])
    ).reshape(groups * lanes, R_DEV, -1)
    got = lax.all_to_all(sent, both_axes, split_axis=0, concat_axis=0, tiled=True)
    mixed = jnp.sum(got.reshape(groups, lanes, R_DEV, -1), axis=0).astype(jnp.bfloat16)
    held_qkv = jnp.swapaxes(mixed, 0, 1).reshape(R_DEV, -1).astype(jnp.float32)

    query = rotate(
        rms_rows(held_qkv[:, : HEADS * HD].reshape(R_DEV, HEADS, HD), query_gain), positions
    ).astype(jnp.bfloat16)
    key_new = rotate(
        rms_rows(held_qkv[:, HEADS * HD : (HEADS + KVH) * HD].reshape(R_DEV, KVH, HD), key_gain),
        positions,
    ).astype(jnp.bfloat16)
    value_new = held_qkv[:, (HEADS + KVH) * HD :].reshape(R_DEV, KVH, HD)
    kept, means, bias = compact_pages(old_cache, keep_rows, drop_weights)
    destination = dest_slots[0]
    fresh_ids = jnp.arange(pages_here, dtype=jnp.int32)
    inverse = jnp.sum(
        jnp.where(destination[None, :] == fresh_ids[:, None], fresh_ids[None, :], 0), axis=1
    )
    compact = kept[inverse].reshape(pages_here // 2, PAGE, KVW)
    summaries = means[inverse]
    per_lane = NP // lanes
    table = page_table.reshape(R_DEV, per_lane, lanes)
    mine = lax.dynamic_slice_in_dim(table, lane, 1, 2)[:, :, 0]
    logical = jnp.arange(per_lane, dtype=jnp.int32) * lanes + lane
    live = logical[None, :] < held_len[:, None]
    owner = jnp.any((mine[:, :, None] == fresh_ids[None, None, :]) & live[:, :, None], axis=1)
    query_groups = query.reshape(R_DEV, KVH, ratio, HD)
    row_keys = kept[:, :, :split].reshape(pages_here, KEEP, KVH, HD)
    row_values = kept[:, :, split:].reshape(pages_here, KEEP, KVH, HD)
    row_live = keep_rows >= 0
    allowed = owner[:, None, None, :, None] & row_live[None, None, None, :, :]
    scores = (
        jnp.einsum("rngd,pmnd->rngpm", query_groups, row_keys, preferred_element_type=jnp.float32)
        * scale
    )
    scores = jnp.where(allowed, scores, negative)
    mean_keys = means[:, :split].reshape(pages_here, KVH, HD)
    mean_values = means[:, split:].reshape(pages_here, KVH, HD)
    mean_scores = (
        jnp.einsum("rngd,pnd->rngp", query_groups, mean_keys, preferred_element_type=jnp.float32)
        * scale
        + bias[None, None, None, :]
    )
    mean_allowed = owner[:, None, None, :]
    mean_scores = jnp.where(mean_allowed, mean_scores, negative)
    own_score = (
        jnp.einsum("rngd,rnd->rng", query_groups, key_new, preferred_element_type=jnp.float32)
        * scale
    )
    own_score = jnp.where(lane == 0, own_score, negative)
    top = jnp.maximum(jnp.max(scores, axis=(3, 4)), jnp.max(mean_scores, axis=3))
    top = jnp.maximum(top, own_score)
    row_weight = jnp.where(allowed, jnp.exp(scores - top[..., None, None]), 0.0)
    mean_weight = jnp.where(mean_allowed, jnp.exp(mean_scores - top[..., None]), 0.0)
    own_weight = jnp.where(lane == 0, jnp.exp(own_score - top), 0.0)
    mass = jnp.sum(row_weight, axis=(3, 4)) + jnp.sum(mean_weight, axis=3) + own_weight
    total = jnp.einsum(
        "rngpm,pmnd->rngd",
        row_weight,
        row_values.astype(jnp.float32),
        precision=lax.Precision.HIGHEST,
    )
    total = total + jnp.einsum(
        "rngp,pnd->rngd",
        mean_weight,
        mean_values.astype(jnp.float32),
        precision=lax.Precision.HIGHEST,
    )
    total = total + own_weight[..., None] * value_new[:, :, None, :]

    some = mass > 0.0
    level = jnp.where(some, top + jnp.log(jnp.where(some, mass, 1.0)), negative)
    means_out = total / jnp.where(some, mass, 1.0)[..., None]
    own = HEADS * HD // groups
    parts = jnp.stack([means_out, jnp.broadcast_to(level[..., None], total.shape)])
    parts = jnp.transpose(parts.reshape(2, R_DEV, groups, own), (2, 1, 0, 3))
    parts = jnp.broadcast_to(
        parts.reshape(groups, 1, R_DEV, 2 * own), (groups, lanes, R_DEV, 2 * own)
    ).reshape(groups * lanes, R_DEV, 2 * own)
    came = lax.all_to_all(parts, both_axes, 0, 0, tiled=True)
    came = came.reshape(groups, lanes, R_DEV, 2 * own)
    outs, levels = came[..., :own], came[..., own:]
    weights = jnp.exp(levels - jnp.max(levels, axis=1, keepdims=True))
    attention = jnp.sum(outs * weights, axis=1) / jnp.sum(weights, axis=1)
    attention = attention.reshape(requests, own).astype(jnp.bfloat16)
    back = jnp.sum(
        jnp.where(holders[None, :] == everyone[:, None], everyone[None, :], 0), axis=1
    )
    projected = jnp.dot(
        pick_rows(back, attention), output_weight, preferred_element_type=jnp.float32
    )
    projected = projected + jnp.where(group == 0, hidden_in.astype(jnp.float32), 0.0)

    share = groups // lanes
    blocks = jnp.moveaxis(projected.reshape(requests, share, 1, features), 0, 2)
    blocks = jnp.broadcast_to(blocks, (share, lanes, requests, features))
    mid = jnp.sum(exchange(blocks.reshape(groups, requests, features)), axis=0)
    mid = to_block_owner(mid.astype(jnp.bfloat16)).astype(jnp.float32)
    squares = jnp.sum(mid * mid, axis=1, keepdims=True)
    gain_here = lax.dynamic_slice_in_dim(feedforward_gain, group * features, features, 0)
    inputs_mid = (mid * gain_here).astype(jnp.bfloat16)
    local_units = gate_weight.shape[1]
    piece = local_units // groups
    gates = jnp.dot(inputs_mid, gate_weight, preferred_element_type=jnp.float32)
    ups = jnp.dot(inputs_mid, up_weight, preferred_element_type=jnp.float32)
    both = jnp.concatenate(
        [
            gates.reshape(requests, groups, piece),
            ups.reshape(requests, groups, piece),
            jnp.broadcast_to(squares[:, :, None], (requests, groups, 1)),
        ],
        axis=2,
    )
    sums = jnp.sum(exchange(jnp.swapaxes(both, 0, 1)), axis=0)
    factor = lax.rsqrt(sums[:, 2 * piece :] / D + epsilon)
    gate = sums[:, :piece] * factor
    active = (jax.nn.silu(gate) * (sums[:, piece : 2 * piece] * factor)).astype(jnp.bfloat16)
    active_here = lax.all_gather(to_block_owner(active), "head", axis=1, tiled=True)
    down = jnp.dot(active_here, down_weight, preferred_element_type=jnp.float32)
    residual = [jnp.where(group == lane * share + k, mid, 0.0) for k in range(share)]
    down = down + jnp.concatenate(residual, axis=1)
    result = whole_sum(down).astype(jnp.bfloat16)
    return (compact, summaries, result)


TILE = 128
bfloat = jnp.bfloat16
single = jnp.float32


TERMS = 4


def three_terms(value, place):
    high = value.astype(bfloat).astype(single)
    rest = value - high
    middle = rest.astype(bfloat).astype(single)
    low = jnp.where(place == 2, rest - middle, 0.0)
    return jnp.where(place == 0, high, jnp.where(place == 1, middle, low))


def iota(shape, axis):
    return lax.broadcasted_iota(jnp.int32, shape, axis)


def run(kernel, outs, far, near, scratch=(), flops=0):
    in_specs = [pl.BlockSpec(memory_space=pltpu.HBM) for _ in far]
    in_specs += [pl.BlockSpec(memory_space=pltpu.VMEM) for _ in near]
    moved = sum(a.size * a.dtype.itemsize for a in [*far, *near, *outs])
    return pl.pallas_call(
        kernel,
        out_shape=list(outs),
        in_specs=in_specs,
        out_specs=[pl.BlockSpec(memory_space=pltpu.VMEM) for _ in outs],
        scratch_shapes=list(scratch),
        compiler_params=pltpu.CompilerParams(vmem_limit_bytes=16 * 2**20),
        cost_estimate=pl.CostEstimate(flops=flops, bytes_accessed=moved, transcendentals=0),
    )(*[pltpu.with_memory_space_constraint(a, pltpu.HBM) for a in far], *near)


def fetch(sources, targets, done):
    copies = [
        pltpu.make_async_copy(source, target, done.at[k])
        for k, (source, target) in enumerate(zip(sources, targets))
    ]
    for copy in copies:
        copy.start()
    return copies


def local_like(*arrays):
    return [pltpu.VMEM(a.shape, a.dtype) for a in arrays]


def scalar_like(*arrays):
    return [pltpu.SMEM(a.shape, a.dtype) for a in arrays]


def row_order(source, count, to_holder):
    first, second = iota((count, count), 0), iota((count, count), 1)
    if not to_holder:
        first, second = second, first
    order = (first == second) & (first % R_DEV == 0)
    for c in range(source.shape[1]):
        order = order | ((first == source[0, c] * R_DEV + 1) & (second == c * R_DEV + 1))
    return order.astype(single).astype(bfloat)


def shaped(shape, dtype):
    return jax.ShapeDtypeStruct(shape, dtype)


def first_kernel(
    source_far, gain_far, weight_far, hidden_far, one, two, three, sent, block, source, gain,
    weight, hidden, lanes_of, wide, done
):
    copies = fetch(
        (source_far, gain_far, weight_far, hidden_far), (source, gain, weight, hidden), done
    )
    rows = hidden.shape[0]
    groups = rows // R_DEV
    lanes = sent.shape[0] // groups
    columns, features = weight.shape
    group = lax.axis_index("req")
    share = groups // lanes
    squares = 0.0
    for turn, values in enumerate((one, two, three)):
        values = values[...].astype(single)
        lanes_of[turn + 1] = values
        squares = squares + jnp.sum(values * values, axis=1, keepdims=True)
    copies[3].wait()
    values = hidden[...].astype(single)
    lanes_of[0] = values
    squares = squares + jnp.sum(values * values, axis=1, keepdims=True)
    factor = lax.rsqrt(squares / D + epsilon)
    here = pl.ds(pl.multiple_of(group * features, features), features)
    within = pl.ds(pl.multiple_of(group % share * features, features), features)
    mine = lanes_of[group // share ^ lax.axis_index("head"), :, within]
    block[...] = mine.astype(bfloat)
    wide[...] = jnp.zeros_like(wide)
    for copy in copies[:3]:
        copy.wait()
    normed = (mine * factor * gain[:, here]).astype(bfloat)
    order = row_order(source, rows, True)
    normed = jnp.dot(order, normed, preferred_element_type=single).astype(bfloat)
    wide[:, :columns] = dot_rows(normed, weight[...])
    for g in range(groups):
        tile = jnp.concatenate(
            [
                wide[R_DEV * g : R_DEV * (g + 1), TILE * j : TILE * (j + 1)]
                for j in range(wide.shape[1] // TILE)
            ],
            axis=0,
        )
        for k in range(lanes):
            sent[g * lanes + k] = tile


def dot_rows(left, right):
    return lax.dot_general(left, right, (((1,), (1,)), ((), ())), preferred_element_type=single)


def prepare_kernel(*refs):
    far, refs = refs[:12], refs[12:]
    (compact, summaries, kept, added, tables, mine, theirs), refs = refs[:7], refs[7:]
    near, (ordered, plain, dealt, done) = refs[:12], refs[12:]
    copies = fetch(far, near, done)
    (dest, lengths, source, table, keep, weights, query_gain, key_gain, turns) = near[:9]
    pages, gate, up = near[9:]
    group = lax.axis_index("req")
    lane = lax.axis_index("head")
    lanes = lax.axis_size("head")
    for copy in copies[:9]:
        copy.wait()

    carried = 0
    for c in range(source.shape[1]):
        carried = carried + jnp.where(source[0, c] == group, c, 0)
    held_len = (lengths[0, group * R_DEV], lengths[0, carried * R_DEV + 1])
    count, rows, _ = pages.shape
    owned = []
    for r in range(R_DEV):
        slots = []
        for i in range(table.shape[1] // lanes):
            j = i * lanes + lane
            slots.append(jnp.where(j < held_len[r], table[r, j], -1))
        owned.append(slots)

    def owner(r, p):
        found = owned[r][0] == p
        for slot in owned[r][1:]:
            found = found | (slot == p)
        return found

    row = iota((32, TILE), 0)
    odd = (row & 1) == 1
    half_rows = turns.shape[0] // 2
    for part in range(2):
        pair = [turns[pl.ds(part * half_rows + held_len[r], 1), :] for r in range(R_DEV)]
        tables[32 * part : 32 * (part + 1), :] = jnp.where(odd, pair[1], pair[0])
    query_rows = HEADS * HD // TILE * R_DEV
    for c in range(TILE // HD):
        columns = slice(HD * c, HD * (c + 1))
        tables[64 : 64 + query_rows, columns] = jnp.broadcast_to(
            query_gain[...], (query_rows, HD)
        )
        tables[64 + query_rows : 96, columns] = jnp.broadcast_to(
            key_gain[...], (32 - query_rows, HD)
        )

    column = iota((1, TILE), 1)
    entries = count * KEEP
    added[...] = jnp.full_like(added, negative)
    extra = [
        jnp.where((column == count + r) & (lane == 0), 0.0, negative) for r in range(R_DEV)
    ]
    weight_columns = weights[...].T
    rows_of = iota((rows, KEEP), 0)
    place = iota((rows, 16), 1)
    copies[9].wait()
    for p in range(count):
        picks = (keep[p : p + 1, :] == rows_of).astype(single)
        dropped = weight_columns[:, p : p + 1] * (1.0 - jnp.sum(picks, axis=1, keepdims=True))
        total = jnp.sum(dropped, axis=0, keepdims=True)
        left = jnp.concatenate([picks, three_terms(dropped, place)], axis=1).astype(bfloat)
        both = lax.dot_general(
            left, pages[p], (((0,), (0,)), ((), ())), preferred_element_type=single
        )
        rows_kept = both[:KEEP].astype(bfloat)
        kept[KEEP * p : KEEP * (p + 1), :] = rows_kept
        slot = dest[0, p]
        start = pl.multiple_of((slot & 1) * KEEP, KEEP)
        compact[slot >> 1, pl.ds(start, KEEP), :] = rows_kept
        mean = both[KEEP : KEEP + 1] + both[KEEP + 1 : KEEP + 2] + both[KEEP + 2 : KEEP + 3]
        mean = mean / total
        plain[p : p + 1, :] = mean
        ordered[pl.ds(slot, 1), :] = mean
        live = jnp.where(keep[p : p + 1, :] >= 0, 0.0, negative)
        for r in range(R_DEV):
            here = owner(r, p)
            added[r : r + 1, KEEP * p : KEEP * (p + 1)] = jnp.where(here, live, negative)
            level = jnp.where(here, jnp.log(total), negative)
            extra[r] = jnp.where(column == p, level, extra[r])
    for r in range(R_DEV):
        added[r : r + 1, entries : entries + TILE] = extra[r]
    plain[count:, :] = jnp.zeros_like(plain[count:, :])
    kept[entries:, :] = plain[...].astype(bfloat)
    summaries[...] = ordered[...].astype(bfloat)

    for copy in copies[10:]:
        copy.wait()
    block = gate.shape[1] // 2
    piece = block // 2
    for k in range(2):
        for b in range(2):
            columns = slice(b * block + k * piece, b * block + (k + 1) * piece)
            start = b * block
            dealt[k, :, start : start + piece] = gate[:, columns].astype(single)
            dealt[k, :, start + piece : start + block] = up[:, columns].astype(single)
    mine[...] = dealt[lane & 1].astype(bfloat)
    theirs[...] = dealt[1 - (lane & 1)].astype(bfloat)


def attend_kernel(came, kept, added, tables, sent, x, extra_k, extra_v, out, logs):
    lanes = lax.axis_size("head")
    groups = came.shape[0] // lanes
    width = (HEADS + 2 * KVH) * HD // lanes
    span = -(-KVH * HD // TILE) * TILE
    key_cols = slice(0, span)
    value_cols = slice(KVW - span, KVW)
    first_key = HEADS * HD // TILE * R_DEV
    scale = HD ** (-0.5)
    x[...] = jnp.zeros_like(x)
    column = iota((8, TILE), 1)
    for k in range(lanes):
        tile = came[k].astype(single)
        for g in range(1, groups):
            tile = tile + came[g * lanes + k].astype(single)
        tile = tile.astype(bfloat).astype(single)
        base, shift = divmod(width * k, TILE)
        base = base * R_DEV
        if shift:
            tile = pltpu.roll(tile, shift, 1)
            x[base + 2 : base + 10, :] += jnp.where(column < shift, tile, 0.0)
        x[base : base + 8, :] += jnp.where(column >= shift, tile, 0.0)
    values = x[...]
    same_head = (iota((TILE, TILE), 0) // HD == iota((TILE, TILE), 1) // HD).astype(single)
    squares = jnp.dot(
        values * values, same_head, precision=lax.Precision.HIGHEST, preferred_element_type=single
    )
    normed = values * lax.rsqrt(squares / HD + epsilon) * tables[64:96, :]
    early = iota(values.shape, 1) % HD < HD // 2
    swapped = jnp.where(
        early, pltpu.roll(normed, TILE - HD // 2, 1), pltpu.roll(normed, HD // 2, 1)
    )
    turned = normed * tables[0:32, :] + swapped * tables[32:64, :]
    turned = turned.astype(bfloat).astype(single)

    rows = 24
    row = iota((rows, TILE), 0)
    half = iota((rows, TILE), 1) // HD
    key_head = row >> 2
    query = jnp.where(row < first_key, turned[:rows], 0.0)
    other = pltpu.roll(query, HD, 1)
    queries = []
    for u in range(2):
        placed = jnp.where(
            half == (key_head & 1), jnp.where((key_head & 1) == u, query, other), 0.0
        )
        queries.append(
            jnp.concatenate(
                [jnp.where((key_head >> 1) == c, placed, 0.0) for c in range(span // TILE)], axis=1
            )
        )
    queries = jnp.concatenate(queries, axis=0).astype(bfloat)

    extras = extra_k.shape[0]
    entries = kept.shape[0] - extras
    count = entries // KEEP
    extra_k[...] = kept[entries:, key_cols].astype(single)
    extra_v[...] = kept[entries:, value_cols].astype(single)
    first_value = first_key + KVH * HD // TILE * R_DEV
    for c in range(span // TILE):
        at = slice(c * TILE, (c + 1) * TILE)
        r = first_key + R_DEV * c
        extra_k[count : count + R_DEV, at] = turned[r : r + R_DEV]
        r = first_value + R_DEV * c
        extra_v[count : count + R_DEV, at] = values[r : r + R_DEV]

    def by_request(columns, size):
        odd = (iota((2 * rows, size), 0) & 1) == 1
        return jnp.where(odd, added[1:2, columns], added[0:1, columns])

    scores = dot_rows(queries, kept[:entries, key_cols]) * scale
    scores = scores + by_request(slice(0, entries), entries)
    extra = dot_rows(queries, extra_k[...].astype(bfloat)) * scale
    extra = extra + by_request(slice(entries, entries + extras), extras)
    top = jnp.maximum(
        jnp.max(scores, axis=1, keepdims=True), jnp.max(extra, axis=1, keepdims=True)
    )
    weight = jnp.where(scores > 0.5 * negative, jnp.exp(scores - top), 0.0)
    extra_weight = jnp.where(extra > 0.5 * negative, jnp.exp(extra - top), 0.0)
    mass = jnp.sum(weight, axis=1, keepdims=True) + jnp.sum(extra_weight, axis=1, keepdims=True)

    def weighted(parts, right):
        high = parts.astype(bfloat)
        low = (parts - high.astype(single)).astype(bfloat)
        return jnp.dot(high, right, preferred_element_type=single) + jnp.dot(
            low, right, preferred_element_type=single
        )

    total = weighted(weight, kept[:entries, value_cols]) + weighted(
        extra_weight, extra_v[...].astype(bfloat)
    )
    some = mass > 0.0
    mass = jnp.where(some, mass, 1.0)
    total = total / mass
    level = jnp.where(some, top + jnp.log(mass), negative)

    slot = key_head + (KVW // 2 - (KVW - span)) // HD
    results = []
    for u in range(2):
        mine = total[rows * u : rows * (u + 1)]
        picked = mine[:, :TILE]
        for c in range(1, span // TILE):
            picked = jnp.where((slot >> 1) == c, mine[:, c * TILE : (c + 1) * TILE], picked)
        results.append(jnp.where((slot & 1) == u, picked, pltpu.roll(picked, HD, 1)))
    out[...] = jnp.where(half == 0, results[0], results[1])
    logs[...] = jnp.broadcast_to(level, logs.shape)
    own = HEADS * HD // lanes
    size = 6
    column = iota((size, TILE), 1)
    here = column // TERMS == iota((size, TILE), 0)
    for k in range(lanes):
        r = own * k // TILE * R_DEV
        tile = [out[r : r + size, :]]
        for u in range(2):
            coded = three_terms(logs[rows * u + r : rows * u + r + size, :], column % TERMS)
            tile.append(jnp.sum(jnp.where(here, coded, 0.0), axis=0, keepdims=True))
        tile = jnp.concatenate(tile, axis=0).astype(bfloat)
        for g in range(groups):
            sent[g * lanes + k] = tile


def blocks_kernel(weight_far, same, other, done):
    width = same.shape[1]
    group = lax.axis_index("req")
    starts = [pl.multiple_of(((group & 1) ^ turn) * width, width) for turn in range(2)]
    parts = [weight_far.at[:, pl.ds(start, width)] for start in starts]
    for copy in fetch(parts, (same, other), done):
        copy.wait()


def project_kernel(source_far, came, first, second, sent, source, logs, rows, pieces, done):
    (copy,) = fetch((source_far,), (source,), done)
    lanes = lax.axis_size("head")
    groups = came.shape[0] // lanes
    group = lax.axis_index("req")
    features = first.shape[0]
    requests = rows.shape[0]
    size = 6
    tiles = [came[d].astype(single) for d in range(groups * lanes)]
    for g in range(groups):
        for k in range(lanes):
            logs[k, 2 * g : 2 * g + 2, :] = tiles[g * lanes + k][size:]
    spread = (iota((8, TILE), 1) // TERMS == iota((8, TILE), 0)).astype(single).astype(bfloat)
    levels = [dot_rows(spread, logs[k].astype(bfloat)) for k in range(lanes)]
    top = jnp.maximum(jnp.maximum(levels[0], levels[1]), jnp.maximum(levels[2], levels[3]))
    shares = [jnp.exp(level - top) for level in levels]
    mass = sum(shares)
    shares = [share / mass for share in shares]
    lower = iota((8, TILE), 1) < HD
    for g in range(groups):
        mixed = 0.0
        for k in range(lanes):
            share = shares[k]
            share = jnp.where(lower, share[:, 2 * g : 2 * g + 1], share[:, 2 * g + 1 : 2 * g + 2])
            mixed = mixed + share * tiles[g * lanes + k]
        for j in range(size // R_DEV):
            rows[R_DEV * g : R_DEV * (g + 1), TILE * j : TILE * (j + 1)] = mixed[
                R_DEV * j : R_DEV * (j + 1)
            ]
    width = rows.shape[1]
    shift = lax.rem(lax.axis_index("head") * (2 * features), TILE)
    attention = rows[...].astype(bfloat).astype(single)
    attention = pltpu.roll(attention, lax.rem(width - shift, width), 1)
    copy.wait()
    order = row_order(source, requests, False)
    attention = jnp.dot(order, attention.astype(bfloat), preferred_element_type=single)
    for b in range(2):
        pieces[b] = attention[:, features * b : features * (b + 1)]
    total = 0.0
    for turn, weight in enumerate((first, second)):
        piece = pieces[(group & 1) ^ turn].astype(bfloat)
        total = total + jnp.dot(piece, weight[...], preferred_element_type=single)
    sent[...] = total


def units_kernel(
    gain_far, own, one, two, three, hidden, mine, theirs, sent, mid_out, gain, done
):
    (copy,) = fetch((gain_far,), (gain,), done)
    rows, features = own.shape
    share = sent.shape[0] // lax.axis_size("head")
    group = lax.axis_index("req")
    lane = lax.axis_index("head")
    here = pl.ds(pl.multiple_of(group * features, features), features)
    mid = (own[...] + one[...]) + (two[...] + three[...])
    mid = (hidden[...].astype(single) + mid).astype(bfloat)
    mid_out[...] = mid
    mid = mid.astype(single)
    squares = jnp.sum(mid * mid, axis=1, keepdims=True)
    block = mine.shape[1] // share
    terms = three_terms(squares, iota((rows, sent.shape[2] - block), 1)).astype(bfloat)
    copy.wait()
    inputs = (mid * gain[:, here]).astype(bfloat)
    for turn, weight in enumerate((mine, theirs)):
        units = jnp.dot(inputs, weight[...], preferred_element_type=single).astype(bfloat)
        target = (lane ^ turn) * share
        for b in range(share):
            sent[target + b, :, :block] = units[:, block * b : block * (b + 1)]
            sent[target + b, :, block:] = terms


def active_kernel(came, active):
    total = came[0].astype(single)
    for g in range(1, came.shape[0]):
        total = total + came[g].astype(single)
    piece = active.shape[1]
    squares = jnp.sum(total[:, 2 * piece : 2 * piece + 3], axis=1, keepdims=True)
    factor = lax.rsqrt(squares / D + epsilon)
    gate = total[:, :piece] * factor
    up = total[:, piece : 2 * piece] * factor
    active[...] = (gate / (1.0 + jnp.exp(-gate)) * up).astype(bfloat)


def down_kernel(own, one, two, three, weight, mid, sent, active):
    groups, rows, width = sent.shape
    piece = own.shape[1]
    half = mid.shape[1]
    for turn, values in enumerate((own, one, two, three)):
        active[turn] = values[...]
    share = width // half
    group = lax.axis_index("req")
    lane = lax.axis_index("head")
    first = group // (2 * share) * 2 ^ lane
    down = jnp.dot(active[first], weight[:piece, :], preferred_element_type=single)
    down = down + jnp.dot(active[first ^ 1], weight[piece:, :], preferred_element_type=single)
    residual = mid[...].astype(single)
    for b in range(share):
        columns = slice(half * b, half * (b + 1))
        mine = group == lane * share + b
        total = (down[:, columns] + jnp.where(mine, residual, 0.0)).astype(bfloat)
        for g in range(groups):
            sent[g, :, columns] = total


def result_kernel(came, result):
    total = came[0].astype(single)
    for g in range(1, came.shape[0]):
        total = total + came[g].astype(single)
    result[...] = total.astype(bfloat)


def rotation_table():
    half = HD // 2
    size = -(-(NP + 1) // 8) * 8
    frequency = 10000.0 ** (-np.arange(half) / half)
    angles = PAGE * np.arange(size)[:, None] * frequency[None, :]
    cosine, sine = np.cos(angles), np.sin(angles)
    wide = [np.tile(np.concatenate(pair, axis=1), (1, TILE // HD)) for pair in
            ((cosine, cosine), (-sine, sine))]
    return jnp.asarray(np.concatenate(wide), dtype=single)


def swapped_lanes(value, turn):
    lanes = lax.axis_size("head")
    return lax.ppermute(value, "head", [(k, k ^ turn) for k in range(lanes)])


def from_lanes(value):
    return [value] + [swapped_lanes(value, turn) for turn in range(1, lax.axis_size("head"))]


def handed_over(value, turn):
    groups = lax.axis_size("req")
    lanes = lax.axis_size("head")
    share = groups // lanes
    pairs = [
        (g * lanes + h, (share * h + ((g & 1) ^ turn)) * lanes + g // share)
        for g in range(groups)
        for h in range(lanes)
    ]
    return lax.ppermute(value, both_axes, pairs)


def on_device(
    hidden_in,
    attention_gain,
    query_gain,
    key_gain,
    feedforward_gain,
    input_weight,
    output_weight,
    gate_weight,
    up_weight,
    down_weight,
    old_cache,
    keep_rows,
    drop_weights,
    dest_slots,
    lengths,
    page_table,
    source,
):
    groups = lax.axis_size("req")
    lanes = lax.axis_size("head")
    requests = hidden_in.shape[0]
    pages_here = old_cache.shape[0]
    devices = groups * lanes
    features = D // groups
    copies = pltpu.SemaphoreType.DMA

    others = from_lanes(hidden_in)[1:]
    blocks = run(
        blocks_kernel,
        [shaped((output_weight.shape[0], features), bfloat)] * 2,
        [output_weight],
        [],
        [copies((2,))],
    )
    handed = [handed_over(block, turn) for turn, block in enumerate(blocks)]
    scalars = [dest_slots, lengths[None, :], source[None, :], page_table]
    arrays = [
        keep_rows,
        drop_weights,
        query_gain[None, :],
        key_gain[None, :],
        rotation_table(),
        old_cache,
        gate_weight,
        up_weight,
    ]
    entries = pages_here * KEEP
    extras = 16
    compact, summaries, kept, added, tables, mine, theirs = run(
        prepare_kernel,
        [
            shaped((pages_here // 2, PAGE, KVW), bfloat),
            shaped((pages_here, KVW), bfloat),
            shaped((entries + extras, KVW), bfloat),
            shaped((8, entries + TILE), single),
            shaped((96, TILE), single),
            shaped(gate_weight.shape, bfloat),
            shaped(gate_weight.shape, bfloat),
        ],
        scalars + arrays,
        [],
        [
            *scalar_like(*scalars),
            *local_like(*arrays),
            pltpu.VMEM((pages_here, KVW), single),
            pltpu.VMEM((extras, KVW), single),
            pltpu.VMEM((2,) + gate_weight.shape, single),
            copies((len(scalars + arrays),)),
        ],
        2 * pages_here * TILE * PAGE * KVW,
    )
    tables, *moved = lax.optimization_barrier((tables, *others, *handed))
    others, handed = moved[: lanes - 1], moved[lanes - 1 :]

    holds = source[None, :]
    columns = input_weight.shape[1]
    padded = -(-columns // TILE) * TILE
    gain = attention_gain[None, :]
    weight = input_weight.T
    far = [holds, gain, weight, hidden_in]
    sent, hidden_block = run(
        first_kernel,
        [
            shaped((devices, R_DEV * padded // TILE, TILE), single),
            shaped((requests, features), bfloat),
        ],
        far,
        others,
        [
            *scalar_like(holds),
            *local_like(*far[1:]),
            pltpu.VMEM((lanes,) + hidden_in.shape, single),
            pltpu.VMEM((requests, padded), single),
            copies((len(far),)),
        ],
        2 * requests * features * columns,
    )
    came = lax.all_to_all(sent, both_axes, 0, 0, tiled=True)
    theirs, _ = lax.optimization_barrier((theirs, sent))
    theirs = swapped_lanes(theirs, 1)
    came, theirs = lax.optimization_barrier((came, theirs))
    span = -(-KVH * HD // TILE) * TILE
    (parts,) = run(
        attend_kernel,
        [shaped((devices, 8, TILE), bfloat)],
        [],
        [came, kept, added, tables],
        [
            pltpu.VMEM((32, TILE), single),
            pltpu.VMEM((extras, span), single),
            pltpu.VMEM((extras, span), single),
            pltpu.VMEM((24, TILE), single),
            pltpu.VMEM((48, TILE), single),
        ],
        6 * 48 * entries * span,
    )
    came = lax.all_to_all(parts, both_axes, 0, 0, tiled=True)
    (sent,) = run(
        project_kernel,
        [shaped((requests, features), single)],
        [holds],
        [came, *handed],
        [
            *scalar_like(holds),
            pltpu.VMEM((lanes, 2 * groups, TILE), single),
            pltpu.VMEM((requests, 3 * TILE), single),
            pltpu.VMEM((2, requests, output_weight.shape[0]), single),
            copies((1,)),
        ],
        2 * requests * output_weight.size,
    )
    gain = feedforward_gain[None, :]
    block = gate_weight.shape[1] // 2
    sent, mid = run(
        units_kernel,
        [
            shaped((groups, requests, block + TILE), bfloat),
            shaped((requests, features), bfloat),
        ],
        [gain],
        [*from_lanes(sent), hidden_block, mine, theirs],
        [*local_like(gain), copies((1,))],
        4 * requests * gate_weight.size,
    )
    (active,) = run(
        active_kernel, [shaped((requests, block // 2), bfloat)], [], [exchange(sent)]
    )
    (sent,) = run(
        down_kernel,
        [shaped((groups, requests, down_weight.shape[1]), bfloat)],
        [],
        [*from_lanes(active), down_weight, mid],
        [pltpu.VMEM((lanes,) + active.shape, bfloat)],
        2 * requests * down_weight.size,
    )
    (result,) = run(
        result_kernel, [shaped((requests, down_weight.shape[1]), bfloat)], [], [exchange(sent)]
    )
    return (compact, summaries, result)


def solution(mesh):
    placed = (
        P(None, "head"),
        P(),
        P(),
        P(),
        P(),
        P("req", "head"),
        P("req", "head"),
        P("req", "head"),
        P("req", "head"),
        P("req", "head"),
        P(("req", "head"), None, None),
        P(("req", "head"), None),
        P(("req", "head"), None),
        P(("req", "head"), None),
        P(),
        P("req", None),
        P(),
    )
    return jax.shard_map(
        on_device if mesh.shape["req"] <= DIRECT else on_device_wide,
        mesh=mesh,
        in_specs=placed,
        out_specs=(P(("req", "head"), None, None), P(("req", "head"), None), P(None, "head")),
        check_vma=False,
    )
```

```python
import jax
import jax.numpy as jnp
import numpy as np
from jax import lax
from jax.experimental import pallas as pl
from jax.experimental.pallas import tpu as pltpu
from jax.sharding import PartitionSpec as P

D = 2048
HEADS = 20
KVH = 5
HD = 64
FF = 5120
PAGE = 128
KEEP = 64
NP = 16
R_DEV = 2
KVW = 640

DIRECT = 8

epsilon = 1e-06
negative = -1e30
both_axes = ("req", "head")


def rms_scale(values):
    return lax.rsqrt(jnp.mean(values * values, axis=-1, keepdims=True) + epsilon)


def rms_rows(values, gain):
    return values * rms_scale(values) * gain


def rotate(vectors, positions):
    half = vectors.shape[-1] // 2
    frequency = 10000.0 ** (-jnp.arange(half, dtype=jnp.float32) / half)
    angles = positions.astype(jnp.float32)[:, None] * frequency[None, :]
    cosine = jnp.cos(angles)[:, None, :]
    sine = jnp.sin(angles)[:, None, :]
    first = vectors[..., :half]
    second = vectors[..., half:]
    return jnp.concatenate(
        [first * cosine - second * sine, second * cosine + first * sine], axis=-1
    )


def compact_pages(pages, keep, weights):
    rows = jnp.arange(pages.shape[1], dtype=jnp.int32)
    picks = keep[:, :, None] == rows[None, None, :]
    kept = jnp.einsum(
        "pkr,prc->pkc", picks.astype(jnp.bfloat16), pages, preferred_element_type=jnp.float32
    ).astype(jnp.bfloat16)
    dropped = weights * (1.0 - jnp.sum(picks.astype(jnp.float32), axis=1))
    total = jnp.sum(dropped, axis=1)
    means = (
        jnp.einsum(
            "pr,prc->pc", dropped, pages.astype(jnp.float32), precision=lax.Precision.HIGHEST
        )
        / total[:, None]
    )
    return (kept, means.astype(jnp.bfloat16), jnp.log(total))


def held_request(rows, source):
    half = R_DEV // 2
    position = rows % R_DEV
    slot = rows // R_DEV * half + position - half
    continued = jnp.arange(source.shape[0], dtype=jnp.int32)
    matches = source[None, :] == slot[:, None]
    owner_cont = jnp.sum(jnp.where(matches, continued[None, :], 0), axis=1)
    carried = owner_cont // half * R_DEV + half + owner_cont % half
    return jnp.where(position < half, rows, carried)


def pick_rows(order, rows):
    chosen = order[:, None] == jnp.arange(rows.shape[0], dtype=jnp.int32)[None, :]
    return jnp.dot(
        chosen.astype(jnp.bfloat16), rows, preferred_element_type=jnp.float32
    ).astype(jnp.bfloat16)


def exchange(parts):
    return lax.all_to_all(parts, "req", split_axis=0, concat_axis=0, tiled=True)


def to_block_owner(rows):
    groups = lax.axis_size("req")
    lanes = lax.axis_size("head")
    per_lane = groups // lanes
    pairs = [
        (g * lanes + h, (per_lane * h + g // lanes) * lanes + g % lanes)
        for g in range(groups)
        for h in range(lanes)
    ]
    return lax.ppermute(rows, both_axes, pairs)


def whole_sum(partial):
    if lax.axis_size("req") > DIRECT:
        return lax.psum(partial, "req")
    groups = lax.axis_size("req")
    return jnp.sum(exchange(jnp.broadcast_to(partial[None], (groups,) + partial.shape)), axis=0)


def on_device_wide(
    hidden_in,
    attention_gain,
    query_gain,
    key_gain,
    feedforward_gain,
    input_weight,
    output_weight,
    gate_weight,
    up_weight,
    down_weight,
    old_cache,
    keep_rows,
    drop_weights,
    dest_slots,
    lengths,
    page_table,
    source,
):
    groups = lax.axis_size("req")
    lanes = lax.axis_size("head")
    group = lax.axis_index("req")
    lane = lax.axis_index("head")
    requests = hidden_in.shape[0]
    half = R_DEV // 2
    split = KVH * HD
    ratio = HEADS // KVH
    scale = HD ** (-0.5)
    pages_here = old_cache.shape[0]
    everyone = jnp.arange(requests, dtype=jnp.int32)
    holders = held_request(everyone, source)
    held = lax.dynamic_slice_in_dim(holders, group * R_DEV, R_DEV, 0)
    held_len = lengths[held]
    positions = held_len * PAGE

    whole = lax.all_gather(hidden_in, "head", axis=1, tiled=True)
    normed = rms_rows(whole.astype(jnp.float32), attention_gain).astype(jnp.bfloat16)
    features = D // groups
    inputs = pick_rows(holders, lax.dynamic_slice_in_dim(normed, group * features, features, 1))
    partial_qkv = jnp.dot(inputs, input_weight, preferred_element_type=jnp.float32)
    sent = jnp.broadcast_to(
        partial_qkv.reshape(groups, 1, R_DEV, -1), (groups, lanes, R_DEV, partial_qkv.shape[1])
    ).reshape(groups * lanes, R_DEV, -1)
    got = lax.all_to_all(sent, both_axes, split_axis=0, concat_axis=0, tiled=True)
    mixed = jnp.sum(got.reshape(groups, lanes, R_DEV, -1), axis=0).astype(jnp.bfloat16)
    held_qkv = jnp.swapaxes(mixed, 0, 1).reshape(R_DEV, -1).astype(jnp.float32)

    query = rotate(
        rms_rows(held_qkv[:, : HEADS * HD].reshape(R_DEV, HEADS, HD), query_gain), positions
    ).astype(jnp.bfloat16)
    key_new = rotate(
        rms_rows(held_qkv[:, HEADS * HD : (HEADS + KVH) * HD].reshape(R_DEV, KVH, HD), key_gain),
        positions,
    ).astype(jnp.bfloat16)
    value_new = held_qkv[:, (HEADS + KVH) * HD :].reshape(R_DEV, KVH, HD)
    kept, means, bias = compact_pages(old_cache, keep_rows, drop_weights)
    destination = dest_slots[0]
    fresh_ids = jnp.arange(pages_here, dtype=jnp.int32)
    inverse = jnp.sum(
        jnp.where(destination[None, :] == fresh_ids[:, None], fresh_ids[None, :], 0), axis=1
    )
    compact = kept[inverse].reshape(pages_here // 2, PAGE, KVW)
    summaries = means[inverse]
    per_lane = NP // lanes
    table = page_table.reshape(R_DEV, per_lane, lanes)
    mine = lax.dynamic_slice_in_dim(table, lane, 1, 2)[:, :, 0]
    logical = jnp.arange(per_lane, dtype=jnp.int32) * lanes + lane
    live = logical[None, :] < held_len[:, None]
    owner = jnp.any((mine[:, :, None] == fresh_ids[None, None, :]) & live[:, :, None], axis=1)
    query_groups = query.reshape(R_DEV, KVH, ratio, HD)
    row_keys = kept[:, :, :split].reshape(pages_here, KEEP, KVH, HD)
    row_values = kept[:, :, split:].reshape(pages_here, KEEP, KVH, HD)
    row_live = keep_rows >= 0
    allowed = owner[:, None, None, :, None] & row_live[None, None, None, :, :]
    scores = (
        jnp.einsum("rngd,pmnd->rngpm", query_groups, row_keys, preferred_element_type=jnp.float32)
        * scale
    )
    scores = jnp.where(allowed, scores, negative)
    mean_keys = means[:, :split].reshape(pages_here, KVH, HD)
    mean_values = means[:, split:].reshape(pages_here, KVH, HD)
    mean_scores = (
        jnp.einsum("rngd,pnd->rngp", query_groups, mean_keys, preferred_element_type=jnp.float32)
        * scale
        + bias[None, None, None, :]
    )
    mean_allowed = owner[:, None, None, :]
    mean_scores = jnp.where(mean_allowed, mean_scores, negative)
    own_score = (
        jnp.einsum("rngd,rnd->rng", query_groups, key_new, preferred_element_type=jnp.float32)
        * scale
    )
    own_score = jnp.where(lane == 0, own_score, negative)
    top = jnp.maximum(jnp.max(scores, axis=(3, 4)), jnp.max(mean_scores, axis=3))
    top = jnp.maximum(top, own_score)
    row_weight = jnp.where(allowed, jnp.exp(scores - top[..., None, None]), 0.0)
    mean_weight = jnp.where(mean_allowed, jnp.exp(mean_scores - top[..., None]), 0.0)
    own_weight = jnp.where(lane == 0, jnp.exp(own_score - top), 0.0)
    mass = jnp.sum(row_weight, axis=(3, 4)) + jnp.sum(mean_weight, axis=3) + own_weight
    total = jnp.einsum(
        "rngpm,pmnd->rngd",
        row_weight,
        row_values.astype(jnp.float32),
        precision=lax.Precision.HIGHEST,
    )
    total = total + jnp.einsum(
        "rngp,pnd->rngd",
        mean_weight,
        mean_values.astype(jnp.float32),
        precision=lax.Precision.HIGHEST,
    )
    total = total + own_weight[..., None] * value_new[:, :, None, :]

    some = mass > 0.0
    level = jnp.where(some, top + jnp.log(jnp.where(some, mass, 1.0)), negative)
    means_out = total / jnp.where(some, mass, 1.0)[..., None]
    own = HEADS * HD // groups
    parts = jnp.stack([means_out, jnp.broadcast_to(level[..., None], total.shape)])
    parts = jnp.transpose(parts.reshape(2, R_DEV, groups, own), (2, 1, 0, 3))
    parts = jnp.broadcast_to(
        parts.reshape(groups, 1, R_DEV, 2 * own), (groups, lanes, R_DEV, 2 * own)
    ).reshape(groups * lanes, R_DEV, 2 * own)
    came = lax.all_to_all(parts, both_axes, 0, 0, tiled=True)
    came = came.reshape(groups, lanes, R_DEV, 2 * own)
    outs, levels = came[..., :own], came[..., own:]
    weights = jnp.exp(levels - jnp.max(levels, axis=1, keepdims=True))
    attention = jnp.sum(outs * weights, axis=1) / jnp.sum(weights, axis=1)
    attention = attention.reshape(requests, own).astype(jnp.bfloat16)
    back = jnp.sum(
        jnp.where(holders[None, :] == everyone[:, None], everyone[None, :], 0), axis=1
    )
    projected = jnp.dot(
        pick_rows(back, attention), output_weight, preferred_element_type=jnp.float32
    )
    projected = projected + jnp.where(group == 0, hidden_in.astype(jnp.float32), 0.0)

    share = groups // lanes
    blocks = jnp.moveaxis(projected.reshape(requests, share, 1, features), 0, 2)
    blocks = jnp.broadcast_to(blocks, (share, lanes, requests, features))
    mid = jnp.sum(exchange(blocks.reshape(groups, requests, features)), axis=0)
    mid = to_block_owner(mid.astype(jnp.bfloat16)).astype(jnp.float32)
    squares = jnp.sum(mid * mid, axis=1, keepdims=True)
    gain_here = lax.dynamic_slice_in_dim(feedforward_gain, group * features, features, 0)
    inputs_mid = (mid * gain_here).astype(jnp.bfloat16)
    local_units = gate_weight.shape[1]
    piece = local_units // groups
    gates = jnp.dot(inputs_mid, gate_weight, preferred_element_type=jnp.float32)
    ups = jnp.dot(inputs_mid, up_weight, preferred_element_type=jnp.float32)
    both = jnp.concatenate(
        [
            gates.reshape(requests, groups, piece),
            ups.reshape(requests, groups, piece),
            jnp.broadcast_to(squares[:, :, None], (requests, groups, 1)),
        ],
        axis=2,
    )
    sums = jnp.sum(exchange(jnp.swapaxes(both, 0, 1)), axis=0)
    factor = lax.rsqrt(sums[:, 2 * piece :] / D + epsilon)
    gate = sums[:, :piece] * factor
    active = (jax.nn.silu(gate) * (sums[:, piece : 2 * piece] * factor)).astype(jnp.bfloat16)
    active_here = lax.all_gather(to_block_owner(active), "head", axis=1, tiled=True)
    down = jnp.dot(active_here, down_weight, preferred_element_type=jnp.float32)
    residual = [jnp.where(group == lane * share + k, mid, 0.0) for k in range(share)]
    down = down + jnp.concatenate(residual, axis=1)
    result = whole_sum(down).astype(jnp.bfloat16)
    return (compact, summaries, result)


TILE = 128
bfloat = jnp.bfloat16
single = jnp.float32


TERMS = 4


def three_terms(value, place):
    high = value.astype(bfloat).astype(single)
    rest = value - high
    middle = rest.astype(bfloat).astype(single)
    low = jnp.where(place == 2, rest - middle, 0.0)
    return jnp.where(place == 0, high, jnp.where(place == 1, middle, low))


def iota(shape, axis):
    return lax.broadcasted_iota(jnp.int32, shape, axis)


def run(kernel, outs, far, near, scratch=(), flops=0):
    in_specs = [pl.BlockSpec(memory_space=pltpu.HBM) for _ in far]
    in_specs += [pl.BlockSpec(memory_space=pltpu.VMEM) for _ in near]
    moved = sum(a.size * a.dtype.itemsize for a in [*far, *near, *outs])
    return pl.pallas_call(
        kernel,
        out_shape=list(outs),
        in_specs=in_specs,
        out_specs=[pl.BlockSpec(memory_space=pltpu.VMEM) for _ in outs],
        scratch_shapes=list(scratch),
        compiler_params=pltpu.CompilerParams(vmem_limit_bytes=16 * 2**20),
        cost_estimate=pl.CostEstimate(flops=flops, bytes_accessed=moved, transcendentals=0),
    )(*[pltpu.with_memory_space_constraint(a, pltpu.HBM) for a in far], *near)


def fetch(sources, targets, done):
    copies = [
        pltpu.make_async_copy(source, target, done.at[k])
        for k, (source, target) in enumerate(zip(sources, targets))
    ]
    for copy in copies:
        copy.start()
    return copies


def local_like(*arrays):
    return [pltpu.VMEM(a.shape, a.dtype) for a in arrays]


def scalar_like(*arrays):
    return [pltpu.SMEM(a.shape, a.dtype) for a in arrays]


def row_order(source, count, to_holder):
    first, second = iota((count, count), 0), iota((count, count), 1)
    if not to_holder:
        first, second = second, first
    order = (first == second) & (first % R_DEV == 0)
    for c in range(source.shape[1]):
        order = order | ((first == source[0, c] * R_DEV + 1) & (second == c * R_DEV + 1))
    return order.astype(single).astype(bfloat)


def shaped(shape, dtype):
    return jax.ShapeDtypeStruct(shape, dtype)


def first_kernel(
    source_far, gain_far, weight_far, hidden_far, one, two, three, sent, block, source, gain,
    weight, hidden, lanes_of, wide, done
):
    copies = fetch(
        (source_far, gain_far, weight_far, hidden_far), (source, gain, weight, hidden), done
    )
    rows = hidden.shape[0]
    groups = rows // R_DEV
    lanes = sent.shape[0] // groups
    columns, features = weight.shape
    group = lax.axis_index("req")
    share = groups // lanes
    squares = 0.0
    for turn, values in enumerate((one, two, three)):
        values = values[...].astype(single)
        lanes_of[turn + 1] = values
        squares = squares + jnp.sum(values * values, axis=1, keepdims=True)
    copies[3].wait()
    values = hidden[...].astype(single)
    lanes_of[0] = values
    squares = squares + jnp.sum(values * values, axis=1, keepdims=True)
    factor = lax.rsqrt(squares / D + epsilon)
    here = pl.ds(pl.multiple_of(group * features, features), features)
    within = pl.ds(pl.multiple_of(group % share * features, features), features)
    mine = lanes_of[group // share ^ lax.axis_index("head"), :, within]
    block[...] = mine.astype(bfloat)
    wide[...] = jnp.zeros_like(wide)
    for copy in copies[:3]:
        copy.wait()
    normed = (mine * factor * gain[:, here]).astype(bfloat)
    order = row_order(source, rows, True)
    normed = jnp.dot(order, normed, preferred_element_type=single).astype(bfloat)
    wide[:, :columns] = dot_rows(normed, weight[...])
    for g in range(groups):
        tile = jnp.concatenate(
            [
                wide[R_DEV * g : R_DEV * (g + 1), TILE * j : TILE * (j + 1)]
                for j in range(wide.shape[1] // TILE)
            ],
            axis=0,
        )
        for k in range(lanes):
            sent[g * lanes + k] = tile


def dot_rows(left, right):
    return lax.dot_general(left, right, (((1,), (1,)), ((), ())), preferred_element_type=single)


def prepare_kernel(*refs):
    far, (handed, *refs) = refs[:12], refs[12:]
    (compact, summaries, kept, added, tables, mine, theirs, given), refs = refs[:8], refs[8:]
    near, (ordered, plain, dealt, done) = refs[:12], refs[12:]
    copies = fetch(far, near, done)
    (dest, lengths, source, table, keep, weights, query_gain, key_gain, turns) = near[:9]
    pages, gate, up = near[9:]
    group = lax.axis_index("req")
    lane = lax.axis_index("head")
    lanes = lax.axis_size("head")
    for copy in copies[:9]:
        copy.wait()

    carried = 0
    for c in range(source.shape[1]):
        carried = carried + jnp.where(source[0, c] == group, c, 0)
    held_len = (lengths[0, group * R_DEV], lengths[0, carried * R_DEV + 1])
    count, rows, _ = pages.shape
    owned = []
    for r in range(R_DEV):
        slots = []
        for i in range(table.shape[1] // lanes):
            j = i * lanes + lane
            slots.append(jnp.where(j < held_len[r], table[r, j], -1))
        owned.append(slots)

    def owner(r, p):
        found = owned[r][0] == p
        for slot in owned[r][1:]:
            found = found | (slot == p)
        return found

    row = iota((32, TILE), 0)
    odd = (row & 1) == 1
    half_rows = turns.shape[0] // 2
    for part in range(2):
        pair = [turns[pl.ds(part * half_rows + held_len[r], 1), :] for r in range(R_DEV)]
        tables[32 * part : 32 * (part + 1), :] = jnp.where(odd, pair[1], pair[0])
    query_rows = HEADS * HD // TILE * R_DEV
    for c in range(TILE // HD):
        columns = slice(HD * c, HD * (c + 1))
        tables[64 : 64 + query_rows, columns] = jnp.broadcast_to(
            query_gain[...], (query_rows, HD)
        )
        tables[64 + query_rows : 96, columns] = jnp.broadcast_to(
            key_gain[...], (32 - query_rows, HD)
        )

    column = iota((1, TILE), 1)
    entries = count * KEEP
    added[...] = jnp.full_like(added, negative)
    extra = [
        jnp.where((column == count + r) & (lane == 0), 0.0, negative) for r in range(R_DEV)
    ]
    weight_columns = weights[...].T
    rows_of = iota((rows, KEEP), 0)
    place = iota((rows, 16), 1)
    copies[9].wait()
    for p in range(count):
        picks = (keep[p : p + 1, :] == rows_of).astype(single)
        dropped = weight_columns[:, p : p + 1] * (1.0 - jnp.sum(picks, axis=1, keepdims=True))
        total = jnp.sum(dropped, axis=0, keepdims=True)
        left = jnp.concatenate([picks, three_terms(dropped, place)], axis=1).astype(bfloat)
        both = lax.dot_general(
            left, pages[p], (((0,), (0,)), ((), ())), preferred_element_type=single
        )
        rows_kept = both[:KEEP].astype(bfloat)
        kept[KEEP * p : KEEP * (p + 1), :] = rows_kept
        slot = dest[0, p]
        start = pl.multiple_of((slot & 1) * KEEP, KEEP)
        compact[slot >> 1, pl.ds(start, KEEP), :] = rows_kept
        mean = both[KEEP : KEEP + 1] + both[KEEP + 1 : KEEP + 2] + both[KEEP + 2 : KEEP + 3]
        mean = mean / total
        plain[p : p + 1, :] = mean
        ordered[pl.ds(slot, 1), :] = mean
        live = jnp.where(keep[p : p + 1, :] >= 0, 0.0, negative)
        for r in range(R_DEV):
            here = owner(r, p)
            added[r : r + 1, KEEP * p : KEEP * (p + 1)] = jnp.where(here, live, negative)
            level = jnp.where(here, jnp.log(total), negative)
            extra[r] = jnp.where(column == p, level, extra[r])
    for r in range(R_DEV):
        added[r : r + 1, entries : entries + TILE] = extra[r]
    plain[count:, :] = jnp.zeros_like(plain[count:, :])
    kept[entries:, :] = plain[...].astype(bfloat)
    summaries[...] = ordered[...].astype(bfloat)

    for copy in copies[10:]:
        copy.wait()
    block = gate.shape[1] // 2
    piece = block // 2
    for k in range(2):
        for b in range(2):
            columns = slice(b * block + k * piece, b * block + (k + 1) * piece)
            start = b * block
            dealt[k, :, start : start + piece] = gate[:, columns].astype(single)
            dealt[k, :, start + piece : start + block] = up[:, columns].astype(single)
    mine[...] = dealt[lane & 1].astype(bfloat)
    theirs[...] = dealt[1 - (lane & 1)].astype(bfloat)
    width = given.shape[1]
    other = pl.multiple_of((1 - (group & 1)) * width, width)
    given[...] = handed[:, pl.ds(other, width)]


def attend_kernel(came, kept, added, tables, sent, x, extra_k, extra_v, out, logs):
    lanes = lax.axis_size("head")
    groups = came.shape[0] // lanes
    width = (HEADS + 2 * KVH) * HD // lanes
    span = -(-KVH * HD // TILE) * TILE
    key_cols = slice(0, span)
    value_cols = slice(KVW - span, KVW)
    first_key = HEADS * HD // TILE * R_DEV
    scale = HD ** (-0.5)
    x[...] = jnp.zeros_like(x)
    column = iota((8, TILE), 1)
    for k in range(lanes):
        tile = came[k].astype(single)
        for g in range(1, groups):
            tile = tile + came[g * lanes + k].astype(single)
        tile = tile.astype(bfloat).astype(single)
        base, shift = divmod(width * k, TILE)
        base = base * R_DEV
        if shift:
            tile = pltpu.roll(tile, shift, 1)
            x[base + 2 : base + 10, :] += jnp.where(column < shift, tile, 0.0)
        x[base : base + 8, :] += jnp.where(column >= shift, tile, 0.0)
    values = x[...]
    same_head = (iota((TILE, TILE), 0) // HD == iota((TILE, TILE), 1) // HD).astype(single)
    squares = jnp.dot(
        values * values, same_head, precision=lax.Precision.HIGHEST, preferred_element_type=single
    )
    normed = values * lax.rsqrt(squares / HD + epsilon) * tables[64:96, :]
    early = iota(values.shape, 1) % HD < HD // 2
    swapped = jnp.where(
        early, pltpu.roll(normed, TILE - HD // 2, 1), pltpu.roll(normed, HD // 2, 1)
    )
    turned = normed * tables[0:32, :] + swapped * tables[32:64, :]
    turned = turned.astype(bfloat).astype(single)

    rows = 24
    row = iota((rows, TILE), 0)
    half = iota((rows, TILE), 1) // HD
    key_head = row >> 2
    query = jnp.where(row < first_key, turned[:rows], 0.0)
    other = pltpu.roll(query, HD, 1)
    queries = []
    for u in range(2):
        placed = jnp.where(
            half == (key_head & 1), jnp.where((key_head & 1) == u, query, other), 0.0
        )
        queries.append(
            jnp.concatenate(
                [jnp.where((key_head >> 1) == c, placed, 0.0) for c in range(span // TILE)], axis=1
            )
        )
    queries = jnp.concatenate(queries, axis=0).astype(bfloat)

    extras = extra_k.shape[0]
    entries = kept.shape[0] - extras
    count = entries // KEEP
    extra_k[...] = kept[entries:, key_cols].astype(single)
    extra_v[...] = kept[entries:, value_cols].astype(single)
    first_value = first_key + KVH * HD // TILE * R_DEV
    for c in range(span // TILE):
        at = slice(c * TILE, (c + 1) * TILE)
        r = first_key + R_DEV * c
        extra_k[count : count + R_DEV, at] = turned[r : r + R_DEV]
        r = first_value + R_DEV * c
        extra_v[count : count + R_DEV, at] = values[r : r + R_DEV]

    def by_request(columns, size):
        odd = (iota((2 * rows, size), 0) & 1) == 1
        return jnp.where(odd, added[1:2, columns], added[0:1, columns])

    scores = dot_rows(queries, kept[:entries, key_cols]) * scale
    scores = scores + by_request(slice(0, entries), entries)
    extra = dot_rows(queries, extra_k[...].astype(bfloat)) * scale
    extra = extra + by_request(slice(entries, entries + extras), extras)
    top = jnp.maximum(
        jnp.max(scores, axis=1, keepdims=True), jnp.max(extra, axis=1, keepdims=True)
    )
    weight = jnp.where(scores > 0.5 * negative, jnp.exp(scores - top), 0.0)
    extra_weight = jnp.where(extra > 0.5 * negative, jnp.exp(extra - top), 0.0)
    mass = jnp.sum(weight, axis=1, keepdims=True) + jnp.sum(extra_weight, axis=1, keepdims=True)

    def weighted(parts, right):
        high = parts.astype(bfloat)
        low = (parts - high.astype(single)).astype(bfloat)
        return jnp.dot(high, right, preferred_element_type=single) + jnp.dot(
            low, right, preferred_element_type=single
        )

    total = weighted(weight, kept[:entries, value_cols]) + weighted(
        extra_weight, extra_v[...].astype(bfloat)
    )
    some = mass > 0.0
    mass = jnp.where(some, mass, 1.0)
    total = total / mass
    level = jnp.where(some, top + jnp.log(mass), negative)

    slot = key_head + (KVW // 2 - (KVW - span)) // HD
    results = []
    for u in range(2):
        mine = total[rows * u : rows * (u + 1)]
        picked = mine[:, :TILE]
        for c in range(1, span // TILE):
            picked = jnp.where((slot >> 1) == c, mine[:, c * TILE : (c + 1) * TILE], picked)
        results.append(jnp.where((slot & 1) == u, picked, pltpu.roll(picked, HD, 1)))
    out[...] = jnp.where(half == 0, results[0], results[1])
    logs[...] = jnp.broadcast_to(level, logs.shape)
    own = HEADS * HD // lanes
    size = 6
    column = iota((size, TILE), 1)
    here = column // TERMS == iota((size, TILE), 0)
    for k in range(lanes):
        r = own * k // TILE * R_DEV
        tile = [out[r : r + size, :]]
        for u in range(2):
            coded = three_terms(logs[rows * u + r : rows * u + r + size, :], column % TERMS)
            tile.append(jnp.sum(jnp.where(here, coded, 0.0), axis=0, keepdims=True))
        tile = jnp.concatenate(tile, axis=0).astype(bfloat)
        for g in range(groups):
            sent[g * lanes + k] = tile


def project_kernel(source_far, came, first, second, sent, source, logs, rows, pieces, done):
    (copy,) = fetch((source_far,), (source,), done)
    lanes = lax.axis_size("head")
    groups = came.shape[0] // lanes
    group = lax.axis_index("req")
    features = first.shape[0]
    requests = rows.shape[0]
    size = 6
    tiles = [came[d].astype(single) for d in range(groups * lanes)]
    for g in range(groups):
        for k in range(lanes):
            logs[k, 2 * g : 2 * g + 2, :] = tiles[g * lanes + k][size:]
    spread = (iota((8, TILE), 1) // TERMS == iota((8, TILE), 0)).astype(single).astype(bfloat)
    levels = [dot_rows(spread, logs[k].astype(bfloat)) for k in range(lanes)]
    top = jnp.maximum(jnp.maximum(levels[0], levels[1]), jnp.maximum(levels[2], levels[3]))
    shares = [jnp.exp(level - top) for level in levels]
    mass = sum(shares)
    shares = [share / mass for share in shares]
    lower = iota((8, TILE), 1) < HD
    for g in range(groups):
        mixed = 0.0
        for k in range(lanes):
            share = shares[k]
            share = jnp.where(lower, share[:, 2 * g : 2 * g + 1], share[:, 2 * g + 1 : 2 * g + 2])
            mixed = mixed + share * tiles[g * lanes + k]
        for j in range(size // R_DEV):
            rows[R_DEV * g : R_DEV * (g + 1), TILE * j : TILE * (j + 1)] = mixed[
                R_DEV * j : R_DEV * (j + 1)
            ]
    width = rows.shape[1]
    shift = lax.rem(lax.axis_index("head") * (2 * features), TILE)
    attention = rows[...].astype(bfloat).astype(single)
    attention = pltpu.roll(attention, lax.rem(width - shift, width), 1)
    copy.wait()
    order = row_order(source, requests, False)
    attention = jnp.dot(order, attention.astype(bfloat), preferred_element_type=single)
    for b in range(2):
        pieces[b] = attention[:, features * b : features * (b + 1)]
    total = 0.0
    width = sent.shape[1]
    here = pl.multiple_of((group & 1) * width, width)
    for turn, weight in enumerate((first[:, pl.ds(here, width)], second[...])):
        piece = pieces[(group & 1) ^ turn].astype(bfloat)
        total = total + jnp.dot(piece, weight, preferred_element_type=single)
    sent[...] = total


def units_kernel(
    gain_far, own, one, two, three, hidden, mine, theirs, sent, mid_out, gain, done
):
    (copy,) = fetch((gain_far,), (gain,), done)
    rows, features = own.shape
    share = sent.shape[0] // lax.axis_size("head")
    group = lax.axis_index("req")
    lane = lax.axis_index("head")
    here = pl.ds(pl.multiple_of(group * features, features), features)
    mid = (own[...] + one[...]) + (two[...] + three[...])
    mid = (hidden[...].astype(single) + mid).astype(bfloat)
    mid_out[...] = mid
    mid = mid.astype(single)
    squares = jnp.sum(mid * mid, axis=1, keepdims=True)
    block = mine.shape[1] // share
    terms = three_terms(squares, iota((rows, sent.shape[2] - block), 1)).astype(bfloat)
    copy.wait()
    inputs = (mid * gain[:, here]).astype(bfloat)
    for turn, weight in enumerate((mine, theirs)):
        units = jnp.dot(inputs, weight[...], preferred_element_type=single).astype(bfloat)
        target = (lane ^ turn) * share
        for b in range(share):
            sent[target + b, :, :block] = units[:, block * b : block * (b + 1)]
            sent[target + b, :, block:] = terms


def active_kernel(came, active):
    total = came[0].astype(single)
    for g in range(1, came.shape[0]):
        total = total + came[g].astype(single)
    piece = active.shape[1]
    squares = jnp.sum(total[:, 2 * piece : 2 * piece + 3], axis=1, keepdims=True)
    factor = lax.rsqrt(squares / D + epsilon)
    gate = total[:, :piece] * factor
    up = total[:, piece : 2 * piece] * factor
    active[...] = (gate / (1.0 + jnp.exp(-gate)) * up).astype(bfloat)


def down_kernel(own, one, two, three, weight, mid, sent, active):
    groups, rows, width = sent.shape
    piece = own.shape[1]
    half = mid.shape[1]
    for turn, values in enumerate((own, one, two, three)):
        active[turn] = values[...]
    share = width // half
    group = lax.axis_index("req")
    lane = lax.axis_index("head")
    first = group // (2 * share) * 2 ^ lane
    down = jnp.dot(active[first], weight[:piece, :], preferred_element_type=single)
    down = down + jnp.dot(active[first ^ 1], weight[piece:, :], preferred_element_type=single)
    residual = mid[...].astype(single)
    for b in range(share):
        columns = slice(half * b, half * (b + 1))
        mine = group == lane * share + b
        total = (down[:, columns] + jnp.where(mine, residual, 0.0)).astype(bfloat)
        for g in range(groups):
            sent[g, :, columns] = total


def result_kernel(came, result):
    total = came[0].astype(single)
    for g in range(1, came.shape[0]):
        total = total + came[g].astype(single)
    result[...] = total.astype(bfloat)


def rotation_table():
    half = HD // 2
    size = -(-(NP + 1) // 8) * 8
    frequency = 10000.0 ** (-np.arange(half) / half)
    angles = PAGE * np.arange(size)[:, None] * frequency[None, :]
    cosine, sine = np.cos(angles), np.sin(angles)
    wide = [np.tile(np.concatenate(pair, axis=1), (1, TILE // HD)) for pair in
            ((cosine, cosine), (-sine, sine))]
    return jnp.asarray(np.concatenate(wide), dtype=single)


def swapped_lanes(value, turn):
    lanes = lax.axis_size("head")
    return lax.ppermute(value, "head", [(k, k ^ turn) for k in range(lanes)])


def from_lanes(value):
    return [value] + [swapped_lanes(value, turn) for turn in range(1, lax.axis_size("head"))]


def transposed(value):
    groups = lax.axis_size("req")
    lanes = lax.axis_size("head")
    pairs = [
        (g * lanes + h, (2 * h + (g & 1)) * lanes + g // 2)
        for g in range(groups)
        for h in range(lanes)
    ]
    return lax.ppermute(value, both_axes, pairs)


def swapped_y(value):
    return lax.ppermute(value, "req", [(g, g ^ 1) for g in range(lax.axis_size("req"))])


def on_device(
    hidden_in,
    attention_gain,
    query_gain,
    key_gain,
    feedforward_gain,
    input_weight,
    output_weight,
    gate_weight,
    up_weight,
    down_weight,
    old_cache,
    keep_rows,
    drop_weights,
    dest_slots,
    lengths,
    page_table,
    source,
):
    groups = lax.axis_size("req")
    lanes = lax.axis_size("head")
    requests = hidden_in.shape[0]
    pages_here = old_cache.shape[0]
    devices = groups * lanes
    features = D // groups
    copies = pltpu.SemaphoreType.DMA

    handed = transposed(output_weight)
    columns = input_weight.shape[1]
    padded = -(-columns // TILE) * TILE
    holds = source[None, :]
    gain = attention_gain[None, :]
    weight = input_weight.T
    far = [holds, gain, weight, hidden_in]
    sent, hidden_block = run(
        first_kernel,
        [
            shaped((devices, R_DEV * padded // TILE, TILE), single),
            shaped((requests, features), bfloat),
        ],
        far,
        from_lanes(hidden_in)[1:],
        [
            *scalar_like(holds),
            *local_like(*far[1:]),
            pltpu.VMEM((lanes,) + hidden_in.shape, single),
            pltpu.VMEM((requests, padded), single),
            copies((len(far),)),
        ],
        2 * requests * features * columns,
    )
    came = lax.all_to_all(sent, both_axes, 0, 0, tiled=True)
    handed, _ = lax.optimization_barrier((handed, sent))
    scalars = [dest_slots, lengths[None, :], holds, page_table]
    arrays = [
        keep_rows,
        drop_weights,
        query_gain[None, :],
        key_gain[None, :],
        rotation_table(),
        old_cache,
        gate_weight,
        up_weight,
    ]
    entries = pages_here * KEEP
    extras = 16
    compact, summaries, kept, added, tables, mine, theirs, given = run(
        prepare_kernel,
        [
            shaped((pages_here // 2, PAGE, KVW), bfloat),
            shaped((pages_here, KVW), bfloat),
            shaped((entries + extras, KVW), bfloat),
            shaped((8, entries + TILE), single),
            shaped((96, TILE), single),
            shaped(gate_weight.shape, bfloat),
            shaped(gate_weight.shape, bfloat),
            shaped((output_weight.shape[0], features), bfloat),
        ],
        scalars + arrays,
        [handed],
        [
            *scalar_like(*scalars),
            *local_like(*arrays),
            pltpu.VMEM((pages_here, KVW), single),
            pltpu.VMEM((extras, KVW), single),
            pltpu.VMEM((2,) + gate_weight.shape, single),
            copies((len(scalars + arrays),)),
        ],
        2 * pages_here * TILE * PAGE * KVW,
    )
    theirs = swapped_lanes(theirs, 1)
    came, theirs = lax.optimization_barrier((came, theirs))
    span = -(-KVH * HD // TILE) * TILE
    (parts,) = run(
        attend_kernel,
        [shaped((devices, 8, TILE), bfloat)],
        [],
        [came, kept, added, tables],
        [
            pltpu.VMEM((32, TILE), single),
            pltpu.VMEM((extras, span), single),
            pltpu.VMEM((extras, span), single),
            pltpu.VMEM((24, TILE), single),
            pltpu.VMEM((48, TILE), single),
        ],
        6 * 48 * entries * span,
    )
    given, _ = lax.optimization_barrier((given, parts))
    given = swapped_y(given)
    came = lax.all_to_all(parts, both_axes, 0, 0, tiled=True)
    (sent,) = run(
        project_kernel,
        [shaped((requests, features), single)],
        [holds],
        [came, handed, given],
        [
            *scalar_like(holds),
            pltpu.VMEM((lanes, 2 * groups, TILE), single),
            pltpu.VMEM((requests, 3 * TILE), single),
            pltpu.VMEM((2, requests, output_weight.shape[0]), single),
            copies((1,)),
        ],
        2 * requests * output_weight.size,
    )
    gain = feedforward_gain[None, :]
    block = gate_weight.shape[1] // 2
    sent, mid = run(
        units_kernel,
        [
            shaped((groups, requests, block + TILE), bfloat),
            shaped((requests, features), bfloat),
        ],
        [gain],
        [*from_lanes(sent), hidden_block, mine, theirs],
        [*local_like(gain), copies((1,))],
        4 * requests * gate_weight.size,
    )
    (active,) = run(
        active_kernel, [shaped((requests, block // 2), bfloat)], [], [exchange(sent)]
    )
    (sent,) = run(
        down_kernel,
        [shaped((groups, requests, down_weight.shape[1]), bfloat)],
        [],
        [*from_lanes(active), down_weight, mid],
        [pltpu.VMEM((lanes,) + active.shape, bfloat)],
        2 * requests * down_weight.size,
    )
    (result,) = run(
        result_kernel, [shaped((requests, down_weight.shape[1]), bfloat)], [], [exchange(sent)]
    )
    return (compact, summaries, result)


def solution(mesh):
    placed = (
        P(None, "head"),
        P(),
        P(),
        P(),
        P(),
        P("req", "head"),
        P("req", "head"),
        P("req", "head"),
        P("req", "head"),
        P("req", "head"),
        P(("req", "head"), None, None),
        P(("req", "head"), None),
        P(("req", "head"), None),
        P(("req", "head"), None),
        P(),
        P("req", None),
        P(),
    )
    return jax.shard_map(
        on_device if mesh.shape["req"] <= DIRECT else on_device_wide,
        mesh=mesh,
        in_specs=placed,
        out_specs=(P(("req", "head"), None, None), P(("req", "head"), None), P(None, "head")),
        check_vma=False,
    )
```

```python
import jax
import jax.numpy as jnp
import numpy as np
from jax import lax
from jax.experimental import pallas as pl
from jax.experimental.pallas import tpu as pltpu
from jax.sharding import PartitionSpec as P

D = 2048
HEADS = 20
KVH = 5
HD = 64
FF = 5120
PAGE = 128
KEEP = 64
NP = 16
R_DEV = 2
KVW = 640

DIRECT = 8

epsilon = 1e-06
negative = -1e30
both_axes = ("req", "head")


def rms_scale(values):
    return lax.rsqrt(jnp.mean(values * values, axis=-1, keepdims=True) + epsilon)


def rms_rows(values, gain):
    return values * rms_scale(values) * gain


def rotate(vectors, positions):
    half = vectors.shape[-1] // 2
    frequency = 10000.0 ** (-jnp.arange(half, dtype=jnp.float32) / half)
    angles = positions.astype(jnp.float32)[:, None] * frequency[None, :]
    cosine = jnp.cos(angles)[:, None, :]
    sine = jnp.sin(angles)[:, None, :]
    first = vectors[..., :half]
    second = vectors[..., half:]
    return jnp.concatenate(
        [first * cosine - second * sine, second * cosine + first * sine], axis=-1
    )


def compact_pages(pages, keep, weights):
    rows = jnp.arange(pages.shape[1], dtype=jnp.int32)
    picks = keep[:, :, None] == rows[None, None, :]
    kept = jnp.einsum(
        "pkr,prc->pkc", picks.astype(jnp.bfloat16), pages, preferred_element_type=jnp.float32
    ).astype(jnp.bfloat16)
    dropped = weights * (1.0 - jnp.sum(picks.astype(jnp.float32), axis=1))
    total = jnp.sum(dropped, axis=1)
    means = (
        jnp.einsum(
            "pr,prc->pc", dropped, pages.astype(jnp.float32), precision=lax.Precision.HIGHEST
        )
        / total[:, None]
    )
    return (kept, means.astype(jnp.bfloat16), jnp.log(total))


def held_request(rows, source):
    half = R_DEV // 2
    position = rows % R_DEV
    slot = rows // R_DEV * half + position - half
    continued = jnp.arange(source.shape[0], dtype=jnp.int32)
    matches = source[None, :] == slot[:, None]
    owner_cont = jnp.sum(jnp.where(matches, continued[None, :], 0), axis=1)
    carried = owner_cont // half * R_DEV + half + owner_cont % half
    return jnp.where(position < half, rows, carried)


def pick_rows(order, rows):
    chosen = order[:, None] == jnp.arange(rows.shape[0], dtype=jnp.int32)[None, :]
    return jnp.dot(
        chosen.astype(jnp.bfloat16), rows, preferred_element_type=jnp.float32
    ).astype(jnp.bfloat16)


def exchange(parts):
    return lax.all_to_all(parts, "req", split_axis=0, concat_axis=0, tiled=True)


def to_block_owner(rows):
    groups = lax.axis_size("req")
    lanes = lax.axis_size("head")
    per_lane = groups // lanes
    pairs = [
        (g * lanes + h, (per_lane * h + g // lanes) * lanes + g % lanes)
        for g in range(groups)
        for h in range(lanes)
    ]
    return lax.ppermute(rows, both_axes, pairs)


def whole_sum(partial):
    if lax.axis_size("req") > DIRECT:
        return lax.psum(partial, "req")
    groups = lax.axis_size("req")
    return jnp.sum(exchange(jnp.broadcast_to(partial[None], (groups,) + partial.shape)), axis=0)


def on_device_wide(
    hidden_in,
    attention_gain,
    query_gain,
    key_gain,
    feedforward_gain,
    input_weight,
    output_weight,
    gate_weight,
    up_weight,
    down_weight,
    old_cache,
    keep_rows,
    drop_weights,
    dest_slots,
    lengths,
    page_table,
    source,
):
    groups = lax.axis_size("req")
    lanes = lax.axis_size("head")
    group = lax.axis_index("req")
    lane = lax.axis_index("head")
    requests = hidden_in.shape[0]
    half = R_DEV // 2
    split = KVH * HD
    ratio = HEADS // KVH
    scale = HD ** (-0.5)
    pages_here = old_cache.shape[0]
    everyone = jnp.arange(requests, dtype=jnp.int32)
    holders = held_request(everyone, source)
    held = lax.dynamic_slice_in_dim(holders, group * R_DEV, R_DEV, 0)
    held_len = lengths[held]
    positions = held_len * PAGE

    whole = lax.all_gather(hidden_in, "head", axis=1, tiled=True)
    normed = rms_rows(whole.astype(jnp.float32), attention_gain).astype(jnp.bfloat16)
    features = D // groups
    inputs = pick_rows(holders, lax.dynamic_slice_in_dim(normed, group * features, features, 1))
    partial_qkv = jnp.dot(inputs, input_weight, preferred_element_type=jnp.float32)
    sent = jnp.broadcast_to(
        partial_qkv.reshape(groups, 1, R_DEV, -1), (groups, lanes, R_DEV, partial_qkv.shape[1])
    ).reshape(groups * lanes, R_DEV, -1)
    got = lax.all_to_all(sent, both_axes, split_axis=0, concat_axis=0, tiled=True)
    mixed = jnp.sum(got.reshape(groups, lanes, R_DEV, -1), axis=0).astype(jnp.bfloat16)
    held_qkv = jnp.swapaxes(mixed, 0, 1).reshape(R_DEV, -1).astype(jnp.float32)

    query = rotate(
        rms_rows(held_qkv[:, : HEADS * HD].reshape(R_DEV, HEADS, HD), query_gain), positions
    ).astype(jnp.bfloat16)
    key_new = rotate(
        rms_rows(held_qkv[:, HEADS * HD : (HEADS + KVH) * HD].reshape(R_DEV, KVH, HD), key_gain),
        positions,
    ).astype(jnp.bfloat16)
    value_new = held_qkv[:, (HEADS + KVH) * HD :].reshape(R_DEV, KVH, HD)
    kept, means, bias = compact_pages(old_cache, keep_rows, drop_weights)
    destination = dest_slots[0]
    fresh_ids = jnp.arange(pages_here, dtype=jnp.int32)
    inverse = jnp.sum(
        jnp.where(destination[None, :] == fresh_ids[:, None], fresh_ids[None, :], 0), axis=1
    )
    compact = kept[inverse].reshape(pages_here // 2, PAGE, KVW)
    summaries = means[inverse]
    per_lane = NP // lanes
    table = page_table.reshape(R_DEV, per_lane, lanes)
    mine = lax.dynamic_slice_in_dim(table, lane, 1, 2)[:, :, 0]
    logical = jnp.arange(per_lane, dtype=jnp.int32) * lanes + lane
    live = logical[None, :] < held_len[:, None]
    owner = jnp.any((mine[:, :, None] == fresh_ids[None, None, :]) & live[:, :, None], axis=1)
    query_groups = query.reshape(R_DEV, KVH, ratio, HD)
    row_keys = kept[:, :, :split].reshape(pages_here, KEEP, KVH, HD)
    row_values = kept[:, :, split:].reshape(pages_here, KEEP, KVH, HD)
    row_live = keep_rows >= 0
    allowed = owner[:, None, None, :, None] & row_live[None, None, None, :, :]
    scores = (
        jnp.einsum("rngd,pmnd->rngpm", query_groups, row_keys, preferred_element_type=jnp.float32)
        * scale
    )
    scores = jnp.where(allowed, scores, negative)
    mean_keys = means[:, :split].reshape(pages_here, KVH, HD)
    mean_values = means[:, split:].reshape(pages_here, KVH, HD)
    mean_scores = (
        jnp.einsum("rngd,pnd->rngp", query_groups, mean_keys, preferred_element_type=jnp.float32)
        * scale
        + bias[None, None, None, :]
    )
    mean_allowed = owner[:, None, None, :]
    mean_scores = jnp.where(mean_allowed, mean_scores, negative)
    own_score = (
        jnp.einsum("rngd,rnd->rng", query_groups, key_new, preferred_element_type=jnp.float32)
        * scale
    )
    own_score = jnp.where(lane == 0, own_score, negative)
    top = jnp.maximum(jnp.max(scores, axis=(3, 4)), jnp.max(mean_scores, axis=3))
    top = jnp.maximum(top, own_score)
    row_weight = jnp.where(allowed, jnp.exp(scores - top[..., None, None]), 0.0)
    mean_weight = jnp.where(mean_allowed, jnp.exp(mean_scores - top[..., None]), 0.0)
    own_weight = jnp.where(lane == 0, jnp.exp(own_score - top), 0.0)
    mass = jnp.sum(row_weight, axis=(3, 4)) + jnp.sum(mean_weight, axis=3) + own_weight
    total = jnp.einsum(
        "rngpm,pmnd->rngd",
        row_weight,
        row_values.astype(jnp.float32),
        precision=lax.Precision.HIGHEST,
    )
    total = total + jnp.einsum(
        "rngp,pnd->rngd",
        mean_weight,
        mean_values.astype(jnp.float32),
        precision=lax.Precision.HIGHEST,
    )
    total = total + own_weight[..., None] * value_new[:, :, None, :]

    some = mass > 0.0
    level = jnp.where(some, top + jnp.log(jnp.where(some, mass, 1.0)), negative)
    means_out = total / jnp.where(some, mass, 1.0)[..., None]
    own = HEADS * HD // groups
    parts = jnp.stack([means_out, jnp.broadcast_to(level[..., None], total.shape)])
    parts = jnp.transpose(parts.reshape(2, R_DEV, groups, own), (2, 1, 0, 3))
    parts = jnp.broadcast_to(
        parts.reshape(groups, 1, R_DEV, 2 * own), (groups, lanes, R_DEV, 2 * own)
    ).reshape(groups * lanes, R_DEV, 2 * own)
    came = lax.all_to_all(parts, both_axes, 0, 0, tiled=True)
    came = came.reshape(groups, lanes, R_DEV, 2 * own)
    outs, levels = came[..., :own], came[..., own:]
    weights = jnp.exp(levels - jnp.max(levels, axis=1, keepdims=True))
    attention = jnp.sum(outs * weights, axis=1) / jnp.sum(weights, axis=1)
    attention = attention.reshape(requests, own).astype(jnp.bfloat16)
    back = jnp.sum(
        jnp.where(holders[None, :] == everyone[:, None], everyone[None, :], 0), axis=1
    )
    projected = jnp.dot(
        pick_rows(back, attention), output_weight, preferred_element_type=jnp.float32
    )
    projected = projected + jnp.where(group == 0, hidden_in.astype(jnp.float32), 0.0)

    share = groups // lanes
    blocks = jnp.moveaxis(projected.reshape(requests, share, 1, features), 0, 2)
    blocks = jnp.broadcast_to(blocks, (share, lanes, requests, features))
    mid = jnp.sum(exchange(blocks.reshape(groups, requests, features)), axis=0)
    mid = to_block_owner(mid.astype(jnp.bfloat16)).astype(jnp.float32)
    squares = jnp.sum(mid * mid, axis=1, keepdims=True)
    gain_here = lax.dynamic_slice_in_dim(feedforward_gain, group * features, features, 0)
    inputs_mid = (mid * gain_here).astype(jnp.bfloat16)
    local_units = gate_weight.shape[1]
    piece = local_units // groups
    gates = jnp.dot(inputs_mid, gate_weight, preferred_element_type=jnp.float32)
    ups = jnp.dot(inputs_mid, up_weight, preferred_element_type=jnp.float32)
    both = jnp.concatenate(
        [
            gates.reshape(requests, groups, piece),
            ups.reshape(requests, groups, piece),
            jnp.broadcast_to(squares[:, :, None], (requests, groups, 1)),
        ],
        axis=2,
    )
    sums = jnp.sum(exchange(jnp.swapaxes(both, 0, 1)), axis=0)
    factor = lax.rsqrt(sums[:, 2 * piece :] / D + epsilon)
    gate = sums[:, :piece] * factor
    active = (jax.nn.silu(gate) * (sums[:, piece : 2 * piece] * factor)).astype(jnp.bfloat16)
    active_here = lax.all_gather(to_block_owner(active), "head", axis=1, tiled=True)
    down = jnp.dot(active_here, down_weight, preferred_element_type=jnp.float32)
    residual = [jnp.where(group == lane * share + k, mid, 0.0) for k in range(share)]
    down = down + jnp.concatenate(residual, axis=1)
    result = whole_sum(down).astype(jnp.bfloat16)
    return (compact, summaries, result)


TILE = 128
bfloat = jnp.bfloat16
single = jnp.float32


TERMS = 4


def three_terms(value, place):
    high = value.astype(bfloat).astype(single)
    rest = value - high
    middle = rest.astype(bfloat).astype(single)
    low = jnp.where(place == 2, rest - middle, 0.0)
    return jnp.where(place == 0, high, jnp.where(place == 1, middle, low))


def iota(shape, axis):
    return lax.broadcasted_iota(jnp.int32, shape, axis)


def run(kernel, outs, far, near, scratch=(), flops=0):
    in_specs = [pl.BlockSpec(memory_space=pltpu.HBM) for _ in far]
    in_specs += [pl.BlockSpec(memory_space=pltpu.VMEM) for _ in near]
    moved = sum(a.size * a.dtype.itemsize for a in [*far, *near, *outs])
    return pl.pallas_call(
        kernel,
        out_shape=list(outs),
        in_specs=in_specs,
        out_specs=[pl.BlockSpec(memory_space=pltpu.VMEM) for _ in outs],
        scratch_shapes=list(scratch),
        compiler_params=pltpu.CompilerParams(vmem_limit_bytes=16 * 2**20),
        cost_estimate=pl.CostEstimate(flops=flops, bytes_accessed=moved, transcendentals=0),
    )(*[pltpu.with_memory_space_constraint(a, pltpu.HBM) for a in far], *near)


def fetch(sources, targets, done):
    copies = [
        pltpu.make_async_copy(source, target, done.at[k])
        for k, (source, target) in enumerate(zip(sources, targets))
    ]
    for copy in copies:
        copy.start()
    return copies


def local_like(*arrays):
    return [pltpu.VMEM(a.shape, a.dtype) for a in arrays]


def scalar_like(*arrays):
    return [pltpu.SMEM(a.shape, a.dtype) for a in arrays]


def row_order(source, count, to_holder):
    first, second = iota((count, count), 0), iota((count, count), 1)
    if not to_holder:
        first, second = second, first
    order = (first == second) & (first % R_DEV == 0)
    for c in range(source.shape[1]):
        order = order | ((first == source[0, c] * R_DEV + 1) & (second == c * R_DEV + 1))
    return order.astype(single).astype(bfloat)


def shaped(shape, dtype):
    return jax.ShapeDtypeStruct(shape, dtype)


def first_kernel(
    source_far, gain_far, weight_far, hidden_far, one, two, three, sent, block, source, gain,
    weight, hidden, lanes_of, wide, done
):
    copies = fetch(
        (source_far, gain_far, weight_far, hidden_far), (source, gain, weight, hidden), done
    )
    rows = hidden.shape[0]
    groups = rows // R_DEV
    lanes = sent.shape[0] // groups
    columns, features = weight.shape
    group = lax.axis_index("req")
    share = groups // lanes
    squares = 0.0
    for turn, values in enumerate((one, two, three)):
        values = values[...].astype(single)
        lanes_of[turn + 1] = values
        squares = squares + jnp.sum(values * values, axis=1, keepdims=True)
    copies[3].wait()
    values = hidden[...].astype(single)
    lanes_of[0] = values
    squares = squares + jnp.sum(values * values, axis=1, keepdims=True)
    factor = lax.rsqrt(squares / D + epsilon)
    here = pl.ds(pl.multiple_of(group * features, features), features)
    within = pl.ds(pl.multiple_of(group % share * features, features), features)
    mine = lanes_of[group // share ^ lax.axis_index("head"), :, within]
    block[...] = mine.astype(bfloat)
    wide[...] = jnp.zeros_like(wide)
    for copy in copies[:3]:
        copy.wait()
    normed = (mine * factor * gain[:, here]).astype(bfloat)
    order = row_order(source, rows, True)
    normed = jnp.dot(order, normed, preferred_element_type=single).astype(bfloat)
    wide[:, :columns] = dot_rows(normed, weight[...])
    for g in range(groups):
        tile = jnp.concatenate(
            [
                wide[R_DEV * g : R_DEV * (g + 1), TILE * j : TILE * (j + 1)]
                for j in range(wide.shape[1] // TILE)
            ],
            axis=0,
        )
        for k in range(lanes):
            sent[g * lanes + k] = tile


def dot_rows(left, right):
    return lax.dot_general(left, right, (((1,), (1,)), ((), ())), preferred_element_type=single)


def prepare_kernel(*refs):
    far, refs = refs[:12], refs[12:]
    (compact, summaries, kept, added, tables, mine, theirs), refs = refs[:7], refs[7:]
    near, (ordered, plain, done) = refs[:12], refs[12:]
    count = far[9].shape[0]
    sources = [*far[:9], *[far[9].at[p] for p in range(count)], *far[10:]]
    targets = [*near[:9], *[near[9].at[p] for p in range(count)], *near[10:]]
    copies = fetch(sources, targets, done)
    (dest, lengths, source, table, keep, weights, query_gain, key_gain, turns) = near[:9]
    pages, gate, up = near[9:]
    group = lax.axis_index("req")
    lane = lax.axis_index("head")
    lanes = lax.axis_size("head")
    for copy in copies[:9]:
        copy.wait()

    carried = 0
    for c in range(source.shape[1]):
        carried = carried + jnp.where(source[0, c] == group, c, 0)
    held_len = (lengths[0, group * R_DEV], lengths[0, carried * R_DEV + 1])
    rows = pages.shape[1]
    owned = []
    for r in range(R_DEV):
        slots = []
        for i in range(table.shape[1] // lanes):
            j = i * lanes + lane
            slots.append(jnp.where(j < held_len[r], table[r, j], -1))
        owned.append(slots)

    def owner(r, p):
        found = owned[r][0] == p
        for slot in owned[r][1:]:
            found = found | (slot == p)
        return found

    row = iota((32, TILE), 0)
    odd = (row & 1) == 1
    half_rows = turns.shape[0] // 2
    for part in range(2):
        pair = [turns[pl.ds(part * half_rows + held_len[r], 1), :] for r in range(R_DEV)]
        tables[32 * part : 32 * (part + 1), :] = jnp.where(odd, pair[1], pair[0])
    query_rows = HEADS * HD // TILE * R_DEV
    for c in range(TILE // HD):
        columns = slice(HD * c, HD * (c + 1))
        tables[64 : 64 + query_rows, columns] = jnp.broadcast_to(
            query_gain[...], (query_rows, HD)
        )
        tables[64 + query_rows : 96, columns] = jnp.broadcast_to(
            key_gain[...], (32 - query_rows, HD)
        )

    column = iota((1, TILE), 1)
    entries = count * KEEP
    added[...] = jnp.full_like(added, negative)
    extra = [
        jnp.where((column == count + r) & (lane == 0), 0.0, negative) for r in range(R_DEV)
    ]
    weight_columns = weights[...].T
    rows_of = iota((rows, KEEP), 0)
    place = iota((rows, 16), 1)
    for p in range(count):
        copies[9 + p].wait()
        picks = (keep[p : p + 1, :] == rows_of).astype(single)
        dropped = weight_columns[:, p : p + 1] * (1.0 - jnp.sum(picks, axis=1, keepdims=True))
        total = jnp.sum(dropped, axis=0, keepdims=True)
        left = jnp.concatenate([picks, three_terms(dropped, place)], axis=1).astype(bfloat)
        both = lax.dot_general(
            left, pages[p], (((0,), (0,)), ((), ())), preferred_element_type=single
        )
        rows_kept = both[:KEEP].astype(bfloat)
        kept[KEEP * p : KEEP * (p + 1), :] = rows_kept
        slot = dest[0, p]
        start = pl.multiple_of((slot & 1) * KEEP, KEEP)
        compact[slot >> 1, pl.ds(start, KEEP), :] = rows_kept
        mean = both[KEEP : KEEP + 1] + both[KEEP + 1 : KEEP + 2] + both[KEEP + 2 : KEEP + 3]
        mean = mean / total
        plain[p : p + 1, :] = mean
        ordered[pl.ds(slot, 1), :] = mean
        live = jnp.where(keep[p : p + 1, :] >= 0, 0.0, negative)
        for r in range(R_DEV):
            here = owner(r, p)
            added[r : r + 1, KEEP * p : KEEP * (p + 1)] = jnp.where(here, live, negative)
            level = jnp.where(here, jnp.log(total), negative)
            extra[r] = jnp.where(column == p, level, extra[r])
    for r in range(R_DEV):
        added[r : r + 1, entries : entries + TILE] = extra[r]
    plain[count:, :] = jnp.zeros_like(plain[count:, :])
    kept[entries:, :] = plain[...].astype(bfloat)
    summaries[...] = ordered[...].astype(bfloat)

    for copy in copies[9 + count :]:
        copy.wait()
    block = gate.shape[1] // 2
    piece = block // 2

    def deal(target, k):
        for b in range(2):
            columns = slice(b * block + k * piece, b * block + (k + 1) * piece)
            parts = [gate[:, columns].astype(single), up[:, columns].astype(single)]
            target[:, b * block : (b + 1) * block] = jnp.concatenate(parts, axis=1).astype(bfloat)

    for core in range(2):

        @pl.when((lane & 1) == core)
        def _():
            deal(mine, core)
            deal(theirs, 1 - core)


def attend_kernel(came, kept, added, tables, sent, x, extra_k, extra_v, out, logs):
    lanes = lax.axis_size("head")
    groups = came.shape[0] // lanes
    width = (HEADS + 2 * KVH) * HD // lanes
    span = -(-KVH * HD // TILE) * TILE
    key_cols = slice(0, span)
    value_cols = slice(KVW - span, KVW)
    first_key = HEADS * HD // TILE * R_DEV
    scale = HD ** (-0.5)
    x[...] = jnp.zeros_like(x)
    column = iota((8, TILE), 1)
    for k in range(lanes):
        tile = came[k].astype(single)
        for g in range(1, groups):
            tile = tile + came[g * lanes + k].astype(single)
        tile = tile.astype(bfloat).astype(single)
        base, shift = divmod(width * k, TILE)
        base = base * R_DEV
        if shift:
            tile = pltpu.roll(tile, shift, 1)
            x[base + 2 : base + 10, :] += jnp.where(column < shift, tile, 0.0)
        x[base : base + 8, :] += jnp.where(column >= shift, tile, 0.0)
    values = x[...]
    same_head = (iota((TILE, TILE), 0) // HD == iota((TILE, TILE), 1) // HD).astype(single)
    squares = jnp.dot(
        values * values, same_head, precision=lax.Precision.HIGHEST, preferred_element_type=single
    )
    normed = values * lax.rsqrt(squares / HD + epsilon) * tables[64:96, :]
    early = iota(values.shape, 1) % HD < HD // 2
    swapped = jnp.where(
        early, pltpu.roll(normed, TILE - HD // 2, 1), pltpu.roll(normed, HD // 2, 1)
    )
    turned = normed * tables[0:32, :] + swapped * tables[32:64, :]
    turned = turned.astype(bfloat).astype(single)

    rows = 24
    row = iota((rows, TILE), 0)
    half = iota((rows, TILE), 1) // HD
    key_head = row >> 2
    query = jnp.where(row < first_key, turned[:rows], 0.0)
    other = pltpu.roll(query, HD, 1)
    queries = []
    for u in range(2):
        placed = jnp.where(
            half == (key_head & 1), jnp.where((key_head & 1) == u, query, other), 0.0
        )
        queries.append(
            jnp.concatenate(
                [jnp.where((key_head >> 1) == c, placed, 0.0) for c in range(span // TILE)], axis=1
            )
        )
    queries = jnp.concatenate(queries, axis=0).astype(bfloat)

    extras = extra_k.shape[0]
    entries = kept.shape[0] - extras
    count = entries // KEEP
    extra_k[...] = kept[entries:, key_cols].astype(single)
    extra_v[...] = kept[entries:, value_cols].astype(single)
    first_value = first_key + KVH * HD // TILE * R_DEV
    for c in range(span // TILE):
        at = slice(c * TILE, (c + 1) * TILE)
        r = first_key + R_DEV * c
        extra_k[count : count + R_DEV, at] = turned[r : r + R_DEV]
        r = first_value + R_DEV * c
        extra_v[count : count + R_DEV, at] = values[r : r + R_DEV]

    def by_request(columns, size):
        odd = (iota((2 * rows, size), 0) & 1) == 1
        return jnp.where(odd, added[1:2, columns], added[0:1, columns])

    scores = dot_rows(queries, kept[:entries, key_cols]) * scale
    scores = scores + by_request(slice(0, entries), entries)
    extra = dot_rows(queries, extra_k[...].astype(bfloat)) * scale
    extra = extra + by_request(slice(entries, entries + extras), extras)
    top = jnp.maximum(
        jnp.max(scores, axis=1, keepdims=True), jnp.max(extra, axis=1, keepdims=True)
    )
    weight = jnp.where(scores > 0.5 * negative, jnp.exp(scores - top), 0.0)
    extra_weight = jnp.where(extra > 0.5 * negative, jnp.exp(extra - top), 0.0)
    mass = jnp.sum(weight, axis=1, keepdims=True) + jnp.sum(extra_weight, axis=1, keepdims=True)

    def weighted(parts, right):
        high = parts.astype(bfloat)
        low = (parts - high.astype(single)).astype(bfloat)
        return jnp.dot(high, right, preferred_element_type=single) + jnp.dot(
            low, right, preferred_element_type=single
        )

    total = weighted(weight, kept[:entries, value_cols]) + weighted(
        extra_weight, extra_v[...].astype(bfloat)
    )
    some = mass > 0.0
    mass = jnp.where(some, mass, 1.0)
    total = total / mass
    level = jnp.where(some, top + jnp.log(mass), negative)

    slot = key_head + (KVW // 2 - (KVW - span)) // HD
    results = []
    for u in range(2):
        mine = total[rows * u : rows * (u + 1)]
        picked = mine[:, :TILE]
        for c in range(1, span // TILE):
            picked = jnp.where((slot >> 1) == c, mine[:, c * TILE : (c + 1) * TILE], picked)
        results.append(jnp.where((slot & 1) == u, picked, pltpu.roll(picked, HD, 1)))
    out[...] = jnp.where(half == 0, results[0], results[1])
    logs[...] = jnp.broadcast_to(level, logs.shape)
    own = HEADS * HD // lanes
    size = 6
    column = iota((size, TILE), 1)
    here = column // TERMS == iota((size, TILE), 0)
    for k in range(lanes):
        r = own * k // TILE * R_DEV
        tile = [out[r : r + size, :]]
        for u in range(2):
            coded = three_terms(logs[rows * u + r : rows * u + r + size, :], column % TERMS)
            tile.append(jnp.sum(jnp.where(here, coded, 0.0), axis=0, keepdims=True))
        tile = jnp.concatenate(tile, axis=0).astype(bfloat)
        for g in range(groups):
            sent[g * lanes + k] = tile


def blocks_kernel(weight_far, same, other, done):
    width = same.shape[1]
    group = lax.axis_index("req")
    starts = [pl.multiple_of(((group & 1) ^ turn) * width, width) for turn in range(2)]
    parts = [weight_far.at[:, pl.ds(start, width)] for start in starts]
    for copy in fetch(parts, (same, other), done):
        copy.wait()


def project_kernel(source_far, came, first, second, sent, source, logs, rows, pieces, done):
    (copy,) = fetch((source_far,), (source,), done)
    lanes = lax.axis_size("head")
    groups = came.shape[0] // lanes
    group = lax.axis_index("req")
    features = first.shape[0]
    requests = rows.shape[0]
    size = 6
    tiles = [came[d].astype(single) for d in range(groups * lanes)]
    for g in range(groups):
        for k in range(lanes):
            logs[k, 2 * g : 2 * g + 2, :] = tiles[g * lanes + k][size:]
    spread = (iota((8, TILE), 1) // TERMS == iota((8, TILE), 0)).astype(single).astype(bfloat)
    levels = [dot_rows(spread, logs[k].astype(bfloat)) for k in range(lanes)]
    top = jnp.maximum(jnp.maximum(levels[0], levels[1]), jnp.maximum(levels[2], levels[3]))
    shares = [jnp.exp(level - top) for level in levels]
    mass = sum(shares)
    shares = [share / mass for share in shares]
    lower = iota((8, TILE), 1) < HD
    for g in range(groups):
        mixed = 0.0
        for k in range(lanes):
            share = shares[k]
            share = jnp.where(lower, share[:, 2 * g : 2 * g + 1], share[:, 2 * g + 1 : 2 * g + 2])
            mixed = mixed + share * tiles[g * lanes + k]
        for j in range(size // R_DEV):
            rows[R_DEV * g : R_DEV * (g + 1), TILE * j : TILE * (j + 1)] = mixed[
                R_DEV * j : R_DEV * (j + 1)
            ]
    width = rows.shape[1]
    shift = lax.rem(lax.axis_index("head") * (2 * features), TILE)
    attention = rows[...].astype(bfloat).astype(single)
    attention = pltpu.roll(attention, lax.rem(width - shift, width), 1)
    copy.wait()
    order = row_order(source, requests, False)
    attention = jnp.dot(order, attention.astype(bfloat), preferred_element_type=single)
    for b in range(2):
        pieces[b] = attention[:, features * b : features * (b + 1)]
    total = 0.0
    for turn, weight in enumerate((first, second)):
        piece = pieces[(group & 1) ^ turn].astype(bfloat)
        total = total + jnp.dot(piece, weight[...], preferred_element_type=single)
    sent[...] = total


def units_kernel(
    gain_far, own, one, two, three, hidden, mine, theirs, sent, mid_out, gain, done
):
    (copy,) = fetch((gain_far,), (gain,), done)
    rows, features = own.shape
    share = sent.shape[0] // lax.axis_size("head")
    group = lax.axis_index("req")
    lane = lax.axis_index("head")
    here = pl.ds(pl.multiple_of(group * features, features), features)
    mid = (own[...] + one[...]) + (two[...] + three[...])
    mid = (hidden[...].astype(single) + mid).astype(bfloat)
    mid_out[...] = mid
    mid = mid.astype(single)
    squares = jnp.sum(mid * mid, axis=1, keepdims=True)
    block = mine.shape[1] // share
    terms = three_terms(squares, iota((rows, sent.shape[2] - block), 1)).astype(bfloat)
    copy.wait()
    inputs = (mid * gain[:, here]).astype(bfloat)
    for turn, weight in enumerate((mine, theirs)):
        units = jnp.dot(inputs, weight[...], preferred_element_type=single).astype(bfloat)
        target = (lane ^ turn) * share
        for b in range(share):
            sent[target + b, :, :block] = units[:, block * b : block * (b + 1)]
            sent[target + b, :, block:] = terms


def active_kernel(came, active):
    total = came[0].astype(single)
    for g in range(1, came.shape[0]):
        total = total + came[g].astype(single)
    piece = active.shape[1]
    squares = jnp.sum(total[:, 2 * piece : 2 * piece + 3], axis=1, keepdims=True)
    factor = lax.rsqrt(squares / D + epsilon)
    gate = total[:, :piece] * factor
    up = total[:, piece : 2 * piece] * factor
    active[...] = (gate / (1.0 + jnp.exp(-gate)) * up).astype(bfloat)


def down_kernel(own, one, two, three, weight, mid, sent, active):
    groups, rows, width = sent.shape
    piece = own.shape[1]
    half = mid.shape[1]
    for turn, values in enumerate((own, one, two, three)):
        active[turn] = values[...]
    share = width // half
    group = lax.axis_index("req")
    lane = lax.axis_index("head")
    first = group // (2 * share) * 2 ^ lane
    down = jnp.dot(active[first], weight[:piece, :], preferred_element_type=single)
    down = down + jnp.dot(active[first ^ 1], weight[piece:, :], preferred_element_type=single)
    residual = mid[...].astype(single)
    for b in range(share):
        columns = slice(half * b, half * (b + 1))
        mine = group == lane * share + b
        total = (down[:, columns] + jnp.where(mine, residual, 0.0)).astype(bfloat)
        for g in range(groups):
            sent[g, :, columns] = total


def result_kernel(came, result):
    total = came[0].astype(single)
    for g in range(1, came.shape[0]):
        total = total + came[g].astype(single)
    result[...] = total.astype(bfloat)


def rotation_table():
    half = HD // 2
    size = -(-(NP + 1) // 8) * 8
    frequency = 10000.0 ** (-np.arange(half) / half)
    angles = PAGE * np.arange(size)[:, None] * frequency[None, :]
    cosine, sine = np.cos(angles), np.sin(angles)
    wide = [np.tile(np.concatenate(pair, axis=1), (1, TILE // HD)) for pair in
            ((cosine, cosine), (-sine, sine))]
    return jnp.asarray(np.concatenate(wide), dtype=single)


def swapped_lanes(value, turn):
    lanes = lax.axis_size("head")
    return lax.ppermute(value, "head", [(k, k ^ turn) for k in range(lanes)])


def from_lanes(value):
    return [value] + [swapped_lanes(value, turn) for turn in range(1, lax.axis_size("head"))]


def handed_over(value, turn):
    groups = lax.axis_size("req")
    lanes = lax.axis_size("head")
    share = groups // lanes
    pairs = [
        (g * lanes + h, (share * h + ((g & 1) ^ turn)) * lanes + g // share)
        for g in range(groups)
        for h in range(lanes)
    ]
    return lax.ppermute(value, both_axes, pairs)


def on_device(
    hidden_in,
    attention_gain,
    query_gain,
    key_gain,
    feedforward_gain,
    input_weight,
    output_weight,
    gate_weight,
    up_weight,
    down_weight,
    old_cache,
    keep_rows,
    drop_weights,
    dest_slots,
    lengths,
    page_table,
    source,
):
    groups = lax.axis_size("req")
    lanes = lax.axis_size("head")
    requests = hidden_in.shape[0]
    pages_here = old_cache.shape[0]
    devices = groups * lanes
    features = D // groups
    copies = pltpu.SemaphoreType.DMA

    others = from_lanes(hidden_in)[1:]
    blocks = run(
        blocks_kernel,
        [shaped((output_weight.shape[0], features), bfloat)] * 2,
        [output_weight],
        [],
        [copies((2,))],
    )
    handed = [handed_over(block, turn) for turn, block in enumerate(blocks)]
    holds = source[None, :]
    columns = input_weight.shape[1]
    padded = -(-columns // TILE) * TILE
    gain = attention_gain[None, :]
    weight = input_weight.T
    far = [holds, gain, weight, hidden_in]
    sent, hidden_block = run(
        first_kernel,
        [
            shaped((devices, R_DEV * padded // TILE, TILE), single),
            shaped((requests, features), bfloat),
        ],
        far,
        others,
        [
            *scalar_like(holds),
            *local_like(*far[1:]),
            pltpu.VMEM((lanes,) + hidden_in.shape, single),
            pltpu.VMEM((requests, padded), single),
            copies((len(far),)),
        ],
        2 * requests * features * columns,
    )
    sent, *handed = lax.optimization_barrier((sent, *handed))
    came = lax.all_to_all(sent, both_axes, 0, 0, tiled=True)

    slots, _ = lax.optimization_barrier((dest_slots, sent))
    scalars = [slots, lengths[None, :], source[None, :], page_table]
    arrays = [
        keep_rows,
        drop_weights,
        query_gain[None, :],
        key_gain[None, :],
        rotation_table(),
        old_cache,
        gate_weight,
        up_weight,
    ]
    entries = pages_here * KEEP
    extras = 16
    compact, summaries, kept, added, tables, mine, theirs = run(
        prepare_kernel,
        [
            shaped((pages_here // 2, PAGE, KVW), bfloat),
            shaped((pages_here, KVW), bfloat),
            shaped((entries + extras, KVW), bfloat),
            shaped((8, entries + TILE), single),
            shaped((96, TILE), single),
            shaped(gate_weight.shape, bfloat),
            shaped(gate_weight.shape, bfloat),
        ],
        scalars + arrays,
        [],
        [
            *scalar_like(*scalars),
            *local_like(*arrays),
            pltpu.VMEM((pages_here, KVW), single),
            pltpu.VMEM((extras, KVW), single),
            copies((len(scalars + arrays) + pages_here - 1,)),
        ],
        2 * pages_here * TILE * PAGE * KVW,
    )
    span = -(-KVH * HD // TILE) * TILE
    (parts,) = run(
        attend_kernel,
        [shaped((devices, 8, TILE), bfloat)],
        [],
        [came, kept, added, tables],
        [
            pltpu.VMEM((32, TILE), single),
            pltpu.VMEM((extras, span), single),
            pltpu.VMEM((extras, span), single),
            pltpu.VMEM((24, TILE), single),
            pltpu.VMEM((48, TILE), single),
        ],
        6 * 48 * entries * span,
    )
    theirs, _ = lax.optimization_barrier((theirs, parts))
    theirs = swapped_lanes(theirs, 1)
    came = lax.all_to_all(parts, both_axes, 0, 0, tiled=True)
    came, theirs = lax.optimization_barrier((came, theirs))
    (sent,) = run(
        project_kernel,
        [shaped((requests, features), single)],
        [holds],
        [came, *handed],
        [
            *scalar_like(holds),
            pltpu.VMEM((lanes, 2 * groups, TILE), single),
            pltpu.VMEM((requests, 3 * TILE), single),
            pltpu.VMEM((2, requests, output_weight.shape[0]), single),
            copies((1,)),
        ],
        2 * requests * output_weight.size,
    )
    gain = feedforward_gain[None, :]
    block = gate_weight.shape[1] // 2
    sent, mid = run(
        units_kernel,
        [
            shaped((groups, requests, block + TILE), bfloat),
            shaped((requests, features), bfloat),
        ],
        [gain],
        [*from_lanes(sent), hidden_block, mine, theirs],
        [*local_like(gain), copies((1,))],
        4 * requests * gate_weight.size,
    )
    (active,) = run(
        active_kernel, [shaped((requests, block // 2), bfloat)], [], [exchange(sent)]
    )
    (sent,) = run(
        down_kernel,
        [shaped((groups, requests, down_weight.shape[1]), bfloat)],
        [],
        [*from_lanes(active), down_weight, mid],
        [pltpu.VMEM((lanes,) + active.shape, bfloat)],
        2 * requests * down_weight.size,
    )
    (result,) = run(
        result_kernel, [shaped((requests, down_weight.shape[1]), bfloat)], [], [exchange(sent)]
    )
    return (compact, summaries, result)


def solution(mesh):
    placed = (
        P(None, "head"),
        P(),
        P(),
        P(),
        P(),
        P("req", "head"),
        P("req", "head"),
        P("req", "head"),
        P("req", "head"),
        P("req", "head"),
        P(("req", "head"), None, None),
        P(("req", "head"), None),
        P(("req", "head"), None),
        P(("req", "head"), None),
        P(),
        P("req", None),
        P(),
    )
    return jax.shard_map(
        on_device if mesh.shape["req"] <= DIRECT else on_device_wide,
        mesh=mesh,
        in_specs=placed,
        out_specs=(P(("req", "head"), None, None), P(("req", "head"), None), P(None, "head")),
        check_vma=False,
    )
```

```python
import jax
import jax.numpy as jnp
import numpy as np
from jax import lax
from jax.experimental import pallas as pl
from jax.experimental.pallas import tpu as pltpu
from jax.sharding import PartitionSpec as P

D = 2048
HEADS = 20
KVH = 5
HD = 64
FF = 5120
PAGE = 128
KEEP = 64
NP = 16
R_DEV = 2
KVW = 640

DIRECT = 8

epsilon = 1e-06
negative = -1e30
both_axes = ("req", "head")


def rms_scale(values):
    return lax.rsqrt(jnp.mean(values * values, axis=-1, keepdims=True) + epsilon)


def rms_rows(values, gain):
    return values * rms_scale(values) * gain


def rotate(vectors, positions):
    half = vectors.shape[-1] // 2
    frequency = 10000.0 ** (-jnp.arange(half, dtype=jnp.float32) / half)
    angles = positions.astype(jnp.float32)[:, None] * frequency[None, :]
    cosine = jnp.cos(angles)[:, None, :]
    sine = jnp.sin(angles)[:, None, :]
    first = vectors[..., :half]
    second = vectors[..., half:]
    return jnp.concatenate(
        [first * cosine - second * sine, second * cosine + first * sine], axis=-1
    )


def compact_pages(pages, keep, weights):
    rows = jnp.arange(pages.shape[1], dtype=jnp.int32)
    picks = keep[:, :, None] == rows[None, None, :]
    kept = jnp.einsum(
        "pkr,prc->pkc", picks.astype(jnp.bfloat16), pages, preferred_element_type=jnp.float32
    ).astype(jnp.bfloat16)
    dropped = weights * (1.0 - jnp.sum(picks.astype(jnp.float32), axis=1))
    total = jnp.sum(dropped, axis=1)
    means = (
        jnp.einsum(
            "pr,prc->pc", dropped, pages.astype(jnp.float32), precision=lax.Precision.HIGHEST
        )
        / total[:, None]
    )
    return (kept, means.astype(jnp.bfloat16), jnp.log(total))


def held_request(rows, source):
    half = R_DEV // 2
    position = rows % R_DEV
    slot = rows // R_DEV * half + position - half
    continued = jnp.arange(source.shape[0], dtype=jnp.int32)
    matches = source[None, :] == slot[:, None]
    owner_cont = jnp.sum(jnp.where(matches, continued[None, :], 0), axis=1)
    carried = owner_cont // half * R_DEV + half + owner_cont % half
    return jnp.where(position < half, rows, carried)


def pick_rows(order, rows):
    chosen = order[:, None] == jnp.arange(rows.shape[0], dtype=jnp.int32)[None, :]
    return jnp.dot(
        chosen.astype(jnp.bfloat16), rows, preferred_element_type=jnp.float32
    ).astype(jnp.bfloat16)


def exchange(parts):
    return lax.all_to_all(parts, "req", split_axis=0, concat_axis=0, tiled=True)


def to_block_owner(rows):
    groups = lax.axis_size("req")
    lanes = lax.axis_size("head")
    per_lane = groups // lanes
    pairs = [
        (g * lanes + h, (per_lane * h + g // lanes) * lanes + g % lanes)
        for g in range(groups)
        for h in range(lanes)
    ]
    return lax.ppermute(rows, both_axes, pairs)


def whole_sum(partial):
    if lax.axis_size("req") > DIRECT:
        return lax.psum(partial, "req")
    groups = lax.axis_size("req")
    return jnp.sum(exchange(jnp.broadcast_to(partial[None], (groups,) + partial.shape)), axis=0)


def on_device_wide(
    hidden_in,
    attention_gain,
    query_gain,
    key_gain,
    feedforward_gain,
    input_weight,
    output_weight,
    gate_weight,
    up_weight,
    down_weight,
    old_cache,
    keep_rows,
    drop_weights,
    dest_slots,
    lengths,
    page_table,
    source,
):
    groups = lax.axis_size("req")
    lanes = lax.axis_size("head")
    group = lax.axis_index("req")
    lane = lax.axis_index("head")
    requests = hidden_in.shape[0]
    half = R_DEV // 2
    split = KVH * HD
    ratio = HEADS // KVH
    scale = HD ** (-0.5)
    pages_here = old_cache.shape[0]
    everyone = jnp.arange(requests, dtype=jnp.int32)
    holders = held_request(everyone, source)
    held = lax.dynamic_slice_in_dim(holders, group * R_DEV, R_DEV, 0)
    held_len = lengths[held]
    positions = held_len * PAGE

    whole = lax.all_gather(hidden_in, "head", axis=1, tiled=True)
    normed = rms_rows(whole.astype(jnp.float32), attention_gain).astype(jnp.bfloat16)
    features = D // groups
    inputs = pick_rows(holders, lax.dynamic_slice_in_dim(normed, group * features, features, 1))
    partial_qkv = jnp.dot(inputs, input_weight, preferred_element_type=jnp.float32)
    sent = jnp.broadcast_to(
        partial_qkv.reshape(groups, 1, R_DEV, -1), (groups, lanes, R_DEV, partial_qkv.shape[1])
    ).reshape(groups * lanes, R_DEV, -1)
    got = lax.all_to_all(sent, both_axes, split_axis=0, concat_axis=0, tiled=True)
    mixed = jnp.sum(got.reshape(groups, lanes, R_DEV, -1), axis=0).astype(jnp.bfloat16)
    held_qkv = jnp.swapaxes(mixed, 0, 1).reshape(R_DEV, -1).astype(jnp.float32)

    query = rotate(
        rms_rows(held_qkv[:, : HEADS * HD].reshape(R_DEV, HEADS, HD), query_gain), positions
    ).astype(jnp.bfloat16)
    key_new = rotate(
        rms_rows(held_qkv[:, HEADS * HD : (HEADS + KVH) * HD].reshape(R_DEV, KVH, HD), key_gain),
        positions,
    ).astype(jnp.bfloat16)
    value_new = held_qkv[:, (HEADS + KVH) * HD :].reshape(R_DEV, KVH, HD)
    kept, means, bias = compact_pages(old_cache, keep_rows, drop_weights)
    destination = dest_slots[0]
    fresh_ids = jnp.arange(pages_here, dtype=jnp.int32)
    inverse = jnp.sum(
        jnp.where(destination[None, :] == fresh_ids[:, None], fresh_ids[None, :], 0), axis=1
    )
    compact = kept[inverse].reshape(pages_here // 2, PAGE, KVW)
    summaries = means[inverse]
    per_lane = NP // lanes
    table = page_table.reshape(R_DEV, per_lane, lanes)
    mine = lax.dynamic_slice_in_dim(table, lane, 1, 2)[:, :, 0]
    logical = jnp.arange(per_lane, dtype=jnp.int32) * lanes + lane
    live = logical[None, :] < held_len[:, None]
    owner = jnp.any((mine[:, :, None] == fresh_ids[None, None, :]) & live[:, :, None], axis=1)
    query_groups = query.reshape(R_DEV, KVH, ratio, HD)
    row_keys = kept[:, :, :split].reshape(pages_here, KEEP, KVH, HD)
    row_values = kept[:, :, split:].reshape(pages_here, KEEP, KVH, HD)
    row_live = keep_rows >= 0
    allowed = owner[:, None, None, :, None] & row_live[None, None, None, :, :]
    scores = (
        jnp.einsum("rngd,pmnd->rngpm", query_groups, row_keys, preferred_element_type=jnp.float32)
        * scale
    )
    scores = jnp.where(allowed, scores, negative)
    mean_keys = means[:, :split].reshape(pages_here, KVH, HD)
    mean_values = means[:, split:].reshape(pages_here, KVH, HD)
    mean_scores = (
        jnp.einsum("rngd,pnd->rngp", query_groups, mean_keys, preferred_element_type=jnp.float32)
        * scale
        + bias[None, None, None, :]
    )
    mean_allowed = owner[:, None, None, :]
    mean_scores = jnp.where(mean_allowed, mean_scores, negative)
    own_score = (
        jnp.einsum("rngd,rnd->rng", query_groups, key_new, preferred_element_type=jnp.float32)
        * scale
    )
    own_score = jnp.where(lane == 0, own_score, negative)
    top = jnp.maximum(jnp.max(scores, axis=(3, 4)), jnp.max(mean_scores, axis=3))
    top = jnp.maximum(top, own_score)
    row_weight = jnp.where(allowed, jnp.exp(scores - top[..., None, None]), 0.0)
    mean_weight = jnp.where(mean_allowed, jnp.exp(mean_scores - top[..., None]), 0.0)
    own_weight = jnp.where(lane == 0, jnp.exp(own_score - top), 0.0)
    mass = jnp.sum(row_weight, axis=(3, 4)) + jnp.sum(mean_weight, axis=3) + own_weight
    total = jnp.einsum(
        "rngpm,pmnd->rngd",
        row_weight,
        row_values.astype(jnp.float32),
        precision=lax.Precision.HIGHEST,
    )
    total = total + jnp.einsum(
        "rngp,pnd->rngd",
        mean_weight,
        mean_values.astype(jnp.float32),
        precision=lax.Precision.HIGHEST,
    )
    total = total + own_weight[..., None] * value_new[:, :, None, :]

    some = mass > 0.0
    level = jnp.where(some, top + jnp.log(jnp.where(some, mass, 1.0)), negative)
    means_out = total / jnp.where(some, mass, 1.0)[..., None]
    own = HEADS * HD // groups
    parts = jnp.stack([means_out, jnp.broadcast_to(level[..., None], total.shape)])
    parts = jnp.transpose(parts.reshape(2, R_DEV, groups, own), (2, 1, 0, 3))
    parts = jnp.broadcast_to(
        parts.reshape(groups, 1, R_DEV, 2 * own), (groups, lanes, R_DEV, 2 * own)
    ).reshape(groups * lanes, R_DEV, 2 * own)
    came = lax.all_to_all(parts, both_axes, 0, 0, tiled=True)
    came = came.reshape(groups, lanes, R_DEV, 2 * own)
    outs, levels = came[..., :own], came[..., own:]
    weights = jnp.exp(levels - jnp.max(levels, axis=1, keepdims=True))
    attention = jnp.sum(outs * weights, axis=1) / jnp.sum(weights, axis=1)
    attention = attention.reshape(requests, own).astype(jnp.bfloat16)
    back = jnp.sum(
        jnp.where(holders[None, :] == everyone[:, None], everyone[None, :], 0), axis=1
    )
    projected = jnp.dot(
        pick_rows(back, attention), output_weight, preferred_element_type=jnp.float32
    )
    projected = projected + jnp.where(group == 0, hidden_in.astype(jnp.float32), 0.0)

    share = groups // lanes
    blocks = jnp.moveaxis(projected.reshape(requests, share, 1, features), 0, 2)
    blocks = jnp.broadcast_to(blocks, (share, lanes, requests, features))
    mid = jnp.sum(exchange(blocks.reshape(groups, requests, features)), axis=0)
    mid = to_block_owner(mid.astype(jnp.bfloat16)).astype(jnp.float32)
    squares = jnp.sum(mid * mid, axis=1, keepdims=True)
    gain_here = lax.dynamic_slice_in_dim(feedforward_gain, group * features, features, 0)
    inputs_mid = (mid * gain_here).astype(jnp.bfloat16)
    local_units = gate_weight.shape[1]
    piece = local_units // groups
    gates = jnp.dot(inputs_mid, gate_weight, preferred_element_type=jnp.float32)
    ups = jnp.dot(inputs_mid, up_weight, preferred_element_type=jnp.float32)
    both = jnp.concatenate(
        [
            gates.reshape(requests, groups, piece),
            ups.reshape(requests, groups, piece),
            jnp.broadcast_to(squares[:, :, None], (requests, groups, 1)),
        ],
        axis=2,
    )
    sums = jnp.sum(exchange(jnp.swapaxes(both, 0, 1)), axis=0)
    factor = lax.rsqrt(sums[:, 2 * piece :] / D + epsilon)
    gate = sums[:, :piece] * factor
    active = (jax.nn.silu(gate) * (sums[:, piece : 2 * piece] * factor)).astype(jnp.bfloat16)
    active_here = lax.all_gather(to_block_owner(active), "head", axis=1, tiled=True)
    down = jnp.dot(active_here, down_weight, preferred_element_type=jnp.float32)
    residual = [jnp.where(group == lane * share + k, mid, 0.0) for k in range(share)]
    down = down + jnp.concatenate(residual, axis=1)
    result = whole_sum(down).astype(jnp.bfloat16)
    return (compact, summaries, result)


TILE = 128
bfloat = jnp.bfloat16
single = jnp.float32


TERMS = 4


def three_terms(value, place):
    high = value.astype(bfloat).astype(single)
    rest = value - high
    middle = rest.astype(bfloat).astype(single)
    low = jnp.where(place == 2, rest - middle, 0.0)
    return jnp.where(place == 0, high, jnp.where(place == 1, middle, low))


def iota(shape, axis):
    return lax.broadcasted_iota(jnp.int32, shape, axis)


def run(kernel, outs, far, near, scratch=(), flops=0):
    in_specs = [pl.BlockSpec(memory_space=pltpu.HBM) for _ in far]
    in_specs += [pl.BlockSpec(memory_space=pltpu.VMEM) for _ in near]
    moved = sum(a.size * a.dtype.itemsize for a in [*far, *near, *outs])
    return pl.pallas_call(
        kernel,
        out_shape=list(outs),
        in_specs=in_specs,
        out_specs=[pl.BlockSpec(memory_space=pltpu.VMEM) for _ in outs],
        scratch_shapes=list(scratch),
        compiler_params=pltpu.CompilerParams(vmem_limit_bytes=16 * 2**20),
        cost_estimate=pl.CostEstimate(flops=flops, bytes_accessed=moved, transcendentals=0),
    )(*[pltpu.with_memory_space_constraint(a, pltpu.HBM) for a in far], *near)


def fetch(sources, targets, done):
    copies = [
        pltpu.make_async_copy(source, target, done.at[k])
        for k, (source, target) in enumerate(zip(sources, targets))
    ]
    for copy in copies:
        copy.start()
    return copies


def local_like(*arrays):
    return [pltpu.VMEM(a.shape, a.dtype) for a in arrays]


def scalar_like(*arrays):
    return [pltpu.SMEM(a.shape, a.dtype) for a in arrays]


def row_order(source, count, to_holder):
    first, second = iota((count, count), 0), iota((count, count), 1)
    if not to_holder:
        first, second = second, first
    order = (first == second) & (first % R_DEV == 0)
    for c in range(source.shape[1]):
        order = order | ((first == source[0, c] * R_DEV + 1) & (second == c * R_DEV + 1))
    return order.astype(single).astype(bfloat)


def shaped(shape, dtype):
    return jax.ShapeDtypeStruct(shape, dtype)


def first_kernel(
    source_far, gain_far, weight_far, hidden_far, one, two, three, sent, block, source, gain,
    weight, hidden, lanes_of, wide, done
):
    copies = fetch(
        (source_far, gain_far, weight_far, hidden_far), (source, gain, weight, hidden), done
    )
    rows = hidden.shape[0]
    groups = rows // R_DEV
    lanes = sent.shape[0] // groups
    columns, features = weight.shape
    group = lax.axis_index("req")
    share = groups // lanes
    squares = 0.0
    for turn, values in enumerate((one, two, three)):
        values = values[...].astype(single)
        lanes_of[turn + 1] = values
        squares = squares + jnp.sum(values * values, axis=1, keepdims=True)
    copies[3].wait()
    values = hidden[...].astype(single)
    lanes_of[0] = values
    squares = squares + jnp.sum(values * values, axis=1, keepdims=True)
    factor = lax.rsqrt(squares / D + epsilon)
    here = pl.ds(pl.multiple_of(group * features, features), features)
    within = pl.ds(pl.multiple_of(group % share * features, features), features)
    mine = lanes_of[group // share ^ lax.axis_index("head"), :, within]
    block[...] = mine.astype(bfloat)
    wide[...] = jnp.zeros_like(wide)
    for copy in copies[:3]:
        copy.wait()
    normed = (mine * factor * gain[:, here]).astype(bfloat)
    order = row_order(source, rows, True)
    normed = jnp.dot(order, normed, preferred_element_type=single).astype(bfloat)
    wide[:, :columns] = dot_rows(normed, weight[...])
    for g in range(groups):
        tile = jnp.concatenate(
            [
                wide[R_DEV * g : R_DEV * (g + 1), TILE * j : TILE * (j + 1)]
                for j in range(wide.shape[1] // TILE)
            ],
            axis=0,
        )
        for k in range(lanes):
            sent[g * lanes + k] = tile


def dot_rows(left, right):
    return lax.dot_general(left, right, (((1,), (1,)), ((), ())), preferred_element_type=single)


def prepare_kernel(*refs):
    far, refs = refs[:13], refs[13:]
    (compact, summaries, kept, added, tables, mine, theirs, *handed), refs = refs[:9], refs[9:]
    near, (ordered, plain, dealt, done) = refs[:13], refs[13:]
    copies = fetch(far, near, done)
    (dest, lengths, source, table, keep, weights, query_gain, key_gain, turns) = near[:9]
    pages, gate, up, output = near[9:]
    group = lax.axis_index("req")
    lane = lax.axis_index("head")
    lanes = lax.axis_size("head")
    for copy in copies[:9]:
        copy.wait()

    carried = 0
    for c in range(source.shape[1]):
        carried = carried + jnp.where(source[0, c] == group, c, 0)
    held_len = (lengths[0, group * R_DEV], lengths[0, carried * R_DEV + 1])
    count, rows, _ = pages.shape
    owned = []
    for r in range(R_DEV):
        slots = []
        for i in range(table.shape[1] // lanes):
            j = i * lanes + lane
            slots.append(jnp.where(j < held_len[r], table[r, j], -1))
        owned.append(slots)

    def owner(r, p):
        found = owned[r][0] == p
        for slot in owned[r][1:]:
            found = found | (slot == p)
        return found

    row = iota((32, TILE), 0)
    odd = (row & 1) == 1
    half_rows = turns.shape[0] // 2
    for part in range(2):
        pair = [turns[pl.ds(part * half_rows + held_len[r], 1), :] for r in range(R_DEV)]
        tables[32 * part : 32 * (part + 1), :] = jnp.where(odd, pair[1], pair[0])
    query_rows = HEADS * HD // TILE * R_DEV
    for c in range(TILE // HD):
        columns = slice(HD * c, HD * (c + 1))
        tables[64 : 64 + query_rows, columns] = jnp.broadcast_to(
            query_gain[...], (query_rows, HD)
        )
        tables[64 + query_rows : 96, columns] = jnp.broadcast_to(
            key_gain[...], (32 - query_rows, HD)
        )

    column = iota((1, TILE), 1)
    entries = count * KEEP
    added[...] = jnp.full_like(added, negative)
    extra = [
        jnp.where((column == count + r) & (lane == 0), 0.0, negative) for r in range(R_DEV)
    ]
    weight_columns = weights[...].T
    rows_of = iota((rows, KEEP), 0)
    place = iota((rows, 16), 1)
    copies[9].wait()
    for p in range(count):
        picks = (keep[p : p + 1, :] == rows_of).astype(single)
        dropped = weight_columns[:, p : p + 1] * (1.0 - jnp.sum(picks, axis=1, keepdims=True))
        total = jnp.sum(dropped, axis=0, keepdims=True)
        left = jnp.concatenate([picks, three_terms(dropped, place)], axis=1).astype(bfloat)
        both = lax.dot_general(
            left, pages[p], (((0,), (0,)), ((), ())), preferred_element_type=single
        )
        rows_kept = both[:KEEP].astype(bfloat)
        kept[KEEP * p : KEEP * (p + 1), :] = rows_kept
        slot = dest[0, p]
        start = pl.multiple_of((slot & 1) * KEEP, KEEP)
        compact[slot >> 1, pl.ds(start, KEEP), :] = rows_kept
        mean = both[KEEP : KEEP + 1] + both[KEEP + 1 : KEEP + 2] + both[KEEP + 2 : KEEP + 3]
        mean = mean / total
        plain[p : p + 1, :] = mean
        ordered[pl.ds(slot, 1), :] = mean
        live = jnp.where(keep[p : p + 1, :] >= 0, 0.0, negative)
        for r in range(R_DEV):
            here = owner(r, p)
            added[r : r + 1, KEEP * p : KEEP * (p + 1)] = jnp.where(here, live, negative)
            level = jnp.where(here, jnp.log(total), negative)
            extra[r] = jnp.where(column == p, level, extra[r])
    for r in range(R_DEV):
        added[r : r + 1, entries : entries + TILE] = extra[r]
    plain[count:, :] = jnp.zeros_like(plain[count:, :])
    kept[entries:, :] = plain[...].astype(bfloat)
    summaries[...] = ordered[...].astype(bfloat)

    for copy in copies[10:]:
        copy.wait()
    block = gate.shape[1] // 2
    piece = block // 2
    for k in range(2):
        for b in range(2):
            columns = slice(b * block + k * piece, b * block + (k + 1) * piece)
            start = b * block
            dealt[k, :, start : start + piece] = gate[:, columns].astype(single)
            dealt[k, :, start + piece : start + block] = up[:, columns].astype(single)
    mine[...] = dealt[lane & 1].astype(bfloat)
    theirs[...] = dealt[1 - (lane & 1)].astype(bfloat)
    width = handed[0].shape[1]
    for turn, block in enumerate(handed):
        start = pl.multiple_of(((group & 1) ^ turn) * width, width)
        block[...] = output[:, pl.ds(start, width)]


def attend_kernel(came, kept, added, tables, sent, x, extra_k, extra_v, out, logs):
    lanes = lax.axis_size("head")
    groups = came.shape[0] // lanes
    width = (HEADS + 2 * KVH) * HD // lanes
    span = -(-KVH * HD // TILE) * TILE
    key_cols = slice(0, span)
    value_cols = slice(KVW - span, KVW)
    first_key = HEADS * HD // TILE * R_DEV
    scale = HD ** (-0.5)
    x[...] = jnp.zeros_like(x)
    column = iota((8, TILE), 1)
    for k in range(lanes):
        tile = came[k].astype(single)
        for g in range(1, groups):
            tile = tile + came[g * lanes + k].astype(single)
        tile = tile.astype(bfloat).astype(single)
        base, shift = divmod(width * k, TILE)
        base = base * R_DEV
        if shift:
            tile = pltpu.roll(tile, shift, 1)
            x[base + 2 : base + 10, :] += jnp.where(column < shift, tile, 0.0)
        x[base : base + 8, :] += jnp.where(column >= shift, tile, 0.0)
    values = x[...]
    same_head = (iota((TILE, TILE), 0) // HD == iota((TILE, TILE), 1) // HD).astype(single)
    squares = jnp.dot(
        values * values, same_head, precision=lax.Precision.HIGHEST, preferred_element_type=single
    )
    normed = values * lax.rsqrt(squares / HD + epsilon) * tables[64:96, :]
    early = iota(values.shape, 1) % HD < HD // 2
    swapped = jnp.where(
        early, pltpu.roll(normed, TILE - HD // 2, 1), pltpu.roll(normed, HD // 2, 1)
    )
    turned = normed * tables[0:32, :] + swapped * tables[32:64, :]
    turned = turned.astype(bfloat).astype(single)

    rows = 24
    row = iota((rows, TILE), 0)
    half = iota((rows, TILE), 1) // HD
    key_head = row >> 2
    query = jnp.where(row < first_key, turned[:rows], 0.0)
    other = pltpu.roll(query, HD, 1)
    queries = []
    for u in range(2):
        placed = jnp.where(
            half == (key_head & 1), jnp.where((key_head & 1) == u, query, other), 0.0
        )
        queries.append(
            jnp.concatenate(
                [jnp.where((key_head >> 1) == c, placed, 0.0) for c in range(span // TILE)], axis=1
            )
        )
    queries = jnp.concatenate(queries, axis=0).astype(bfloat)

    extras = extra_k.shape[0]
    entries = kept.shape[0] - extras
    count = entries // KEEP
    extra_k[...] = kept[entries:, key_cols].astype(single)
    extra_v[...] = kept[entries:, value_cols].astype(single)
    first_value = first_key + KVH * HD // TILE * R_DEV
    for c in range(span // TILE):
        at = slice(c * TILE, (c + 1) * TILE)
        r = first_key + R_DEV * c
        extra_k[count : count + R_DEV, at] = turned[r : r + R_DEV]
        r = first_value + R_DEV * c
        extra_v[count : count + R_DEV, at] = values[r : r + R_DEV]

    def by_request(columns, size):
        odd = (iota((2 * rows, size), 0) & 1) == 1
        return jnp.where(odd, added[1:2, columns], added[0:1, columns])

    scores = dot_rows(queries, kept[:entries, key_cols]) * scale
    scores = scores + by_request(slice(0, entries), entries)
    extra = dot_rows(queries, extra_k[...].astype(bfloat)) * scale
    extra = extra + by_request(slice(entries, entries + extras), extras)
    top = jnp.maximum(
        jnp.max(scores, axis=1, keepdims=True), jnp.max(extra, axis=1, keepdims=True)
    )
    weight = jnp.where(scores > 0.5 * negative, jnp.exp(scores - top), 0.0)
    extra_weight = jnp.where(extra > 0.5 * negative, jnp.exp(extra - top), 0.0)
    mass = jnp.sum(weight, axis=1, keepdims=True) + jnp.sum(extra_weight, axis=1, keepdims=True)

    def weighted(parts, right):
        high = parts.astype(bfloat)
        low = (parts - high.astype(single)).astype(bfloat)
        return jnp.dot(high, right, preferred_element_type=single) + jnp.dot(
            low, right, preferred_element_type=single
        )

    total = weighted(weight, kept[:entries, value_cols]) + weighted(
        extra_weight, extra_v[...].astype(bfloat)
    )
    some = mass > 0.0
    mass = jnp.where(some, mass, 1.0)
    total = total / mass
    level = jnp.where(some, top + jnp.log(mass), negative)

    slot = key_head + (KVW // 2 - (KVW - span)) // HD
    results = []
    for u in range(2):
        mine = total[rows * u : rows * (u + 1)]
        picked = mine[:, :TILE]
        for c in range(1, span // TILE):
            picked = jnp.where((slot >> 1) == c, mine[:, c * TILE : (c + 1) * TILE], picked)
        results.append(jnp.where((slot & 1) == u, picked, pltpu.roll(picked, HD, 1)))
    out[...] = jnp.where(half == 0, results[0], results[1])
    logs[...] = jnp.broadcast_to(level, logs.shape)
    own = HEADS * HD // lanes
    size = 6
    column = iota((size, TILE), 1)
    here = column // TERMS == iota((size, TILE), 0)
    for k in range(lanes):
        r = own * k // TILE * R_DEV
        tile = [out[r : r + size, :]]
        for u in range(2):
            coded = three_terms(logs[rows * u + r : rows * u + r + size, :], column % TERMS)
            tile.append(jnp.sum(jnp.where(here, coded, 0.0), axis=0, keepdims=True))
        tile = jnp.concatenate(tile, axis=0).astype(bfloat)
        for g in range(groups):
            sent[g * lanes + k] = tile


def project_kernel(source_far, came, first, second, sent, source, logs, rows, pieces, done):
    (copy,) = fetch((source_far,), (source,), done)
    lanes = lax.axis_size("head")
    groups = came.shape[0] // lanes
    group = lax.axis_index("req")
    features = first.shape[0]
    requests = rows.shape[0]
    size = 6
    tiles = [came[d].astype(single) for d in range(groups * lanes)]
    for g in range(groups):
        for k in range(lanes):
            logs[k, 2 * g : 2 * g + 2, :] = tiles[g * lanes + k][size:]
    spread = (iota((8, TILE), 1) // TERMS == iota((8, TILE), 0)).astype(single).astype(bfloat)
    levels = [dot_rows(spread, logs[k].astype(bfloat)) for k in range(lanes)]
    top = jnp.maximum(jnp.maximum(levels[0], levels[1]), jnp.maximum(levels[2], levels[3]))
    shares = [jnp.exp(level - top) for level in levels]
    mass = sum(shares)
    shares = [share / mass for share in shares]
    lower = iota((8, TILE), 1) < HD
    for g in range(groups):
        mixed = 0.0
        for k in range(lanes):
            share = shares[k]
            share = jnp.where(lower, share[:, 2 * g : 2 * g + 1], share[:, 2 * g + 1 : 2 * g + 2])
            mixed = mixed + share * tiles[g * lanes + k]
        for j in range(size // R_DEV):
            rows[R_DEV * g : R_DEV * (g + 1), TILE * j : TILE * (j + 1)] = mixed[
                R_DEV * j : R_DEV * (j + 1)
            ]
    width = rows.shape[1]
    shift = lax.rem(lax.axis_index("head") * (2 * features), TILE)
    attention = rows[...].astype(bfloat).astype(single)
    attention = pltpu.roll(attention, lax.rem(width - shift, width), 1)
    copy.wait()
    order = row_order(source, requests, False)
    attention = jnp.dot(order, attention.astype(bfloat), preferred_element_type=single)
    for b in range(2):
        pieces[b] = attention[:, features * b : features * (b + 1)]
    total = 0.0
    for turn, weight in enumerate((first, second)):
        piece = pieces[(group & 1) ^ turn].astype(bfloat)
        total = total + jnp.dot(piece, weight[...], preferred_element_type=single)
    sent[...] = total


def units_kernel(
    gain_far, own, one, two, three, hidden, mine, theirs, sent, mid_out, gain, done
):
    (copy,) = fetch((gain_far,), (gain,), done)
    rows, features = own.shape
    share = sent.shape[0] // lax.axis_size("head")
    group = lax.axis_index("req")
    lane = lax.axis_index("head")
    here = pl.ds(pl.multiple_of(group * features, features), features)
    mid = (own[...] + one[...]) + (two[...] + three[...])
    mid = (hidden[...].astype(single) + mid).astype(bfloat)
    mid_out[...] = mid
    mid = mid.astype(single)
    squares = jnp.sum(mid * mid, axis=1, keepdims=True)
    block = mine.shape[1] // share
    terms = three_terms(squares, iota((rows, sent.shape[2] - block), 1)).astype(bfloat)
    copy.wait()
    inputs = (mid * gain[:, here]).astype(bfloat)
    for turn, weight in enumerate((mine, theirs)):
        units = jnp.dot(inputs, weight[...], preferred_element_type=single).astype(bfloat)
        target = (lane ^ turn) * share
        for b in range(share):
            sent[target + b, :, :block] = units[:, block * b : block * (b + 1)]
            sent[target + b, :, block:] = terms


def active_kernel(came, active):
    total = came[0].astype(single)
    for g in range(1, came.shape[0]):
        total = total + came[g].astype(single)
    piece = active.shape[1]
    squares = jnp.sum(total[:, 2 * piece : 2 * piece + 3], axis=1, keepdims=True)
    factor = lax.rsqrt(squares / D + epsilon)
    gate = total[:, :piece] * factor
    up = total[:, piece : 2 * piece] * factor
    active[...] = (gate / (1.0 + jnp.exp(-gate)) * up).astype(bfloat)


def down_kernel(own, one, two, three, weight, mid, sent, active):
    groups, rows, width = sent.shape
    piece = own.shape[1]
    half = mid.shape[1]
    for turn, values in enumerate((own, one, two, three)):
        active[turn] = values[...]
    share = width // half
    group = lax.axis_index("req")
    lane = lax.axis_index("head")
    first = group // (2 * share) * 2 ^ lane
    down = jnp.dot(active[first], weight[:piece, :], preferred_element_type=single)
    down = down + jnp.dot(active[first ^ 1], weight[piece:, :], preferred_element_type=single)
    residual = mid[...].astype(single)
    for b in range(share):
        columns = slice(half * b, half * (b + 1))
        mine = group == lane * share + b
        total = (down[:, columns] + jnp.where(mine, residual, 0.0)).astype(bfloat)
        for g in range(groups):
            sent[g, :, columns] = total


def result_kernel(came, result):
    total = came[0].astype(single)
    for g in range(1, came.shape[0]):
        total = total + came[g].astype(single)
    result[...] = total.astype(bfloat)


def rotation_table():
    half = HD // 2
    size = -(-(NP + 1) // 8) * 8
    frequency = 10000.0 ** (-np.arange(half) / half)
    angles = PAGE * np.arange(size)[:, None] * frequency[None, :]
    cosine, sine = np.cos(angles), np.sin(angles)
    wide = [np.tile(np.concatenate(pair, axis=1), (1, TILE // HD)) for pair in
            ((cosine, cosine), (-sine, sine))]
    return jnp.asarray(np.concatenate(wide), dtype=single)


def swapped_lanes(value, turn):
    lanes = lax.axis_size("head")
    return lax.ppermute(value, "head", [(k, k ^ turn) for k in range(lanes)])


def from_lanes(value):
    return [value] + [swapped_lanes(value, turn) for turn in range(1, lax.axis_size("head"))]


def handed_over(value, turn):
    groups = lax.axis_size("req")
    lanes = lax.axis_size("head")
    share = groups // lanes
    pairs = [
        (g * lanes + h, (share * h + ((g & 1) ^ turn)) * lanes + g // share)
        for g in range(groups)
        for h in range(lanes)
    ]
    return lax.ppermute(value, both_axes, pairs)


def on_device(
    hidden_in,
    attention_gain,
    query_gain,
    key_gain,
    feedforward_gain,
    input_weight,
    output_weight,
    gate_weight,
    up_weight,
    down_weight,
    old_cache,
    keep_rows,
    drop_weights,
    dest_slots,
    lengths,
    page_table,
    source,
):
    groups = lax.axis_size("req")
    lanes = lax.axis_size("head")
    requests = hidden_in.shape[0]
    pages_here = old_cache.shape[0]
    devices = groups * lanes
    features = D // groups
    copies = pltpu.SemaphoreType.DMA

    others = from_lanes(hidden_in)[1:]
    scalars = [dest_slots, lengths[None, :], source[None, :], page_table]
    arrays = [
        keep_rows,
        drop_weights,
        query_gain[None, :],
        key_gain[None, :],
        rotation_table(),
        old_cache,
        gate_weight,
        up_weight,
        output_weight,
    ]
    entries = pages_here * KEEP
    extras = 16
    compact, summaries, kept, added, tables, mine, theirs, *handed = run(
        prepare_kernel,
        [
            shaped((pages_here // 2, PAGE, KVW), bfloat),
            shaped((pages_here, KVW), bfloat),
            shaped((entries + extras, KVW), bfloat),
            shaped((8, entries + TILE), single),
            shaped((96, TILE), single),
            shaped(gate_weight.shape, bfloat),
            shaped(gate_weight.shape, bfloat),
            shaped((output_weight.shape[0], features), bfloat),
            shaped((output_weight.shape[0], features), bfloat),
        ],
        scalars + arrays,
        [],
        [
            *scalar_like(*scalars),
            *local_like(*arrays),
            pltpu.VMEM((pages_here, KVW), single),
            pltpu.VMEM((extras, KVW), single),
            pltpu.VMEM((2,) + gate_weight.shape, single),
            copies((len(scalars + arrays),)),
        ],
        2 * pages_here * TILE * PAGE * KVW,
    )
    tables, *others = lax.optimization_barrier((tables, *others))

    holds = source[None, :]
    columns = input_weight.shape[1]
    padded = -(-columns // TILE) * TILE
    gain = attention_gain[None, :]
    weight = input_weight.T
    far = [holds, gain, weight, hidden_in]
    sent, hidden_block = run(
        first_kernel,
        [
            shaped((devices, R_DEV * padded // TILE, TILE), single),
            shaped((requests, features), bfloat),
        ],
        far,
        others,
        [
            *scalar_like(holds),
            *local_like(*far[1:]),
            pltpu.VMEM((lanes,) + hidden_in.shape, single),
            pltpu.VMEM((requests, padded), single),
            copies((len(far),)),
        ],
        2 * requests * features * columns,
    )
    came = lax.all_to_all(sent, both_axes, 0, 0, tiled=True)
    theirs = swapped_lanes(theirs, 1)
    handed = [handed_over(block, turn) for turn, block in enumerate(handed)]
    came, theirs, *handed = lax.optimization_barrier((came, theirs, *handed))
    span = -(-KVH * HD // TILE) * TILE
    (parts,) = run(
        attend_kernel,
        [shaped((devices, 8, TILE), bfloat)],
        [],
        [came, kept, added, tables],
        [
            pltpu.VMEM((32, TILE), single),
            pltpu.VMEM((extras, span), single),
            pltpu.VMEM((extras, span), single),
            pltpu.VMEM((24, TILE), single),
            pltpu.VMEM((48, TILE), single),
        ],
        6 * 48 * entries * span,
    )
    came = lax.all_to_all(parts, both_axes, 0, 0, tiled=True)
    (sent,) = run(
        project_kernel,
        [shaped((requests, features), single)],
        [holds],
        [came, *handed],
        [
            *scalar_like(holds),
            pltpu.VMEM((lanes, 2 * groups, TILE), single),
            pltpu.VMEM((requests, 3 * TILE), single),
            pltpu.VMEM((2, requests, output_weight.shape[0]), single),
            copies((1,)),
        ],
        2 * requests * output_weight.size,
    )
    gain = feedforward_gain[None, :]
    block = gate_weight.shape[1] // 2
    sent, mid = run(
        units_kernel,
        [
            shaped((groups, requests, block + TILE), bfloat),
            shaped((requests, features), bfloat),
        ],
        [gain],
        [*from_lanes(sent), hidden_block, mine, theirs],
        [*local_like(gain), copies((1,))],
        4 * requests * gate_weight.size,
    )
    (active,) = run(
        active_kernel, [shaped((requests, block // 2), bfloat)], [], [exchange(sent)]
    )
    (sent,) = run(
        down_kernel,
        [shaped((groups, requests, down_weight.shape[1]), bfloat)],
        [],
        [*from_lanes(active), down_weight, mid],
        [pltpu.VMEM((lanes,) + active.shape, bfloat)],
        2 * requests * down_weight.size,
    )
    (result,) = run(
        result_kernel, [shaped((requests, down_weight.shape[1]), bfloat)], [], [exchange(sent)]
    )
    return (compact, summaries, result)


def solution(mesh):
    placed = (
        P(None, "head"),
        P(),
        P(),
        P(),
        P(),
        P("req", "head"),
        P("req", "head"),
        P("req", "head"),
        P("req", "head"),
        P("req", "head"),
        P(("req", "head"), None, None),
        P(("req", "head"), None),
        P(("req", "head"), None),
        P(("req", "head"), None),
        P(),
        P("req", None),
        P(),
    )
    return jax.shard_map(
        on_device if mesh.shape["req"] <= DIRECT else on_device_wide,
        mesh=mesh,
        in_specs=placed,
        out_specs=(P(("req", "head"), None, None), P(("req", "head"), None), P(None, "head")),
        check_vma=False,
    )
```

```python
import jax
import jax.numpy as jnp
import numpy as np
from jax import lax
from jax.experimental import pallas as pl
from jax.experimental.pallas import tpu as pltpu
from jax.sharding import PartitionSpec as P

D = 2048
HEADS = 20
KVH = 5
HD = 64
FF = 5120
PAGE = 128
KEEP = 64
NP = 16
R_DEV = 2
KVW = 640

DIRECT = 8

epsilon = 1e-06
negative = -1e30
both_axes = ("req", "head")


def rms_scale(values):
    return lax.rsqrt(jnp.mean(values * values, axis=-1, keepdims=True) + epsilon)


def rms_rows(values, gain):
    return values * rms_scale(values) * gain


def rotate(vectors, positions):
    half = vectors.shape[-1] // 2
    frequency = 10000.0 ** (-jnp.arange(half, dtype=jnp.float32) / half)
    angles = positions.astype(jnp.float32)[:, None] * frequency[None, :]
    cosine = jnp.cos(angles)[:, None, :]
    sine = jnp.sin(angles)[:, None, :]
    first = vectors[..., :half]
    second = vectors[..., half:]
    return jnp.concatenate(
        [first * cosine - second * sine, second * cosine + first * sine], axis=-1
    )


def compact_pages(pages, keep, weights):
    rows = jnp.arange(pages.shape[1], dtype=jnp.int32)
    picks = keep[:, :, None] == rows[None, None, :]
    kept = jnp.einsum(
        "pkr,prc->pkc", picks.astype(jnp.bfloat16), pages, preferred_element_type=jnp.float32
    ).astype(jnp.bfloat16)
    dropped = weights * (1.0 - jnp.sum(picks.astype(jnp.float32), axis=1))
    total = jnp.sum(dropped, axis=1)
    means = (
        jnp.einsum(
            "pr,prc->pc", dropped, pages.astype(jnp.float32), precision=lax.Precision.HIGHEST
        )
        / total[:, None]
    )
    return (kept, means.astype(jnp.bfloat16), jnp.log(total))


def held_request(rows, source):
    half = R_DEV // 2
    position = rows % R_DEV
    slot = rows // R_DEV * half + position - half
    continued = jnp.arange(source.shape[0], dtype=jnp.int32)
    matches = source[None, :] == slot[:, None]
    owner_cont = jnp.sum(jnp.where(matches, continued[None, :], 0), axis=1)
    carried = owner_cont // half * R_DEV + half + owner_cont % half
    return jnp.where(position < half, rows, carried)


def pick_rows(order, rows):
    chosen = order[:, None] == jnp.arange(rows.shape[0], dtype=jnp.int32)[None, :]
    return jnp.dot(
        chosen.astype(jnp.bfloat16), rows, preferred_element_type=jnp.float32
    ).astype(jnp.bfloat16)


def exchange(parts):
    return lax.all_to_all(parts, "req", split_axis=0, concat_axis=0, tiled=True)


def to_block_owner(rows):
    groups = lax.axis_size("req")
    lanes = lax.axis_size("head")
    per_lane = groups // lanes
    pairs = [
        (g * lanes + h, (per_lane * h + g // lanes) * lanes + g % lanes)
        for g in range(groups)
        for h in range(lanes)
    ]
    return lax.ppermute(rows, both_axes, pairs)


def whole_sum(partial):
    if lax.axis_size("req") > DIRECT:
        return lax.psum(partial, "req")
    groups = lax.axis_size("req")
    return jnp.sum(exchange(jnp.broadcast_to(partial[None], (groups,) + partial.shape)), axis=0)


def on_device_wide(
    hidden_in,
    attention_gain,
    query_gain,
    key_gain,
    feedforward_gain,
    input_weight,
    output_weight,
    gate_weight,
    up_weight,
    down_weight,
    old_cache,
    keep_rows,
    drop_weights,
    dest_slots,
    lengths,
    page_table,
    source,
):
    groups = lax.axis_size("req")
    lanes = lax.axis_size("head")
    group = lax.axis_index("req")
    lane = lax.axis_index("head")
    requests = hidden_in.shape[0]
    half = R_DEV // 2
    split = KVH * HD
    ratio = HEADS // KVH
    scale = HD ** (-0.5)
    pages_here = old_cache.shape[0]
    everyone = jnp.arange(requests, dtype=jnp.int32)
    holders = held_request(everyone, source)
    held = lax.dynamic_slice_in_dim(holders, group * R_DEV, R_DEV, 0)
    held_len = lengths[held]
    positions = held_len * PAGE

    whole = lax.all_gather(hidden_in, "head", axis=1, tiled=True)
    normed = rms_rows(whole.astype(jnp.float32), attention_gain).astype(jnp.bfloat16)
    features = D // groups
    inputs = pick_rows(holders, lax.dynamic_slice_in_dim(normed, group * features, features, 1))
    partial_qkv = jnp.dot(inputs, input_weight, preferred_element_type=jnp.float32)
    sent = jnp.broadcast_to(
        partial_qkv.reshape(groups, 1, R_DEV, -1), (groups, lanes, R_DEV, partial_qkv.shape[1])
    ).reshape(groups * lanes, R_DEV, -1)
    got = lax.all_to_all(sent, both_axes, split_axis=0, concat_axis=0, tiled=True)
    mixed = jnp.sum(got.reshape(groups, lanes, R_DEV, -1), axis=0).astype(jnp.bfloat16)
    held_qkv = jnp.swapaxes(mixed, 0, 1).reshape(R_DEV, -1).astype(jnp.float32)

    query = rotate(
        rms_rows(held_qkv[:, : HEADS * HD].reshape(R_DEV, HEADS, HD), query_gain), positions
    ).astype(jnp.bfloat16)
    key_new = rotate(
        rms_rows(held_qkv[:, HEADS * HD : (HEADS + KVH) * HD].reshape(R_DEV, KVH, HD), key_gain),
        positions,
    ).astype(jnp.bfloat16)
    value_new = held_qkv[:, (HEADS + KVH) * HD :].reshape(R_DEV, KVH, HD)
    kept, means, bias = compact_pages(old_cache, keep_rows, drop_weights)
    destination = dest_slots[0]
    fresh_ids = jnp.arange(pages_here, dtype=jnp.int32)
    inverse = jnp.sum(
        jnp.where(destination[None, :] == fresh_ids[:, None], fresh_ids[None, :], 0), axis=1
    )
    compact = kept[inverse].reshape(pages_here // 2, PAGE, KVW)
    summaries = means[inverse]
    per_lane = NP // lanes
    table = page_table.reshape(R_DEV, per_lane, lanes)
    mine = lax.dynamic_slice_in_dim(table, lane, 1, 2)[:, :, 0]
    logical = jnp.arange(per_lane, dtype=jnp.int32) * lanes + lane
    live = logical[None, :] < held_len[:, None]
    owner = jnp.any((mine[:, :, None] == fresh_ids[None, None, :]) & live[:, :, None], axis=1)
    query_groups = query.reshape(R_DEV, KVH, ratio, HD)
    row_keys = kept[:, :, :split].reshape(pages_here, KEEP, KVH, HD)
    row_values = kept[:, :, split:].reshape(pages_here, KEEP, KVH, HD)
    row_live = keep_rows >= 0
    allowed = owner[:, None, None, :, None] & row_live[None, None, None, :, :]
    scores = (
        jnp.einsum("rngd,pmnd->rngpm", query_groups, row_keys, preferred_element_type=jnp.float32)
        * scale
    )
    scores = jnp.where(allowed, scores, negative)
    mean_keys = means[:, :split].reshape(pages_here, KVH, HD)
    mean_values = means[:, split:].reshape(pages_here, KVH, HD)
    mean_scores = (
        jnp.einsum("rngd,pnd->rngp", query_groups, mean_keys, preferred_element_type=jnp.float32)
        * scale
        + bias[None, None, None, :]
    )
    mean_allowed = owner[:, None, None, :]
    mean_scores = jnp.where(mean_allowed, mean_scores, negative)
    own_score = (
        jnp.einsum("rngd,rnd->rng", query_groups, key_new, preferred_element_type=jnp.float32)
        * scale
    )
    own_score = jnp.where(lane == 0, own_score, negative)
    top = jnp.maximum(jnp.max(scores, axis=(3, 4)), jnp.max(mean_scores, axis=3))
    top = jnp.maximum(top, own_score)
    row_weight = jnp.where(allowed, jnp.exp(scores - top[..., None, None]), 0.0)
    mean_weight = jnp.where(mean_allowed, jnp.exp(mean_scores - top[..., None]), 0.0)
    own_weight = jnp.where(lane == 0, jnp.exp(own_score - top), 0.0)
    mass = jnp.sum(row_weight, axis=(3, 4)) + jnp.sum(mean_weight, axis=3) + own_weight
    total = jnp.einsum(
        "rngpm,pmnd->rngd",
        row_weight,
        row_values.astype(jnp.float32),
        precision=lax.Precision.HIGHEST,
    )
    total = total + jnp.einsum(
        "rngp,pnd->rngd",
        mean_weight,
        mean_values.astype(jnp.float32),
        precision=lax.Precision.HIGHEST,
    )
    total = total + own_weight[..., None] * value_new[:, :, None, :]

    some = mass > 0.0
    level = jnp.where(some, top + jnp.log(jnp.where(some, mass, 1.0)), negative)
    means_out = total / jnp.where(some, mass, 1.0)[..., None]
    own = HEADS * HD // groups
    parts = jnp.stack([means_out, jnp.broadcast_to(level[..., None], total.shape)])
    parts = jnp.transpose(parts.reshape(2, R_DEV, groups, own), (2, 1, 0, 3))
    parts = jnp.broadcast_to(
        parts.reshape(groups, 1, R_DEV, 2 * own), (groups, lanes, R_DEV, 2 * own)
    ).reshape(groups * lanes, R_DEV, 2 * own)
    came = lax.all_to_all(parts, both_axes, 0, 0, tiled=True)
    came = came.reshape(groups, lanes, R_DEV, 2 * own)
    outs, levels = came[..., :own], came[..., own:]
    weights = jnp.exp(levels - jnp.max(levels, axis=1, keepdims=True))
    attention = jnp.sum(outs * weights, axis=1) / jnp.sum(weights, axis=1)
    attention = attention.reshape(requests, own).astype(jnp.bfloat16)
    back = jnp.sum(
        jnp.where(holders[None, :] == everyone[:, None], everyone[None, :], 0), axis=1
    )
    projected = jnp.dot(
        pick_rows(back, attention), output_weight, preferred_element_type=jnp.float32
    )
    projected = projected + jnp.where(group == 0, hidden_in.astype(jnp.float32), 0.0)

    share = groups // lanes
    blocks = jnp.moveaxis(projected.reshape(requests, share, 1, features), 0, 2)
    blocks = jnp.broadcast_to(blocks, (share, lanes, requests, features))
    mid = jnp.sum(exchange(blocks.reshape(groups, requests, features)), axis=0)
    mid = to_block_owner(mid.astype(jnp.bfloat16)).astype(jnp.float32)
    squares = jnp.sum(mid * mid, axis=1, keepdims=True)
    gain_here = lax.dynamic_slice_in_dim(feedforward_gain, group * features, features, 0)
    inputs_mid = (mid * gain_here).astype(jnp.bfloat16)
    local_units = gate_weight.shape[1]
    piece = local_units // groups
    gates = jnp.dot(inputs_mid, gate_weight, preferred_element_type=jnp.float32)
    ups = jnp.dot(inputs_mid, up_weight, preferred_element_type=jnp.float32)
    both = jnp.concatenate(
        [
            gates.reshape(requests, groups, piece),
            ups.reshape(requests, groups, piece),
            jnp.broadcast_to(squares[:, :, None], (requests, groups, 1)),
        ],
        axis=2,
    )
    sums = jnp.sum(exchange(jnp.swapaxes(both, 0, 1)), axis=0)
    factor = lax.rsqrt(sums[:, 2 * piece :] / D + epsilon)
    gate = sums[:, :piece] * factor
    active = (jax.nn.silu(gate) * (sums[:, piece : 2 * piece] * factor)).astype(jnp.bfloat16)
    active_here = lax.all_gather(to_block_owner(active), "head", axis=1, tiled=True)
    down = jnp.dot(active_here, down_weight, preferred_element_type=jnp.float32)
    residual = [jnp.where(group == lane * share + k, mid, 0.0) for k in range(share)]
    down = down + jnp.concatenate(residual, axis=1)
    result = whole_sum(down).astype(jnp.bfloat16)
    return (compact, summaries, result)


TILE = 128
bfloat = jnp.bfloat16
single = jnp.float32


TERMS = 4


def three_terms(value, place):
    high = value.astype(bfloat).astype(single)
    rest = value - high
    middle = rest.astype(bfloat).astype(single)
    low = jnp.where(place == 2, rest - middle, 0.0)
    return jnp.where(place == 0, high, jnp.where(place == 1, middle, low))


def iota(shape, axis):
    return lax.broadcasted_iota(jnp.int32, shape, axis)


def run(kernel, outs, far, near, scratch=(), flops=0):
    in_specs = [pl.BlockSpec(memory_space=pltpu.HBM) for _ in far]
    in_specs += [pl.BlockSpec(memory_space=pltpu.VMEM) for _ in near]
    moved = sum(a.size * a.dtype.itemsize for a in [*far, *near, *outs])
    return pl.pallas_call(
        kernel,
        out_shape=list(outs),
        in_specs=in_specs,
        out_specs=[pl.BlockSpec(memory_space=pltpu.VMEM) for _ in outs],
        scratch_shapes=list(scratch),
        compiler_params=pltpu.CompilerParams(vmem_limit_bytes=16 * 2**20),
        cost_estimate=pl.CostEstimate(flops=flops, bytes_accessed=moved, transcendentals=0),
    )(*[pltpu.with_memory_space_constraint(a, pltpu.HBM) for a in far], *near)


def fetch(sources, targets, done):
    copies = [
        pltpu.make_async_copy(source, target, done.at[k])
        for k, (source, target) in enumerate(zip(sources, targets))
    ]
    for copy in copies:
        copy.start()
    return copies


def local_like(*arrays):
    return [pltpu.VMEM(a.shape, a.dtype) for a in arrays]


def scalar_like(*arrays):
    return [pltpu.SMEM(a.shape, a.dtype) for a in arrays]


def row_order(source, count, to_holder):
    first, second = iota((count, count), 0), iota((count, count), 1)
    if not to_holder:
        first, second = second, first
    order = (first == second) & (first % R_DEV == 0)
    for c in range(source.shape[1]):
        order = order | ((first == source[0, c] * R_DEV + 1) & (second == c * R_DEV + 1))
    return order.astype(single).astype(bfloat)


def shaped(shape, dtype):
    return jax.ShapeDtypeStruct(shape, dtype)


def first_kernel(
    source_far, gain_far, weight_far, hidden_far, one, two, three, sent, block, source, gain,
    weight, hidden, lanes_of, wide, done
):
    copies = fetch(
        (source_far, gain_far, weight_far, hidden_far), (source, gain, weight, hidden), done
    )
    rows = hidden.shape[0]
    groups = rows // R_DEV
    lanes = sent.shape[0] // groups
    columns, features = weight.shape
    group = lax.axis_index("req")
    share = groups // lanes
    squares = 0.0
    for turn, values in enumerate((one, two, three)):
        values = values[...].astype(single)
        lanes_of[turn + 1] = values
        squares = squares + jnp.sum(values * values, axis=1, keepdims=True)
    copies[3].wait()
    values = hidden[...].astype(single)
    lanes_of[0] = values
    squares = squares + jnp.sum(values * values, axis=1, keepdims=True)
    factor = lax.rsqrt(squares / D + epsilon)
    here = pl.ds(pl.multiple_of(group * features, features), features)
    within = pl.ds(pl.multiple_of(group % share * features, features), features)
    mine = lanes_of[group // share ^ lax.axis_index("head"), :, within]
    block[...] = mine.astype(bfloat)
    wide[...] = jnp.zeros_like(wide)
    for copy in copies[:3]:
        copy.wait()
    normed = (mine * factor * gain[:, here]).astype(bfloat)
    order = row_order(source, rows, True)
    normed = jnp.dot(order, normed, preferred_element_type=single).astype(bfloat)
    wide[:, :columns] = dot_rows(normed, weight[...])
    for g in range(groups):
        tile = jnp.concatenate(
            [
                wide[R_DEV * g : R_DEV * (g + 1), TILE * j : TILE * (j + 1)]
                for j in range(wide.shape[1] // TILE)
            ],
            axis=0,
        )
        for k in range(lanes):
            sent[g * lanes + k] = tile


def dot_rows(left, right):
    return lax.dot_general(left, right, (((1,), (1,)), ((), ())), preferred_element_type=single)


def prepare_kernel(*refs):
    far, refs = refs[:10], refs[10:]
    (compact, summaries, kept, added, tables), refs = refs[:5], refs[5:]
    near, (ordered, plain, done) = refs[:10], refs[10:]
    copies = fetch(far, near, done)
    (dest, lengths, source, table, keep, weights, query_gain, key_gain, turns) = near[:9]
    pages = near[9]
    group = lax.axis_index("req")
    lane = lax.axis_index("head")
    lanes = lax.axis_size("head")
    for copy in copies[:9]:
        copy.wait()

    carried = 0
    for c in range(source.shape[1]):
        carried = carried + jnp.where(source[0, c] == group, c, 0)
    held_len = (lengths[0, group * R_DEV], lengths[0, carried * R_DEV + 1])
    count, rows, _ = pages.shape
    owned = []
    for r in range(R_DEV):
        slots = []
        for i in range(table.shape[1] // lanes):
            j = i * lanes + lane
            slots.append(jnp.where(j < held_len[r], table[r, j], -1))
        owned.append(slots)

    def owner(r, p):
        found = owned[r][0] == p
        for slot in owned[r][1:]:
            found = found | (slot == p)
        return found

    row = iota((32, TILE), 0)
    odd = (row & 1) == 1
    half_rows = turns.shape[0] // 2
    for part in range(2):
        pair = [turns[pl.ds(part * half_rows + held_len[r], 1), :] for r in range(R_DEV)]
        tables[32 * part : 32 * (part + 1), :] = jnp.where(odd, pair[1], pair[0])
    query_rows = HEADS * HD // TILE * R_DEV
    for c in range(TILE // HD):
        columns = slice(HD * c, HD * (c + 1))
        tables[64 : 64 + query_rows, columns] = jnp.broadcast_to(
            query_gain[...], (query_rows, HD)
        )
        tables[64 + query_rows : 96, columns] = jnp.broadcast_to(
            key_gain[...], (32 - query_rows, HD)
        )

    column = iota((1, TILE), 1)
    entries = count * KEEP
    added[...] = jnp.full_like(added, negative)
    extra = [
        jnp.where((column == count + r) & (lane == 0), 0.0, negative) for r in range(R_DEV)
    ]
    weight_columns = weights[...].T
    rows_of = iota((rows, KEEP), 0)
    place = iota((rows, 16), 1)
    copies[9].wait()
    for p in range(count):
        picks = (keep[p : p + 1, :] == rows_of).astype(single)
        dropped = weight_columns[:, p : p + 1] * (1.0 - jnp.sum(picks, axis=1, keepdims=True))
        total = jnp.sum(dropped, axis=0, keepdims=True)
        left = jnp.concatenate([picks, three_terms(dropped, place)], axis=1).astype(bfloat)
        both = lax.dot_general(
            left, pages[p], (((0,), (0,)), ((), ())), preferred_element_type=single
        )
        rows_kept = both[:KEEP].astype(bfloat)
        kept[KEEP * p : KEEP * (p + 1), :] = rows_kept
        slot = dest[0, p]
        start = pl.multiple_of((slot & 1) * KEEP, KEEP)
        compact[slot >> 1, pl.ds(start, KEEP), :] = rows_kept
        mean = both[KEEP : KEEP + 1] + both[KEEP + 1 : KEEP + 2] + both[KEEP + 2 : KEEP + 3]
        mean = mean / total
        plain[p : p + 1, :] = mean
        ordered[pl.ds(slot, 1), :] = mean
        live = jnp.where(keep[p : p + 1, :] >= 0, 0.0, negative)
        for r in range(R_DEV):
            here = owner(r, p)
            added[r : r + 1, KEEP * p : KEEP * (p + 1)] = jnp.where(here, live, negative)
            level = jnp.where(here, jnp.log(total), negative)
            extra[r] = jnp.where(column == p, level, extra[r])
    for r in range(R_DEV):
        added[r : r + 1, entries : entries + TILE] = extra[r]
    plain[count:, :] = jnp.zeros_like(plain[count:, :])
    kept[entries:, :] = plain[...].astype(bfloat)
    summaries[...] = ordered[...].astype(bfloat)


def deal_kernel(gate_far, up_far, mine, theirs, gate, up, dealt, done):
    for copy in fetch((gate_far, up_far), (gate, up), done):
        copy.wait()
    block = gate.shape[1] // 2
    piece = block // 2
    for k in range(2):
        for b in range(2):
            columns = slice(b * block + k * piece, b * block + (k + 1) * piece)
            start = b * block
            dealt[k, :, start : start + piece] = gate[:, columns].astype(single)
            dealt[k, :, start + piece : start + block] = up[:, columns].astype(single)
    core = lax.axis_index("head") & 1
    mine[...] = dealt[core].astype(bfloat)
    theirs[...] = dealt[1 - core].astype(bfloat)


def attend_kernel(came, kept, added, tables, sent, x, extra_k, extra_v, out, logs):
    lanes = lax.axis_size("head")
    groups = came.shape[0] // lanes
    width = (HEADS + 2 * KVH) * HD // lanes
    span = -(-KVH * HD // TILE) * TILE
    key_cols = slice(0, span)
    value_cols = slice(KVW - span, KVW)
    first_key = HEADS * HD // TILE * R_DEV
    scale = HD ** (-0.5)
    x[...] = jnp.zeros_like(x)
    column = iota((8, TILE), 1)
    for k in range(lanes):
        tile = came[k].astype(single)
        for g in range(1, groups):
            tile = tile + came[g * lanes + k].astype(single)
        tile = tile.astype(bfloat).astype(single)
        base, shift = divmod(width * k, TILE)
        base = base * R_DEV
        if shift:
            tile = pltpu.roll(tile, shift, 1)
            x[base + 2 : base + 10, :] += jnp.where(column < shift, tile, 0.0)
        x[base : base + 8, :] += jnp.where(column >= shift, tile, 0.0)
    values = x[...]
    same_head = (iota((TILE, TILE), 0) // HD == iota((TILE, TILE), 1) // HD).astype(single)
    squares = jnp.dot(
        values * values, same_head, precision=lax.Precision.HIGHEST, preferred_element_type=single
    )
    normed = values * lax.rsqrt(squares / HD + epsilon) * tables[64:96, :]
    early = iota(values.shape, 1) % HD < HD // 2
    swapped = jnp.where(
        early, pltpu.roll(normed, TILE - HD // 2, 1), pltpu.roll(normed, HD // 2, 1)
    )
    turned = normed * tables[0:32, :] + swapped * tables[32:64, :]
    turned = turned.astype(bfloat).astype(single)

    rows = 24
    row = iota((rows, TILE), 0)
    half = iota((rows, TILE), 1) // HD
    key_head = row >> 2
    query = jnp.where(row < first_key, turned[:rows], 0.0)
    other = pltpu.roll(query, HD, 1)
    queries = []
    for u in range(2):
        placed = jnp.where(
            half == (key_head & 1), jnp.where((key_head & 1) == u, query, other), 0.0
        )
        queries.append(
            jnp.concatenate(
                [jnp.where((key_head >> 1) == c, placed, 0.0) for c in range(span // TILE)], axis=1
            )
        )
    queries = jnp.concatenate(queries, axis=0).astype(bfloat)

    extras = extra_k.shape[0]
    entries = kept.shape[0] - extras
    count = entries // KEEP
    extra_k[...] = kept[entries:, key_cols].astype(single)
    extra_v[...] = kept[entries:, value_cols].astype(single)
    first_value = first_key + KVH * HD // TILE * R_DEV
    for c in range(span // TILE):
        at = slice(c * TILE, (c + 1) * TILE)
        r = first_key + R_DEV * c
        extra_k[count : count + R_DEV, at] = turned[r : r + R_DEV]
        r = first_value + R_DEV * c
        extra_v[count : count + R_DEV, at] = values[r : r + R_DEV]

    def by_request(columns, size):
        odd = (iota((2 * rows, size), 0) & 1) == 1
        return jnp.where(odd, added[1:2, columns], added[0:1, columns])

    scores = dot_rows(queries, kept[:entries, key_cols]) * scale
    scores = scores + by_request(slice(0, entries), entries)
    extra = dot_rows(queries, extra_k[...].astype(bfloat)) * scale
    extra = extra + by_request(slice(entries, entries + extras), extras)
    top = jnp.maximum(
        jnp.max(scores, axis=1, keepdims=True), jnp.max(extra, axis=1, keepdims=True)
    )
    weight = jnp.where(scores > 0.5 * negative, jnp.exp(scores - top), 0.0)
    extra_weight = jnp.where(extra > 0.5 * negative, jnp.exp(extra - top), 0.0)
    mass = jnp.sum(weight, axis=1, keepdims=True) + jnp.sum(extra_weight, axis=1, keepdims=True)

    def weighted(parts, right):
        high = parts.astype(bfloat)
        low = (parts - high.astype(single)).astype(bfloat)
        return jnp.dot(high, right, preferred_element_type=single) + jnp.dot(
            low, right, preferred_element_type=single
        )

    total = weighted(weight, kept[:entries, value_cols]) + weighted(
        extra_weight, extra_v[...].astype(bfloat)
    )
    some = mass > 0.0
    mass = jnp.where(some, mass, 1.0)
    total = total / mass
    level = jnp.where(some, top + jnp.log(mass), negative)

    slot = key_head + (KVW // 2 - (KVW - span)) // HD
    results = []
    for u in range(2):
        mine = total[rows * u : rows * (u + 1)]
        picked = mine[:, :TILE]
        for c in range(1, span // TILE):
            picked = jnp.where((slot >> 1) == c, mine[:, c * TILE : (c + 1) * TILE], picked)
        results.append(jnp.where((slot & 1) == u, picked, pltpu.roll(picked, HD, 1)))
    out[...] = jnp.where(half == 0, results[0], results[1])
    logs[...] = jnp.broadcast_to(level, logs.shape)
    own = HEADS * HD // lanes
    size = 6
    column = iota((size, TILE), 1)
    here = column // TERMS == iota((size, TILE), 0)
    for k in range(lanes):
        r = own * k // TILE * R_DEV
        tile = [out[r : r + size, :]]
        for u in range(2):
            coded = three_terms(logs[rows * u + r : rows * u + r + size, :], column % TERMS)
            tile.append(jnp.sum(jnp.where(here, coded, 0.0), axis=0, keepdims=True))
        tile = jnp.concatenate(tile, axis=0).astype(bfloat)
        for g in range(groups):
            sent[g * lanes + k] = tile


def blocks_kernel(weight_far, same, other, done):
    width = same.shape[1]
    group = lax.axis_index("req")
    starts = [pl.multiple_of(((group & 1) ^ turn) * width, width) for turn in range(2)]
    parts = [weight_far.at[:, pl.ds(start, width)] for start in starts]
    for copy in fetch(parts, (same, other), done):
        copy.wait()


def project_kernel(source_far, came, first, second, sent, source, logs, rows, pieces, done):
    (copy,) = fetch((source_far,), (source,), done)
    lanes = lax.axis_size("head")
    groups = came.shape[0] // lanes
    group = lax.axis_index("req")
    features = first.shape[0]
    requests = rows.shape[0]
    size = 6
    tiles = [came[d].astype(single) for d in range(groups * lanes)]
    for g in range(groups):
        for k in range(lanes):
            logs[k, 2 * g : 2 * g + 2, :] = tiles[g * lanes + k][size:]
    spread = (iota((8, TILE), 1) // TERMS == iota((8, TILE), 0)).astype(single).astype(bfloat)
    levels = [dot_rows(spread, logs[k].astype(bfloat)) for k in range(lanes)]
    top = jnp.maximum(jnp.maximum(levels[0], levels[1]), jnp.maximum(levels[2], levels[3]))
    shares = [jnp.exp(level - top) for level in levels]
    mass = sum(shares)
    shares = [share / mass for share in shares]
    lower = iota((8, TILE), 1) < HD
    for g in range(groups):
        mixed = 0.0
        for k in range(lanes):
            share = shares[k]
            share = jnp.where(lower, share[:, 2 * g : 2 * g + 1], share[:, 2 * g + 1 : 2 * g + 2])
            mixed = mixed + share * tiles[g * lanes + k]
        for j in range(size // R_DEV):
            rows[R_DEV * g : R_DEV * (g + 1), TILE * j : TILE * (j + 1)] = mixed[
                R_DEV * j : R_DEV * (j + 1)
            ]
    width = rows.shape[1]
    shift = lax.rem(lax.axis_index("head") * (2 * features), TILE)
    attention = rows[...].astype(bfloat).astype(single)
    attention = pltpu.roll(attention, lax.rem(width - shift, width), 1)
    copy.wait()
    order = row_order(source, requests, False)
    attention = jnp.dot(order, attention.astype(bfloat), preferred_element_type=single)
    for b in range(2):
        pieces[b] = attention[:, features * b : features * (b + 1)]
    total = 0.0
    for turn, weight in enumerate((first, second)):
        piece = pieces[(group & 1) ^ turn].astype(bfloat)
        total = total + jnp.dot(piece, weight[...], preferred_element_type=single)
    sent[...] = total


def units_kernel(
    gain_far, own, one, two, three, hidden, mine, theirs, sent, mid_out, gain, done
):
    (copy,) = fetch((gain_far,), (gain,), done)
    rows, features = own.shape
    share = sent.shape[0] // lax.axis_size("head")
    group = lax.axis_index("req")
    lane = lax.axis_index("head")
    here = pl.ds(pl.multiple_of(group * features, features), features)
    mid = (own[...] + one[...]) + (two[...] + three[...])
    mid = (hidden[...].astype(single) + mid).astype(bfloat)
    mid_out[...] = mid
    mid = mid.astype(single)
    squares = jnp.sum(mid * mid, axis=1, keepdims=True)
    block = mine.shape[1] // share
    terms = three_terms(squares, iota((rows, sent.shape[2] - block), 1)).astype(bfloat)
    copy.wait()
    inputs = (mid * gain[:, here]).astype(bfloat)
    for turn, weight in enumerate((mine, theirs)):
        units = jnp.dot(inputs, weight[...], preferred_element_type=single).astype(bfloat)
        target = (lane ^ turn) * share
        for b in range(share):
            sent[target + b, :, :block] = units[:, block * b : block * (b + 1)]
            sent[target + b, :, block:] = terms


def active_kernel(came, active):
    total = came[0].astype(single)
    for g in range(1, came.shape[0]):
        total = total + came[g].astype(single)
    piece = active.shape[1]
    squares = jnp.sum(total[:, 2 * piece : 2 * piece + 3], axis=1, keepdims=True)
    factor = lax.rsqrt(squares / D + epsilon)
    gate = total[:, :piece] * factor
    up = total[:, piece : 2 * piece] * factor
    active[...] = (gate / (1.0 + jnp.exp(-gate)) * up).astype(bfloat)


def down_kernel(own, one, two, three, weight, mid, sent, active):
    groups, rows, width = sent.shape
    piece = own.shape[1]
    half = mid.shape[1]
    for turn, values in enumerate((own, one, two, three)):
        active[turn] = values[...]
    share = width // half
    group = lax.axis_index("req")
    lane = lax.axis_index("head")
    first = group // (2 * share) * 2 ^ lane
    down = jnp.dot(active[first], weight[:piece, :], preferred_element_type=single)
    down = down + jnp.dot(active[first ^ 1], weight[piece:, :], preferred_element_type=single)
    residual = mid[...].astype(single)
    for b in range(share):
        columns = slice(half * b, half * (b + 1))
        mine = group == lane * share + b
        total = (down[:, columns] + jnp.where(mine, residual, 0.0)).astype(bfloat)
        for g in range(groups):
            sent[g, :, columns] = total


def result_kernel(came, result):
    total = came[0].astype(single)
    for g in range(1, came.shape[0]):
        total = total + came[g].astype(single)
    result[...] = total.astype(bfloat)


def rotation_table():
    half = HD // 2
    size = -(-(NP + 1) // 8) * 8
    frequency = 10000.0 ** (-np.arange(half) / half)
    angles = PAGE * np.arange(size)[:, None] * frequency[None, :]
    cosine, sine = np.cos(angles), np.sin(angles)
    wide = [np.tile(np.concatenate(pair, axis=1), (1, TILE // HD)) for pair in
            ((cosine, cosine), (-sine, sine))]
    return jnp.asarray(np.concatenate(wide), dtype=single)


def swapped_lanes(value, turn):
    lanes = lax.axis_size("head")
    return lax.ppermute(value, "head", [(k, k ^ turn) for k in range(lanes)])


def from_lanes(value):
    return [value] + [swapped_lanes(value, turn) for turn in range(1, lax.axis_size("head"))]


def handed_over(value, turn):
    groups = lax.axis_size("req")
    lanes = lax.axis_size("head")
    share = groups // lanes
    pairs = [
        (g * lanes + h, (share * h + ((g & 1) ^ turn)) * lanes + g // share)
        for g in range(groups)
        for h in range(lanes)
    ]
    return lax.ppermute(value, both_axes, pairs)


def on_device(
    hidden_in,
    attention_gain,
    query_gain,
    key_gain,
    feedforward_gain,
    input_weight,
    output_weight,
    gate_weight,
    up_weight,
    down_weight,
    old_cache,
    keep_rows,
    drop_weights,
    dest_slots,
    lengths,
    page_table,
    source,
):
    groups = lax.axis_size("req")
    lanes = lax.axis_size("head")
    requests = hidden_in.shape[0]
    pages_here = old_cache.shape[0]
    devices = groups * lanes
    features = D // groups
    copies = pltpu.SemaphoreType.DMA

    others = from_lanes(hidden_in)[1:]
    blocks = run(
        blocks_kernel,
        [shaped((output_weight.shape[0], features), bfloat)] * 2,
        [output_weight],
        [],
        [copies((2,))],
    )
    handed = [handed_over(block, turn) for turn, block in enumerate(blocks)]
    scalars = [dest_slots, lengths[None, :], source[None, :], page_table]
    arrays = [
        keep_rows,
        drop_weights,
        query_gain[None, :],
        key_gain[None, :],
        rotation_table(),
        old_cache,
    ]
    entries = pages_here * KEEP
    extras = 16
    compact, summaries, kept, added, tables = run(
        prepare_kernel,
        [
            shaped((pages_here // 2, PAGE, KVW), bfloat),
            shaped((pages_here, KVW), bfloat),
            shaped((entries + extras, KVW), bfloat),
            shaped((8, entries + TILE), single),
            shaped((96, TILE), single),
        ],
        scalars + arrays,
        [],
        [
            *scalar_like(*scalars),
            *local_like(*arrays),
            pltpu.VMEM((pages_here, KVW), single),
            pltpu.VMEM((extras, KVW), single),
            copies((len(scalars + arrays),)),
        ],
        2 * pages_here * TILE * PAGE * KVW,
    )
    tables, *moved = lax.optimization_barrier((tables, *others, *handed))
    others, handed = moved[: lanes - 1], moved[lanes - 1 :]

    holds = source[None, :]
    columns = input_weight.shape[1]
    padded = -(-columns // TILE) * TILE
    gain = attention_gain[None, :]
    weight = input_weight.T
    far = [holds, gain, weight, hidden_in]
    sent, hidden_block = run(
        first_kernel,
        [
            shaped((devices, R_DEV * padded // TILE, TILE), single),
            shaped((requests, features), bfloat),
        ],
        far,
        others,
        [
            *scalar_like(holds),
            *local_like(*far[1:]),
            pltpu.VMEM((lanes,) + hidden_in.shape, single),
            pltpu.VMEM((requests, padded), single),
            copies((len(far),)),
        ],
        2 * requests * features * columns,
    )
    came = lax.all_to_all(sent, both_axes, 0, 0, tiled=True)
    gates, _ = lax.optimization_barrier((gate_weight, sent))
    mine, theirs = run(
        deal_kernel,
        [shaped(gate_weight.shape, bfloat)] * 2,
        [gates, up_weight],
        [],
        [
            *local_like(gate_weight, up_weight),
            pltpu.VMEM((2,) + gate_weight.shape, single),
            copies((2,)),
        ],
    )
    span = -(-KVH * HD // TILE) * TILE
    (parts,) = run(
        attend_kernel,
        [shaped((devices, 8, TILE), bfloat)],
        [],
        [came, kept, added, tables],
        [
            pltpu.VMEM((32, TILE), single),
            pltpu.VMEM((extras, span), single),
            pltpu.VMEM((extras, span), single),
            pltpu.VMEM((24, TILE), single),
            pltpu.VMEM((48, TILE), single),
        ],
        6 * 48 * entries * span,
    )
    theirs, _ = lax.optimization_barrier((theirs, parts))
    theirs = swapped_lanes(theirs, 1)
    came = lax.all_to_all(parts, both_axes, 0, 0, tiled=True)
    came, theirs = lax.optimization_barrier((came, theirs))
    (sent,) = run(
        project_kernel,
        [shaped((requests, features), single)],
        [holds],
        [came, *handed],
        [
            *scalar_like(holds),
            pltpu.VMEM((lanes, 2 * groups, TILE), single),
            pltpu.VMEM((requests, 3 * TILE), single),
            pltpu.VMEM((2, requests, output_weight.shape[0]), single),
            copies((1,)),
        ],
        2 * requests * output_weight.size,
    )
    gain = feedforward_gain[None, :]
    block = gate_weight.shape[1] // 2
    sent, mid = run(
        units_kernel,
        [
            shaped((groups, requests, block + TILE), bfloat),
            shaped((requests, features), bfloat),
        ],
        [gain],
        [*from_lanes(sent), hidden_block, mine, theirs],
        [*local_like(gain), copies((1,))],
        4 * requests * gate_weight.size,
    )
    (active,) = run(
        active_kernel, [shaped((requests, block // 2), bfloat)], [], [exchange(sent)]
    )
    (sent,) = run(
        down_kernel,
        [shaped((groups, requests, down_weight.shape[1]), bfloat)],
        [],
        [*from_lanes(active), down_weight, mid],
        [pltpu.VMEM((lanes,) + active.shape, bfloat)],
        2 * requests * down_weight.size,
    )
    (result,) = run(
        result_kernel, [shaped((requests, down_weight.shape[1]), bfloat)], [], [exchange(sent)]
    )
    return (compact, summaries, result)


def solution(mesh):
    placed = (
        P(None, "head"),
        P(),
        P(),
        P(),
        P(),
        P("req", "head"),
        P("req", "head"),
        P("req", "head"),
        P("req", "head"),
        P("req", "head"),
        P(("req", "head"), None, None),
        P(("req", "head"), None),
        P(("req", "head"), None),
        P(("req", "head"), None),
        P(),
        P("req", None),
        P(),
    )
    return jax.shard_map(
        on_device if mesh.shape["req"] <= DIRECT else on_device_wide,
        mesh=mesh,
        in_specs=placed,
        out_specs=(P(("req", "head"), None, None), P(("req", "head"), None), P(None, "head")),
        check_vma=False,
    )
```

```python
import jax
import jax.numpy as jnp
import numpy as np
from jax import lax
from jax.experimental import pallas as pl
from jax.experimental.pallas import tpu as pltpu
from jax.sharding import PartitionSpec as P

D = 2048
HEADS = 20
KVH = 5
HD = 64
FF = 5120
PAGE = 128
KEEP = 64
NP = 16
R_DEV = 2
KVW = 640

DIRECT = 8

epsilon = 1e-06
negative = -1e30
both_axes = ("req", "head")


def rms_scale(values):
    return lax.rsqrt(jnp.mean(values * values, axis=-1, keepdims=True) + epsilon)


def rms_rows(values, gain):
    return values * rms_scale(values) * gain


def rotate(vectors, positions):
    half = vectors.shape[-1] // 2
    frequency = 10000.0 ** (-jnp.arange(half, dtype=jnp.float32) / half)
    angles = positions.astype(jnp.float32)[:, None] * frequency[None, :]
    cosine = jnp.cos(angles)[:, None, :]
    sine = jnp.sin(angles)[:, None, :]
    first = vectors[..., :half]
    second = vectors[..., half:]
    return jnp.concatenate(
        [first * cosine - second * sine, second * cosine + first * sine], axis=-1
    )


def compact_pages(pages, keep, weights):
    rows = jnp.arange(pages.shape[1], dtype=jnp.int32)
    picks = keep[:, :, None] == rows[None, None, :]
    kept = jnp.einsum(
        "pkr,prc->pkc", picks.astype(jnp.bfloat16), pages, preferred_element_type=jnp.float32
    ).astype(jnp.bfloat16)
    dropped = weights * (1.0 - jnp.sum(picks.astype(jnp.float32), axis=1))
    total = jnp.sum(dropped, axis=1)
    means = (
        jnp.einsum(
            "pr,prc->pc", dropped, pages.astype(jnp.float32), precision=lax.Precision.HIGHEST
        )
        / total[:, None]
    )
    return (kept, means.astype(jnp.bfloat16), jnp.log(total))


def held_request(rows, source):
    half = R_DEV // 2
    position = rows % R_DEV
    slot = rows // R_DEV * half + position - half
    continued = jnp.arange(source.shape[0], dtype=jnp.int32)
    matches = source[None, :] == slot[:, None]
    owner_cont = jnp.sum(jnp.where(matches, continued[None, :], 0), axis=1)
    carried = owner_cont // half * R_DEV + half + owner_cont % half
    return jnp.where(position < half, rows, carried)


def pick_rows(order, rows):
    chosen = order[:, None] == jnp.arange(rows.shape[0], dtype=jnp.int32)[None, :]
    return jnp.dot(
        chosen.astype(jnp.bfloat16), rows, preferred_element_type=jnp.float32
    ).astype(jnp.bfloat16)


def exchange(parts):
    return lax.all_to_all(parts, "req", split_axis=0, concat_axis=0, tiled=True)


def to_block_owner(rows):
    groups = lax.axis_size("req")
    lanes = lax.axis_size("head")
    per_lane = groups // lanes
    pairs = [
        (g * lanes + h, (per_lane * h + g // lanes) * lanes + g % lanes)
        for g in range(groups)
        for h in range(lanes)
    ]
    return lax.ppermute(rows, both_axes, pairs)


def whole_sum(partial):
    if lax.axis_size("req") > DIRECT:
        return lax.psum(partial, "req")
    groups = lax.axis_size("req")
    return jnp.sum(exchange(jnp.broadcast_to(partial[None], (groups,) + partial.shape)), axis=0)


def on_device_wide(
    hidden_in,
    attention_gain,
    query_gain,
    key_gain,
    feedforward_gain,
    input_weight,
    output_weight,
    gate_weight,
    up_weight,
    down_weight,
    old_cache,
    keep_rows,
    drop_weights,
    dest_slots,
    lengths,
    page_table,
    source,
):
    groups = lax.axis_size("req")
    lanes = lax.axis_size("head")
    group = lax.axis_index("req")
    lane = lax.axis_index("head")
    requests = hidden_in.shape[0]
    half = R_DEV // 2
    split = KVH * HD
    ratio = HEADS // KVH
    scale = HD ** (-0.5)
    pages_here = old_cache.shape[0]
    everyone = jnp.arange(requests, dtype=jnp.int32)
    holders = held_request(everyone, source)
    held = lax.dynamic_slice_in_dim(holders, group * R_DEV, R_DEV, 0)
    held_len = lengths[held]
    positions = held_len * PAGE

    whole = lax.all_gather(hidden_in, "head", axis=1, tiled=True)
    normed = rms_rows(whole.astype(jnp.float32), attention_gain).astype(jnp.bfloat16)
    features = D // groups
    inputs = pick_rows(holders, lax.dynamic_slice_in_dim(normed, group * features, features, 1))
    partial_qkv = jnp.dot(inputs, input_weight, preferred_element_type=jnp.float32)
    sent = jnp.broadcast_to(
        partial_qkv.reshape(groups, 1, R_DEV, -1), (groups, lanes, R_DEV, partial_qkv.shape[1])
    ).reshape(groups * lanes, R_DEV, -1)
    got = lax.all_to_all(sent, both_axes, split_axis=0, concat_axis=0, tiled=True)
    mixed = jnp.sum(got.reshape(groups, lanes, R_DEV, -1), axis=0).astype(jnp.bfloat16)
    held_qkv = jnp.swapaxes(mixed, 0, 1).reshape(R_DEV, -1).astype(jnp.float32)

    query = rotate(
        rms_rows(held_qkv[:, : HEADS * HD].reshape(R_DEV, HEADS, HD), query_gain), positions
    ).astype(jnp.bfloat16)
    key_new = rotate(
        rms_rows(held_qkv[:, HEADS * HD : (HEADS + KVH) * HD].reshape(R_DEV, KVH, HD), key_gain),
        positions,
    ).astype(jnp.bfloat16)
    value_new = held_qkv[:, (HEADS + KVH) * HD :].reshape(R_DEV, KVH, HD)
    kept, means, bias = compact_pages(old_cache, keep_rows, drop_weights)
    destination = dest_slots[0]
    fresh_ids = jnp.arange(pages_here, dtype=jnp.int32)
    inverse = jnp.sum(
        jnp.where(destination[None, :] == fresh_ids[:, None], fresh_ids[None, :], 0), axis=1
    )
    compact = kept[inverse].reshape(pages_here // 2, PAGE, KVW)
    summaries = means[inverse]
    per_lane = NP // lanes
    table = page_table.reshape(R_DEV, per_lane, lanes)
    mine = lax.dynamic_slice_in_dim(table, lane, 1, 2)[:, :, 0]
    logical = jnp.arange(per_lane, dtype=jnp.int32) * lanes + lane
    live = logical[None, :] < held_len[:, None]
    owner = jnp.any((mine[:, :, None] == fresh_ids[None, None, :]) & live[:, :, None], axis=1)
    query_groups = query.reshape(R_DEV, KVH, ratio, HD)
    row_keys = kept[:, :, :split].reshape(pages_here, KEEP, KVH, HD)
    row_values = kept[:, :, split:].reshape(pages_here, KEEP, KVH, HD)
    row_live = keep_rows >= 0
    allowed = owner[:, None, None, :, None] & row_live[None, None, None, :, :]
    scores = (
        jnp.einsum("rngd,pmnd->rngpm", query_groups, row_keys, preferred_element_type=jnp.float32)
        * scale
    )
    scores = jnp.where(allowed, scores, negative)
    mean_keys = means[:, :split].reshape(pages_here, KVH, HD)
    mean_values = means[:, split:].reshape(pages_here, KVH, HD)
    mean_scores = (
        jnp.einsum("rngd,pnd->rngp", query_groups, mean_keys, preferred_element_type=jnp.float32)
        * scale
        + bias[None, None, None, :]
    )
    mean_allowed = owner[:, None, None, :]
    mean_scores = jnp.where(mean_allowed, mean_scores, negative)
    own_score = (
        jnp.einsum("rngd,rnd->rng", query_groups, key_new, preferred_element_type=jnp.float32)
        * scale
    )
    own_score = jnp.where(lane == 0, own_score, negative)
    top = jnp.maximum(jnp.max(scores, axis=(3, 4)), jnp.max(mean_scores, axis=3))
    top = jnp.maximum(top, own_score)
    row_weight = jnp.where(allowed, jnp.exp(scores - top[..., None, None]), 0.0)
    mean_weight = jnp.where(mean_allowed, jnp.exp(mean_scores - top[..., None]), 0.0)
    own_weight = jnp.where(lane == 0, jnp.exp(own_score - top), 0.0)
    mass = jnp.sum(row_weight, axis=(3, 4)) + jnp.sum(mean_weight, axis=3) + own_weight
    total = jnp.einsum(
        "rngpm,pmnd->rngd",
        row_weight,
        row_values.astype(jnp.float32),
        precision=lax.Precision.HIGHEST,
    )
    total = total + jnp.einsum(
        "rngp,pnd->rngd",
        mean_weight,
        mean_values.astype(jnp.float32),
        precision=lax.Precision.HIGHEST,
    )
    total = total + own_weight[..., None] * value_new[:, :, None, :]

    some = mass > 0.0
    level = jnp.where(some, top + jnp.log(jnp.where(some, mass, 1.0)), negative)
    means_out = total / jnp.where(some, mass, 1.0)[..., None]
    own = HEADS * HD // groups
    parts = jnp.stack([means_out, jnp.broadcast_to(level[..., None], total.shape)])
    parts = jnp.transpose(parts.reshape(2, R_DEV, groups, own), (2, 1, 0, 3))
    parts = jnp.broadcast_to(
        parts.reshape(groups, 1, R_DEV, 2 * own), (groups, lanes, R_DEV, 2 * own)
    ).reshape(groups * lanes, R_DEV, 2 * own)
    came = lax.all_to_all(parts, both_axes, 0, 0, tiled=True)
    came = came.reshape(groups, lanes, R_DEV, 2 * own)
    outs, levels = came[..., :own], came[..., own:]
    weights = jnp.exp(levels - jnp.max(levels, axis=1, keepdims=True))
    attention = jnp.sum(outs * weights, axis=1) / jnp.sum(weights, axis=1)
    attention = attention.reshape(requests, own).astype(jnp.bfloat16)
    back = jnp.sum(
        jnp.where(holders[None, :] == everyone[:, None], everyone[None, :], 0), axis=1
    )
    projected = jnp.dot(
        pick_rows(back, attention), output_weight, preferred_element_type=jnp.float32
    )
    projected = projected + jnp.where(group == 0, hidden_in.astype(jnp.float32), 0.0)

    share = groups // lanes
    blocks = jnp.moveaxis(projected.reshape(requests, share, 1, features), 0, 2)
    blocks = jnp.broadcast_to(blocks, (share, lanes, requests, features))
    mid = jnp.sum(exchange(blocks.reshape(groups, requests, features)), axis=0)
    mid = to_block_owner(mid.astype(jnp.bfloat16)).astype(jnp.float32)
    squares = jnp.sum(mid * mid, axis=1, keepdims=True)
    gain_here = lax.dynamic_slice_in_dim(feedforward_gain, group * features, features, 0)
    inputs_mid = (mid * gain_here).astype(jnp.bfloat16)
    local_units = gate_weight.shape[1]
    piece = local_units // groups
    gates = jnp.dot(inputs_mid, gate_weight, preferred_element_type=jnp.float32)
    ups = jnp.dot(inputs_mid, up_weight, preferred_element_type=jnp.float32)
    both = jnp.concatenate(
        [
            gates.reshape(requests, groups, piece),
            ups.reshape(requests, groups, piece),
            jnp.broadcast_to(squares[:, :, None], (requests, groups, 1)),
        ],
        axis=2,
    )
    sums = jnp.sum(exchange(jnp.swapaxes(both, 0, 1)), axis=0)
    factor = lax.rsqrt(sums[:, 2 * piece :] / D + epsilon)
    gate = sums[:, :piece] * factor
    active = (jax.nn.silu(gate) * (sums[:, piece : 2 * piece] * factor)).astype(jnp.bfloat16)
    active_here = lax.all_gather(to_block_owner(active), "head", axis=1, tiled=True)
    down = jnp.dot(active_here, down_weight, preferred_element_type=jnp.float32)
    residual = [jnp.where(group == lane * share + k, mid, 0.0) for k in range(share)]
    down = down + jnp.concatenate(residual, axis=1)
    result = whole_sum(down).astype(jnp.bfloat16)
    return (compact, summaries, result)


TILE = 128
bfloat = jnp.bfloat16
single = jnp.float32


TERMS = 4


def three_terms(value, place):
    high = value.astype(bfloat).astype(single)
    rest = value - high
    middle = rest.astype(bfloat).astype(single)
    low = jnp.where(place == 2, rest - middle, 0.0)
    return jnp.where(place == 0, high, jnp.where(place == 1, middle, low))


def iota(shape, axis):
    return lax.broadcasted_iota(jnp.int32, shape, axis)


def run(kernel, outs, far, near, scratch=(), flops=0):
    in_specs = [pl.BlockSpec(memory_space=pltpu.HBM) for _ in far]
    in_specs += [pl.BlockSpec(memory_space=pltpu.VMEM) for _ in near]
    moved = sum(a.size * a.dtype.itemsize for a in [*far, *near, *outs])
    return pl.pallas_call(
        kernel,
        out_shape=list(outs),
        in_specs=in_specs,
        out_specs=[pl.BlockSpec(memory_space=pltpu.VMEM) for _ in outs],
        scratch_shapes=list(scratch),
        compiler_params=pltpu.CompilerParams(vmem_limit_bytes=16 * 2**20),
        cost_estimate=pl.CostEstimate(flops=flops, bytes_accessed=moved, transcendentals=0),
    )(*[pltpu.with_memory_space_constraint(a, pltpu.HBM) for a in far], *near)


def fetch(sources, targets, done):
    copies = [
        pltpu.make_async_copy(source, target, done.at[k])
        for k, (source, target) in enumerate(zip(sources, targets))
    ]
    for copy in copies:
        copy.start()
    return copies


def local_like(*arrays):
    return [pltpu.VMEM(a.shape, a.dtype) for a in arrays]


def scalar_like(*arrays):
    return [pltpu.SMEM(a.shape, a.dtype) for a in arrays]


def row_order(source, count, to_holder):
    first, second = iota((count, count), 0), iota((count, count), 1)
    if not to_holder:
        first, second = second, first
    order = (first == second) & (first % R_DEV == 0)
    for c in range(source.shape[1]):
        order = order | ((first == source[0, c] * R_DEV + 1) & (second == c * R_DEV + 1))
    return order.astype(single).astype(bfloat)


def shaped(shape, dtype):
    return jax.ShapeDtypeStruct(shape, dtype)


def first_kernel(
    source_far, gain_far, weight_far, hidden_far, one, two, three, sent, block, source, gain,
    weight, hidden, lanes_of, wide, done
):
    copies = fetch(
        (source_far, gain_far, weight_far, hidden_far), (source, gain, weight, hidden), done
    )
    rows = hidden.shape[0]
    groups = rows // R_DEV
    lanes = sent.shape[0] // groups
    columns, features = weight.shape
    group = lax.axis_index("req")
    share = groups // lanes
    squares = 0.0
    for turn, values in enumerate((one, two, three)):
        values = values[...].astype(single)
        lanes_of[turn + 1] = values
        squares = squares + jnp.sum(values * values, axis=1, keepdims=True)
    copies[3].wait()
    values = hidden[...].astype(single)
    lanes_of[0] = values
    squares = squares + jnp.sum(values * values, axis=1, keepdims=True)
    factor = lax.rsqrt(squares / D + epsilon)
    here = pl.ds(pl.multiple_of(group * features, features), features)
    within = pl.ds(pl.multiple_of(group % share * features, features), features)
    mine = lanes_of[group // share ^ lax.axis_index("head"), :, within]
    block[...] = mine.astype(bfloat)
    wide[...] = jnp.zeros_like(wide)
    for copy in copies[:3]:
        copy.wait()
    normed = (mine * factor * gain[:, here]).astype(bfloat)
    order = row_order(source, rows, True)
    normed = jnp.dot(order, normed, preferred_element_type=single).astype(bfloat)
    wide[:, :columns] = dot_rows(normed, weight[...])
    for g in range(groups):
        tile = jnp.concatenate(
            [
                wide[R_DEV * g : R_DEV * (g + 1), TILE * j : TILE * (j + 1)]
                for j in range(wide.shape[1] // TILE)
            ],
            axis=0,
        )
        for k in range(lanes):
            sent[g * lanes + k] = tile


def dot_rows(left, right):
    return lax.dot_general(left, right, (((1,), (1,)), ((), ())), preferred_element_type=single)


def prepare_kernel(*refs):
    far, (handed, *refs) = refs[:12], refs[12:]
    (compact, summaries, kept, added, tables, mine, theirs, given), refs = refs[:8], refs[8:]
    near, (ordered, plain, dealt, done) = refs[:12], refs[12:]
    copies = fetch(far, near, done)
    (dest, lengths, source, table, keep, weights, query_gain, key_gain, turns) = near[:9]
    pages, gate, up = near[9:]
    group = lax.axis_index("req")
    lane = lax.axis_index("head")
    lanes = lax.axis_size("head")
    for copy in copies[:9]:
        copy.wait()

    carried = 0
    for c in range(source.shape[1]):
        carried = carried + jnp.where(source[0, c] == group, c, 0)
    held_len = (lengths[0, group * R_DEV], lengths[0, carried * R_DEV + 1])
    count, rows, _ = pages.shape
    owned = []
    for r in range(R_DEV):
        slots = []
        for i in range(table.shape[1] // lanes):
            j = i * lanes + lane
            slots.append(jnp.where(j < held_len[r], table[r, j], -1))
        owned.append(slots)

    def owner(r, p):
        found = owned[r][0] == p
        for slot in owned[r][1:]:
            found = found | (slot == p)
        return found

    row = iota((32, TILE), 0)
    odd = (row & 1) == 1
    half_rows = turns.shape[0] // 2
    for part in range(2):
        pair = [turns[pl.ds(part * half_rows + held_len[r], 1), :] for r in range(R_DEV)]
        tables[32 * part : 32 * (part + 1), :] = jnp.where(odd, pair[1], pair[0])
    query_rows = HEADS * HD // TILE * R_DEV
    for c in range(TILE // HD):
        columns = slice(HD * c, HD * (c + 1))
        tables[64 : 64 + query_rows, columns] = jnp.broadcast_to(
            query_gain[...], (query_rows, HD)
        )
        tables[64 + query_rows : 96, columns] = jnp.broadcast_to(
            key_gain[...], (32 - query_rows, HD)
        )

    column = iota((1, TILE), 1)
    entries = count * KEEP
    added[...] = jnp.full_like(added, negative)
    extra = [
        jnp.where((column == count + r) & (lane == 0), 0.0, negative) for r in range(R_DEV)
    ]
    weight_columns = weights[...].T
    rows_of = iota((rows, KEEP), 0)
    place = iota((rows, 16), 1)
    copies[9].wait()
    for p in range(count):
        picks = (keep[p : p + 1, :] == rows_of).astype(single)
        dropped = weight_columns[:, p : p + 1] * (1.0 - jnp.sum(picks, axis=1, keepdims=True))
        total = jnp.sum(dropped, axis=0, keepdims=True)
        left = jnp.concatenate([picks, three_terms(dropped, place)], axis=1).astype(bfloat)
        both = lax.dot_general(
            left, pages[p], (((0,), (0,)), ((), ())), preferred_element_type=single
        )
        rows_kept = both[:KEEP].astype(bfloat)
        kept[KEEP * p : KEEP * (p + 1), :] = rows_kept
        slot = dest[0, p]
        start = pl.multiple_of((slot & 1) * KEEP, KEEP)
        compact[slot >> 1, pl.ds(start, KEEP), :] = rows_kept
        mean = both[KEEP : KEEP + 1] + both[KEEP + 1 : KEEP + 2] + both[KEEP + 2 : KEEP + 3]
        mean = mean / total
        plain[p : p + 1, :] = mean
        ordered[pl.ds(slot, 1), :] = mean
        live = jnp.where(keep[p : p + 1, :] >= 0, 0.0, negative)
        for r in range(R_DEV):
            here = owner(r, p)
            added[r : r + 1, KEEP * p : KEEP * (p + 1)] = jnp.where(here, live, negative)
            level = jnp.where(here, jnp.log(total), negative)
            extra[r] = jnp.where(column == p, level, extra[r])
    for r in range(R_DEV):
        added[r : r + 1, entries : entries + TILE] = extra[r]
    plain[count:, :] = jnp.zeros_like(plain[count:, :])
    kept[entries:, :] = plain[...].astype(bfloat)
    summaries[...] = ordered[...].astype(bfloat)

    for copy in copies[10:]:
        copy.wait()
    block = gate.shape[1] // 2
    piece = block // 2
    for k in range(2):
        for b in range(2):
            columns = slice(b * block + k * piece, b * block + (k + 1) * piece)
            start = b * block
            dealt[k, :, start : start + piece] = gate[:, columns].astype(single)
            dealt[k, :, start + piece : start + block] = up[:, columns].astype(single)
    mine[...] = dealt[lane & 1].astype(bfloat)
    theirs[...] = dealt[1 - (lane & 1)].astype(bfloat)
    width = given.shape[1]
    other = pl.multiple_of((1 - (group & 1)) * width, width)
    given[...] = handed[:, pl.ds(other, width)]


def attend_kernel(came, kept, added, tables, sent, x, extra_k, extra_v, out, logs):
    lanes = lax.axis_size("head")
    groups = came.shape[0] // lanes
    width = (HEADS + 2 * KVH) * HD // lanes
    span = -(-KVH * HD // TILE) * TILE
    key_cols = slice(0, span)
    value_cols = slice(KVW - span, KVW)
    first_key = HEADS * HD // TILE * R_DEV
    scale = HD ** (-0.5)
    x[...] = jnp.zeros_like(x)
    column = iota((8, TILE), 1)
    for k in range(lanes):
        tile = came[k].astype(single)
        for g in range(1, groups):
            tile = tile + came[g * lanes + k].astype(single)
        tile = tile.astype(bfloat).astype(single)
        base, shift = divmod(width * k, TILE)
        base = base * R_DEV
        if shift:
            tile = pltpu.roll(tile, shift, 1)
            x[base + 2 : base + 10, :] += jnp.where(column < shift, tile, 0.0)
        x[base : base + 8, :] += jnp.where(column >= shift, tile, 0.0)
    values = x[...]
    same_head = (iota((TILE, TILE), 0) // HD == iota((TILE, TILE), 1) // HD).astype(single)
    squares = jnp.dot(
        values * values, same_head, precision=lax.Precision.HIGHEST, preferred_element_type=single
    )
    normed = values * lax.rsqrt(squares / HD + epsilon) * tables[64:96, :]
    early = iota(values.shape, 1) % HD < HD // 2
    swapped = jnp.where(
        early, pltpu.roll(normed, TILE - HD // 2, 1), pltpu.roll(normed, HD // 2, 1)
    )
    turned = normed * tables[0:32, :] + swapped * tables[32:64, :]
    turned = turned.astype(bfloat).astype(single)

    rows = 24
    row = iota((rows, TILE), 0)
    half = iota((rows, TILE), 1) // HD
    key_head = row >> 2
    query = jnp.where(row < first_key, turned[:rows], 0.0)
    other = pltpu.roll(query, HD, 1)
    queries = []
    for u in range(2):
        placed = jnp.where(
            half == (key_head & 1), jnp.where((key_head & 1) == u, query, other), 0.0
        )
        queries.append(
            jnp.concatenate(
                [jnp.where((key_head >> 1) == c, placed, 0.0) for c in range(span // TILE)], axis=1
            )
        )
    queries = jnp.concatenate(queries, axis=0).astype(bfloat)

    extras = extra_k.shape[0]
    entries = kept.shape[0] - extras
    count = entries // KEEP
    extra_k[...] = kept[entries:, key_cols].astype(single)
    extra_v[...] = kept[entries:, value_cols].astype(single)
    first_value = first_key + KVH * HD // TILE * R_DEV
    for c in range(span // TILE):
        at = slice(c * TILE, (c + 1) * TILE)
        r = first_key + R_DEV * c
        extra_k[count : count + R_DEV, at] = turned[r : r + R_DEV]
        r = first_value + R_DEV * c
        extra_v[count : count + R_DEV, at] = values[r : r + R_DEV]

    def by_request(columns, size):
        odd = (iota((2 * rows, size), 0) & 1) == 1
        return jnp.where(odd, added[1:2, columns], added[0:1, columns])

    scores = dot_rows(queries, kept[:entries, key_cols]) * scale
    scores = scores + by_request(slice(0, entries), entries)
    extra = dot_rows(queries, extra_k[...].astype(bfloat)) * scale
    extra = extra + by_request(slice(entries, entries + extras), extras)
    top = jnp.maximum(
        jnp.max(scores, axis=1, keepdims=True), jnp.max(extra, axis=1, keepdims=True)
    )
    weight = jnp.where(scores > 0.5 * negative, jnp.exp(scores - top), 0.0)
    extra_weight = jnp.where(extra > 0.5 * negative, jnp.exp(extra - top), 0.0)
    mass = jnp.sum(weight, axis=1, keepdims=True) + jnp.sum(extra_weight, axis=1, keepdims=True)

    def weighted(parts, right):
        high = parts.astype(bfloat)
        low = (parts - high.astype(single)).astype(bfloat)
        return jnp.dot(high, right, preferred_element_type=single) + jnp.dot(
            low, right, preferred_element_type=single
        )

    total = weighted(weight, kept[:entries, value_cols]) + weighted(
        extra_weight, extra_v[...].astype(bfloat)
    )
    some = mass > 0.0
    mass = jnp.where(some, mass, 1.0)
    total = total / mass
    level = jnp.where(some, top + jnp.log(mass), negative)

    slot = key_head + (KVW // 2 - (KVW - span)) // HD
    results = []
    for u in range(2):
        mine = total[rows * u : rows * (u + 1)]
        picked = mine[:, :TILE]
        for c in range(1, span // TILE):
            picked = jnp.where((slot >> 1) == c, mine[:, c * TILE : (c + 1) * TILE], picked)
        results.append(jnp.where((slot & 1) == u, picked, pltpu.roll(picked, HD, 1)))
    out[...] = jnp.where(half == 0, results[0], results[1])
    logs[...] = jnp.broadcast_to(level, logs.shape)
    own = HEADS * HD // lanes
    size = 6
    column = iota((size, TILE), 1)
    here = column // TERMS == iota((size, TILE), 0)
    for k in range(lanes):
        r = own * k // TILE * R_DEV
        tile = [out[r : r + size, :]]
        for u in range(2):
            coded = three_terms(logs[rows * u + r : rows * u + r + size, :], column % TERMS)
            tile.append(jnp.sum(jnp.where(here, coded, 0.0), axis=0, keepdims=True))
        tile = jnp.concatenate(tile, axis=0).astype(bfloat)
        for g in range(groups):
            sent[g * lanes + k] = tile


def project_kernel(source_far, came, first, second, sent, source, logs, rows, pieces, done):
    (copy,) = fetch((source_far,), (source,), done)
    lanes = lax.axis_size("head")
    groups = came.shape[0] // lanes
    group = lax.axis_index("req")
    features = first.shape[0]
    requests = rows.shape[0]
    size = 6
    tiles = [came[d].astype(single) for d in range(groups * lanes)]
    for g in range(groups):
        for k in range(lanes):
            logs[k, 2 * g : 2 * g + 2, :] = tiles[g * lanes + k][size:]
    spread = (iota((8, TILE), 1) // TERMS == iota((8, TILE), 0)).astype(single).astype(bfloat)
    levels = [dot_rows(spread, logs[k].astype(bfloat)) for k in range(lanes)]
    top = jnp.maximum(jnp.maximum(levels[0], levels[1]), jnp.maximum(levels[2], levels[3]))
    shares = [jnp.exp(level - top) for level in levels]
    mass = sum(shares)
    shares = [share / mass for share in shares]
    lower = iota((8, TILE), 1) < HD
    for g in range(groups):
        mixed = 0.0
        for k in range(lanes):
            share = shares[k]
            share = jnp.where(lower, share[:, 2 * g : 2 * g + 1], share[:, 2 * g + 1 : 2 * g + 2])
            mixed = mixed + share * tiles[g * lanes + k]
        for j in range(size // R_DEV):
            rows[R_DEV * g : R_DEV * (g + 1), TILE * j : TILE * (j + 1)] = mixed[
                R_DEV * j : R_DEV * (j + 1)
            ]
    width = rows.shape[1]
    shift = lax.rem(lax.axis_index("head") * (2 * features), TILE)
    attention = rows[...].astype(bfloat).astype(single)
    attention = pltpu.roll(attention, lax.rem(width - shift, width), 1)
    copy.wait()
    order = row_order(source, requests, False)
    attention = jnp.dot(order, attention.astype(bfloat), preferred_element_type=single)
    for b in range(2):
        pieces[b] = attention[:, features * b : features * (b + 1)]
    total = 0.0
    width = sent.shape[1]
    here = pl.multiple_of((group & 1) * width, width)
    for turn, weight in enumerate((first[:, pl.ds(here, width)], second[...])):
        piece = pieces[(group & 1) ^ turn].astype(bfloat)
        total = total + jnp.dot(piece, weight, preferred_element_type=single)
    sent[...] = total


def units_kernel(
    gain_far, own, one, two, three, hidden, mine, theirs, sent, mid_out, gain, done
):
    (copy,) = fetch((gain_far,), (gain,), done)
    rows, features = own.shape
    share = sent.shape[0] // lax.axis_size("head")
    group = lax.axis_index("req")
    lane = lax.axis_index("head")
    here = pl.ds(pl.multiple_of(group * features, features), features)
    mid = (own[...] + one[...]) + (two[...] + three[...])
    mid = (hidden[...].astype(single) + mid).astype(bfloat)
    mid_out[...] = mid
    mid = mid.astype(single)
    squares = jnp.sum(mid * mid, axis=1, keepdims=True)
    block = mine.shape[1] // share
    terms = three_terms(squares, iota((rows, sent.shape[2] - block), 1)).astype(bfloat)
    copy.wait()
    inputs = (mid * gain[:, here]).astype(bfloat)
    for turn, weight in enumerate((mine, theirs)):
        units = jnp.dot(inputs, weight[...], preferred_element_type=single).astype(bfloat)
        target = (lane ^ turn) * share
        for b in range(share):
            sent[target + b, :, :block] = units[:, block * b : block * (b + 1)]
            sent[target + b, :, block:] = terms


def active_kernel(came, active):
    total = came[0].astype(single)
    for g in range(1, came.shape[0]):
        total = total + came[g].astype(single)
    piece = active.shape[1]
    squares = jnp.sum(total[:, 2 * piece : 2 * piece + 3], axis=1, keepdims=True)
    factor = lax.rsqrt(squares / D + epsilon)
    gate = total[:, :piece] * factor
    up = total[:, piece : 2 * piece] * factor
    active[...] = (gate / (1.0 + jnp.exp(-gate)) * up).astype(bfloat)


def down_kernel(own, one, two, three, weight, mid, sent, active):
    groups, rows, width = sent.shape
    piece = own.shape[1]
    half = mid.shape[1]
    for turn, values in enumerate((own, one, two, three)):
        active[turn] = values[...]
    share = width // half
    group = lax.axis_index("req")
    lane = lax.axis_index("head")
    first = group // (2 * share) * 2 ^ lane
    down = jnp.dot(active[first], weight[:piece, :], preferred_element_type=single)
    down = down + jnp.dot(active[first ^ 1], weight[piece:, :], preferred_element_type=single)
    residual = mid[...].astype(single)
    for b in range(share):
        columns = slice(half * b, half * (b + 1))
        mine = group == lane * share + b
        total = (down[:, columns] + jnp.where(mine, residual, 0.0)).astype(bfloat)
        for g in range(groups):
            sent[g, :, columns] = total


def result_kernel(came, result):
    total = came[0].astype(single)
    for g in range(1, came.shape[0]):
        total = total + came[g].astype(single)
    result[...] = total.astype(bfloat)


def rotation_table():
    half = HD // 2
    size = -(-(NP + 1) // 8) * 8
    frequency = 10000.0 ** (-np.arange(half) / half)
    angles = PAGE * np.arange(size)[:, None] * frequency[None, :]
    cosine, sine = np.cos(angles), np.sin(angles)
    wide = [np.tile(np.concatenate(pair, axis=1), (1, TILE // HD)) for pair in
            ((cosine, cosine), (-sine, sine))]
    return jnp.asarray(np.concatenate(wide), dtype=single)


def swapped_lanes(value, turn):
    lanes = lax.axis_size("head")
    return lax.ppermute(value, "head", [(k, k ^ turn) for k in range(lanes)])


def from_lanes(value):
    return [value] + [swapped_lanes(value, turn) for turn in range(1, lax.axis_size("head"))]


def transposed(value):
    groups = lax.axis_size("req")
    lanes = lax.axis_size("head")
    pairs = [
        (g * lanes + h, (2 * h + (g & 1)) * lanes + g // 2)
        for g in range(groups)
        for h in range(lanes)
    ]
    return lax.ppermute(value, both_axes, pairs)


def swapped_y(value):
    return lax.ppermute(value, "req", [(g, g ^ 1) for g in range(lax.axis_size("req"))])


def on_device(
    hidden_in,
    attention_gain,
    query_gain,
    key_gain,
    feedforward_gain,
    input_weight,
    output_weight,
    gate_weight,
    up_weight,
    down_weight,
    old_cache,
    keep_rows,
    drop_weights,
    dest_slots,
    lengths,
    page_table,
    source,
):
    groups = lax.axis_size("req")
    lanes = lax.axis_size("head")
    requests = hidden_in.shape[0]
    pages_here = old_cache.shape[0]
    devices = groups * lanes
    features = D // groups
    copies = pltpu.SemaphoreType.DMA

    handed = transposed(output_weight)
    columns = input_weight.shape[1]
    padded = -(-columns // TILE) * TILE
    holds = source[None, :]
    gain = attention_gain[None, :]
    weight = input_weight.T
    far = [holds, gain, weight, hidden_in]
    sent, hidden_block = run(
        first_kernel,
        [
            shaped((devices, R_DEV * padded // TILE, TILE), single),
            shaped((requests, features), bfloat),
        ],
        far,
        from_lanes(hidden_in)[1:],
        [
            *scalar_like(holds),
            *local_like(*far[1:]),
            pltpu.VMEM((lanes,) + hidden_in.shape, single),
            pltpu.VMEM((requests, padded), single),
            copies((len(far),)),
        ],
        2 * requests * features * columns,
    )
    came = lax.all_to_all(sent, both_axes, 0, 0, tiled=True)
    handed, _ = lax.optimization_barrier((handed, sent))
    scalars = [dest_slots, lengths[None, :], holds, page_table]
    arrays = [
        keep_rows,
        drop_weights,
        query_gain[None, :],
        key_gain[None, :],
        rotation_table(),
        old_cache,
        gate_weight,
        up_weight,
    ]
    entries = pages_here * KEEP
    extras = 16
    compact, summaries, kept, added, tables, mine, theirs, given = run(
        prepare_kernel,
        [
            shaped((pages_here // 2, PAGE, KVW), bfloat),
            shaped((pages_here, KVW), bfloat),
            shaped((entries + extras, KVW), bfloat),
            shaped((8, entries + TILE), single),
            shaped((96, TILE), single),
            shaped(gate_weight.shape, bfloat),
            shaped(gate_weight.shape, bfloat),
            shaped((output_weight.shape[0], features), bfloat),
        ],
        scalars + arrays,
        [handed],
        [
            *scalar_like(*scalars),
            *local_like(*arrays),
            pltpu.VMEM((pages_here, KVW), single),
            pltpu.VMEM((extras, KVW), single),
            pltpu.VMEM((2,) + gate_weight.shape, single),
            copies((len(scalars + arrays),)),
        ],
        2 * pages_here * TILE * PAGE * KVW,
    )
    span = -(-KVH * HD // TILE) * TILE
    (parts,) = run(
        attend_kernel,
        [shaped((devices, 8, TILE), bfloat)],
        [],
        [came, kept, added, tables],
        [
            pltpu.VMEM((32, TILE), single),
            pltpu.VMEM((extras, span), single),
            pltpu.VMEM((extras, span), single),
            pltpu.VMEM((24, TILE), single),
            pltpu.VMEM((48, TILE), single),
        ],
        6 * 48 * entries * span,
    )
    theirs, given, _ = lax.optimization_barrier((theirs, given, parts))
    theirs = swapped_lanes(theirs, 1)
    given = swapped_y(given)
    came = lax.all_to_all(parts, both_axes, 0, 0, tiled=True)
    came, theirs = lax.optimization_barrier((came, theirs))
    (sent,) = run(
        project_kernel,
        [shaped((requests, features), single)],
        [holds],
        [came, handed, given],
        [
            *scalar_like(holds),
            pltpu.VMEM((lanes, 2 * groups, TILE), single),
            pltpu.VMEM((requests, 3 * TILE), single),
            pltpu.VMEM((2, requests, output_weight.shape[0]), single),
            copies((1,)),
        ],
        2 * requests * output_weight.size,
    )
    gain = feedforward_gain[None, :]
    block = gate_weight.shape[1] // 2
    sent, mid = run(
        units_kernel,
        [
            shaped((groups, requests, block + TILE), bfloat),
            shaped((requests, features), bfloat),
        ],
        [gain],
        [*from_lanes(sent), hidden_block, mine, theirs],
        [*local_like(gain), copies((1,))],
        4 * requests * gate_weight.size,
    )
    (active,) = run(
        active_kernel, [shaped((requests, block // 2), bfloat)], [], [exchange(sent)]
    )
    (sent,) = run(
        down_kernel,
        [shaped((groups, requests, down_weight.shape[1]), bfloat)],
        [],
        [*from_lanes(active), down_weight, mid],
        [pltpu.VMEM((lanes,) + active.shape, bfloat)],
        2 * requests * down_weight.size,
    )
    (result,) = run(
        result_kernel, [shaped((requests, down_weight.shape[1]), bfloat)], [], [exchange(sent)]
    )
    return (compact, summaries, result)


def solution(mesh):
    placed = (
        P(None, "head"),
        P(),
        P(),
        P(),
        P(),
        P("req", "head"),
        P("req", "head"),
        P("req", "head"),
        P("req", "head"),
        P("req", "head"),
        P(("req", "head"), None, None),
        P(("req", "head"), None),
        P(("req", "head"), None),
        P(("req", "head"), None),
        P(),
        P("req", None),
        P(),
    )
    return jax.shard_map(
        on_device if mesh.shape["req"] <= DIRECT else on_device_wide,
        mesh=mesh,
        in_specs=placed,
        out_specs=(P(("req", "head"), None, None), P(("req", "head"), None), P(None, "head")),
        check_vma=False,
    )
```

```python
import jax
import jax.numpy as jnp
import numpy as np
from jax import lax
from jax.experimental import pallas as pl
from jax.experimental.pallas import tpu as pltpu
from jax.sharding import PartitionSpec as P

D = 2048
HEADS = 20
KVH = 5
HD = 64
FF = 5120
PAGE = 128
KEEP = 64
NP = 16
R_DEV = 2
KVW = 640

DIRECT = 8

epsilon = 1e-06
negative = -1e30
both_axes = ("req", "head")


def rms_scale(values):
    return lax.rsqrt(jnp.mean(values * values, axis=-1, keepdims=True) + epsilon)


def rms_rows(values, gain):
    return values * rms_scale(values) * gain


def rotate(vectors, positions):
    half = vectors.shape[-1] // 2
    frequency = 10000.0 ** (-jnp.arange(half, dtype=jnp.float32) / half)
    angles = positions.astype(jnp.float32)[:, None] * frequency[None, :]
    cosine = jnp.cos(angles)[:, None, :]
    sine = jnp.sin(angles)[:, None, :]
    first = vectors[..., :half]
    second = vectors[..., half:]
    return jnp.concatenate(
        [first * cosine - second * sine, second * cosine + first * sine], axis=-1
    )


def compact_pages(pages, keep, weights):
    rows = jnp.arange(pages.shape[1], dtype=jnp.int32)
    picks = keep[:, :, None] == rows[None, None, :]
    kept = jnp.einsum(
        "pkr,prc->pkc", picks.astype(jnp.bfloat16), pages, preferred_element_type=jnp.float32
    ).astype(jnp.bfloat16)
    dropped = weights * (1.0 - jnp.sum(picks.astype(jnp.float32), axis=1))
    total = jnp.sum(dropped, axis=1)
    means = (
        jnp.einsum(
            "pr,prc->pc", dropped, pages.astype(jnp.float32), precision=lax.Precision.HIGHEST
        )
        / total[:, None]
    )
    return (kept, means.astype(jnp.bfloat16), jnp.log(total))


def held_request(rows, source):
    half = R_DEV // 2
    position = rows % R_DEV
    slot = rows // R_DEV * half + position - half
    continued = jnp.arange(source.shape[0], dtype=jnp.int32)
    matches = source[None, :] == slot[:, None]
    owner_cont = jnp.sum(jnp.where(matches, continued[None, :], 0), axis=1)
    carried = owner_cont // half * R_DEV + half + owner_cont % half
    return jnp.where(position < half, rows, carried)


def pick_rows(order, rows):
    chosen = order[:, None] == jnp.arange(rows.shape[0], dtype=jnp.int32)[None, :]
    return jnp.dot(
        chosen.astype(jnp.bfloat16), rows, preferred_element_type=jnp.float32
    ).astype(jnp.bfloat16)


def exchange(parts):
    return lax.all_to_all(parts, "req", split_axis=0, concat_axis=0, tiled=True)


def to_block_owner(rows):
    groups = lax.axis_size("req")
    lanes = lax.axis_size("head")
    per_lane = groups // lanes
    pairs = [
        (g * lanes + h, (per_lane * h + g // lanes) * lanes + g % lanes)
        for g in range(groups)
        for h in range(lanes)
    ]
    return lax.ppermute(rows, both_axes, pairs)


def whole_sum(partial):
    if lax.axis_size("req") > DIRECT:
        return lax.psum(partial, "req")
    groups = lax.axis_size("req")
    return jnp.sum(exchange(jnp.broadcast_to(partial[None], (groups,) + partial.shape)), axis=0)


def on_device_wide(
    hidden_in,
    attention_gain,
    query_gain,
    key_gain,
    feedforward_gain,
    input_weight,
    output_weight,
    gate_weight,
    up_weight,
    down_weight,
    old_cache,
    keep_rows,
    drop_weights,
    dest_slots,
    lengths,
    page_table,
    source,
):
    groups = lax.axis_size("req")
    lanes = lax.axis_size("head")
    group = lax.axis_index("req")
    lane = lax.axis_index("head")
    requests = hidden_in.shape[0]
    half = R_DEV // 2
    split = KVH * HD
    ratio = HEADS // KVH
    scale = HD ** (-0.5)
    pages_here = old_cache.shape[0]
    everyone = jnp.arange(requests, dtype=jnp.int32)
    holders = held_request(everyone, source)
    held = lax.dynamic_slice_in_dim(holders, group * R_DEV, R_DEV, 0)
    held_len = lengths[held]
    positions = held_len * PAGE

    whole = lax.all_gather(hidden_in, "head", axis=1, tiled=True)
    normed = rms_rows(whole.astype(jnp.float32), attention_gain).astype(jnp.bfloat16)
    features = D // groups
    inputs = pick_rows(holders, lax.dynamic_slice_in_dim(normed, group * features, features, 1))
    partial_qkv = jnp.dot(inputs, input_weight, preferred_element_type=jnp.float32)
    sent = jnp.broadcast_to(
        partial_qkv.reshape(groups, 1, R_DEV, -1), (groups, lanes, R_DEV, partial_qkv.shape[1])
    ).reshape(groups * lanes, R_DEV, -1)
    got = lax.all_to_all(sent, both_axes, split_axis=0, concat_axis=0, tiled=True)
    mixed = jnp.sum(got.reshape(groups, lanes, R_DEV, -1), axis=0).astype(jnp.bfloat16)
    held_qkv = jnp.swapaxes(mixed, 0, 1).reshape(R_DEV, -1).astype(jnp.float32)

    query = rotate(
        rms_rows(held_qkv[:, : HEADS * HD].reshape(R_DEV, HEADS, HD), query_gain), positions
    ).astype(jnp.bfloat16)
    key_new = rotate(
        rms_rows(held_qkv[:, HEADS * HD : (HEADS + KVH) * HD].reshape(R_DEV, KVH, HD), key_gain),
        positions,
    ).astype(jnp.bfloat16)
    value_new = held_qkv[:, (HEADS + KVH) * HD :].reshape(R_DEV, KVH, HD)
    kept, means, bias = compact_pages(old_cache, keep_rows, drop_weights)
    destination = dest_slots[0]
    fresh_ids = jnp.arange(pages_here, dtype=jnp.int32)
    inverse = jnp.sum(
        jnp.where(destination[None, :] == fresh_ids[:, None], fresh_ids[None, :], 0), axis=1
    )
    compact = kept[inverse].reshape(pages_here // 2, PAGE, KVW)
    summaries = means[inverse]
    per_lane = NP // lanes
    table = page_table.reshape(R_DEV, per_lane, lanes)
    mine = lax.dynamic_slice_in_dim(table, lane, 1, 2)[:, :, 0]
    logical = jnp.arange(per_lane, dtype=jnp.int32) * lanes + lane
    live = logical[None, :] < held_len[:, None]
    owner = jnp.any((mine[:, :, None] == fresh_ids[None, None, :]) & live[:, :, None], axis=1)
    query_groups = query.reshape(R_DEV, KVH, ratio, HD)
    row_keys = kept[:, :, :split].reshape(pages_here, KEEP, KVH, HD)
    row_values = kept[:, :, split:].reshape(pages_here, KEEP, KVH, HD)
    row_live = keep_rows >= 0
    allowed = owner[:, None, None, :, None] & row_live[None, None, None, :, :]
    scores = (
        jnp.einsum("rngd,pmnd->rngpm", query_groups, row_keys, preferred_element_type=jnp.float32)
        * scale
    )
    scores = jnp.where(allowed, scores, negative)
    mean_keys = means[:, :split].reshape(pages_here, KVH, HD)
    mean_values = means[:, split:].reshape(pages_here, KVH, HD)
    mean_scores = (
        jnp.einsum("rngd,pnd->rngp", query_groups, mean_keys, preferred_element_type=jnp.float32)
        * scale
        + bias[None, None, None, :]
    )
    mean_allowed = owner[:, None, None, :]
    mean_scores = jnp.where(mean_allowed, mean_scores, negative)
    own_score = (
        jnp.einsum("rngd,rnd->rng", query_groups, key_new, preferred_element_type=jnp.float32)
        * scale
    )
    own_score = jnp.where(lane == 0, own_score, negative)
    top = jnp.maximum(jnp.max(scores, axis=(3, 4)), jnp.max(mean_scores, axis=3))
    top = jnp.maximum(top, own_score)
    row_weight = jnp.where(allowed, jnp.exp(scores - top[..., None, None]), 0.0)
    mean_weight = jnp.where(mean_allowed, jnp.exp(mean_scores - top[..., None]), 0.0)
    own_weight = jnp.where(lane == 0, jnp.exp(own_score - top), 0.0)
    mass = jnp.sum(row_weight, axis=(3, 4)) + jnp.sum(mean_weight, axis=3) + own_weight
    total = jnp.einsum(
        "rngpm,pmnd->rngd",
        row_weight,
        row_values.astype(jnp.float32),
        precision=lax.Precision.HIGHEST,
    )
    total = total + jnp.einsum(
        "rngp,pnd->rngd",
        mean_weight,
        mean_values.astype(jnp.float32),
        precision=lax.Precision.HIGHEST,
    )
    total = total + own_weight[..., None] * value_new[:, :, None, :]

    some = mass > 0.0
    level = jnp.where(some, top + jnp.log(jnp.where(some, mass, 1.0)), negative)
    means_out = total / jnp.where(some, mass, 1.0)[..., None]
    own = HEADS * HD // groups
    parts = jnp.stack([means_out, jnp.broadcast_to(level[..., None], total.shape)])
    parts = jnp.transpose(parts.reshape(2, R_DEV, groups, own), (2, 1, 0, 3))
    parts = jnp.broadcast_to(
        parts.reshape(groups, 1, R_DEV, 2 * own), (groups, lanes, R_DEV, 2 * own)
    ).reshape(groups * lanes, R_DEV, 2 * own)
    came = lax.all_to_all(parts, both_axes, 0, 0, tiled=True)
    came = came.reshape(groups, lanes, R_DEV, 2 * own)
    outs, levels = came[..., :own], came[..., own:]
    weights = jnp.exp(levels - jnp.max(levels, axis=1, keepdims=True))
    attention = jnp.sum(outs * weights, axis=1) / jnp.sum(weights, axis=1)
    attention = attention.reshape(requests, own).astype(jnp.bfloat16)
    back = jnp.sum(
        jnp.where(holders[None, :] == everyone[:, None], everyone[None, :], 0), axis=1
    )
    projected = jnp.dot(
        pick_rows(back, attention), output_weight, preferred_element_type=jnp.float32
    )
    projected = projected + jnp.where(group == 0, hidden_in.astype(jnp.float32), 0.0)

    share = groups // lanes
    blocks = jnp.moveaxis(projected.reshape(requests, share, 1, features), 0, 2)
    blocks = jnp.broadcast_to(blocks, (share, lanes, requests, features))
    mid = jnp.sum(exchange(blocks.reshape(groups, requests, features)), axis=0)
    mid = to_block_owner(mid.astype(jnp.bfloat16)).astype(jnp.float32)
    squares = jnp.sum(mid * mid, axis=1, keepdims=True)
    gain_here = lax.dynamic_slice_in_dim(feedforward_gain, group * features, features, 0)
    inputs_mid = (mid * gain_here).astype(jnp.bfloat16)
    local_units = gate_weight.shape[1]
    piece = local_units // groups
    gates = jnp.dot(inputs_mid, gate_weight, preferred_element_type=jnp.float32)
    ups = jnp.dot(inputs_mid, up_weight, preferred_element_type=jnp.float32)
    both = jnp.concatenate(
        [
            gates.reshape(requests, groups, piece),
            ups.reshape(requests, groups, piece),
            jnp.broadcast_to(squares[:, :, None], (requests, groups, 1)),
        ],
        axis=2,
    )
    sums = jnp.sum(exchange(jnp.swapaxes(both, 0, 1)), axis=0)
    factor = lax.rsqrt(sums[:, 2 * piece :] / D + epsilon)
    gate = sums[:, :piece] * factor
    active = (jax.nn.silu(gate) * (sums[:, piece : 2 * piece] * factor)).astype(jnp.bfloat16)
    active_here = lax.all_gather(to_block_owner(active), "head", axis=1, tiled=True)
    down = jnp.dot(active_here, down_weight, preferred_element_type=jnp.float32)
    residual = [jnp.where(group == lane * share + k, mid, 0.0) for k in range(share)]
    down = down + jnp.concatenate(residual, axis=1)
    result = whole_sum(down).astype(jnp.bfloat16)
    return (compact, summaries, result)


TILE = 128
bfloat = jnp.bfloat16
single = jnp.float32


TERMS = 4


def three_terms(value, place):
    high = value.astype(bfloat).astype(single)
    rest = value - high
    middle = rest.astype(bfloat).astype(single)
    low = jnp.where(place == 2, rest - middle, 0.0)
    return jnp.where(place == 0, high, jnp.where(place == 1, middle, low))


def iota(shape, axis):
    return lax.broadcasted_iota(jnp.int32, shape, axis)


def run(kernel, outs, far, near, scratch=(), flops=0):
    in_specs = [pl.BlockSpec(memory_space=pltpu.HBM) for _ in far]
    in_specs += [pl.BlockSpec(memory_space=pltpu.VMEM) for _ in near]
    moved = sum(a.size * a.dtype.itemsize for a in [*far, *near, *outs])
    return pl.pallas_call(
        kernel,
        out_shape=list(outs),
        in_specs=in_specs,
        out_specs=[pl.BlockSpec(memory_space=pltpu.VMEM) for _ in outs],
        scratch_shapes=list(scratch),
        compiler_params=pltpu.CompilerParams(vmem_limit_bytes=16 * 2**20),
        cost_estimate=pl.CostEstimate(flops=flops, bytes_accessed=moved, transcendentals=0),
    )(*[pltpu.with_memory_space_constraint(a, pltpu.HBM) for a in far], *near)


def fetch(sources, targets, done):
    copies = [
        pltpu.make_async_copy(source, target, done.at[k])
        for k, (source, target) in enumerate(zip(sources, targets))
    ]
    for copy in copies:
        copy.start()
    return copies


def local_like(*arrays):
    return [pltpu.VMEM(a.shape, a.dtype) for a in arrays]


def scalar_like(*arrays):
    return [pltpu.SMEM(a.shape, a.dtype) for a in arrays]


def row_order(source, count, to_holder):
    first, second = iota((count, count), 0), iota((count, count), 1)
    if not to_holder:
        first, second = second, first
    order = (first == second) & (first % R_DEV == 0)
    for c in range(source.shape[1]):
        order = order | ((first == source[0, c] * R_DEV + 1) & (second == c * R_DEV + 1))
    return order.astype(single).astype(bfloat)


def shaped(shape, dtype):
    return jax.ShapeDtypeStruct(shape, dtype)


def first_kernel(
    source_far, gain_far, weight_far, hidden_far, one, two, three, sent, block, source, gain,
    weight, hidden, lanes_of, wide, done
):
    copies = fetch(
        (source_far, gain_far, weight_far, hidden_far), (source, gain, weight, hidden), done
    )
    rows = hidden.shape[0]
    groups = rows // R_DEV
    lanes = sent.shape[0] // groups
    columns, features = weight.shape
    group = lax.axis_index("req")
    share = groups // lanes
    squares = 0.0
    for turn, values in enumerate((one, two, three)):
        values = values[...].astype(single)
        lanes_of[turn + 1] = values
        squares = squares + jnp.sum(values * values, axis=1, keepdims=True)
    copies[3].wait()
    values = hidden[...].astype(single)
    lanes_of[0] = values
    squares = squares + jnp.sum(values * values, axis=1, keepdims=True)
    factor = lax.rsqrt(squares / D + epsilon)
    here = pl.ds(pl.multiple_of(group * features, features), features)
    within = pl.ds(pl.multiple_of(group % share * features, features), features)
    mine = lanes_of[group // share ^ lax.axis_index("head"), :, within]
    block[...] = mine.astype(bfloat)
    wide[...] = jnp.zeros_like(wide)
    for copy in copies[:3]:
        copy.wait()
    normed = (mine * factor * gain[:, here]).astype(bfloat)
    order = row_order(source, rows, True)
    normed = jnp.dot(order, normed, preferred_element_type=single).astype(bfloat)
    wide[:, :columns] = dot_rows(normed, weight[...])
    for g in range(groups):
        tile = jnp.concatenate(
            [
                wide[R_DEV * g : R_DEV * (g + 1), TILE * j : TILE * (j + 1)]
                for j in range(wide.shape[1] // TILE)
            ],
            axis=0,
        )
        for k in range(lanes):
            sent[g * lanes + k] = tile


def dot_rows(left, right):
    return lax.dot_general(left, right, (((1,), (1,)), ((), ())), preferred_element_type=single)


def prepare_kernel(*refs):
    far, refs = refs[:12], refs[12:]
    (compact, summaries, kept, added, tables, mine, theirs), refs = refs[:7], refs[7:]
    near, (ordered, plain, dealt, done) = refs[:12], refs[12:]
    copies = fetch(far, near, done)
    (dest, lengths, source, table, keep, weights, query_gain, key_gain, turns) = near[:9]
    pages, gate, up = near[9:]
    group = lax.axis_index("req")
    lane = lax.axis_index("head")
    lanes = lax.axis_size("head")
    for copy in copies[:9]:
        copy.wait()

    carried = 0
    for c in range(source.shape[1]):
        carried = carried + jnp.where(source[0, c] == group, c, 0)
    held_len = (lengths[0, group * R_DEV], lengths[0, carried * R_DEV + 1])
    count, rows, _ = pages.shape
    owned = []
    for r in range(R_DEV):
        slots = []
        for i in range(table.shape[1] // lanes):
            j = i * lanes + lane
            slots.append(jnp.where(j < held_len[r], table[r, j], -1))
        owned.append(slots)

    def owner(r, p):
        found = owned[r][0] == p
        for slot in owned[r][1:]:
            found = found | (slot == p)
        return found

    row = iota((32, TILE), 0)
    odd = (row & 1) == 1
    half_rows = turns.shape[0] // 2
    for part in range(2):
        pair = [turns[pl.ds(part * half_rows + held_len[r], 1), :] for r in range(R_DEV)]
        tables[32 * part : 32 * (part + 1), :] = jnp.where(odd, pair[1], pair[0])
    query_rows = HEADS * HD // TILE * R_DEV
    for c in range(TILE // HD):
        columns = slice(HD * c, HD * (c + 1))
        tables[64 : 64 + query_rows, columns] = jnp.broadcast_to(
            query_gain[...], (query_rows, HD)
        )
        tables[64 + query_rows : 96, columns] = jnp.broadcast_to(
            key_gain[...], (32 - query_rows, HD)
        )

    column = iota((1, TILE), 1)
    entries = count * KEEP
    added[...] = jnp.full_like(added, negative)
    extra = [
        jnp.where((column == count + r) & (lane == 0), 0.0, negative) for r in range(R_DEV)
    ]
    weight_columns = weights[...].T
    rows_of = iota((rows, KEEP), 0)
    place = iota((rows, 16), 1)
    ones = jnp.ones((KEEP, 16), bfloat)
    copies[9].wait()
    for p in range(count):
        picks = (keep[p : p + 1, :] == rows_of).astype(single)
        listed = jnp.dot(picks.astype(bfloat), ones, preferred_element_type=single)
        dropped = weight_columns[:, p : p + 1] * (1.0 - listed)
        total = jnp.sum(dropped, axis=0, keepdims=True)[:, :1]
        left = jnp.concatenate([picks, three_terms(dropped, place)], axis=1).astype(bfloat)
        both = lax.dot_general(
            left, pages[p], (((0,), (0,)), ((), ())), preferred_element_type=single
        )
        rows_kept = both[:KEEP].astype(bfloat)
        kept[KEEP * p : KEEP * (p + 1), :] = rows_kept
        slot = dest[0, p]
        start = pl.multiple_of((slot & 1) * KEEP, KEEP)
        compact[slot >> 1, pl.ds(start, KEEP), :] = rows_kept
        mean = both[KEEP : KEEP + 1] + both[KEEP + 1 : KEEP + 2] + both[KEEP + 2 : KEEP + 3]
        mean = mean / total
        plain[p : p + 1, :] = mean
        ordered[pl.ds(slot, 1), :] = mean
        live = jnp.where(keep[p : p + 1, :] >= 0, 0.0, negative)
        for r in range(R_DEV):
            here = owner(r, p)
            added[r : r + 1, KEEP * p : KEEP * (p + 1)] = jnp.where(here, live, negative)
            level = jnp.where(here, jnp.log(total), negative)
            extra[r] = jnp.where(column == p, level, extra[r])
    for r in range(R_DEV):
        added[r : r + 1, entries : entries + TILE] = extra[r]
    plain[count:, :] = jnp.zeros_like(plain[count:, :])
    kept[entries:, :] = plain[...].astype(bfloat)
    summaries[...] = ordered[...].astype(bfloat)

    for copy in copies[10:]:
        copy.wait()
    block = gate.shape[1] // 2
    piece = block // 2
    for k in range(2):
        for b in range(2):
            columns = slice(b * block + k * piece, b * block + (k + 1) * piece)
            start = b * block
            dealt[k, :, start : start + piece] = gate[:, columns].astype(single)
            dealt[k, :, start + piece : start + block] = up[:, columns].astype(single)
    mine[...] = dealt[lane & 1].astype(bfloat)
    theirs[...] = dealt[1 - (lane & 1)].astype(bfloat)


def attend_kernel(came, kept, added, tables, sent, x, extra_k, extra_v, out, logs):
    lanes = lax.axis_size("head")
    groups = came.shape[0] // lanes
    width = (HEADS + 2 * KVH) * HD // lanes
    span = -(-KVH * HD // TILE) * TILE
    key_cols = slice(0, span)
    value_cols = slice(KVW - span, KVW)
    first_key = HEADS * HD // TILE * R_DEV
    scale = HD ** (-0.5)
    x[...] = jnp.zeros_like(x)
    column = iota((8, TILE), 1)
    for k in range(lanes):
        tile = came[k].astype(single)
        for g in range(1, groups):
            tile = tile + came[g * lanes + k].astype(single)
        tile = tile.astype(bfloat).astype(single)
        base, shift = divmod(width * k, TILE)
        base = base * R_DEV
        if shift:
            tile = pltpu.roll(tile, shift, 1)
            x[base + 2 : base + 10, :] += jnp.where(column < shift, tile, 0.0)
        x[base : base + 8, :] += jnp.where(column >= shift, tile, 0.0)
    values = x[...]
    same_head = (iota((TILE, TILE), 0) // HD == iota((TILE, TILE), 1) // HD).astype(single)
    squares = jnp.dot(
        values * values, same_head, precision=lax.Precision.HIGHEST, preferred_element_type=single
    )
    normed = values * lax.rsqrt(squares / HD + epsilon) * tables[64:96, :]
    early = iota(values.shape, 1) % HD < HD // 2
    swapped = jnp.where(
        early, pltpu.roll(normed, TILE - HD // 2, 1), pltpu.roll(normed, HD // 2, 1)
    )
    turned = normed * tables[0:32, :] + swapped * tables[32:64, :]
    turned = turned.astype(bfloat).astype(single)

    rows = 24
    row = iota((rows, TILE), 0)
    half = iota((rows, TILE), 1) // HD
    key_head = row >> 2
    query = jnp.where(row < first_key, turned[:rows], 0.0)
    other = pltpu.roll(query, HD, 1)
    queries = []
    for u in range(2):
        placed = jnp.where(
            half == (key_head & 1), jnp.where((key_head & 1) == u, query, other), 0.0
        )
        queries.append(
            jnp.concatenate(
                [jnp.where((key_head >> 1) == c, placed, 0.0) for c in range(span // TILE)], axis=1
            )
        )
    queries = jnp.concatenate(queries, axis=0).astype(bfloat)

    extras = extra_k.shape[0]
    entries = kept.shape[0] - extras
    count = entries // KEEP
    extra_k[...] = kept[entries:, key_cols].astype(single)
    extra_v[...] = kept[entries:, value_cols].astype(single)
    first_value = first_key + KVH * HD // TILE * R_DEV
    for c in range(span // TILE):
        at = slice(c * TILE, (c + 1) * TILE)
        r = first_key + R_DEV * c
        extra_k[count : count + R_DEV, at] = turned[r : r + R_DEV]
        r = first_value + R_DEV * c
        extra_v[count : count + R_DEV, at] = values[r : r + R_DEV]

    def by_request(columns, size):
        odd = (iota((2 * rows, size), 0) & 1) == 1
        return jnp.where(odd, added[1:2, columns], added[0:1, columns])

    scores = dot_rows(queries, kept[:entries, key_cols]) * scale
    scores = scores + by_request(slice(0, entries), entries)
    extra = dot_rows(queries, extra_k[...].astype(bfloat)) * scale
    extra = extra + by_request(slice(entries, entries + extras), extras)
    top = jnp.maximum(
        jnp.max(scores, axis=1, keepdims=True), jnp.max(extra, axis=1, keepdims=True)
    )
    weight = jnp.where(scores > 0.5 * negative, jnp.exp(scores - top), 0.0)
    extra_weight = jnp.where(extra > 0.5 * negative, jnp.exp(extra - top), 0.0)
    mass = jnp.sum(weight, axis=1, keepdims=True) + jnp.sum(extra_weight, axis=1, keepdims=True)

    def weighted(parts, right):
        high = parts.astype(bfloat)
        low = (parts - high.astype(single)).astype(bfloat)
        return jnp.dot(high, right, preferred_element_type=single) + jnp.dot(
            low, right, preferred_element_type=single
        )

    total = weighted(weight, kept[:entries, value_cols]) + weighted(
        extra_weight, extra_v[...].astype(bfloat)
    )
    some = mass > 0.0
    mass = jnp.where(some, mass, 1.0)
    total = total / mass
    level = jnp.where(some, top + jnp.log(mass), negative)

    slot = key_head + (KVW // 2 - (KVW - span)) // HD
    results = []
    for u in range(2):
        mine = total[rows * u : rows * (u + 1)]
        picked = mine[:, :TILE]
        for c in range(1, span // TILE):
            picked = jnp.where((slot >> 1) == c, mine[:, c * TILE : (c + 1) * TILE], picked)
        results.append(jnp.where((slot & 1) == u, picked, pltpu.roll(picked, HD, 1)))
    out[...] = jnp.where(half == 0, results[0], results[1])
    logs[...] = jnp.broadcast_to(level, logs.shape)
    own = HEADS * HD // lanes
    size = 6
    column = iota((size, TILE), 1)
    here = column // TERMS == iota((size, TILE), 0)
    for k in range(lanes):
        r = own * k // TILE * R_DEV
        tile = [out[r : r + size, :]]
        for u in range(2):
            coded = three_terms(logs[rows * u + r : rows * u + r + size, :], column % TERMS)
            tile.append(jnp.sum(jnp.where(here, coded, 0.0), axis=0, keepdims=True))
        tile = jnp.concatenate(tile, axis=0).astype(bfloat)
        for g in range(groups):
            sent[g * lanes + k] = tile


def blocks_kernel(weight_far, same, other, done):
    width = same.shape[1]
    group = lax.axis_index("req")
    starts = [pl.multiple_of(((group & 1) ^ turn) * width, width) for turn in range(2)]
    parts = [weight_far.at[:, pl.ds(start, width)] for start in starts]
    for copy in fetch(parts, (same, other), done):
        copy.wait()


def project_kernel(source_far, came, first, second, sent, source, logs, rows, pieces, done):
    (copy,) = fetch((source_far,), (source,), done)
    lanes = lax.axis_size("head")
    groups = came.shape[0] // lanes
    group = lax.axis_index("req")
    features = first.shape[0]
    requests = rows.shape[0]
    size = 6
    tiles = [came[d].astype(single) for d in range(groups * lanes)]
    for g in range(groups):
        for k in range(lanes):
            logs[k, 2 * g : 2 * g + 2, :] = tiles[g * lanes + k][size:]
    spread = (iota((8, TILE), 1) // TERMS == iota((8, TILE), 0)).astype(single).astype(bfloat)
    levels = [dot_rows(spread, logs[k].astype(bfloat)) for k in range(lanes)]
    top = jnp.maximum(jnp.maximum(levels[0], levels[1]), jnp.maximum(levels[2], levels[3]))
    shares = [jnp.exp(level - top) for level in levels]
    mass = sum(shares)
    shares = [share / mass for share in shares]
    lower = iota((8, TILE), 1) < HD
    for g in range(groups):
        mixed = 0.0
        for k in range(lanes):
            share = shares[k]
            share = jnp.where(lower, share[:, 2 * g : 2 * g + 1], share[:, 2 * g + 1 : 2 * g + 2])
            mixed = mixed + share * tiles[g * lanes + k]
        for j in range(size // R_DEV):
            rows[R_DEV * g : R_DEV * (g + 1), TILE * j : TILE * (j + 1)] = mixed[
                R_DEV * j : R_DEV * (j + 1)
            ]
    width = rows.shape[1]
    shift = lax.rem(lax.axis_index("head") * (2 * features), TILE)
    attention = rows[...].astype(bfloat).astype(single)
    attention = pltpu.roll(attention, lax.rem(width - shift, width), 1)
    copy.wait()
    order = row_order(source, requests, False)
    attention = jnp.dot(order, attention.astype(bfloat), preferred_element_type=single)
    for b in range(2):
        pieces[b] = attention[:, features * b : features * (b + 1)]
    total = 0.0
    for turn, weight in enumerate((first, second)):
        piece = pieces[(group & 1) ^ turn].astype(bfloat)
        total = total + jnp.dot(piece, weight[...], preferred_element_type=single)
    sent[...] = total


def units_kernel(
    gain_far, own, one, two, three, hidden, mine, theirs, sent, mid_out, gain, done
):
    (copy,) = fetch((gain_far,), (gain,), done)
    rows, features = own.shape
    share = sent.shape[0] // lax.axis_size("head")
    group = lax.axis_index("req")
    lane = lax.axis_index("head")
    here = pl.ds(pl.multiple_of(group * features, features), features)
    mid = (own[...] + one[...]) + (two[...] + three[...])
    mid = (hidden[...].astype(single) + mid).astype(bfloat)
    mid_out[...] = mid
    mid = mid.astype(single)
    squares = jnp.sum(mid * mid, axis=1, keepdims=True)
    block = mine.shape[1] // share
    terms = three_terms(squares, iota((rows, sent.shape[2] - block), 1)).astype(bfloat)
    copy.wait()
    inputs = (mid * gain[:, here]).astype(bfloat)
    for turn, weight in enumerate((mine, theirs)):
        units = jnp.dot(inputs, weight[...], preferred_element_type=single).astype(bfloat)
        target = (lane ^ turn) * share
        for b in range(share):
            sent[target + b, :, :block] = units[:, block * b : block * (b + 1)]
            sent[target + b, :, block:] = terms


def active_kernel(came, active):
    total = came[0].astype(single)
    for g in range(1, came.shape[0]):
        total = total + came[g].astype(single)
    piece = active.shape[1]
    squares = jnp.sum(total[:, 2 * piece : 2 * piece + 3], axis=1, keepdims=True)
    factor = lax.rsqrt(squares / D + epsilon)
    gate = total[:, :piece] * factor
    up = total[:, piece : 2 * piece] * factor
    active[...] = (gate / (1.0 + jnp.exp(-gate)) * up).astype(bfloat)


def down_kernel(own, one, two, three, weight, mid, sent, active):
    groups, rows, width = sent.shape
    piece = own.shape[1]
    half = mid.shape[1]
    for turn, values in enumerate((own, one, two, three)):
        active[turn] = values[...]
    share = width // half
    group = lax.axis_index("req")
    lane = lax.axis_index("head")
    first = group // (2 * share) * 2 ^ lane
    down = jnp.dot(active[first], weight[:piece, :], preferred_element_type=single)
    down = down + jnp.dot(active[first ^ 1], weight[piece:, :], preferred_element_type=single)
    residual = mid[...].astype(single)
    for b in range(share):
        columns = slice(half * b, half * (b + 1))
        mine = group == lane * share + b
        total = (down[:, columns] + jnp.where(mine, residual, 0.0)).astype(bfloat)
        for g in range(groups):
            sent[g, :, columns] = total


def result_kernel(came, result):
    total = came[0].astype(single)
    for g in range(1, came.shape[0]):
        total = total + came[g].astype(single)
    result[...] = total.astype(bfloat)


def rotation_table():
    half = HD // 2
    size = -(-(NP + 1) // 8) * 8
    frequency = 10000.0 ** (-np.arange(half) / half)
    angles = PAGE * np.arange(size)[:, None] * frequency[None, :]
    cosine, sine = np.cos(angles), np.sin(angles)
    wide = [np.tile(np.concatenate(pair, axis=1), (1, TILE // HD)) for pair in
            ((cosine, cosine), (-sine, sine))]
    return jnp.asarray(np.concatenate(wide), dtype=single)


def swapped_lanes(value, turn):
    lanes = lax.axis_size("head")
    return lax.ppermute(value, "head", [(k, k ^ turn) for k in range(lanes)])


def from_lanes(value):
    return [value] + [swapped_lanes(value, turn) for turn in range(1, lax.axis_size("head"))]


def handed_over(value, turn):
    groups = lax.axis_size("req")
    lanes = lax.axis_size("head")
    share = groups // lanes
    pairs = [
        (g * lanes + h, (share * h + ((g & 1) ^ turn)) * lanes + g // share)
        for g in range(groups)
        for h in range(lanes)
    ]
    return lax.ppermute(value, both_axes, pairs)


def on_device(
    hidden_in,
    attention_gain,
    query_gain,
    key_gain,
    feedforward_gain,
    input_weight,
    output_weight,
    gate_weight,
    up_weight,
    down_weight,
    old_cache,
    keep_rows,
    drop_weights,
    dest_slots,
    lengths,
    page_table,
    source,
):
    groups = lax.axis_size("req")
    lanes = lax.axis_size("head")
    requests = hidden_in.shape[0]
    pages_here = old_cache.shape[0]
    devices = groups * lanes
    features = D // groups
    copies = pltpu.SemaphoreType.DMA

    others = from_lanes(hidden_in)[1:]
    blocks = run(
        blocks_kernel,
        [shaped((output_weight.shape[0], features), bfloat)] * 2,
        [output_weight],
        [],
        [copies((2,))],
    )
    handed = [handed_over(block, turn) for turn, block in enumerate(blocks)]
    scalars = [dest_slots, lengths[None, :], source[None, :], page_table]
    arrays = [
        keep_rows,
        drop_weights,
        query_gain[None, :],
        key_gain[None, :],
        rotation_table(),
        old_cache,
        gate_weight,
        up_weight,
    ]
    entries = pages_here * KEEP
    extras = 16
    compact, summaries, kept, added, tables, mine, theirs = run(
        prepare_kernel,
        [
            shaped((pages_here // 2, PAGE, KVW), bfloat),
            shaped((pages_here, KVW), bfloat),
            shaped((entries + extras, KVW), bfloat),
            shaped((8, entries + TILE), single),
            shaped((96, TILE), single),
            shaped(gate_weight.shape, bfloat),
            shaped(gate_weight.shape, bfloat),
        ],
        scalars + arrays,
        [],
        [
            *scalar_like(*scalars),
            *local_like(*arrays),
            pltpu.VMEM((pages_here, KVW), single),
            pltpu.VMEM((extras, KVW), single),
            pltpu.VMEM((2,) + gate_weight.shape, single),
            copies((len(scalars + arrays),)),
        ],
        2 * pages_here * TILE * PAGE * KVW,
    )
    tables, *moved = lax.optimization_barrier((tables, *others, *handed))
    others, handed = moved[: lanes - 1], moved[lanes - 1 :]

    holds = source[None, :]
    columns = input_weight.shape[1]
    padded = -(-columns // TILE) * TILE
    gain = attention_gain[None, :]
    weight = input_weight.T
    far = [holds, gain, weight, hidden_in]
    sent, hidden_block = run(
        first_kernel,
        [
            shaped((devices, R_DEV * padded // TILE, TILE), single),
            shaped((requests, features), bfloat),
        ],
        far,
        others,
        [
            *scalar_like(holds),
            *local_like(*far[1:]),
            pltpu.VMEM((lanes,) + hidden_in.shape, single),
            pltpu.VMEM((requests, padded), single),
            copies((len(far),)),
        ],
        2 * requests * features * columns,
    )
    came = lax.all_to_all(sent, both_axes, 0, 0, tiled=True)
    theirs, _ = lax.optimization_barrier((theirs, sent))
    theirs = swapped_lanes(theirs, 1)
    came, theirs = lax.optimization_barrier((came, theirs))
    span = -(-KVH * HD // TILE) * TILE
    (parts,) = run(
        attend_kernel,
        [shaped((devices, 8, TILE), bfloat)],
        [],
        [came, kept, added, tables],
        [
            pltpu.VMEM((32, TILE), single),
            pltpu.VMEM((extras, span), single),
            pltpu.VMEM((extras, span), single),
            pltpu.VMEM((24, TILE), single),
            pltpu.VMEM((48, TILE), single),
        ],
        6 * 48 * entries * span,
    )
    came = lax.all_to_all(parts, both_axes, 0, 0, tiled=True)
    (sent,) = run(
        project_kernel,
        [shaped((requests, features), single)],
        [holds],
        [came, *handed],
        [
            *scalar_like(holds),
            pltpu.VMEM((lanes, 2 * groups, TILE), single),
            pltpu.VMEM((requests, 3 * TILE), single),
            pltpu.VMEM((2, requests, output_weight.shape[0]), single),
            copies((1,)),
        ],
        2 * requests * output_weight.size,
    )
    gain = feedforward_gain[None, :]
    block = gate_weight.shape[1] // 2
    sent, mid = run(
        units_kernel,
        [
            shaped((groups, requests, block + TILE), bfloat),
            shaped((requests, features), bfloat),
        ],
        [gain],
        [*from_lanes(sent), hidden_block, mine, theirs],
        [*local_like(gain), copies((1,))],
        4 * requests * gate_weight.size,
    )
    (active,) = run(
        active_kernel, [shaped((requests, block // 2), bfloat)], [], [exchange(sent)]
    )
    (sent,) = run(
        down_kernel,
        [shaped((groups, requests, down_weight.shape[1]), bfloat)],
        [],
        [*from_lanes(active), down_weight, mid],
        [pltpu.VMEM((lanes,) + active.shape, bfloat)],
        2 * requests * down_weight.size,
    )
    (result,) = run(
        result_kernel, [shaped((requests, down_weight.shape[1]), bfloat)], [], [exchange(sent)]
    )
    return (compact, summaries, result)


def solution(mesh):
    placed = (
        P(None, "head"),
        P(),
        P(),
        P(),
        P(),
        P("req", "head"),
        P("req", "head"),
        P("req", "head"),
        P("req", "head"),
        P("req", "head"),
        P(("req", "head"), None, None),
        P(("req", "head"), None),
        P(("req", "head"), None),
        P(("req", "head"), None),
        P(),
        P("req", None),
        P(),
    )
    return jax.shard_map(
        on_device if mesh.shape["req"] <= DIRECT else on_device_wide,
        mesh=mesh,
        in_specs=placed,
        out_specs=(P(("req", "head"), None, None), P(("req", "head"), None), P(None, "head")),
        check_vma=False,
    )
```

```python
import jax
import jax.numpy as jnp
import numpy as np
from jax import lax
from jax.experimental import pallas as pl
from jax.experimental.pallas import tpu as pltpu
from jax.sharding import PartitionSpec as P

D = 2048
HEADS = 20
KVH = 5
HD = 64
FF = 5120
PAGE = 128
KEEP = 64
NP = 16
R_DEV = 2
KVW = 640

DIRECT = 8

epsilon = 1e-06
negative = -1e30
both_axes = ("req", "head")


def rms_scale(values):
    return lax.rsqrt(jnp.mean(values * values, axis=-1, keepdims=True) + epsilon)


def rms_rows(values, gain):
    return values * rms_scale(values) * gain


def rotate(vectors, positions):
    half = vectors.shape[-1] // 2
    frequency = 10000.0 ** (-jnp.arange(half, dtype=jnp.float32) / half)
    angles = positions.astype(jnp.float32)[:, None] * frequency[None, :]
    cosine = jnp.cos(angles)[:, None, :]
    sine = jnp.sin(angles)[:, None, :]
    first = vectors[..., :half]
    second = vectors[..., half:]
    return jnp.concatenate(
        [first * cosine - second * sine, second * cosine + first * sine], axis=-1
    )


def compact_pages(pages, keep, weights):
    rows = jnp.arange(pages.shape[1], dtype=jnp.int32)
    picks = keep[:, :, None] == rows[None, None, :]
    kept = jnp.einsum(
        "pkr,prc->pkc", picks.astype(jnp.bfloat16), pages, preferred_element_type=jnp.float32
    ).astype(jnp.bfloat16)
    dropped = weights * (1.0 - jnp.sum(picks.astype(jnp.float32), axis=1))
    total = jnp.sum(dropped, axis=1)
    means = (
        jnp.einsum(
            "pr,prc->pc", dropped, pages.astype(jnp.float32), precision=lax.Precision.HIGHEST
        )
        / total[:, None]
    )
    return (kept, means.astype(jnp.bfloat16), jnp.log(total))


def held_request(rows, source):
    half = R_DEV // 2
    position = rows % R_DEV
    slot = rows // R_DEV * half + position - half
    continued = jnp.arange(source.shape[0], dtype=jnp.int32)
    matches = source[None, :] == slot[:, None]
    owner_cont = jnp.sum(jnp.where(matches, continued[None, :], 0), axis=1)
    carried = owner_cont // half * R_DEV + half + owner_cont % half
    return jnp.where(position < half, rows, carried)


def pick_rows(order, rows):
    chosen = order[:, None] == jnp.arange(rows.shape[0], dtype=jnp.int32)[None, :]
    return jnp.dot(
        chosen.astype(jnp.bfloat16), rows, preferred_element_type=jnp.float32
    ).astype(jnp.bfloat16)


def exchange(parts):
    return lax.all_to_all(parts, "req", split_axis=0, concat_axis=0, tiled=True)


def to_block_owner(rows):
    groups = lax.axis_size("req")
    lanes = lax.axis_size("head")
    per_lane = groups // lanes
    pairs = [
        (g * lanes + h, (per_lane * h + g // lanes) * lanes + g % lanes)
        for g in range(groups)
        for h in range(lanes)
    ]
    return lax.ppermute(rows, both_axes, pairs)


def whole_sum(partial):
    if lax.axis_size("req") > DIRECT:
        return lax.psum(partial, "req")
    groups = lax.axis_size("req")
    return jnp.sum(exchange(jnp.broadcast_to(partial[None], (groups,) + partial.shape)), axis=0)


def on_device_wide(
    hidden_in,
    attention_gain,
    query_gain,
    key_gain,
    feedforward_gain,
    input_weight,
    output_weight,
    gate_weight,
    up_weight,
    down_weight,
    old_cache,
    keep_rows,
    drop_weights,
    dest_slots,
    lengths,
    page_table,
    source,
):
    groups = lax.axis_size("req")
    lanes = lax.axis_size("head")
    group = lax.axis_index("req")
    lane = lax.axis_index("head")
    requests = hidden_in.shape[0]
    half = R_DEV // 2
    split = KVH * HD
    ratio = HEADS // KVH
    scale = HD ** (-0.5)
    pages_here = old_cache.shape[0]
    everyone = jnp.arange(requests, dtype=jnp.int32)
    holders = held_request(everyone, source)
    held = lax.dynamic_slice_in_dim(holders, group * R_DEV, R_DEV, 0)
    held_len = lengths[held]
    positions = held_len * PAGE

    whole = lax.all_gather(hidden_in, "head", axis=1, tiled=True)
    normed = rms_rows(whole.astype(jnp.float32), attention_gain).astype(jnp.bfloat16)
    features = D // groups
    inputs = pick_rows(holders, lax.dynamic_slice_in_dim(normed, group * features, features, 1))
    partial_qkv = jnp.dot(inputs, input_weight, preferred_element_type=jnp.float32)
    sent = jnp.broadcast_to(
        partial_qkv.reshape(groups, 1, R_DEV, -1), (groups, lanes, R_DEV, partial_qkv.shape[1])
    ).reshape(groups * lanes, R_DEV, -1)
    got = lax.all_to_all(sent, both_axes, split_axis=0, concat_axis=0, tiled=True)
    mixed = jnp.sum(got.reshape(groups, lanes, R_DEV, -1), axis=0).astype(jnp.bfloat16)
    held_qkv = jnp.swapaxes(mixed, 0, 1).reshape(R_DEV, -1).astype(jnp.float32)

    query = rotate(
        rms_rows(held_qkv[:, : HEADS * HD].reshape(R_DEV, HEADS, HD), query_gain), positions
    ).astype(jnp.bfloat16)
    key_new = rotate(
        rms_rows(held_qkv[:, HEADS * HD : (HEADS + KVH) * HD].reshape(R_DEV, KVH, HD), key_gain),
        positions,
    ).astype(jnp.bfloat16)
    value_new = held_qkv[:, (HEADS + KVH) * HD :].reshape(R_DEV, KVH, HD)
    kept, means, bias = compact_pages(old_cache, keep_rows, drop_weights)
    destination = dest_slots[0]
    fresh_ids = jnp.arange(pages_here, dtype=jnp.int32)
    inverse = jnp.sum(
        jnp.where(destination[None, :] == fresh_ids[:, None], fresh_ids[None, :], 0), axis=1
    )
    compact = kept[inverse].reshape(pages_here // 2, PAGE, KVW)
    summaries = means[inverse]
    per_lane = NP // lanes
    table = page_table.reshape(R_DEV, per_lane, lanes)
    mine = lax.dynamic_slice_in_dim(table, lane, 1, 2)[:, :, 0]
    logical = jnp.arange(per_lane, dtype=jnp.int32) * lanes + lane
    live = logical[None, :] < held_len[:, None]
    owner = jnp.any((mine[:, :, None] == fresh_ids[None, None, :]) & live[:, :, None], axis=1)
    query_groups = query.reshape(R_DEV, KVH, ratio, HD)
    row_keys = kept[:, :, :split].reshape(pages_here, KEEP, KVH, HD)
    row_values = kept[:, :, split:].reshape(pages_here, KEEP, KVH, HD)
    row_live = keep_rows >= 0
    allowed = owner[:, None, None, :, None] & row_live[None, None, None, :, :]
    scores = (
        jnp.einsum("rngd,pmnd->rngpm", query_groups, row_keys, preferred_element_type=jnp.float32)
        * scale
    )
    scores = jnp.where(allowed, scores, negative)
    mean_keys = means[:, :split].reshape(pages_here, KVH, HD)
    mean_values = means[:, split:].reshape(pages_here, KVH, HD)
    mean_scores = (
        jnp.einsum("rngd,pnd->rngp", query_groups, mean_keys, preferred_element_type=jnp.float32)
        * scale
        + bias[None, None, None, :]
    )
    mean_allowed = owner[:, None, None, :]
    mean_scores = jnp.where(mean_allowed, mean_scores, negative)
    own_score = (
        jnp.einsum("rngd,rnd->rng", query_groups, key_new, preferred_element_type=jnp.float32)
        * scale
    )
    own_score = jnp.where(lane == 0, own_score, negative)
    top = jnp.maximum(jnp.max(scores, axis=(3, 4)), jnp.max(mean_scores, axis=3))
    top = jnp.maximum(top, own_score)
    row_weight = jnp.where(allowed, jnp.exp(scores - top[..., None, None]), 0.0)
    mean_weight = jnp.where(mean_allowed, jnp.exp(mean_scores - top[..., None]), 0.0)
    own_weight = jnp.where(lane == 0, jnp.exp(own_score - top), 0.0)
    mass = jnp.sum(row_weight, axis=(3, 4)) + jnp.sum(mean_weight, axis=3) + own_weight
    total = jnp.einsum(
        "rngpm,pmnd->rngd",
        row_weight,
        row_values.astype(jnp.float32),
        precision=lax.Precision.HIGHEST,
    )
    total = total + jnp.einsum(
        "rngp,pnd->rngd",
        mean_weight,
        mean_values.astype(jnp.float32),
        precision=lax.Precision.HIGHEST,
    )
    total = total + own_weight[..., None] * value_new[:, :, None, :]

    some = mass > 0.0
    level = jnp.where(some, top + jnp.log(jnp.where(some, mass, 1.0)), negative)
    means_out = total / jnp.where(some, mass, 1.0)[..., None]
    own = HEADS * HD // groups
    parts = jnp.stack([means_out, jnp.broadcast_to(level[..., None], total.shape)])
    parts = jnp.transpose(parts.reshape(2, R_DEV, groups, own), (2, 1, 0, 3))
    parts = jnp.broadcast_to(
        parts.reshape(groups, 1, R_DEV, 2 * own), (groups, lanes, R_DEV, 2 * own)
    ).reshape(groups * lanes, R_DEV, 2 * own)
    came = lax.all_to_all(parts, both_axes, 0, 0, tiled=True)
    came = came.reshape(groups, lanes, R_DEV, 2 * own)
    outs, levels = came[..., :own], came[..., own:]
    weights = jnp.exp(levels - jnp.max(levels, axis=1, keepdims=True))
    attention = jnp.sum(outs * weights, axis=1) / jnp.sum(weights, axis=1)
    attention = attention.reshape(requests, own).astype(jnp.bfloat16)
    back = jnp.sum(
        jnp.where(holders[None, :] == everyone[:, None], everyone[None, :], 0), axis=1
    )
    projected = jnp.dot(
        pick_rows(back, attention), output_weight, preferred_element_type=jnp.float32
    )
    projected = projected + jnp.where(group == 0, hidden_in.astype(jnp.float32), 0.0)

    share = groups // lanes
    blocks = jnp.moveaxis(projected.reshape(requests, share, 1, features), 0, 2)
    blocks = jnp.broadcast_to(blocks, (share, lanes, requests, features))
    mid = jnp.sum(exchange(blocks.reshape(groups, requests, features)), axis=0)
    mid = to_block_owner(mid.astype(jnp.bfloat16)).astype(jnp.float32)
    squares = jnp.sum(mid * mid, axis=1, keepdims=True)
    gain_here = lax.dynamic_slice_in_dim(feedforward_gain, group * features, features, 0)
    inputs_mid = (mid * gain_here).astype(jnp.bfloat16)
    local_units = gate_weight.shape[1]
    piece = local_units // groups
    gates = jnp.dot(inputs_mid, gate_weight, preferred_element_type=jnp.float32)
    ups = jnp.dot(inputs_mid, up_weight, preferred_element_type=jnp.float32)
    both = jnp.concatenate(
        [
            gates.reshape(requests, groups, piece),
            ups.reshape(requests, groups, piece),
            jnp.broadcast_to(squares[:, :, None], (requests, groups, 1)),
        ],
        axis=2,
    )
    sums = jnp.sum(exchange(jnp.swapaxes(both, 0, 1)), axis=0)
    factor = lax.rsqrt(sums[:, 2 * piece :] / D + epsilon)
    gate = sums[:, :piece] * factor
    active = (jax.nn.silu(gate) * (sums[:, piece : 2 * piece] * factor)).astype(jnp.bfloat16)
    active_here = lax.all_gather(to_block_owner(active), "head", axis=1, tiled=True)
    down = jnp.dot(active_here, down_weight, preferred_element_type=jnp.float32)
    residual = [jnp.where(group == lane * share + k, mid, 0.0) for k in range(share)]
    down = down + jnp.concatenate(residual, axis=1)
    result = whole_sum(down).astype(jnp.bfloat16)
    return (compact, summaries, result)


TILE = 128
bfloat = jnp.bfloat16
single = jnp.float32


TERMS = 4


def three_terms(value, place):
    high = value.astype(bfloat).astype(single)
    rest = value - high
    middle = rest.astype(bfloat).astype(single)
    low = jnp.where(place == 2, rest - middle, 0.0)
    return jnp.where(place == 0, high, jnp.where(place == 1, middle, low))


def iota(shape, axis):
    return lax.broadcasted_iota(jnp.int32, shape, axis)


def run(kernel, outs, far, near, scratch=(), flops=0):
    in_specs = [pl.BlockSpec(memory_space=pltpu.HBM) for _ in far]
    in_specs += [pl.BlockSpec(memory_space=pltpu.VMEM) for _ in near]
    moved = sum(a.size * a.dtype.itemsize for a in [*far, *near, *outs])
    return pl.pallas_call(
        kernel,
        out_shape=list(outs),
        in_specs=in_specs,
        out_specs=[pl.BlockSpec(memory_space=pltpu.VMEM) for _ in outs],
        scratch_shapes=list(scratch),
        compiler_params=pltpu.CompilerParams(vmem_limit_bytes=16 * 2**20),
        cost_estimate=pl.CostEstimate(flops=flops, bytes_accessed=moved, transcendentals=0),
    )(*[pltpu.with_memory_space_constraint(a, pltpu.HBM) for a in far], *near)


def fetch(sources, targets, done):
    copies = [
        pltpu.make_async_copy(source, target, done.at[k])
        for k, (source, target) in enumerate(zip(sources, targets))
    ]
    for copy in copies:
        copy.start()
    return copies


def local_like(*arrays):
    return [pltpu.VMEM(a.shape, a.dtype) for a in arrays]


def scalar_like(*arrays):
    return [pltpu.SMEM(a.shape, a.dtype) for a in arrays]


def row_order(source, count, to_holder):
    first, second = iota((count, count), 0), iota((count, count), 1)
    if not to_holder:
        first, second = second, first
    order = (first == second) & (first % R_DEV == 0)
    for c in range(source.shape[1]):
        order = order | ((first == source[0, c] * R_DEV + 1) & (second == c * R_DEV + 1))
    return order.astype(single).astype(bfloat)


def shaped(shape, dtype):
    return jax.ShapeDtypeStruct(shape, dtype)


def first_kernel(
    source_far, gain_far, weight_far, hidden_far, one, two, three, sent, block, source, gain,
    weight, hidden, lanes_of, wide, done
):
    copies = fetch(
        (source_far, gain_far, weight_far, hidden_far), (source, gain, weight, hidden), done
    )
    rows = hidden.shape[0]
    groups = rows // R_DEV
    lanes = sent.shape[0] // groups
    columns, features = weight.shape
    group = lax.axis_index("req")
    share = groups // lanes
    squares = 0.0
    for turn, values in enumerate((one, two, three)):
        values = values[...].astype(single)
        lanes_of[turn + 1] = values
        squares = squares + jnp.sum(values * values, axis=1, keepdims=True)
    copies[3].wait()
    values = hidden[...].astype(single)
    lanes_of[0] = values
    squares = squares + jnp.sum(values * values, axis=1, keepdims=True)
    factor = lax.rsqrt(squares / D + epsilon)
    here = pl.ds(pl.multiple_of(group * features, features), features)
    within = pl.ds(pl.multiple_of(group % share * features, features), features)
    mine = lanes_of[group // share ^ lax.axis_index("head"), :, within]
    block[...] = mine.astype(bfloat)
    wide[...] = jnp.zeros_like(wide)
    for copy in copies[:3]:
        copy.wait()
    normed = (mine * factor * gain[:, here]).astype(bfloat)
    order = row_order(source, rows, True)
    normed = jnp.dot(order, normed, preferred_element_type=single).astype(bfloat)
    wide[:, :columns] = dot_rows(normed, weight[...])
    for g in range(groups):
        tile = jnp.concatenate(
            [
                wide[R_DEV * g : R_DEV * (g + 1), TILE * j : TILE * (j + 1)]
                for j in range(wide.shape[1] // TILE)
            ],
            axis=0,
        )
        for k in range(lanes):
            sent[g * lanes + k] = tile


def dot_rows(left, right):
    return lax.dot_general(left, right, (((1,), (1,)), ((), ())), preferred_element_type=single)


def prepare_kernel(*refs):
    far, refs = refs[:12], refs[12:]
    (compact, summaries, kept, added, tables, mine, theirs), refs = refs[:7], refs[7:]
    near, (ordered, plain, dealt, done) = refs[:12], refs[12:]
    copies = fetch(far, near, done)
    (dest, lengths, source, table, keep, weights, query_gain, key_gain, turns) = near[:9]
    pages, gate, up = near[9:]
    group = lax.axis_index("req")
    lane = lax.axis_index("head")
    lanes = lax.axis_size("head")
    for copy in copies[:9]:
        copy.wait()

    carried = 0
    for c in range(source.shape[1]):
        carried = carried + jnp.where(source[0, c] == group, c, 0)
    held_len = (lengths[0, group * R_DEV], lengths[0, carried * R_DEV + 1])
    count, rows, _ = pages.shape
    owned = []
    for r in range(R_DEV):
        slots = []
        for i in range(table.shape[1] // lanes):
            j = i * lanes + lane
            slots.append(jnp.where(j < held_len[r], table[r, j], -1))
        owned.append(slots)

    def owner(r, p):
        found = owned[r][0] == p
        for slot in owned[r][1:]:
            found = found | (slot == p)
        return found

    row = iota((32, TILE), 0)
    odd = (row & 1) == 1
    half_rows = turns.shape[0] // 2
    for part in range(2):
        pair = [turns[pl.ds(part * half_rows + held_len[r], 1), :] for r in range(R_DEV)]
        tables[32 * part : 32 * (part + 1), :] = jnp.where(odd, pair[1], pair[0])
    query_rows = HEADS * HD // TILE * R_DEV
    for c in range(TILE // HD):
        columns = slice(HD * c, HD * (c + 1))
        tables[64 : 64 + query_rows, columns] = jnp.broadcast_to(
            query_gain[...], (query_rows, HD)
        )
        tables[64 + query_rows : 96, columns] = jnp.broadcast_to(
            key_gain[...], (32 - query_rows, HD)
        )

    column = iota((1, TILE), 1)
    entries = count * KEEP
    added[...] = jnp.full_like(added, negative)
    extra = [
        jnp.where((column == count + r) & (lane == 0), 0.0, negative) for r in range(R_DEV)
    ]
    weight_columns = weights[...].T
    rows_of = iota((rows, KEEP), 0)
    place = iota((rows, 16), 1)
    lefts, totals = [], []
    for p in range(count):
        picks = (keep[p : p + 1, :] == rows_of).astype(single)
        dropped = weight_columns[:, p : p + 1] * (1.0 - jnp.sum(picks, axis=1, keepdims=True))
        total = jnp.sum(dropped, axis=0, keepdims=True)
        left = jnp.concatenate([picks, three_terms(dropped, place)], axis=1).astype(bfloat)
        lefts.append(left)
        totals.append(total)
        live = jnp.where(keep[p : p + 1, :] >= 0, 0.0, negative)
        for r in range(R_DEV):
            here = owner(r, p)
            added[r : r + 1, KEEP * p : KEEP * (p + 1)] = jnp.where(here, live, negative)
            level = jnp.where(here, jnp.log(total), negative)
            extra[r] = jnp.where(column == p, level, extra[r])
    copies[9].wait()
    for p in range(count):
        both = lax.dot_general(
            lefts[p], pages[p], (((0,), (0,)), ((), ())), preferred_element_type=single
        )
        rows_kept = both[:KEEP].astype(bfloat)
        kept[KEEP * p : KEEP * (p + 1), :] = rows_kept
        slot = dest[0, p]
        start = pl.multiple_of((slot & 1) * KEEP, KEEP)
        compact[slot >> 1, pl.ds(start, KEEP), :] = rows_kept
        mean = both[KEEP : KEEP + 1] + both[KEEP + 1 : KEEP + 2] + both[KEEP + 2 : KEEP + 3]
        mean = mean / totals[p]
        plain[p : p + 1, :] = mean
        ordered[pl.ds(slot, 1), :] = mean
    for r in range(R_DEV):
        added[r : r + 1, entries : entries + TILE] = extra[r]
    plain[count:, :] = jnp.zeros_like(plain[count:, :])
    kept[entries:, :] = plain[...].astype(bfloat)
    summaries[...] = ordered[...].astype(bfloat)

    for copy in copies[10:]:
        copy.wait()
    block = gate.shape[1] // 2
    piece = block // 2
    for k in range(2):
        for b in range(2):
            columns = slice(b * block + k * piece, b * block + (k + 1) * piece)
            start = b * block
            dealt[k, :, start : start + piece] = gate[:, columns].astype(single)
            dealt[k, :, start + piece : start + block] = up[:, columns].astype(single)
    mine[...] = dealt[lane & 1].astype(bfloat)
    theirs[...] = dealt[1 - (lane & 1)].astype(bfloat)


def attend_kernel(came, kept, added, tables, sent, x, extra_k, extra_v, out, logs):
    lanes = lax.axis_size("head")
    groups = came.shape[0] // lanes
    width = (HEADS + 2 * KVH) * HD // lanes
    span = -(-KVH * HD // TILE) * TILE
    key_cols = slice(0, span)
    value_cols = slice(KVW - span, KVW)
    first_key = HEADS * HD // TILE * R_DEV
    scale = HD ** (-0.5)
    x[...] = jnp.zeros_like(x)
    column = iota((8, TILE), 1)
    for k in range(lanes):
        tile = came[k].astype(single)
        for g in range(1, groups):
            tile = tile + came[g * lanes + k].astype(single)
        tile = tile.astype(bfloat).astype(single)
        base, shift = divmod(width * k, TILE)
        base = base * R_DEV
        if shift:
            tile = pltpu.roll(tile, shift, 1)
            x[base + 2 : base + 10, :] += jnp.where(column < shift, tile, 0.0)
        x[base : base + 8, :] += jnp.where(column >= shift, tile, 0.0)
    values = x[...]
    same_head = (iota((TILE, TILE), 0) // HD == iota((TILE, TILE), 1) // HD).astype(single)
    squares = jnp.dot(
        values * values, same_head, precision=lax.Precision.HIGHEST, preferred_element_type=single
    )
    normed = values * lax.rsqrt(squares / HD + epsilon) * tables[64:96, :]
    early = iota(values.shape, 1) % HD < HD // 2
    swapped = jnp.where(
        early, pltpu.roll(normed, TILE - HD // 2, 1), pltpu.roll(normed, HD // 2, 1)
    )
    turned = normed * tables[0:32, :] + swapped * tables[32:64, :]
    turned = turned.astype(bfloat).astype(single)

    rows = 24
    row = iota((rows, TILE), 0)
    half = iota((rows, TILE), 1) // HD
    key_head = row >> 2
    query = jnp.where(row < first_key, turned[:rows], 0.0)
    other = pltpu.roll(query, HD, 1)
    queries = []
    for u in range(2):
        placed = jnp.where(
            half == (key_head & 1), jnp.where((key_head & 1) == u, query, other), 0.0
        )
        queries.append(
            jnp.concatenate(
                [jnp.where((key_head >> 1) == c, placed, 0.0) for c in range(span // TILE)], axis=1
            )
        )
    queries = jnp.concatenate(queries, axis=0).astype(bfloat)

    extras = extra_k.shape[0]
    entries = kept.shape[0] - extras
    count = entries // KEEP
    extra_k[...] = kept[entries:, key_cols].astype(single)
    extra_v[...] = kept[entries:, value_cols].astype(single)
    first_value = first_key + KVH * HD // TILE * R_DEV
    for c in range(span // TILE):
        at = slice(c * TILE, (c + 1) * TILE)
        r = first_key + R_DEV * c
        extra_k[count : count + R_DEV, at] = turned[r : r + R_DEV]
        r = first_value + R_DEV * c
        extra_v[count : count + R_DEV, at] = values[r : r + R_DEV]

    def by_request(columns, size):
        odd = (iota((2 * rows, size), 0) & 1) == 1
        return jnp.where(odd, added[1:2, columns], added[0:1, columns])

    scores = dot_rows(queries, kept[:entries, key_cols]) * scale
    scores = scores + by_request(slice(0, entries), entries)
    extra = dot_rows(queries, extra_k[...].astype(bfloat)) * scale
    extra = extra + by_request(slice(entries, entries + extras), extras)
    top = jnp.maximum(
        jnp.max(scores, axis=1, keepdims=True), jnp.max(extra, axis=1, keepdims=True)
    )
    weight = jnp.where(scores > 0.5 * negative, jnp.exp(scores - top), 0.0)
    extra_weight = jnp.where(extra > 0.5 * negative, jnp.exp(extra - top), 0.0)
    mass = jnp.sum(weight, axis=1, keepdims=True) + jnp.sum(extra_weight, axis=1, keepdims=True)

    def weighted(parts, right):
        high = parts.astype(bfloat)
        low = (parts - high.astype(single)).astype(bfloat)
        return jnp.dot(high, right, preferred_element_type=single) + jnp.dot(
            low, right, preferred_element_type=single
        )

    total = weighted(weight, kept[:entries, value_cols]) + weighted(
        extra_weight, extra_v[...].astype(bfloat)
    )
    some = mass > 0.0
    mass = jnp.where(some, mass, 1.0)
    total = total / mass
    level = jnp.where(some, top + jnp.log(mass), negative)

    slot = key_head + (KVW // 2 - (KVW - span)) // HD
    results = []
    for u in range(2):
        mine = total[rows * u : rows * (u + 1)]
        picked = mine[:, :TILE]
        for c in range(1, span // TILE):
            picked = jnp.where((slot >> 1) == c, mine[:, c * TILE : (c + 1) * TILE], picked)
        results.append(jnp.where((slot & 1) == u, picked, pltpu.roll(picked, HD, 1)))
    out[...] = jnp.where(half == 0, results[0], results[1])
    logs[...] = jnp.broadcast_to(level, logs.shape)
    own = HEADS * HD // lanes
    size = 6
    column = iota((size, TILE), 1)
    here = column // TERMS == iota((size, TILE), 0)
    for k in range(lanes):
        r = own * k // TILE * R_DEV
        tile = [out[r : r + size, :]]
        for u in range(2):
            coded = three_terms(logs[rows * u + r : rows * u + r + size, :], column % TERMS)
            tile.append(jnp.sum(jnp.where(here, coded, 0.0), axis=0, keepdims=True))
        tile = jnp.concatenate(tile, axis=0).astype(bfloat)
        for g in range(groups):
            sent[g * lanes + k] = tile


def blocks_kernel(weight_far, same, other, done):
    width = same.shape[1]
    group = lax.axis_index("req")
    starts = [pl.multiple_of(((group & 1) ^ turn) * width, width) for turn in range(2)]
    parts = [weight_far.at[:, pl.ds(start, width)] for start in starts]
    for copy in fetch(parts, (same, other), done):
        copy.wait()


def project_kernel(source_far, came, first, second, sent, source, logs, rows, pieces, done):
    (copy,) = fetch((source_far,), (source,), done)
    lanes = lax.axis_size("head")
    groups = came.shape[0] // lanes
    group = lax.axis_index("req")
    features = first.shape[0]
    requests = rows.shape[0]
    size = 6
    tiles = [came[d].astype(single) for d in range(groups * lanes)]
    for g in range(groups):
        for k in range(lanes):
            logs[k, 2 * g : 2 * g + 2, :] = tiles[g * lanes + k][size:]
    spread = (iota((8, TILE), 1) // TERMS == iota((8, TILE), 0)).astype(single).astype(bfloat)
    levels = [dot_rows(spread, logs[k].astype(bfloat)) for k in range(lanes)]
    top = jnp.maximum(jnp.maximum(levels[0], levels[1]), jnp.maximum(levels[2], levels[3]))
    shares = [jnp.exp(level - top) for level in levels]
    mass = sum(shares)
    shares = [share / mass for share in shares]
    lower = iota((8, TILE), 1) < HD
    for g in range(groups):
        mixed = 0.0
        for k in range(lanes):
            share = shares[k]
            share = jnp.where(lower, share[:, 2 * g : 2 * g + 1], share[:, 2 * g + 1 : 2 * g + 2])
            mixed = mixed + share * tiles[g * lanes + k]
        for j in range(size // R_DEV):
            rows[R_DEV * g : R_DEV * (g + 1), TILE * j : TILE * (j + 1)] = mixed[
                R_DEV * j : R_DEV * (j + 1)
            ]
    width = rows.shape[1]
    shift = lax.rem(lax.axis_index("head") * (2 * features), TILE)
    attention = rows[...].astype(bfloat).astype(single)
    attention = pltpu.roll(attention, lax.rem(width - shift, width), 1)
    copy.wait()
    order = row_order(source, requests, False)
    attention = jnp.dot(order, attention.astype(bfloat), preferred_element_type=single)
    for b in range(2):
        pieces[b] = attention[:, features * b : features * (b + 1)]
    total = 0.0
    for turn, weight in enumerate((first, second)):
        piece = pieces[(group & 1) ^ turn].astype(bfloat)
        total = total + jnp.dot(piece, weight[...], preferred_element_type=single)
    sent[...] = total


def units_kernel(
    gain_far, own, one, two, three, hidden, mine, theirs, sent, mid_out, gain, done
):
    (copy,) = fetch((gain_far,), (gain,), done)
    rows, features = own.shape
    share = sent.shape[0] // lax.axis_size("head")
    group = lax.axis_index("req")
    lane = lax.axis_index("head")
    here = pl.ds(pl.multiple_of(group * features, features), features)
    mid = (own[...] + one[...]) + (two[...] + three[...])
    mid = (hidden[...].astype(single) + mid).astype(bfloat)
    mid_out[...] = mid
    mid = mid.astype(single)
    squares = jnp.sum(mid * mid, axis=1, keepdims=True)
    block = mine.shape[1] // share
    terms = three_terms(squares, iota((rows, sent.shape[2] - block), 1)).astype(bfloat)
    copy.wait()
    inputs = (mid * gain[:, here]).astype(bfloat)
    for turn, weight in enumerate((mine, theirs)):
        units = jnp.dot(inputs, weight[...], preferred_element_type=single).astype(bfloat)
        target = (lane ^ turn) * share
        for b in range(share):
            sent[target + b, :, :block] = units[:, block * b : block * (b + 1)]
            sent[target + b, :, block:] = terms


def active_kernel(came, active):
    total = came[0].astype(single)
    for g in range(1, came.shape[0]):
        total = total + came[g].astype(single)
    piece = active.shape[1]
    squares = jnp.sum(total[:, 2 * piece : 2 * piece + 3], axis=1, keepdims=True)
    factor = lax.rsqrt(squares / D + epsilon)
    gate = total[:, :piece] * factor
    up = total[:, piece : 2 * piece] * factor
    active[...] = (gate / (1.0 + jnp.exp(-gate)) * up).astype(bfloat)


def down_kernel(own, one, two, three, weight, mid, sent, active):
    groups, rows, width = sent.shape
    piece = own.shape[1]
    half = mid.shape[1]
    for turn, values in enumerate((own, one, two, three)):
        active[turn] = values[...]
    share = width // half
    group = lax.axis_index("req")
    lane = lax.axis_index("head")
    first = group // (2 * share) * 2 ^ lane
    down = jnp.dot(active[first], weight[:piece, :], preferred_element_type=single)
    down = down + jnp.dot(active[first ^ 1], weight[piece:, :], preferred_element_type=single)
    residual = mid[...].astype(single)
    for b in range(share):
        columns = slice(half * b, half * (b + 1))
        mine = group == lane * share + b
        total = (down[:, columns] + jnp.where(mine, residual, 0.0)).astype(bfloat)
        for g in range(groups):
            sent[g, :, columns] = total


def result_kernel(came, result):
    total = came[0].astype(single)
    for g in range(1, came.shape[0]):
        total = total + came[g].astype(single)
    result[...] = total.astype(bfloat)


def rotation_table():
    half = HD // 2
    size = -(-(NP + 1) // 8) * 8
    frequency = 10000.0 ** (-np.arange(half) / half)
    angles = PAGE * np.arange(size)[:, None] * frequency[None, :]
    cosine, sine = np.cos(angles), np.sin(angles)
    wide = [np.tile(np.concatenate(pair, axis=1), (1, TILE // HD)) for pair in
            ((cosine, cosine), (-sine, sine))]
    return jnp.asarray(np.concatenate(wide), dtype=single)


def swapped_lanes(value, turn):
    lanes = lax.axis_size("head")
    return lax.ppermute(value, "head", [(k, k ^ turn) for k in range(lanes)])


def from_lanes(value):
    return [value] + [swapped_lanes(value, turn) for turn in range(1, lax.axis_size("head"))]


def handed_over(value, turn):
    groups = lax.axis_size("req")
    lanes = lax.axis_size("head")
    share = groups // lanes
    pairs = [
        (g * lanes + h, (share * h + ((g & 1) ^ turn)) * lanes + g // share)
        for g in range(groups)
        for h in range(lanes)
    ]
    return lax.ppermute(value, both_axes, pairs)


def on_device(
    hidden_in,
    attention_gain,
    query_gain,
    key_gain,
    feedforward_gain,
    input_weight,
    output_weight,
    gate_weight,
    up_weight,
    down_weight,
    old_cache,
    keep_rows,
    drop_weights,
    dest_slots,
    lengths,
    page_table,
    source,
):
    groups = lax.axis_size("req")
    lanes = lax.axis_size("head")
    requests = hidden_in.shape[0]
    pages_here = old_cache.shape[0]
    devices = groups * lanes
    features = D // groups
    copies = pltpu.SemaphoreType.DMA

    others = from_lanes(hidden_in)[1:]
    blocks = run(
        blocks_kernel,
        [shaped((output_weight.shape[0], features), bfloat)] * 2,
        [output_weight],
        [],
        [copies((2,))],
    )
    handed = [handed_over(block, turn) for turn, block in enumerate(blocks)]
    scalars = [dest_slots, lengths[None, :], source[None, :], page_table]
    arrays = [
        keep_rows,
        drop_weights,
        query_gain[None, :],
        key_gain[None, :],
        rotation_table(),
        old_cache,
        gate_weight,
        up_weight,
    ]
    entries = pages_here * KEEP
    extras = 16
    compact, summaries, kept, added, tables, mine, theirs = run(
        prepare_kernel,
        [
            shaped((pages_here // 2, PAGE, KVW), bfloat),
            shaped((pages_here, KVW), bfloat),
            shaped((entries + extras, KVW), bfloat),
            shaped((8, entries + TILE), single),
            shaped((96, TILE), single),
            shaped(gate_weight.shape, bfloat),
            shaped(gate_weight.shape, bfloat),
        ],
        scalars + arrays,
        [],
        [
            *scalar_like(*scalars),
            *local_like(*arrays),
            pltpu.VMEM((pages_here, KVW), single),
            pltpu.VMEM((extras, KVW), single),
            pltpu.VMEM((2,) + gate_weight.shape, single),
            copies((len(scalars + arrays),)),
        ],
        2 * pages_here * TILE * PAGE * KVW,
    )
    tables, *moved = lax.optimization_barrier((tables, *others, *handed))
    others, handed = moved[: lanes - 1], moved[lanes - 1 :]

    holds = source[None, :]
    columns = input_weight.shape[1]
    padded = -(-columns // TILE) * TILE
    gain = attention_gain[None, :]
    weight = input_weight.T
    far = [holds, gain, weight, hidden_in]
    sent, hidden_block = run(
        first_kernel,
        [
            shaped((devices, R_DEV * padded // TILE, TILE), single),
            shaped((requests, features), bfloat),
        ],
        far,
        others,
        [
            *scalar_like(holds),
            *local_like(*far[1:]),
            pltpu.VMEM((lanes,) + hidden_in.shape, single),
            pltpu.VMEM((requests, padded), single),
            copies((len(far),)),
        ],
        2 * requests * features * columns,
    )
    came = lax.all_to_all(sent, both_axes, 0, 0, tiled=True)
    theirs, _ = lax.optimization_barrier((theirs, sent))
    theirs = swapped_lanes(theirs, 1)
    came, theirs = lax.optimization_barrier((came, theirs))
    span = -(-KVH * HD // TILE) * TILE
    (parts,) = run(
        attend_kernel,
        [shaped((devices, 8, TILE), bfloat)],
        [],
        [came, kept, added, tables],
        [
            pltpu.VMEM((32, TILE), single),
            pltpu.VMEM((extras, span), single),
            pltpu.VMEM((extras, span), single),
            pltpu.VMEM((24, TILE), single),
            pltpu.VMEM((48, TILE), single),
        ],
        6 * 48 * entries * span,
    )
    came = lax.all_to_all(parts, both_axes, 0, 0, tiled=True)
    (sent,) = run(
        project_kernel,
        [shaped((requests, features), single)],
        [holds],
        [came, *handed],
        [
            *scalar_like(holds),
            pltpu.VMEM((lanes, 2 * groups, TILE), single),
            pltpu.VMEM((requests, 3 * TILE), single),
            pltpu.VMEM((2, requests, output_weight.shape[0]), single),
            copies((1,)),
        ],
        2 * requests * output_weight.size,
    )
    gain = feedforward_gain[None, :]
    block = gate_weight.shape[1] // 2
    sent, mid = run(
        units_kernel,
        [
            shaped((groups, requests, block + TILE), bfloat),
            shaped((requests, features), bfloat),
        ],
        [gain],
        [*from_lanes(sent), hidden_block, mine, theirs],
        [*local_like(gain), copies((1,))],
        4 * requests * gate_weight.size,
    )
    (active,) = run(
        active_kernel, [shaped((requests, block // 2), bfloat)], [], [exchange(sent)]
    )
    (sent,) = run(
        down_kernel,
        [shaped((groups, requests, down_weight.shape[1]), bfloat)],
        [],
        [*from_lanes(active), down_weight, mid],
        [pltpu.VMEM((lanes,) + active.shape, bfloat)],
        2 * requests * down_weight.size,
    )
    (result,) = run(
        result_kernel, [shaped((requests, down_weight.shape[1]), bfloat)], [], [exchange(sent)]
    )
    return (compact, summaries, result)


def solution(mesh):
    placed = (
        P(None, "head"),
        P(),
        P(),
        P(),
        P(),
        P("req", "head"),
        P("req", "head"),
        P("req", "head"),
        P("req", "head"),
        P("req", "head"),
        P(("req", "head"), None, None),
        P(("req", "head"), None),
        P(("req", "head"), None),
        P(("req", "head"), None),
        P(),
        P("req", None),
        P(),
    )
    return jax.shard_map(
        on_device if mesh.shape["req"] <= DIRECT else on_device_wide,
        mesh=mesh,
        in_specs=placed,
        out_specs=(P(("req", "head"), None, None), P(("req", "head"), None), P(None, "head")),
        check_vma=False,
    )
```

```python
import jax
import jax.numpy as jnp
import numpy as np
from jax import lax
from jax.experimental import pallas as pl
from jax.experimental.pallas import tpu as pltpu
from jax.sharding import PartitionSpec as P

D = 2048
HEADS = 20
KVH = 5
HD = 64
FF = 5120
PAGE = 128
KEEP = 64
NP = 16
R_DEV = 2
KVW = 640

DIRECT = 8

epsilon = 1e-06
negative = -1e30
both_axes = ("req", "head")


def rms_scale(values):
    return lax.rsqrt(jnp.mean(values * values, axis=-1, keepdims=True) + epsilon)


def rms_rows(values, gain):
    return values * rms_scale(values) * gain


def rotate(vectors, positions):
    half = vectors.shape[-1] // 2
    frequency = 10000.0 ** (-jnp.arange(half, dtype=jnp.float32) / half)
    angles = positions.astype(jnp.float32)[:, None] * frequency[None, :]
    cosine = jnp.cos(angles)[:, None, :]
    sine = jnp.sin(angles)[:, None, :]
    first = vectors[..., :half]
    second = vectors[..., half:]
    return jnp.concatenate(
        [first * cosine - second * sine, second * cosine + first * sine], axis=-1
    )


def compact_pages(pages, keep, weights):
    rows = jnp.arange(pages.shape[1], dtype=jnp.int32)
    picks = keep[:, :, None] == rows[None, None, :]
    kept = jnp.einsum(
        "pkr,prc->pkc", picks.astype(jnp.bfloat16), pages, preferred_element_type=jnp.float32
    ).astype(jnp.bfloat16)
    dropped = weights * (1.0 - jnp.sum(picks.astype(jnp.float32), axis=1))
    total = jnp.sum(dropped, axis=1)
    means = (
        jnp.einsum(
            "pr,prc->pc", dropped, pages.astype(jnp.float32), precision=lax.Precision.HIGHEST
        )
        / total[:, None]
    )
    return (kept, means.astype(jnp.bfloat16), jnp.log(total))


def held_request(rows, source):
    half = R_DEV // 2
    position = rows % R_DEV
    slot = rows // R_DEV * half + position - half
    continued = jnp.arange(source.shape[0], dtype=jnp.int32)
    matches = source[None, :] == slot[:, None]
    owner_cont = jnp.sum(jnp.where(matches, continued[None, :], 0), axis=1)
    carried = owner_cont // half * R_DEV + half + owner_cont % half
    return jnp.where(position < half, rows, carried)


def pick_rows(order, rows):
    chosen = order[:, None] == jnp.arange(rows.shape[0], dtype=jnp.int32)[None, :]
    return jnp.dot(
        chosen.astype(jnp.bfloat16), rows, preferred_element_type=jnp.float32
    ).astype(jnp.bfloat16)


def exchange(parts):
    return lax.all_to_all(parts, "req", split_axis=0, concat_axis=0, tiled=True)


def to_block_owner(rows):
    groups = lax.axis_size("req")
    lanes = lax.axis_size("head")
    per_lane = groups // lanes
    pairs = [
        (g * lanes + h, (per_lane * h + g // lanes) * lanes + g % lanes)
        for g in range(groups)
        for h in range(lanes)
    ]
    return lax.ppermute(rows, both_axes, pairs)


def whole_sum(partial):
    if lax.axis_size("req") > DIRECT:
        return lax.psum(partial, "req")
    groups = lax.axis_size("req")
    return jnp.sum(exchange(jnp.broadcast_to(partial[None], (groups,) + partial.shape)), axis=0)


def on_device_wide(
    hidden_in,
    attention_gain,
    query_gain,
    key_gain,
    feedforward_gain,
    input_weight,
    output_weight,
    gate_weight,
    up_weight,
    down_weight,
    old_cache,
    keep_rows,
    drop_weights,
    dest_slots,
    lengths,
    page_table,
    source,
):
    groups = lax.axis_size("req")
    lanes = lax.axis_size("head")
    group = lax.axis_index("req")
    lane = lax.axis_index("head")
    requests = hidden_in.shape[0]
    half = R_DEV // 2
    split = KVH * HD
    ratio = HEADS // KVH
    scale = HD ** (-0.5)
    pages_here = old_cache.shape[0]
    everyone = jnp.arange(requests, dtype=jnp.int32)
    holders = held_request(everyone, source)
    held = lax.dynamic_slice_in_dim(holders, group * R_DEV, R_DEV, 0)
    held_len = lengths[held]
    positions = held_len * PAGE

    whole = lax.all_gather(hidden_in, "head", axis=1, tiled=True)
    normed = rms_rows(whole.astype(jnp.float32), attention_gain).astype(jnp.bfloat16)
    features = D // groups
    inputs = pick_rows(holders, lax.dynamic_slice_in_dim(normed, group * features, features, 1))
    partial_qkv = jnp.dot(inputs, input_weight, preferred_element_type=jnp.float32)
    sent = jnp.broadcast_to(
        partial_qkv.reshape(groups, 1, R_DEV, -1), (groups, lanes, R_DEV, partial_qkv.shape[1])
    ).reshape(groups * lanes, R_DEV, -1)
    got = lax.all_to_all(sent, both_axes, split_axis=0, concat_axis=0, tiled=True)
    mixed = jnp.sum(got.reshape(groups, lanes, R_DEV, -1), axis=0).astype(jnp.bfloat16)
    held_qkv = jnp.swapaxes(mixed, 0, 1).reshape(R_DEV, -1).astype(jnp.float32)

    query = rotate(
        rms_rows(held_qkv[:, : HEADS * HD].reshape(R_DEV, HEADS, HD), query_gain), positions
    ).astype(jnp.bfloat16)
    key_new = rotate(
        rms_rows(held_qkv[:, HEADS * HD : (HEADS + KVH) * HD].reshape(R_DEV, KVH, HD), key_gain),
        positions,
    ).astype(jnp.bfloat16)
    value_new = held_qkv[:, (HEADS + KVH) * HD :].reshape(R_DEV, KVH, HD)
    kept, means, bias = compact_pages(old_cache, keep_rows, drop_weights)
    destination = dest_slots[0]
    fresh_ids = jnp.arange(pages_here, dtype=jnp.int32)
    inverse = jnp.sum(
        jnp.where(destination[None, :] == fresh_ids[:, None], fresh_ids[None, :], 0), axis=1
    )
    compact = kept[inverse].reshape(pages_here // 2, PAGE, KVW)
    summaries = means[inverse]
    per_lane = NP // lanes
    table = page_table.reshape(R_DEV, per_lane, lanes)
    mine = lax.dynamic_slice_in_dim(table, lane, 1, 2)[:, :, 0]
    logical = jnp.arange(per_lane, dtype=jnp.int32) * lanes + lane
    live = logical[None, :] < held_len[:, None]
    owner = jnp.any((mine[:, :, None] == fresh_ids[None, None, :]) & live[:, :, None], axis=1)
    query_groups = query.reshape(R_DEV, KVH, ratio, HD)
    row_keys = kept[:, :, :split].reshape(pages_here, KEEP, KVH, HD)
    row_values = kept[:, :, split:].reshape(pages_here, KEEP, KVH, HD)
    row_live = keep_rows >= 0
    allowed = owner[:, None, None, :, None] & row_live[None, None, None, :, :]
    scores = (
        jnp.einsum("rngd,pmnd->rngpm", query_groups, row_keys, preferred_element_type=jnp.float32)
        * scale
    )
    scores = jnp.where(allowed, scores, negative)
    mean_keys = means[:, :split].reshape(pages_here, KVH, HD)
    mean_values = means[:, split:].reshape(pages_here, KVH, HD)
    mean_scores = (
        jnp.einsum("rngd,pnd->rngp", query_groups, mean_keys, preferred_element_type=jnp.float32)
        * scale
        + bias[None, None, None, :]
    )
    mean_allowed = owner[:, None, None, :]
    mean_scores = jnp.where(mean_allowed, mean_scores, negative)
    own_score = (
        jnp.einsum("rngd,rnd->rng", query_groups, key_new, preferred_element_type=jnp.float32)
        * scale
    )
    own_score = jnp.where(lane == 0, own_score, negative)
    top = jnp.maximum(jnp.max(scores, axis=(3, 4)), jnp.max(mean_scores, axis=3))
    top = jnp.maximum(top, own_score)
    row_weight = jnp.where(allowed, jnp.exp(scores - top[..., None, None]), 0.0)
    mean_weight = jnp.where(mean_allowed, jnp.exp(mean_scores - top[..., None]), 0.0)
    own_weight = jnp.where(lane == 0, jnp.exp(own_score - top), 0.0)
    mass = jnp.sum(row_weight, axis=(3, 4)) + jnp.sum(mean_weight, axis=3) + own_weight
    total = jnp.einsum(
        "rngpm,pmnd->rngd",
        row_weight,
        row_values.astype(jnp.float32),
        precision=lax.Precision.HIGHEST,
    )
    total = total + jnp.einsum(
        "rngp,pnd->rngd",
        mean_weight,
        mean_values.astype(jnp.float32),
        precision=lax.Precision.HIGHEST,
    )
    total = total + own_weight[..., None] * value_new[:, :, None, :]

    some = mass > 0.0
    level = jnp.where(some, top + jnp.log(jnp.where(some, mass, 1.0)), negative)
    means_out = total / jnp.where(some, mass, 1.0)[..., None]
    own = HEADS * HD // groups
    parts = jnp.stack([means_out, jnp.broadcast_to(level[..., None], total.shape)])
    parts = jnp.transpose(parts.reshape(2, R_DEV, groups, own), (2, 1, 0, 3))
    parts = jnp.broadcast_to(
        parts.reshape(groups, 1, R_DEV, 2 * own), (groups, lanes, R_DEV, 2 * own)
    ).reshape(groups * lanes, R_DEV, 2 * own)
    came = lax.all_to_all(parts, both_axes, 0, 0, tiled=True)
    came = came.reshape(groups, lanes, R_DEV, 2 * own)
    outs, levels = came[..., :own], came[..., own:]
    weights = jnp.exp(levels - jnp.max(levels, axis=1, keepdims=True))
    attention = jnp.sum(outs * weights, axis=1) / jnp.sum(weights, axis=1)
    attention = attention.reshape(requests, own).astype(jnp.bfloat16)
    back = jnp.sum(
        jnp.where(holders[None, :] == everyone[:, None], everyone[None, :], 0), axis=1
    )
    projected = jnp.dot(
        pick_rows(back, attention), output_weight, preferred_element_type=jnp.float32
    )
    projected = projected + jnp.where(group == 0, hidden_in.astype(jnp.float32), 0.0)

    share = groups // lanes
    blocks = jnp.moveaxis(projected.reshape(requests, share, 1, features), 0, 2)
    blocks = jnp.broadcast_to(blocks, (share, lanes, requests, features))
    mid = jnp.sum(exchange(blocks.reshape(groups, requests, features)), axis=0)
    mid = to_block_owner(mid.astype(jnp.bfloat16)).astype(jnp.float32)
    squares = jnp.sum(mid * mid, axis=1, keepdims=True)
    gain_here = lax.dynamic_slice_in_dim(feedforward_gain, group * features, features, 0)
    inputs_mid = (mid * gain_here).astype(jnp.bfloat16)
    local_units = gate_weight.shape[1]
    piece = local_units // groups
    gates = jnp.dot(inputs_mid, gate_weight, preferred_element_type=jnp.float32)
    ups = jnp.dot(inputs_mid, up_weight, preferred_element_type=jnp.float32)
    both = jnp.concatenate(
        [
            gates.reshape(requests, groups, piece),
            ups.reshape(requests, groups, piece),
            jnp.broadcast_to(squares[:, :, None], (requests, groups, 1)),
        ],
        axis=2,
    )
    sums = jnp.sum(exchange(jnp.swapaxes(both, 0, 1)), axis=0)
    factor = lax.rsqrt(sums[:, 2 * piece :] / D + epsilon)
    gate = sums[:, :piece] * factor
    active = (jax.nn.silu(gate) * (sums[:, piece : 2 * piece] * factor)).astype(jnp.bfloat16)
    active_here = lax.all_gather(to_block_owner(active), "head", axis=1, tiled=True)
    down = jnp.dot(active_here, down_weight, preferred_element_type=jnp.float32)
    residual = [jnp.where(group == lane * share + k, mid, 0.0) for k in range(share)]
    down = down + jnp.concatenate(residual, axis=1)
    result = whole_sum(down).astype(jnp.bfloat16)
    return (compact, summaries, result)


TILE = 128
bfloat = jnp.bfloat16
single = jnp.float32


TERMS = 4


def three_terms(value, place):
    high = value.astype(bfloat).astype(single)
    rest = value - high
    middle = rest.astype(bfloat).astype(single)
    low = jnp.where(place == 2, rest - middle, 0.0)
    return jnp.where(place == 0, high, jnp.where(place == 1, middle, low))


def iota(shape, axis):
    return lax.broadcasted_iota(jnp.int32, shape, axis)


def run(kernel, outs, far, near, scratch=(), flops=0):
    in_specs = [pl.BlockSpec(memory_space=pltpu.HBM) for _ in far]
    in_specs += [pl.BlockSpec(memory_space=pltpu.VMEM) for _ in near]
    moved = sum(a.size * a.dtype.itemsize for a in [*far, *near, *outs])
    return pl.pallas_call(
        kernel,
        out_shape=list(outs),
        in_specs=in_specs,
        out_specs=[pl.BlockSpec(memory_space=pltpu.VMEM) for _ in outs],
        scratch_shapes=list(scratch),
        compiler_params=pltpu.CompilerParams(vmem_limit_bytes=16 * 2**20),
        cost_estimate=pl.CostEstimate(flops=flops, bytes_accessed=moved, transcendentals=0),
    )(*[pltpu.with_memory_space_constraint(a, pltpu.HBM) for a in far], *near)


def fetch(sources, targets, done):
    copies = [
        pltpu.make_async_copy(source, target, done.at[k])
        for k, (source, target) in enumerate(zip(sources, targets))
    ]
    for copy in copies:
        copy.start()
    return copies


def local_like(*arrays):
    return [pltpu.VMEM(a.shape, a.dtype) for a in arrays]


def scalar_like(*arrays):
    return [pltpu.SMEM(a.shape, a.dtype) for a in arrays]


def row_order(source, count, to_holder):
    first, second = iota((count, count), 0), iota((count, count), 1)
    if not to_holder:
        first, second = second, first
    order = (first == second) & (first % R_DEV == 0)
    for c in range(source.shape[1]):
        order = order | ((first == source[0, c] * R_DEV + 1) & (second == c * R_DEV + 1))
    return order.astype(single).astype(bfloat)


def shaped(shape, dtype):
    return jax.ShapeDtypeStruct(shape, dtype)


def first_kernel(
    source_far, gain_far, weight_far, hidden_far, one, two, three, sent, block, source, gain,
    weight, hidden, lanes_of, wide, done
):
    copies = fetch(
        (source_far, gain_far, weight_far, hidden_far), (source, gain, weight, hidden), done
    )
    rows = hidden.shape[0]
    groups = rows // R_DEV
    lanes = sent.shape[0] // groups
    columns, features = weight.shape
    group = lax.axis_index("req")
    share = groups // lanes
    squares = 0.0
    for turn, values in enumerate((one, two, three)):
        values = values[...].astype(single)
        lanes_of[turn + 1] = values
        squares = squares + jnp.sum(values * values, axis=1, keepdims=True)
    copies[3].wait()
    values = hidden[...].astype(single)
    lanes_of[0] = values
    squares = squares + jnp.sum(values * values, axis=1, keepdims=True)
    factor = lax.rsqrt(squares / D + epsilon)
    here = pl.ds(pl.multiple_of(group * features, features), features)
    within = pl.ds(pl.multiple_of(group % share * features, features), features)
    mine = lanes_of[group // share ^ lax.axis_index("head"), :, within]
    block[...] = mine.astype(bfloat)
    wide[...] = jnp.zeros_like(wide)
    for copy in copies[:3]:
        copy.wait()
    normed = (mine * factor * gain[:, here]).astype(bfloat)
    order = row_order(source, rows, True)
    normed = jnp.dot(order, normed, preferred_element_type=single).astype(bfloat)
    wide[:, :columns] = dot_rows(normed, weight[...])
    for g in range(groups):
        tile = jnp.concatenate(
            [
                wide[R_DEV * g : R_DEV * (g + 1), TILE * j : TILE * (j + 1)]
                for j in range(wide.shape[1] // TILE)
            ],
            axis=0,
        )
        for k in range(lanes):
            sent[g * lanes + k] = tile


def dot_rows(left, right):
    return lax.dot_general(left, right, (((1,), (1,)), ((), ())), preferred_element_type=single)


def prepare_kernel(*refs):
    far, refs = refs[:12], refs[12:]
    (compact, summaries, kept, added, tables, mine, theirs), refs = refs[:7], refs[7:]
    near, (ordered, plain, dealt, done) = refs[:12], refs[12:]
    copies = fetch(far, near, done)
    (dest, lengths, source, table, keep, weights, query_gain, key_gain, turns) = near[:9]
    pages, gate, up = near[9:]
    group = lax.axis_index("req")
    lane = lax.axis_index("head")
    lanes = lax.axis_size("head")
    for copy in copies[:9]:
        copy.wait()

    carried = 0
    for c in range(source.shape[1]):
        carried = carried + jnp.where(source[0, c] == group, c, 0)
    held_len = (lengths[0, group * R_DEV], lengths[0, carried * R_DEV + 1])
    count, rows, _ = pages.shape
    owned = []
    for r in range(R_DEV):
        slots = []
        for i in range(table.shape[1] // lanes):
            j = i * lanes + lane
            slots.append(jnp.where(j < held_len[r], table[r, j], -1))
        owned.append(slots)

    def owner(r, p):
        found = owned[r][0] == p
        for slot in owned[r][1:]:
            found = found | (slot == p)
        return found

    row = iota((32, TILE), 0)
    odd = (row & 1) == 1
    half_rows = turns.shape[0] // 2
    for part in range(2):
        pair = [turns[pl.ds(part * half_rows + held_len[r], 1), :] for r in range(R_DEV)]
        tables[32 * part : 32 * (part + 1), :] = jnp.where(odd, pair[1], pair[0])
    query_rows = HEADS * HD // TILE * R_DEV
    for c in range(TILE // HD):
        columns = slice(HD * c, HD * (c + 1))
        tables[64 : 64 + query_rows, columns] = jnp.broadcast_to(
            query_gain[...], (query_rows, HD)
        )
        tables[64 + query_rows : 96, columns] = jnp.broadcast_to(
            key_gain[...], (32 - query_rows, HD)
        )

    column = iota((1, TILE), 1)
    entries = count * KEEP
    added[...] = jnp.full_like(added, negative)
    extra = [
        jnp.where((column == count + r) & (lane == 0), 0.0, negative) for r in range(R_DEV)
    ]
    weight_columns = weights[...].T
    rows_of = iota((rows, KEEP), 0)
    place = iota((rows, 16), 1)
    copies[9].wait()
    for p in range(count):
        picks = (keep[p : p + 1, :] == rows_of).astype(single)
        dropped = weight_columns[:, p : p + 1] * (1.0 - jnp.sum(picks, axis=1, keepdims=True))
        total = jnp.sum(dropped, axis=0, keepdims=True)
        left = jnp.concatenate([picks, three_terms(dropped, place)], axis=1).astype(bfloat)
        both = lax.dot_general(
            left, pages[p], (((0,), (0,)), ((), ())), preferred_element_type=single
        )
        rows_kept = both[:KEEP].astype(bfloat)
        kept[KEEP * p : KEEP * (p + 1), :] = rows_kept
        slot = dest[0, p]
        start = pl.multiple_of((slot & 1) * KEEP, KEEP)
        compact[slot >> 1, pl.ds(start, KEEP), :] = rows_kept
        mean = both[KEEP : KEEP + 1] + both[KEEP + 1 : KEEP + 2] + both[KEEP + 2 : KEEP + 3]
        mean = mean / total
        plain[p : p + 1, :] = mean
        ordered[pl.ds(slot, 1), :] = mean
        live = jnp.where(keep[p : p + 1, :] >= 0, 0.0, negative)
        for r in range(R_DEV):
            here = owner(r, p)
            added[r : r + 1, KEEP * p : KEEP * (p + 1)] = jnp.where(here, live, negative)
            level = jnp.where(here, jnp.log(total), negative)
            extra[r] = jnp.where(column == p, level, extra[r])
    for r in range(R_DEV):
        added[r : r + 1, entries : entries + TILE] = extra[r]
    plain[count:, :] = jnp.zeros_like(plain[count:, :])
    kept[entries:, :] = plain[...].astype(bfloat)
    summaries[...] = ordered[...].astype(bfloat)

    for copy in copies[10:]:
        copy.wait()
    block = gate.shape[1] // 2
    piece = block // 2
    for k in range(2):
        for b in range(2):
            columns = slice(b * block + k * piece, b * block + (k + 1) * piece)
            start = b * block
            dealt[k, :, start : start + piece] = gate[:, columns].astype(single)
            dealt[k, :, start + piece : start + block] = up[:, columns].astype(single)
    mine[...] = dealt[lane & 1].astype(bfloat)
    theirs[...] = dealt[1 - (lane & 1)].astype(bfloat)


def attend_kernel(came, kept, added, tables, sent, x, extra_k, extra_v, out, logs):
    lanes = lax.axis_size("head")
    groups = came.shape[0] // lanes
    width = (HEADS + 2 * KVH) * HD // lanes
    span = -(-KVH * HD // TILE) * TILE
    key_cols = slice(0, span)
    value_cols = slice(KVW - span, KVW)
    first_key = HEADS * HD // TILE * R_DEV
    scale = HD ** (-0.5)
    x[...] = jnp.zeros_like(x)
    column = iota((8, TILE), 1)
    for k in range(lanes):
        tile = came[k].astype(single)
        for g in range(1, groups):
            tile = tile + came[g * lanes + k].astype(single)
        tile = tile.astype(bfloat).astype(single)
        base, shift = divmod(width * k, TILE)
        base = base * R_DEV
        if shift:
            tile = pltpu.roll(tile, shift, 1)
            x[base + 2 : base + 10, :] += jnp.where(column < shift, tile, 0.0)
        x[base : base + 8, :] += jnp.where(column >= shift, tile, 0.0)
    values = x[...]
    same_head = (iota((TILE, TILE), 0) // HD == iota((TILE, TILE), 1) // HD).astype(single)
    squares = jnp.dot(
        values * values, same_head, precision=lax.Precision.HIGHEST, preferred_element_type=single
    )
    normed = values * lax.rsqrt(squares / HD + epsilon) * tables[64:96, :]
    early = iota(values.shape, 1) % HD < HD // 2
    swapped = jnp.where(
        early, pltpu.roll(normed, TILE - HD // 2, 1), pltpu.roll(normed, HD // 2, 1)
    )
    turned = normed * tables[0:32, :] + swapped * tables[32:64, :]
    turned = turned.astype(bfloat).astype(single)

    rows = 24
    row = iota((rows, TILE), 0)
    half = iota((rows, TILE), 1) // HD
    key_head = row >> 2
    query = jnp.where(row < first_key, turned[:rows], 0.0)
    other = pltpu.roll(query, HD, 1)
    queries = []
    for u in range(2):
        placed = jnp.where(
            half == (key_head & 1), jnp.where((key_head & 1) == u, query, other), 0.0
        )
        queries.append(
            jnp.concatenate(
                [jnp.where((key_head >> 1) == c, placed, 0.0) for c in range(span // TILE)], axis=1
            )
        )
    queries = jnp.concatenate(queries, axis=0).astype(bfloat)

    extras = extra_k.shape[0]
    entries = kept.shape[0] - extras
    count = entries // KEEP
    extra_k[...] = kept[entries:, key_cols].astype(single)
    extra_v[...] = kept[entries:, value_cols].astype(single)
    first_value = first_key + KVH * HD // TILE * R_DEV
    for c in range(span // TILE):
        at = slice(c * TILE, (c + 1) * TILE)
        r = first_key + R_DEV * c
        extra_k[count : count + R_DEV, at] = turned[r : r + R_DEV]
        r = first_value + R_DEV * c
        extra_v[count : count + R_DEV, at] = values[r : r + R_DEV]

    def by_request(columns, size):
        odd = (iota((2 * rows, size), 0) & 1) == 1
        return jnp.where(odd, added[1:2, columns], added[0:1, columns])

    scores = dot_rows(queries, kept[:entries, key_cols]) * scale
    scores = scores + by_request(slice(0, entries), entries)
    extra = dot_rows(queries, extra_k[...].astype(bfloat)) * scale
    extra = extra + by_request(slice(entries, entries + extras), extras)
    top = jnp.maximum(
        jnp.max(scores, axis=1, keepdims=True), jnp.max(extra, axis=1, keepdims=True)
    )
    weight = jnp.where(scores > 0.5 * negative, jnp.exp(scores - top), 0.0)
    extra_weight = jnp.where(extra > 0.5 * negative, jnp.exp(extra - top), 0.0)
    mass = jnp.sum(weight, axis=1, keepdims=True) + jnp.sum(extra_weight, axis=1, keepdims=True)

    def weighted(parts, right):
        high = parts.astype(bfloat)
        low = (parts - high.astype(single)).astype(bfloat)
        return jnp.dot(high, right, preferred_element_type=single) + jnp.dot(
            low, right, preferred_element_type=single
        )

    total = weighted(weight, kept[:entries, value_cols]) + weighted(
        extra_weight, extra_v[...].astype(bfloat)
    )
    some = mass > 0.0
    mass = jnp.where(some, mass, 1.0)
    total = total / mass
    level = jnp.where(some, top + jnp.log(mass), negative)

    slot = key_head + (KVW // 2 - (KVW - span)) // HD
    results = []
    for u in range(2):
        mine = total[rows * u : rows * (u + 1)]
        picked = mine[:, :TILE]
        for c in range(1, span // TILE):
            picked = jnp.where((slot >> 1) == c, mine[:, c * TILE : (c + 1) * TILE], picked)
        results.append(jnp.where((slot & 1) == u, picked, pltpu.roll(picked, HD, 1)))
    out[...] = jnp.where(half == 0, results[0], results[1])
    logs[...] = jnp.broadcast_to(level, logs.shape)
    own = HEADS * HD // lanes
    size = 6
    column = iota((size, TILE), 1)
    here = column // TERMS == iota((size, TILE), 0)
    for k in range(lanes):
        r = own * k // TILE * R_DEV
        tile = [out[r : r + size, :]]
        for u in range(2):
            coded = three_terms(logs[rows * u + r : rows * u + r + size, :], column % TERMS)
            tile.append(jnp.sum(jnp.where(here, coded, 0.0), axis=0, keepdims=True))
        tile = jnp.concatenate(tile, axis=0).astype(bfloat)
        for g in range(groups):
            sent[g * lanes + k] = tile


def project_kernel(source_far, came, first, second, sent, source, logs, rows, pieces, done):
    (copy,) = fetch((source_far,), (source,), done)
    lanes = lax.axis_size("head")
    groups = came.shape[0] // lanes
    group = lax.axis_index("req")
    features = first.shape[0]
    requests = rows.shape[0]
    size = 6
    tiles = [came[d].astype(single) for d in range(groups * lanes)]
    for g in range(groups):
        for k in range(lanes):
            logs[k, 2 * g : 2 * g + 2, :] = tiles[g * lanes + k][size:]
    spread = (iota((8, TILE), 1) // TERMS == iota((8, TILE), 0)).astype(single).astype(bfloat)
    levels = [dot_rows(spread, logs[k].astype(bfloat)) for k in range(lanes)]
    top = jnp.maximum(jnp.maximum(levels[0], levels[1]), jnp.maximum(levels[2], levels[3]))
    shares = [jnp.exp(level - top) for level in levels]
    mass = sum(shares)
    shares = [share / mass for share in shares]
    lower = iota((8, TILE), 1) < HD
    for g in range(groups):
        mixed = 0.0
        for k in range(lanes):
            share = shares[k]
            share = jnp.where(lower, share[:, 2 * g : 2 * g + 1], share[:, 2 * g + 1 : 2 * g + 2])
            mixed = mixed + share * tiles[g * lanes + k]
        for j in range(size // R_DEV):
            rows[R_DEV * g : R_DEV * (g + 1), TILE * j : TILE * (j + 1)] = mixed[
                R_DEV * j : R_DEV * (j + 1)
            ]
    width = rows.shape[1]
    shift = lax.rem(lax.axis_index("head") * (2 * features), TILE)
    attention = rows[...].astype(bfloat).astype(single)
    attention = pltpu.roll(attention, lax.rem(width - shift, width), 1)
    copy.wait()
    order = row_order(source, requests, False)
    attention = jnp.dot(order, attention.astype(bfloat), preferred_element_type=single)
    for b in range(2):
        pieces[b] = attention[:, features * b : features * (b + 1)]
    total = 0.0
    width = sent.shape[1]
    here = pl.ds(pl.multiple_of((group & 1) * width, width), width)
    for turn, weight in enumerate((first, second)):
        piece = pieces[(group & 1) ^ turn].astype(bfloat)
        total = total + jnp.dot(piece, weight[:, here], preferred_element_type=single)
    sent[...] = total


def units_kernel(
    gain_far, own, one, two, three, hidden, mine, theirs, sent, mid_out, gain, done
):
    (copy,) = fetch((gain_far,), (gain,), done)
    rows, features = own.shape
    share = sent.shape[0] // lax.axis_size("head")
    group = lax.axis_index("req")
    lane = lax.axis_index("head")
    here = pl.ds(pl.multiple_of(group * features, features), features)
    mid = (own[...] + one[...]) + (two[...] + three[...])
    mid = (hidden[...].astype(single) + mid).astype(bfloat)
    mid_out[...] = mid
    mid = mid.astype(single)
    squares = jnp.sum(mid * mid, axis=1, keepdims=True)
    block = mine.shape[1] // share
    terms = three_terms(squares, iota((rows, sent.shape[2] - block), 1)).astype(bfloat)
    copy.wait()
    inputs = (mid * gain[:, here]).astype(bfloat)
    for turn, weight in enumerate((mine, theirs)):
        units = jnp.dot(inputs, weight[...], preferred_element_type=single).astype(bfloat)
        target = (lane ^ turn) * share
        for b in range(share):
            sent[target + b, :, :block] = units[:, block * b : block * (b + 1)]
            sent[target + b, :, block:] = terms


def active_kernel(came, active):
    total = came[0].astype(single)
    for g in range(1, came.shape[0]):
        total = total + came[g].astype(single)
    piece = active.shape[1]
    squares = jnp.sum(total[:, 2 * piece : 2 * piece + 3], axis=1, keepdims=True)
    factor = lax.rsqrt(squares / D + epsilon)
    gate = total[:, :piece] * factor
    up = total[:, piece : 2 * piece] * factor
    active[...] = (gate / (1.0 + jnp.exp(-gate)) * up).astype(bfloat)


def down_kernel(own, one, two, three, weight, mid, sent, active):
    groups, rows, width = sent.shape
    piece = own.shape[1]
    half = mid.shape[1]
    for turn, values in enumerate((own, one, two, three)):
        active[turn] = values[...]
    share = width // half
    group = lax.axis_index("req")
    lane = lax.axis_index("head")
    first = group // (2 * share) * 2 ^ lane
    down = jnp.dot(active[first], weight[:piece, :], preferred_element_type=single)
    down = down + jnp.dot(active[first ^ 1], weight[piece:, :], preferred_element_type=single)
    residual = mid[...].astype(single)
    for b in range(share):
        columns = slice(half * b, half * (b + 1))
        mine = group == lane * share + b
        total = (down[:, columns] + jnp.where(mine, residual, 0.0)).astype(bfloat)
        for g in range(groups):
            sent[g, :, columns] = total


def result_kernel(came, result):
    total = came[0].astype(single)
    for g in range(1, came.shape[0]):
        total = total + came[g].astype(single)
    result[...] = total.astype(bfloat)


def rotation_table():
    half = HD // 2
    size = -(-(NP + 1) // 8) * 8
    frequency = 10000.0 ** (-np.arange(half) / half)
    angles = PAGE * np.arange(size)[:, None] * frequency[None, :]
    cosine, sine = np.cos(angles), np.sin(angles)
    wide = [np.tile(np.concatenate(pair, axis=1), (1, TILE // HD)) for pair in
            ((cosine, cosine), (-sine, sine))]
    return jnp.asarray(np.concatenate(wide), dtype=single)


def swapped_lanes(value, turn):
    lanes = lax.axis_size("head")
    return lax.ppermute(value, "head", [(k, k ^ turn) for k in range(lanes)])


def from_lanes(value):
    return [value] + [swapped_lanes(value, turn) for turn in range(1, lax.axis_size("head"))]


def transposed(value):
    groups = lax.axis_size("req")
    lanes = lax.axis_size("head")
    pairs = [
        (g * lanes + h, (2 * h + (g & 1)) * lanes + g // 2)
        for g in range(groups)
        for h in range(lanes)
    ]
    return lax.ppermute(value, both_axes, pairs)


def swapped_y(value):
    return lax.ppermute(value, "req", [(g, g ^ 1) for g in range(lax.axis_size("req"))])


def on_device(
    hidden_in,
    attention_gain,
    query_gain,
    key_gain,
    feedforward_gain,
    input_weight,
    output_weight,
    gate_weight,
    up_weight,
    down_weight,
    old_cache,
    keep_rows,
    drop_weights,
    dest_slots,
    lengths,
    page_table,
    source,
):
    groups = lax.axis_size("req")
    lanes = lax.axis_size("head")
    requests = hidden_in.shape[0]
    pages_here = old_cache.shape[0]
    devices = groups * lanes
    features = D // groups
    copies = pltpu.SemaphoreType.DMA

    others = from_lanes(hidden_in)[1:]
    handed = transposed(output_weight)
    scalars = [dest_slots, lengths[None, :], source[None, :], page_table]
    arrays = [
        keep_rows,
        drop_weights,
        query_gain[None, :],
        key_gain[None, :],
        rotation_table(),
        old_cache,
        gate_weight,
        up_weight,
    ]
    entries = pages_here * KEEP
    extras = 16
    compact, summaries, kept, added, tables, mine, theirs = run(
        prepare_kernel,
        [
            shaped((pages_here // 2, PAGE, KVW), bfloat),
            shaped((pages_here, KVW), bfloat),
            shaped((entries + extras, KVW), bfloat),
            shaped((8, entries + TILE), single),
            shaped((96, TILE), single),
            shaped(gate_weight.shape, bfloat),
            shaped(gate_weight.shape, bfloat),
        ],
        scalars + arrays,
        [],
        [
            *scalar_like(*scalars),
            *local_like(*arrays),
            pltpu.VMEM((pages_here, KVW), single),
            pltpu.VMEM((extras, KVW), single),
            pltpu.VMEM((2,) + gate_weight.shape, single),
            copies((len(scalars + arrays),)),
        ],
        2 * pages_here * TILE * PAGE * KVW,
    )
    tables, handed, *others = lax.optimization_barrier((tables, handed, *others))

    holds = source[None, :]
    columns = input_weight.shape[1]
    padded = -(-columns // TILE) * TILE
    gain = attention_gain[None, :]
    weight = input_weight.T
    far = [holds, gain, weight, hidden_in]
    sent, hidden_block = run(
        first_kernel,
        [
            shaped((devices, R_DEV * padded // TILE, TILE), single),
            shaped((requests, features), bfloat),
        ],
        far,
        others,
        [
            *scalar_like(holds),
            *local_like(*far[1:]),
            pltpu.VMEM((lanes,) + hidden_in.shape, single),
            pltpu.VMEM((requests, padded), single),
            copies((len(far),)),
        ],
        2 * requests * features * columns,
    )
    came = lax.all_to_all(sent, both_axes, 0, 0, tiled=True)
    theirs, given, _ = lax.optimization_barrier((theirs, handed, sent))
    theirs = swapped_lanes(theirs, 1)
    given = swapped_y(given)
    came, theirs, given = lax.optimization_barrier((came, theirs, given))
    span = -(-KVH * HD // TILE) * TILE
    (parts,) = run(
        attend_kernel,
        [shaped((devices, 8, TILE), bfloat)],
        [],
        [came, kept, added, tables],
        [
            pltpu.VMEM((32, TILE), single),
            pltpu.VMEM((extras, span), single),
            pltpu.VMEM((extras, span), single),
            pltpu.VMEM((24, TILE), single),
            pltpu.VMEM((48, TILE), single),
        ],
        6 * 48 * entries * span,
    )
    came = lax.all_to_all(parts, both_axes, 0, 0, tiled=True)
    (sent,) = run(
        project_kernel,
        [shaped((requests, features), single)],
        [holds],
        [came, handed, given],
        [
            *scalar_like(holds),
            pltpu.VMEM((lanes, 2 * groups, TILE), single),
            pltpu.VMEM((requests, 3 * TILE), single),
            pltpu.VMEM((2, requests, output_weight.shape[0]), single),
            copies((1,)),
        ],
        2 * requests * output_weight.size,
    )
    gain = feedforward_gain[None, :]
    block = gate_weight.shape[1] // 2
    sent, mid = run(
        units_kernel,
        [
            shaped((groups, requests, block + TILE), bfloat),
            shaped((requests, features), bfloat),
        ],
        [gain],
        [*from_lanes(sent), hidden_block, mine, theirs],
        [*local_like(gain), copies((1,))],
        4 * requests * gate_weight.size,
    )
    (active,) = run(
        active_kernel, [shaped((requests, block // 2), bfloat)], [], [exchange(sent)]
    )
    (sent,) = run(
        down_kernel,
        [shaped((groups, requests, down_weight.shape[1]), bfloat)],
        [],
        [*from_lanes(active), down_weight, mid],
        [pltpu.VMEM((lanes,) + active.shape, bfloat)],
        2 * requests * down_weight.size,
    )
    (result,) = run(
        result_kernel, [shaped((requests, down_weight.shape[1]), bfloat)], [], [exchange(sent)]
    )
    return (compact, summaries, result)


def solution(mesh):
    placed = (
        P(None, "head"),
        P(),
        P(),
        P(),
        P(),
        P("req", "head"),
        P("req", "head"),
        P("req", "head"),
        P("req", "head"),
        P("req", "head"),
        P(("req", "head"), None, None),
        P(("req", "head"), None),
        P(("req", "head"), None),
        P(("req", "head"), None),
        P(),
        P("req", None),
        P(),
    )
    return jax.shard_map(
        on_device if mesh.shape["req"] <= DIRECT else on_device_wide,
        mesh=mesh,
        in_specs=placed,
        out_specs=(P(("req", "head"), None, None), P(("req", "head"), None), P(None, "head")),
        check_vma=False,
    )
```

```python
import jax
import jax.numpy as jnp
import numpy as np
from jax import lax
from jax.experimental import pallas as pl
from jax.experimental.pallas import tpu as pltpu
from jax.sharding import PartitionSpec as P

D = 2048
HEADS = 20
KVH = 5
HD = 64
FF = 5120
PAGE = 128
KEEP = 64
NP = 16
R_DEV = 2
KVW = 640

DIRECT = 8

epsilon = 1e-06
negative = -1e30
both_axes = ("req", "head")


def rms_scale(values):
    return lax.rsqrt(jnp.mean(values * values, axis=-1, keepdims=True) + epsilon)


def rms_rows(values, gain):
    return values * rms_scale(values) * gain


def rotate(vectors, positions):
    half = vectors.shape[-1] // 2
    frequency = 10000.0 ** (-jnp.arange(half, dtype=jnp.float32) / half)
    angles = positions.astype(jnp.float32)[:, None] * frequency[None, :]
    cosine = jnp.cos(angles)[:, None, :]
    sine = jnp.sin(angles)[:, None, :]
    first = vectors[..., :half]
    second = vectors[..., half:]
    return jnp.concatenate(
        [first * cosine - second * sine, second * cosine + first * sine], axis=-1
    )


def compact_pages(pages, keep, weights):
    rows = jnp.arange(pages.shape[1], dtype=jnp.int32)
    picks = keep[:, :, None] == rows[None, None, :]
    kept = jnp.einsum(
        "pkr,prc->pkc", picks.astype(jnp.bfloat16), pages, preferred_element_type=jnp.float32
    ).astype(jnp.bfloat16)
    dropped = weights * (1.0 - jnp.sum(picks.astype(jnp.float32), axis=1))
    total = jnp.sum(dropped, axis=1)
    means = (
        jnp.einsum(
            "pr,prc->pc", dropped, pages.astype(jnp.float32), precision=lax.Precision.HIGHEST
        )
        / total[:, None]
    )
    return (kept, means.astype(jnp.bfloat16), jnp.log(total))


def held_request(rows, source):
    half = R_DEV // 2
    position = rows % R_DEV
    slot = rows // R_DEV * half + position - half
    continued = jnp.arange(source.shape[0], dtype=jnp.int32)
    matches = source[None, :] == slot[:, None]
    owner_cont = jnp.sum(jnp.where(matches, continued[None, :], 0), axis=1)
    carried = owner_cont // half * R_DEV + half + owner_cont % half
    return jnp.where(position < half, rows, carried)


def pick_rows(order, rows):
    chosen = order[:, None] == jnp.arange(rows.shape[0], dtype=jnp.int32)[None, :]
    return jnp.dot(
        chosen.astype(jnp.bfloat16), rows, preferred_element_type=jnp.float32
    ).astype(jnp.bfloat16)


def exchange(parts):
    return lax.all_to_all(parts, "req", split_axis=0, concat_axis=0, tiled=True)


def to_block_owner(rows):
    groups = lax.axis_size("req")
    lanes = lax.axis_size("head")
    per_lane = groups // lanes
    pairs = [
        (g * lanes + h, (per_lane * h + g // lanes) * lanes + g % lanes)
        for g in range(groups)
        for h in range(lanes)
    ]
    return lax.ppermute(rows, both_axes, pairs)


def whole_sum(partial):
    if lax.axis_size("req") > DIRECT:
        return lax.psum(partial, "req")
    groups = lax.axis_size("req")
    return jnp.sum(exchange(jnp.broadcast_to(partial[None], (groups,) + partial.shape)), axis=0)


def on_device_wide(
    hidden_in,
    attention_gain,
    query_gain,
    key_gain,
    feedforward_gain,
    input_weight,
    output_weight,
    gate_weight,
    up_weight,
    down_weight,
    old_cache,
    keep_rows,
    drop_weights,
    dest_slots,
    lengths,
    page_table,
    source,
):
    groups = lax.axis_size("req")
    lanes = lax.axis_size("head")
    group = lax.axis_index("req")
    lane = lax.axis_index("head")
    requests = hidden_in.shape[0]
    half = R_DEV // 2
    split = KVH * HD
    ratio = HEADS // KVH
    scale = HD ** (-0.5)
    pages_here = old_cache.shape[0]
    everyone = jnp.arange(requests, dtype=jnp.int32)
    holders = held_request(everyone, source)
    held = lax.dynamic_slice_in_dim(holders, group * R_DEV, R_DEV, 0)
    held_len = lengths[held]
    positions = held_len * PAGE

    whole = lax.all_gather(hidden_in, "head", axis=1, tiled=True)
    normed = rms_rows(whole.astype(jnp.float32), attention_gain).astype(jnp.bfloat16)
    features = D // groups
    inputs = pick_rows(holders, lax.dynamic_slice_in_dim(normed, group * features, features, 1))
    partial_qkv = jnp.dot(inputs, input_weight, preferred_element_type=jnp.float32)
    sent = jnp.broadcast_to(
        partial_qkv.reshape(groups, 1, R_DEV, -1), (groups, lanes, R_DEV, partial_qkv.shape[1])
    ).reshape(groups * lanes, R_DEV, -1)
    got = lax.all_to_all(sent, both_axes, split_axis=0, concat_axis=0, tiled=True)
    mixed = jnp.sum(got.reshape(groups, lanes, R_DEV, -1), axis=0).astype(jnp.bfloat16)
    held_qkv = jnp.swapaxes(mixed, 0, 1).reshape(R_DEV, -1).astype(jnp.float32)

    query = rotate(
        rms_rows(held_qkv[:, : HEADS * HD].reshape(R_DEV, HEADS, HD), query_gain), positions
    ).astype(jnp.bfloat16)
    key_new = rotate(
        rms_rows(held_qkv[:, HEADS * HD : (HEADS + KVH) * HD].reshape(R_DEV, KVH, HD), key_gain),
        positions,
    ).astype(jnp.bfloat16)
    value_new = held_qkv[:, (HEADS + KVH) * HD :].reshape(R_DEV, KVH, HD)
    kept, means, bias = compact_pages(old_cache, keep_rows, drop_weights)
    destination = dest_slots[0]
    fresh_ids = jnp.arange(pages_here, dtype=jnp.int32)
    inverse = jnp.sum(
        jnp.where(destination[None, :] == fresh_ids[:, None], fresh_ids[None, :], 0), axis=1
    )
    compact = kept[inverse].reshape(pages_here // 2, PAGE, KVW)
    summaries = means[inverse]
    per_lane = NP // lanes
    table = page_table.reshape(R_DEV, per_lane, lanes)
    mine = lax.dynamic_slice_in_dim(table, lane, 1, 2)[:, :, 0]
    logical = jnp.arange(per_lane, dtype=jnp.int32) * lanes + lane
    live = logical[None, :] < held_len[:, None]
    owner = jnp.any((mine[:, :, None] == fresh_ids[None, None, :]) & live[:, :, None], axis=1)
    query_groups = query.reshape(R_DEV, KVH, ratio, HD)
    row_keys = kept[:, :, :split].reshape(pages_here, KEEP, KVH, HD)
    row_values = kept[:, :, split:].reshape(pages_here, KEEP, KVH, HD)
    row_live = keep_rows >= 0
    allowed = owner[:, None, None, :, None] & row_live[None, None, None, :, :]
    scores = (
        jnp.einsum("rngd,pmnd->rngpm", query_groups, row_keys, preferred_element_type=jnp.float32)
        * scale
    )
    scores = jnp.where(allowed, scores, negative)
    mean_keys = means[:, :split].reshape(pages_here, KVH, HD)
    mean_values = means[:, split:].reshape(pages_here, KVH, HD)
    mean_scores = (
        jnp.einsum("rngd,pnd->rngp", query_groups, mean_keys, preferred_element_type=jnp.float32)
        * scale
        + bias[None, None, None, :]
    )
    mean_allowed = owner[:, None, None, :]
    mean_scores = jnp.where(mean_allowed, mean_scores, negative)
    own_score = (
        jnp.einsum("rngd,rnd->rng", query_groups, key_new, preferred_element_type=jnp.float32)
        * scale
    )
    own_score = jnp.where(lane == 0, own_score, negative)
    top = jnp.maximum(jnp.max(scores, axis=(3, 4)), jnp.max(mean_scores, axis=3))
    top = jnp.maximum(top, own_score)
    row_weight = jnp.where(allowed, jnp.exp(scores - top[..., None, None]), 0.0)
    mean_weight = jnp.where(mean_allowed, jnp.exp(mean_scores - top[..., None]), 0.0)
    own_weight = jnp.where(lane == 0, jnp.exp(own_score - top), 0.0)
    mass = jnp.sum(row_weight, axis=(3, 4)) + jnp.sum(mean_weight, axis=3) + own_weight
    total = jnp.einsum(
        "rngpm,pmnd->rngd",
        row_weight,
        row_values.astype(jnp.float32),
        precision=lax.Precision.HIGHEST,
    )
    total = total + jnp.einsum(
        "rngp,pnd->rngd",
        mean_weight,
        mean_values.astype(jnp.float32),
        precision=lax.Precision.HIGHEST,
    )
    total = total + own_weight[..., None] * value_new[:, :, None, :]

    some = mass > 0.0
    level = jnp.where(some, top + jnp.log(jnp.where(some, mass, 1.0)), negative)
    means_out = total / jnp.where(some, mass, 1.0)[..., None]
    own = HEADS * HD // groups
    parts = jnp.stack([means_out, jnp.broadcast_to(level[..., None], total.shape)])
    parts = jnp.transpose(parts.reshape(2, R_DEV, groups, own), (2, 1, 0, 3))
    parts = jnp.broadcast_to(
        parts.reshape(groups, 1, R_DEV, 2 * own), (groups, lanes, R_DEV, 2 * own)
    ).reshape(groups * lanes, R_DEV, 2 * own)
    came = lax.all_to_all(parts, both_axes, 0, 0, tiled=True)
    came = came.reshape(groups, lanes, R_DEV, 2 * own)
    outs, levels = came[..., :own], came[..., own:]
    weights = jnp.exp(levels - jnp.max(levels, axis=1, keepdims=True))
    attention = jnp.sum(outs * weights, axis=1) / jnp.sum(weights, axis=1)
    attention = attention.reshape(requests, own).astype(jnp.bfloat16)
    back = jnp.sum(
        jnp.where(holders[None, :] == everyone[:, None], everyone[None, :], 0), axis=1
    )
    projected = jnp.dot(
        pick_rows(back, attention), output_weight, preferred_element_type=jnp.float32
    )
    projected = projected + jnp.where(group == 0, hidden_in.astype(jnp.float32), 0.0)

    share = groups // lanes
    blocks = jnp.moveaxis(projected.reshape(requests, share, 1, features), 0, 2)
    blocks = jnp.broadcast_to(blocks, (share, lanes, requests, features))
    mid = jnp.sum(exchange(blocks.reshape(groups, requests, features)), axis=0)
    mid = to_block_owner(mid.astype(jnp.bfloat16)).astype(jnp.float32)
    squares = jnp.sum(mid * mid, axis=1, keepdims=True)
    gain_here = lax.dynamic_slice_in_dim(feedforward_gain, group * features, features, 0)
    inputs_mid = (mid * gain_here).astype(jnp.bfloat16)
    local_units = gate_weight.shape[1]
    piece = local_units // groups
    gates = jnp.dot(inputs_mid, gate_weight, preferred_element_type=jnp.float32)
    ups = jnp.dot(inputs_mid, up_weight, preferred_element_type=jnp.float32)
    both = jnp.concatenate(
        [
            gates.reshape(requests, groups, piece),
            ups.reshape(requests, groups, piece),
            jnp.broadcast_to(squares[:, :, None], (requests, groups, 1)),
        ],
        axis=2,
    )
    sums = jnp.sum(exchange(jnp.swapaxes(both, 0, 1)), axis=0)
    factor = lax.rsqrt(sums[:, 2 * piece :] / D + epsilon)
    gate = sums[:, :piece] * factor
    active = (jax.nn.silu(gate) * (sums[:, piece : 2 * piece] * factor)).astype(jnp.bfloat16)
    active_here = lax.all_gather(to_block_owner(active), "head", axis=1, tiled=True)
    down = jnp.dot(active_here, down_weight, preferred_element_type=jnp.float32)
    residual = [jnp.where(group == lane * share + k, mid, 0.0) for k in range(share)]
    down = down + jnp.concatenate(residual, axis=1)
    result = whole_sum(down).astype(jnp.bfloat16)
    return (compact, summaries, result)


TILE = 128
bfloat = jnp.bfloat16
single = jnp.float32


TERMS = 4


def three_terms(value, place):
    high = value.astype(bfloat).astype(single)
    rest = value - high
    middle = rest.astype(bfloat).astype(single)
    low = jnp.where(place == 2, rest - middle, 0.0)
    return jnp.where(place == 0, high, jnp.where(place == 1, middle, low))


def iota(shape, axis):
    return lax.broadcasted_iota(jnp.int32, shape, axis)


def run(kernel, outs, far, near, scratch=(), flops=0):
    in_specs = [pl.BlockSpec(memory_space=pltpu.HBM) for _ in far]
    in_specs += [pl.BlockSpec(memory_space=pltpu.VMEM) for _ in near]
    moved = sum(a.size * a.dtype.itemsize for a in [*far, *near, *outs])
    return pl.pallas_call(
        kernel,
        out_shape=list(outs),
        in_specs=in_specs,
        out_specs=[pl.BlockSpec(memory_space=pltpu.VMEM) for _ in outs],
        scratch_shapes=list(scratch),
        compiler_params=pltpu.CompilerParams(vmem_limit_bytes=16 * 2**20),
        cost_estimate=pl.CostEstimate(flops=flops, bytes_accessed=moved, transcendentals=0),
    )(*[pltpu.with_memory_space_constraint(a, pltpu.HBM) for a in far], *near)


def fetch(sources, targets, done):
    copies = [
        pltpu.make_async_copy(source, target, done.at[k])
        for k, (source, target) in enumerate(zip(sources, targets))
    ]
    for copy in copies:
        copy.start()
    return copies


def local_like(*arrays):
    return [pltpu.VMEM(a.shape, a.dtype) for a in arrays]


def scalar_like(*arrays):
    return [pltpu.SMEM(a.shape, a.dtype) for a in arrays]


def row_order(source, count, to_holder):
    first, second = iota((count, count), 0), iota((count, count), 1)
    if not to_holder:
        first, second = second, first
    order = (first == second) & (first % R_DEV == 0)
    for c in range(source.shape[1]):
        order = order | ((first == source[0, c] * R_DEV + 1) & (second == c * R_DEV + 1))
    return order.astype(single).astype(bfloat)


def shaped(shape, dtype):
    return jax.ShapeDtypeStruct(shape, dtype)


def first_kernel(
    source_far, gain_far, weight_far, hidden_far, one, two, three, sent, block, source, gain,
    weight, hidden, lanes_of, wide, done
):
    copies = fetch(
        (source_far, gain_far, weight_far, hidden_far), (source, gain, weight, hidden), done
    )
    rows = hidden.shape[0]
    groups = rows // R_DEV
    lanes = sent.shape[0] // groups
    columns, features = weight.shape
    group = lax.axis_index("req")
    share = groups // lanes
    squares = 0.0
    for turn, values in enumerate((one, two, three)):
        values = values[...].astype(single)
        lanes_of[turn + 1] = values
        squares = squares + jnp.sum(values * values, axis=1, keepdims=True)
    copies[3].wait()
    values = hidden[...].astype(single)
    lanes_of[0] = values
    squares = squares + jnp.sum(values * values, axis=1, keepdims=True)
    factor = lax.rsqrt(squares / D + epsilon)
    here = pl.ds(pl.multiple_of(group * features, features), features)
    within = pl.ds(pl.multiple_of(group % share * features, features), features)
    mine = lanes_of[group // share ^ lax.axis_index("head"), :, within]
    block[...] = mine.astype(bfloat)
    wide[...] = jnp.zeros_like(wide)
    for copy in copies[:3]:
        copy.wait()
    normed = (mine * factor * gain[:, here]).astype(bfloat)
    order = row_order(source, rows, True)
    normed = jnp.dot(order, normed, preferred_element_type=single).astype(bfloat)
    wide[:, :columns] = dot_rows(normed, weight[...])
    for g in range(groups):
        tile = jnp.concatenate(
            [
                wide[R_DEV * g : R_DEV * (g + 1), TILE * j : TILE * (j + 1)]
                for j in range(wide.shape[1] // TILE)
            ],
            axis=0,
        )
        for k in range(lanes):
            sent[g * lanes + k] = tile


def dot_rows(left, right):
    return lax.dot_general(left, right, (((1,), (1,)), ((), ())), preferred_element_type=single)


def prepare_kernel(*refs):
    far, refs = refs[:12], refs[12:]
    (compact, summaries, kept, added, tables, mine, theirs), refs = refs[:7], refs[7:]
    near, (ordered, plain, dealt, done) = refs[:12], refs[12:]
    copies = fetch(far, near, done)
    (dest, lengths, source, table, keep, weights, query_gain, key_gain, turns) = near[:9]
    pages, gate, up = near[9:]
    group = lax.axis_index("req")
    lane = lax.axis_index("head")
    lanes = lax.axis_size("head")
    for copy in copies[:9]:
        copy.wait()

    carried = 0
    for c in range(source.shape[1]):
        carried = carried + jnp.where(source[0, c] == group, c, 0)
    held_len = (lengths[0, group * R_DEV], lengths[0, carried * R_DEV + 1])
    count, rows, _ = pages.shape
    owned = []
    for r in range(R_DEV):
        slots = []
        for i in range(table.shape[1] // lanes):
            j = i * lanes + lane
            slots.append(jnp.where(j < held_len[r], table[r, j], -1))
        owned.append(slots)

    def owner(r, p):
        found = owned[r][0] == p
        for slot in owned[r][1:]:
            found = found | (slot == p)
        return found

    row = iota((32, TILE), 0)
    odd = (row & 1) == 1
    half_rows = turns.shape[0] // 2
    for part in range(2):
        pair = [turns[pl.ds(part * half_rows + held_len[r], 1), :] for r in range(R_DEV)]
        tables[32 * part : 32 * (part + 1), :] = jnp.where(odd, pair[1], pair[0])
    query_rows = HEADS * HD // TILE * R_DEV
    for c in range(TILE // HD):
        columns = slice(HD * c, HD * (c + 1))
        tables[64 : 64 + query_rows, columns] = jnp.broadcast_to(
            query_gain[...], (query_rows, HD)
        )
        tables[64 + query_rows : 96, columns] = jnp.broadcast_to(
            key_gain[...], (32 - query_rows, HD)
        )

    column = iota((1, TILE), 1)
    entries = count * KEEP
    added[...] = jnp.full_like(added, negative)
    extra = [
        jnp.where((column == count + r) & (lane == 0), 0.0, negative) for r in range(R_DEV)
    ]
    weight_columns = weights[...].T
    rows_of = iota((rows, KEEP), 0)
    place = iota((rows, 16), 1)
    lefts, totals = [], []
    for p in range(count):
        picks = (keep[p : p + 1, :] == rows_of).astype(single)
        dropped = weight_columns[:, p : p + 1] * (1.0 - jnp.sum(picks, axis=1, keepdims=True))
        total = jnp.sum(dropped, axis=0, keepdims=True)
        left = jnp.concatenate([picks, three_terms(dropped, place)], axis=1).astype(bfloat)
        lefts.append(left)
        totals.append(total)
        live = jnp.where(keep[p : p + 1, :] >= 0, 0.0, negative)
        for r in range(R_DEV):
            here = owner(r, p)
            added[r : r + 1, KEEP * p : KEEP * (p + 1)] = jnp.where(here, live, negative)
            level = jnp.where(here, jnp.log(total), negative)
            extra[r] = jnp.where(column == p, level, extra[r])
    copies[9].wait()
    for p in range(count):
        both = lax.dot_general(
            lefts[p], pages[p], (((0,), (0,)), ((), ())), preferred_element_type=single
        )
        rows_kept = both[:KEEP].astype(bfloat)
        kept[KEEP * p : KEEP * (p + 1), :] = rows_kept
        slot = dest[0, p]
        start = pl.multiple_of((slot & 1) * KEEP, KEEP)
        compact[slot >> 1, pl.ds(start, KEEP), :] = rows_kept
        mean = both[KEEP : KEEP + 1] + both[KEEP + 1 : KEEP + 2] + both[KEEP + 2 : KEEP + 3]
        mean = mean / totals[p]
        plain[p : p + 1, :] = mean
        ordered[pl.ds(slot, 1), :] = mean
    for r in range(R_DEV):
        added[r : r + 1, entries : entries + TILE] = extra[r]
    plain[count:, :] = jnp.zeros_like(plain[count:, :])
    kept[entries:, :] = plain[...].astype(bfloat)
    summaries[...] = ordered[...].astype(bfloat)

    for copy in copies[10:]:
        copy.wait()
    block = gate.shape[1] // 2
    piece = block // 2
    for k in range(2):
        for b in range(2):
            columns = slice(b * block + k * piece, b * block + (k + 1) * piece)
            start = b * block
            dealt[k, :, start : start + piece] = gate[:, columns].astype(single)
            dealt[k, :, start + piece : start + block] = up[:, columns].astype(single)
    mine[...] = dealt[lane & 1].astype(bfloat)
    theirs[...] = dealt[1 - (lane & 1)].astype(bfloat)


def attend_kernel(came, kept, added, tables, sent, x, extra_k, extra_v, out, logs):
    lanes = lax.axis_size("head")
    groups = came.shape[0] // lanes
    width = (HEADS + 2 * KVH) * HD // lanes
    span = -(-KVH * HD // TILE) * TILE
    key_cols = slice(0, span)
    value_cols = slice(KVW - span, KVW)
    first_key = HEADS * HD // TILE * R_DEV
    scale = HD ** (-0.5)
    x[...] = jnp.zeros_like(x)
    column = iota((8, TILE), 1)
    for k in range(lanes):
        tile = came[k].astype(single)
        for g in range(1, groups):
            tile = tile + came[g * lanes + k].astype(single)
        tile = tile.astype(bfloat).astype(single)
        base, shift = divmod(width * k, TILE)
        base = base * R_DEV
        if shift:
            tile = pltpu.roll(tile, shift, 1)
            x[base + 2 : base + 10, :] += jnp.where(column < shift, tile, 0.0)
        x[base : base + 8, :] += jnp.where(column >= shift, tile, 0.0)
    values = x[...]
    same_head = (iota((TILE, TILE), 0) // HD == iota((TILE, TILE), 1) // HD).astype(single)
    squares = jnp.dot(
        values * values, same_head, precision=lax.Precision.HIGHEST, preferred_element_type=single
    )
    normed = values * lax.rsqrt(squares / HD + epsilon) * tables[64:96, :]
    early = iota(values.shape, 1) % HD < HD // 2
    swapped = jnp.where(
        early, pltpu.roll(normed, TILE - HD // 2, 1), pltpu.roll(normed, HD // 2, 1)
    )
    turned = normed * tables[0:32, :] + swapped * tables[32:64, :]
    turned = turned.astype(bfloat).astype(single)

    rows = 24
    row = iota((rows, TILE), 0)
    half = iota((rows, TILE), 1) // HD
    key_head = row >> 2
    query = jnp.where(row < first_key, turned[:rows], 0.0)
    other = pltpu.roll(query, HD, 1)
    queries = []
    for u in range(2):
        placed = jnp.where(
            half == (key_head & 1), jnp.where((key_head & 1) == u, query, other), 0.0
        )
        queries.append(
            jnp.concatenate(
                [jnp.where((key_head >> 1) == c, placed, 0.0) for c in range(span // TILE)], axis=1
            )
        )
    queries = jnp.concatenate(queries, axis=0).astype(bfloat)

    extras = extra_k.shape[0]
    entries = kept.shape[0] - extras
    count = entries // KEEP
    extra_k[...] = kept[entries:, key_cols].astype(single)
    extra_v[...] = kept[entries:, value_cols].astype(single)
    first_value = first_key + KVH * HD // TILE * R_DEV
    for c in range(span // TILE):
        at = slice(c * TILE, (c + 1) * TILE)
        r = first_key + R_DEV * c
        extra_k[count : count + R_DEV, at] = turned[r : r + R_DEV]
        r = first_value + R_DEV * c
        extra_v[count : count + R_DEV, at] = values[r : r + R_DEV]

    def by_request(columns, size):
        odd = (iota((2 * rows, size), 0) & 1) == 1
        return jnp.where(odd, added[1:2, columns], added[0:1, columns])

    scores = dot_rows(queries, kept[:entries, key_cols]) * scale
    scores = scores + by_request(slice(0, entries), entries)
    extra = dot_rows(queries, extra_k[...].astype(bfloat)) * scale
    extra = extra + by_request(slice(entries, entries + extras), extras)
    top = jnp.maximum(
        jnp.max(scores, axis=1, keepdims=True), jnp.max(extra, axis=1, keepdims=True)
    )
    weight = jnp.where(scores > 0.5 * negative, jnp.exp(scores - top), 0.0)
    extra_weight = jnp.where(extra > 0.5 * negative, jnp.exp(extra - top), 0.0)
    mass = jnp.sum(weight, axis=1, keepdims=True) + jnp.sum(extra_weight, axis=1, keepdims=True)

    def weighted(parts, right):
        high = parts.astype(bfloat)
        low = (parts - high.astype(single)).astype(bfloat)
        return jnp.dot(high, right, preferred_element_type=single) + jnp.dot(
            low, right, preferred_element_type=single
        )

    total = weighted(weight, kept[:entries, value_cols]) + weighted(
        extra_weight, extra_v[...].astype(bfloat)
    )
    some = mass > 0.0
    mass = jnp.where(some, mass, 1.0)
    total = total / mass
    level = jnp.where(some, top + jnp.log(mass), negative)

    slot = key_head + (KVW // 2 - (KVW - span)) // HD
    results = []
    for u in range(2):
        mine = total[rows * u : rows * (u + 1)]
        picked = mine[:, :TILE]
        for c in range(1, span // TILE):
            picked = jnp.where((slot >> 1) == c, mine[:, c * TILE : (c + 1) * TILE], picked)
        results.append(jnp.where((slot & 1) == u, picked, pltpu.roll(picked, HD, 1)))
    out[...] = jnp.where(half == 0, results[0], results[1])
    logs[...] = jnp.broadcast_to(level, logs.shape)
    own = HEADS * HD // lanes
    size = 6
    column = iota((size, TILE), 1)
    here = column // TERMS == iota((size, TILE), 0)
    for k in range(lanes):
        r = own * k // TILE * R_DEV
        tile = [out[r : r + size, :]]
        for u in range(2):
            coded = three_terms(logs[rows * u + r : rows * u + r + size, :], column % TERMS)
            tile.append(jnp.sum(jnp.where(here, coded, 0.0), axis=0, keepdims=True))
        tile = jnp.concatenate(tile, axis=0).astype(bfloat)
        for g in range(groups):
            sent[g * lanes + k] = tile


def blocks_kernel(weight_far, same, other, done):
    width = same.shape[1]
    group = lax.axis_index("req")
    starts = [pl.multiple_of(((group & 1) ^ turn) * width, width) for turn in range(2)]
    parts = [weight_far.at[:, pl.ds(start, width)] for start in starts]
    for copy in fetch(parts, (same, other), done):
        copy.wait()


def project_kernel(source_far, came, first, second, sent, source, logs, rows, pieces, done):
    (copy,) = fetch((source_far,), (source,), done)
    lanes = lax.axis_size("head")
    groups = came.shape[0] // lanes
    group = lax.axis_index("req")
    features = first.shape[0]
    requests = rows.shape[0]
    size = 6
    tiles = [came[d].astype(single) for d in range(groups * lanes)]
    for g in range(groups):
        for k in range(lanes):
            logs[k, 2 * g : 2 * g + 2, :] = tiles[g * lanes + k][size:]
    spread = (iota((8, TILE), 1) // TERMS == iota((8, TILE), 0)).astype(single).astype(bfloat)
    levels = [dot_rows(spread, logs[k].astype(bfloat)) for k in range(lanes)]
    top = jnp.maximum(jnp.maximum(levels[0], levels[1]), jnp.maximum(levels[2], levels[3]))
    shares = [jnp.exp(level - top) for level in levels]
    mass = sum(shares)
    shares = [share / mass for share in shares]
    lower = iota((8, TILE), 1) < HD
    for g in range(groups):
        mixed = 0.0
        for k in range(lanes):
            share = shares[k]
            share = jnp.where(lower, share[:, 2 * g : 2 * g + 1], share[:, 2 * g + 1 : 2 * g + 2])
            mixed = mixed + share * tiles[g * lanes + k]
        for j in range(size // R_DEV):
            rows[R_DEV * g : R_DEV * (g + 1), TILE * j : TILE * (j + 1)] = mixed[
                R_DEV * j : R_DEV * (j + 1)
            ]
    width = rows.shape[1]
    shift = lax.rem(lax.axis_index("head") * (2 * features), TILE)
    attention = rows[...].astype(bfloat).astype(single)
    attention = pltpu.roll(attention, lax.rem(width - shift, width), 1)
    copy.wait()
    order = row_order(source, requests, False)
    attention = jnp.dot(order, attention.astype(bfloat), preferred_element_type=single)
    for b in range(2):
        pieces[b] = attention[:, features * b : features * (b + 1)]
    total = 0.0
    for turn, weight in enumerate((first, second)):
        piece = pieces[(group & 1) ^ turn].astype(bfloat)
        total = total + jnp.dot(piece, weight[...], preferred_element_type=single)
    sent[...] = total


def units_kernel(
    gain_far, own, one, two, three, hidden, mine, theirs, sent, mid_out, gain, done
):
    (copy,) = fetch((gain_far,), (gain,), done)
    rows, features = own.shape
    share = sent.shape[0] // lax.axis_size("head")
    group = lax.axis_index("req")
    lane = lax.axis_index("head")
    here = pl.ds(pl.multiple_of(group * features, features), features)
    mid = (own[...] + one[...]) + (two[...] + three[...])
    mid = (hidden[...].astype(single) + mid).astype(bfloat)
    mid_out[...] = mid
    mid = mid.astype(single)
    squares = jnp.sum(mid * mid, axis=1, keepdims=True)
    block = mine.shape[1] // share
    terms = three_terms(squares, iota((rows, sent.shape[2] - block), 1)).astype(bfloat)
    copy.wait()
    inputs = (mid * gain[:, here]).astype(bfloat)
    for turn, weight in enumerate((mine, theirs)):
        units = jnp.dot(inputs, weight[...], preferred_element_type=single).astype(bfloat)
        target = (lane ^ turn) * share
        for b in range(share):
            sent[target + b, :, :block] = units[:, block * b : block * (b + 1)]
            sent[target + b, :, block:] = terms


def active_kernel(came, active):
    total = came[0].astype(single)
    for g in range(1, came.shape[0]):
        total = total + came[g].astype(single)
    piece = active.shape[1]
    squares = jnp.sum(total[:, 2 * piece : 2 * piece + 3], axis=1, keepdims=True)
    factor = lax.rsqrt(squares / D + epsilon)
    gate = total[:, :piece] * factor
    up = total[:, piece : 2 * piece] * factor
    active[...] = (gate / (1.0 + jnp.exp(-gate)) * up).astype(bfloat)


def down_kernel(own, one, two, three, weight, mid, sent, active):
    groups, rows, width = sent.shape
    piece = own.shape[1]
    half = mid.shape[1]
    for turn, values in enumerate((own, one, two, three)):
        active[turn] = values[...]
    share = width // half
    group = lax.axis_index("req")
    lane = lax.axis_index("head")
    first = group // (2 * share) * 2 ^ lane
    down = jnp.dot(active[first], weight[:piece, :], preferred_element_type=single)
    down = down + jnp.dot(active[first ^ 1], weight[piece:, :], preferred_element_type=single)
    residual = mid[...].astype(single)
    for b in range(share):
        columns = slice(half * b, half * (b + 1))
        mine = group == lane * share + b
        total = (down[:, columns] + jnp.where(mine, residual, 0.0)).astype(bfloat)
        for g in range(groups):
            sent[g, :, columns] = total


def result_kernel(came, result):
    total = came[0].astype(single)
    for g in range(1, came.shape[0]):
        total = total + came[g].astype(single)
    result[...] = total.astype(bfloat)


def rotation_table():
    half = HD // 2
    size = -(-(NP + 1) // 8) * 8
    frequency = 10000.0 ** (-np.arange(half) / half)
    angles = PAGE * np.arange(size)[:, None] * frequency[None, :]
    cosine, sine = np.cos(angles), np.sin(angles)
    wide = [np.tile(np.concatenate(pair, axis=1), (1, TILE // HD)) for pair in
            ((cosine, cosine), (-sine, sine))]
    return jnp.asarray(np.concatenate(wide), dtype=single)


def swapped_lanes(value, turn):
    lanes = lax.axis_size("head")
    return lax.ppermute(value, "head", [(k, k ^ turn) for k in range(lanes)])


def from_lanes(value):
    return [value] + [swapped_lanes(value, turn) for turn in range(1, lax.axis_size("head"))]


def handed_over(value, turn):
    groups = lax.axis_size("req")
    lanes = lax.axis_size("head")
    share = groups // lanes
    pairs = [
        (g * lanes + h, (share * h + ((g & 1) ^ turn)) * lanes + g // share)
        for g in range(groups)
        for h in range(lanes)
    ]
    return lax.ppermute(value, both_axes, pairs)


def on_device(
    hidden_in,
    attention_gain,
    query_gain,
    key_gain,
    feedforward_gain,
    input_weight,
    output_weight,
    gate_weight,
    up_weight,
    down_weight,
    old_cache,
    keep_rows,
    drop_weights,
    dest_slots,
    lengths,
    page_table,
    source,
):
    groups = lax.axis_size("req")
    lanes = lax.axis_size("head")
    requests = hidden_in.shape[0]
    pages_here = old_cache.shape[0]
    devices = groups * lanes
    features = D // groups
    copies = pltpu.SemaphoreType.DMA

    others = from_lanes(hidden_in)[1:]
    blocks = run(
        blocks_kernel,
        [shaped((output_weight.shape[0], features), bfloat)] * 2,
        [output_weight],
        [],
        [copies((2,))],
    )
    handed = [handed_over(block, turn) for turn, block in enumerate(blocks)]
    scalars = [dest_slots, lengths[None, :], source[None, :], page_table]
    arrays = [
        keep_rows,
        drop_weights,
        query_gain[None, :],
        key_gain[None, :],
        rotation_table(),
        old_cache,
        gate_weight,
        up_weight,
    ]
    entries = pages_here * KEEP
    extras = 16
    compact, summaries, kept, added, tables, mine, theirs = run(
        prepare_kernel,
        [
            shaped((pages_here // 2, PAGE, KVW), bfloat),
            shaped((pages_here, KVW), bfloat),
            shaped((entries + extras, KVW), bfloat),
            shaped((8, entries + TILE), single),
            shaped((96, TILE), single),
            shaped(gate_weight.shape, bfloat),
            shaped(gate_weight.shape, bfloat),
        ],
        scalars + arrays,
        [],
        [
            *scalar_like(*scalars),
            *local_like(*arrays),
            pltpu.VMEM((pages_here, KVW), single),
            pltpu.VMEM((extras, KVW), single),
            pltpu.VMEM((2,) + gate_weight.shape, single),
            copies((len(scalars + arrays),)),
        ],
        2 * pages_here * TILE * PAGE * KVW,
    )
    tables, *moved = lax.optimization_barrier((tables, *others, *handed))
    others, handed = moved[: lanes - 1], moved[lanes - 1 :]

    holds = source[None, :]
    columns = input_weight.shape[1]
    padded = -(-columns // TILE) * TILE
    gain = attention_gain[None, :]
    weight = input_weight.T
    far = [holds, gain, weight, hidden_in]
    sent, hidden_block = run(
        first_kernel,
        [
            shaped((devices, R_DEV * padded // TILE, TILE), single),
            shaped((requests, features), bfloat),
        ],
        far,
        others,
        [
            *scalar_like(holds),
            *local_like(*far[1:]),
            pltpu.VMEM((lanes,) + hidden_in.shape, single),
            pltpu.VMEM((requests, padded), single),
            copies((len(far),)),
        ],
        2 * requests * features * columns,
    )
    came = lax.all_to_all(sent, both_axes, 0, 0, tiled=True)
    span = -(-KVH * HD // TILE) * TILE
    (parts,) = run(
        attend_kernel,
        [shaped((devices, 8, TILE), bfloat)],
        [],
        [came, kept, added, tables],
        [
            pltpu.VMEM((32, TILE), single),
            pltpu.VMEM((extras, span), single),
            pltpu.VMEM((extras, span), single),
            pltpu.VMEM((24, TILE), single),
            pltpu.VMEM((48, TILE), single),
        ],
        6 * 48 * entries * span,
    )
    theirs, _ = lax.optimization_barrier((theirs, parts))
    theirs = swapped_lanes(theirs, 1)
    came = lax.all_to_all(parts, both_axes, 0, 0, tiled=True)
    came, theirs = lax.optimization_barrier((came, theirs))
    (sent,) = run(
        project_kernel,
        [shaped((requests, features), single)],
        [holds],
        [came, *handed],
        [
            *scalar_like(holds),
            pltpu.VMEM((lanes, 2 * groups, TILE), single),
            pltpu.VMEM((requests, 3 * TILE), single),
            pltpu.VMEM((2, requests, output_weight.shape[0]), single),
            copies((1,)),
        ],
        2 * requests * output_weight.size,
    )
    gain = feedforward_gain[None, :]
    block = gate_weight.shape[1] // 2
    sent, mid = run(
        units_kernel,
        [
            shaped((groups, requests, block + TILE), bfloat),
            shaped((requests, features), bfloat),
        ],
        [gain],
        [*from_lanes(sent), hidden_block, mine, theirs],
        [*local_like(gain), copies((1,))],
        4 * requests * gate_weight.size,
    )
    (active,) = run(
        active_kernel, [shaped((requests, block // 2), bfloat)], [], [exchange(sent)]
    )
    (sent,) = run(
        down_kernel,
        [shaped((groups, requests, down_weight.shape[1]), bfloat)],
        [],
        [*from_lanes(active), down_weight, mid],
        [pltpu.VMEM((lanes,) + active.shape, bfloat)],
        2 * requests * down_weight.size,
    )
    (result,) = run(
        result_kernel, [shaped((requests, down_weight.shape[1]), bfloat)], [], [exchange(sent)]
    )
    return (compact, summaries, result)


def solution(mesh):
    placed = (
        P(None, "head"),
        P(),
        P(),
        P(),
        P(),
        P("req", "head"),
        P("req", "head"),
        P("req", "head"),
        P("req", "head"),
        P("req", "head"),
        P(("req", "head"), None, None),
        P(("req", "head"), None),
        P(("req", "head"), None),
        P(("req", "head"), None),
        P(),
        P("req", None),
        P(),
    )
    return jax.shard_map(
        on_device if mesh.shape["req"] <= DIRECT else on_device_wide,
        mesh=mesh,
        in_specs=placed,
        out_specs=(P(("req", "head"), None, None), P(("req", "head"), None), P(None, "head")),
        check_vma=False,
    )
```
